32 devices in a mesh: gx: 4 (over x, core), gy: 8 (over z, y).
Axes of the slice: x: 2, y: 2, z: 4, core: 2. Of those that a mesh axis runs over, the one named last changes fastest.
Arguments:
- images: bfloat16 [32, 16, 16, 320], P(('gx', 'gy')), may hold values from -6 to 6
- valid_count: int32 [32], P(('gx', 'gy')), may hold values from 1 to 1, as said below
- pixel_mask: int32 [32, 16, 16], P(('gx', 'gy')), may hold values from 0 to 1, as said below
- gain_entry: float32 [320], replicated, may hold values from 0.5 to 2
- shift_entry: float32 [320], replicated, may hold values from -0.5 to 0.5
- conv_first: bfloat16 [2880, 640], P('gy'), may hold values from -0.109375 to 0.109375
- gain_middle: float32 [640], replicated, may hold values from 0.5 to 2
- shift_middle: float32 [640], replicated, may hold values from -0.5 to 0.5
- conv_second: bfloat16 [5760, 640], P('gy'), may hold values from -0.078125 to 0.078125
- projection: bfloat16 [320, 640], P('gy'), may hold values from -0.3125 to 0.3125
- gain_inner: float32 [640], replicated, may hold values from 0.5 to 2
- shift_inner: float32 [640], replicated, may hold values from -0.5 to 0.5
- conv_third: bfloat16 [5760, 640], P('gy'), may hold values from -0.078125 to 0.078125
- gain_last: float32 [640], replicated, may hold values from 0.5 to 2
- shift_last: float32 [640], replicated, may hold values from -0.5 to 0.5
- conv_fourth: bfloat16 [5760, 640], P('gy'), may hold values from -0.078125 to 0.078125
- cotangent: bfloat16 [32, 8, 8, 640], P(('gx', 'gy')), may hold values from -6 to 6
Outputs:
- result: bfloat16 [32, 8, 8, 640], P(('gx', 'gy'))
- image_grad: float32 [32, 16, 16, 320], P(('gx', 'gy'))
- gain_entry_grad: float32 [320], replicated
- shift_entry_grad: float32 [320], replicated
- conv_first_grad: float32 [2880, 640], P('gy')
- gain_middle_grad: float32 [640], replicated
- shift_middle_grad: float32 [640], replicated
- conv_second_grad: float32 [5760, 640], P('gy')
- projection_grad: float32 [320, 640], P('gy')
- gain_inner_grad: float32 [640], replicated
- shift_inner_grad: float32 [640], replicated
- conv_third_grad: float32 [5760, 640], P('gy')
- gain_last_grad: float32 [640], replicated
- shift_last_grad: float32 [640], replicated
- conv_fourth_grad: float32 [5760, 640], P('gy')
The draws below stay inside these ranges and needn't reach their ends.
Inputs may be any that keep to these rules, and one draw needn't show every extreme that they name: `valid_count`: each device's live slots are its first ones. `pixel_mask`: pixel (0, 0) of every slot is valid.
All inputs are finite; a program needn't handle non-finite values.
Results may differ from the reference program's by a relative error of at most 0.0098.
Values may be sent and summed in bfloat16 or wider, within the bound.
No kernel may reach another device: no remote copies, remote signals or barrier semaphores. Data moves between devices by JAX's collectives and lax.ppermute only.
A program may use at most 192 MiB of HBM per device.

```python
import math
import jax
import jax.numpy as jnp
from jax import lax

C_IN = 320
C_OUT = 640
MAP = 16
IMG_DEV = 1
IMAGES = 32


def draw_valid_count(key, part):
    key = jax.random.fold_in(key, 1)
    groups = IMAGES // IMG_DEV
    keys = jax.random.split(key, 3)
    drawn = jax.random.randint(keys[0], (groups,), 1, IMG_DEV + 1)
    top_spot = jax.random.randint(keys[1], (), 0, groups)
    least_spot = (top_spot + 1 + jax.random.randint(keys[2], (), 0, groups - 1)) % groups
    index = jnp.arange(groups)
    drawn = jnp.where(index == least_spot, 1, drawn)
    return jnp.where(index == top_spot, IMG_DEV, drawn).astype(jnp.int32)


def draw_pixel_mask(key, part):
    key = jax.random.fold_in(key, 2)
    drawn = jax.random.randint(key, (IMAGES, MAP, MAP), 0, 8)
    valid = (drawn < 7).astype(jnp.int32)
    corner = (jnp.arange(MAP)[:, None] + jnp.arange(MAP)[None, :] == 0).astype(jnp.int32)
    return jnp.maximum(valid, corner[None, :, :])


def shard_levels(key, shape, pieces, low, high):
    def one(position, parts):
        draws = jax.random.uniform(jax.random.fold_in(jax.random.fold_in(key, 6), position), (parts,), jnp.float32, low / len(pieces), high / len(pieces))
        return jnp.repeat(jnp.exp(draws), shape[position] // parts).reshape((-1,) + (1,) * (len(shape) - position - 1))

    level = one(*pieces[0])
    for cut in pieces[1:]:
        level = level * one(*cut)
    return level


def scatter_about(rng, shape, scale, reach, pieces=(), kind=jnp.bfloat16):
    level = shard_levels(rng, shape, pieces, -0.22, 0.18) if pieces else 1.0
    array = jax.random.normal(rng, shape, jnp.float32) * scale * level
    return jnp.minimum(jnp.maximum(array, -reach), reach).astype(kind)


def setup_inputs(seed: int = 0) -> dict:
    key_of = jax.random.split(jax.random.key(seed), 18)
    return {
        "images": scatter_about(key_of[0], (IMAGES, MAP, MAP, C_IN), 1.0, 6.0, ((0, 32),)),
        "valid_count": draw_valid_count(jax.random.fold_in(key_of[17], 71), 0),
        "pixel_mask": draw_pixel_mask(jax.random.fold_in(key_of[17], 71), 0),
        "gain_entry": jnp.clip(jnp.exp(jax.random.uniform(key_of[3], (C_IN,), jnp.float32, math.log(0.5), math.log(2.0))), 0.5, 2.0),
        "shift_entry": jnp.clip(jax.random.uniform(key_of[4], (C_IN,), jnp.float32, -0.5, 0.5), -0.5, 0.5),
        "conv_first": scatter_about(key_of[5], (9 * C_IN, C_OUT), (9 * C_IN) ** -0.5, 0.109375, ((0, 8),)),
        "gain_middle": jnp.clip(jnp.exp(jax.random.uniform(key_of[6], (C_OUT,), jnp.float32, math.log(0.5), math.log(2.0))), 0.5, 2.0),
        "shift_middle": jnp.clip(jax.random.uniform(key_of[7], (C_OUT,), jnp.float32, -0.5, 0.5), -0.5, 0.5),
        "conv_second": scatter_about(key_of[8], (9 * C_OUT, C_OUT), (9 * C_OUT) ** -0.5, 0.078125, ((0, 8),)),
        "projection": scatter_about(key_of[9], (C_IN, C_OUT), C_IN ** -0.5, 0.3125, ((0, 8),)),
        "gain_inner": jnp.clip(jnp.exp(jax.random.uniform(key_of[10], (C_OUT,), jnp.float32, math.log(0.5), math.log(2.0))), 0.5, 2.0),
        "shift_inner": jnp.clip(jax.random.uniform(key_of[11], (C_OUT,), jnp.float32, -0.5, 0.5), -0.5, 0.5),
        "conv_third": scatter_about(key_of[12], (9 * C_OUT, C_OUT), (9 * C_OUT) ** -0.5, 0.078125, ((0, 8),)),
        "gain_last": jnp.clip(jnp.exp(jax.random.uniform(key_of[13], (C_OUT,), jnp.float32, math.log(0.5), math.log(2.0))), 0.5, 2.0),
        "shift_last": jnp.clip(jax.random.uniform(key_of[14], (C_OUT,), jnp.float32, -0.5, 0.5), -0.5, 0.5),
        "conv_fourth": scatter_about(key_of[15], (9 * C_OUT, C_OUT), (9 * C_OUT) ** -0.5, 0.078125, ((0, 8),)),
        "cotangent": scatter_about(key_of[16], (IMAGES, MAP // 2, MAP // 2, C_OUT), 1.0, 6.0, ((0, 32),)),
    }


@jax.custom_vjp
def low(v):
    return lax.optimization_barrier(v.astype(jnp.bfloat16)).astype(jnp.float32)

@jax.custom_vjp
def low_back(v):
    return v

def low_keep(v):
    return (low(v), None)

def low_pass(kept, grad):
    return (grad,)

def back_keep(v):
    return (v, None)

def back_low(kept, grad):
    return (low(grad),)
low.defvjp(low_keep, low_pass)
low_back.defvjp(back_keep, back_low)
EPS = 1e-05

def convolve(act, weight, stride, chans):
    kernel = weight.reshape(3, 3, chans, weight.shape[1])
    return lax.conv_general_dilated(act, kernel, (stride, stride), ((1, 1), (1, 1)), dimension_numbers=('NHWC', 'HWIO', 'NHWC'), precision=lax.Precision.HIGHEST)

def batch_norm(values, weight, gain, shift):
    total = jnp.sum(weight)
    mean = lax.optimization_barrier(jnp.sum(weight * values, axis=(0, 1, 2))) / total
    centered = values - mean
    spread = lax.optimization_barrier(jnp.sum(weight * centered * centered, axis=(0, 1, 2))) / total
    return gain * (centered * lax.rsqrt(spread + EPS)) + shift

def forward(images, gain_entry, shift_entry, conv_first, gain_middle, shift_middle, conv_second, projection, gain_inner, shift_inner, conv_third, gain_last, shift_last, conv_fourth, wide_weight, narrow_weight):
    act_one = low(jax.nn.gelu(batch_norm(images, wide_weight, gain_entry, shift_entry)))
    first = low_back(convolve(act_one, conv_first, 2, C_IN))
    skipped = low_back(jnp.einsum('nhwc,cd->nhwd', act_one[:, ::2, ::2, :], projection, precision=lax.Precision.HIGHEST))
    act_two = low(jax.nn.gelu(batch_norm(first, narrow_weight, gain_middle, shift_middle)))
    second = low_back(convolve(act_two, conv_second, 1, C_OUT))
    hidden = second + skipped
    act_three = low(jax.nn.gelu(batch_norm(hidden, narrow_weight, gain_inner, shift_inner)))
    third = low_back(convolve(act_three, conv_third, 1, C_OUT))
    act_four = low(jax.nn.gelu(batch_norm(third, narrow_weight, gain_last, shift_last)))
    fourth = low_back(convolve(act_four, conv_fourth, 1, C_OUT))
    return hidden + fourth

def reference(images, valid_count, pixel_mask, gain_entry, shift_entry, conv_first, gain_middle, shift_middle, conv_second, projection, gain_inner, shift_inner, conv_third, gain_last, shift_last, conv_fourth, cotangent):
    slots = jnp.arange(IMAGES, dtype=jnp.int32) % IMG_DEV
    live = (slots < jnp.repeat(valid_count, IMG_DEV)).astype(jnp.float32)
    wide_weight = (pixel_mask.astype(jnp.float32) * live[:, None, None])[..., None]
    narrow_weight = wide_weight[:, ::2, ::2, :]

    def run(*params):
        return forward(*params, wide_weight, narrow_weight)
    params = (images.astype(jnp.float32), gain_entry, shift_entry, conv_first.astype(jnp.float32), gain_middle, shift_middle, conv_second.astype(jnp.float32), projection.astype(jnp.float32), gain_inner, shift_inner, conv_third.astype(jnp.float32), gain_last, shift_last, conv_fourth.astype(jnp.float32))
    output, pullback = jax.vjp(run, *params)
    grads = pullback(cotangent.astype(jnp.float32))
    return (output.astype(jnp.bfloat16), grads[0], grads[1], grads[2], grads[3], grads[4], grads[5], grads[6], grads[7], grads[8], grads[9], grads[10], grads[11], grads[12], grads[13])
```

```python
import functools

import jax
import jax.numpy as jnp
from jax import lax
from jax.experimental import pallas as pl
from jax.experimental.pallas import tpu as pltpu
from jax.sharding import PartitionSpec as P

EPS = 1e-05
F32 = jnp.float32
BF16 = jnp.bfloat16
PEERS = 8
C0 = 0.7978845608028654
C1 = 0.044715
VMEM = pl.BlockSpec(memory_space=pltpu.VMEM)
SMEM = pl.BlockSpec(memory_space=pltpu.SMEM)


def gelu(v):
    return 0.5 * v * (1.0 + jnp.tanh(C0 * (v + C1 * (v * v * v))))


def gelu_slope(v):
    t = jnp.tanh(C0 * (v + C1 * (v * v * v)))
    return 0.5 * (1.0 + t) + 0.5 * v * (1.0 - t * t) * (C0 * (1.0 + 3.0 * C1 * (v * v)))


def call(kernel, outs, args, scratch=(), flops=1 << 20):
    size = sum(a.size * a.dtype.itemsize for a in args)
    return pl.pallas_call(
        kernel,
        out_shape=outs,
        in_specs=[SMEM] + [VMEM] * (len(args) - 1),
        out_specs=jax.tree.map(lambda _: VMEM, outs),
        scratch_shapes=list(scratch),
        compiler_params=pltpu.CompilerParams(vmem_limit_bytes=48 * 1024 * 1024),
        cost_estimate=pl.CostEstimate(flops=flops, bytes_accessed=size, transcendentals=0),
    )(*args)


def shape(dims, dtype=F32):
    return jax.ShapeDtypeStruct(dims, dtype)


def rows_at(index, count):
    return pl.ds(pl.multiple_of(index * count, count), count)


def columns(parts, height):
    lane = lax.broadcasted_iota(jnp.int32, (height, 128), 1)
    out = jnp.zeros((height, 128), F32)
    for k, part in enumerate(parts):
        out = jnp.where(lane == k, part, out)
    return out


def in_order(refs, me, scratch):
    for k, ref in enumerate(refs):
        scratch[me ^ k] = ref[...]
    return [scratch[k] for k in range(len(refs))]


def merge_moments(stats):
    total = sum(n for _, _, n in stats)
    mean = sum(n * m for m, _, n in stats) / total
    squares = sum(q + n * (m - mean) * (m - mean) for m, q, n in stats)
    return mean, lax.rsqrt(squares / total + EPS), total


def pixel(width, area, small):
    lane = lax.broadcasted_iota(jnp.int32, (1, width), 1) % area
    return lane // small, lane % small


def inside(row, col, drow, dcol, small):
    return (row + drow >= 0) & (row + drow < small) & (col + dcol >= 0) & (col + dcol < small)


def moved(value, step):
    shift = (-step) % value.shape[1]
    return pltpu.roll(value, shift, 1) if shift else value


def offsets(stride):
    out = []
    for krow in range(3):
        for kcol in range(3):
            if stride == 1:
                out.append((0, krow - 1, kcol - 1))
            else:
                phase = (krow != 1) * 2 + (kcol != 1)
                out.append((phase, -(krow == 0), -(kcol == 0)))
    return out


def masked_stats(value, weight, n):
    mean = jnp.sum(value * weight, axis=1, keepdims=True) / n
    centred = value - mean
    return mean, jnp.sum(weight * centred * centred, axis=1, keepdims=True)


def entry_stats(area, idx, *refs):
    images, out = refs[:PEERS], refs[PEERS]
    lanes = out.shape[1]
    first = jnp.zeros((1, lanes), F32)
    wide = jnp.zeros((1, 1), F32)
    narrow = jnp.zeros((1, 1), F32)
    c_in = lanes - 64
    for ref in images:
        x = ref[...].astype(F32)
        w = x[:, c_in : c_in + 1]
        first += jnp.sum(x * w, axis=0, keepdims=True)
        wide += jnp.sum(w, axis=0, keepdims=True)
        narrow += jnp.sum(w[:area], axis=0, keepdims=True)
    mean = first / wide
    squares = jnp.zeros((1, lanes), F32)
    for ref in images:
        x = ref[...].astype(F32)
        w = x[:, c_in : c_in + 1]
        d = x - mean
        squares += jnp.sum(d * d * w, axis=0, keepdims=True)
    out[...] = jnp.zeros_like(out)
    out[0:1, :] = mean
    out[1:2, :] = squares
    out[2:3, :] = jnp.broadcast_to(wide, (1, lanes))
    out[3:4, :] = jnp.broadcast_to(narrow, (1, lanes))


def entry_block(nt, area, small, idx, *refs):
    images = refs[:PEERS]
    stats = refs[PEERS : PEERS + nt]
    gain, shift, w_first = refs[PEERS + nt : PEERS + nt + 3]
    first, skipped, out_stats, norm, narrow, act = refs[PEERS + nt + 3 : PEERS + nt + 9]
    order, masks = refs[PEERS + nt + 9 :]
    me, mine = idx[0], idx[1]
    c_in = gain.shape[1]
    lanes = norm.shape[1]
    cs = first.shape[0]
    width = first.shape[1]
    got = in_order(stats, mine, order)
    mean, scale, total = merge_moments([(g[0:1], g[1:2], g[2:3]) for g in got])
    norm[...] = jnp.zeros_like(norm)
    norm[0:1, :] = mean
    norm[1:2, :] = scale
    norm[2:3, :] = total
    norm[3:4, :] = sum(g[3:4] for g in got)
    for k, ref in enumerate(images):
        x = ref[...]
        v = x[:, :c_in].astype(F32)
        pre = gain[...] * ((v - mean[:, :c_in]) * scale[:, :c_in]) + shift[...]
        a = gelu(pre).astype(BF16)
        for phase in range(4):
            act[phase, rows_at(me ^ k, area), :] = a[phase * area : (phase + 1) * area]
        masks[rows_at(me ^ k, area), :] = x[:area]
    pick = (lax.broadcasted_iota(jnp.int32, (8, lanes), 1) == c_in).astype(BF16)
    weight8 = lax.dot_general(
        pick, masks[...], (((1,), (1,)), ((), ())), preferred_element_type=F32
    )
    narrow[...] = weight8
    weight = weight8[0:1]
    row, col = pixel(width, area, small)
    total_first = jnp.zeros((cs, width), F32)
    for k, (phase, drow, dcol) in enumerate(offsets(2)):
        y = lax.dot_general(
            w_first[k * cs : (k + 1) * cs, :],
            act[phase],
            (((1,), (1,)), ((), ())),
            preferred_element_type=F32,
        )
        y = moved(y, drow * small + dcol)
        total_first += jnp.where(inside(row, col, drow, dcol, small), y, 0.0)
    first[...] = total_first
    skipped[...] = lax.dot_general(
        w_first[9 * cs :, :], act[0], (((1,), (1,)), ((), ())), preferred_element_type=F32
    )
    n = jnp.sum(weight, axis=1, keepdims=True)
    mean2, squares = masked_stats(total_first, weight, n)
    out_stats[...] = columns((mean2, squares, n), cs)


def act_block(nt, idx, *refs):
    value, params = refs[:2]
    stats = refs[2 : 2 + nt]
    act, normed, scales, order = refs[2 + nt :]
    got = in_order(stats, idx[1], order)
    mean, scale, total = merge_moments([(g[:, 0:1], g[:, 1:2], g[:, 2:3]) for g in got])
    norm = (value[...] - mean) * scale
    normed[...] = norm
    act[...] = gelu(params[:, 0:1] * norm + params[:, 1:2]).astype(BF16)
    scales[...] = columns((scale, total), norm.shape[0])


def conv_block(added, stats, area, small, idx, *refs):
    pieces = refs[:PEERS]
    weights, narrow = refs[PEERS : PEERS + 2]
    rest = refs[PEERS + 2 :]
    base, rest = (rest[0], rest[1:]) if added else (None, rest)
    me = idx[0]
    cs, width = pieces[0].shape
    if stats:
        value, out_stats, act, spread = rest
    else:
        value, act, spread = rest
    for k, ref in enumerate(pieces):
        act[rows_at(me ^ k, cs), :] = ref[...]
    spread[...] = jnp.dot(weights[...], act[...], preferred_element_type=F32)
    row, col = pixel(width, area, small)
    total = base[...] if added else jnp.zeros((cs, width), F32)
    for k, (_, drow, dcol) in enumerate(offsets(1)):
        y = moved(spread[k * cs : (k + 1) * cs, :], drow * small + dcol)
        total += jnp.where(inside(row, col, drow, dcol, small), y, 0.0)
    if stats:
        value[...] = total
        weight = narrow[0:1, :]
        n = jnp.sum(weight, axis=1, keepdims=True)
        mean, squares = masked_stats(total, weight, n)
        out_stats[...] = columns((mean, squares, n), cs)
    else:
        value[...] = total.astype(value.dtype)


def split_images(area, idx, *refs):
    value, outs = refs[0], refs[1:]
    me = idx[0]
    width = value.shape[1]
    lane = lax.broadcasted_iota(jnp.int32, (width, 128), 0)
    slot = lax.broadcasted_iota(jnp.int32, (width, 128), 1)
    for k, out in enumerate(outs):
        pick = (lane == (me ^ k) * area + slot).astype(BF16)
        out[...] = jnp.dot(value[...], pick, preferred_element_type=F32).astype(BF16)


def join_result(idx, *refs):
    pieces, (out, stack) = refs[:PEERS], refs[PEERS:]
    cs = pieces[0].shape[0]
    for k, ref in enumerate(pieces):
        stack[rows_at(idx[0] ^ k, cs), :] = ref[...].astype(F32)
    out[...] = stack[...].T[: out.shape[0]].astype(BF16)


def split_cotangent(idx, *refs):
    cot, outs, stack = refs[0], refs[1 : 1 + PEERS], refs[1 + PEERS]
    c = cot[...].astype(F32)
    stack[...] = jnp.concatenate([c, c], axis=0).T
    cs = outs[0].shape[0]
    for k, out in enumerate(outs):
        out[...] = stack[rows_at(idx[0] ^ k, cs), :].astype(BF16)


def spread_grad(grad, shifted, area, small, offs):
    cs, width = grad.shape
    row, col = pixel(width, area, small)
    for k, (_, drow, dcol) in enumerate(offs):
        g = moved(grad, -(drow * small + dcol))
        g = jnp.where(inside(row, col, -drow, -dcol, small), g, 0.0)
        shifted[k * cs : (k + 1) * cs, :] = g.astype(BF16)


def push_back(me, weights, shifted, partial, outs):
    cs = outs[0].shape[0]
    partial[...] = lax.dot_general(
        weights[...], shifted[...], (((0,), (0,)), ((), ())), preferred_element_type=F32
    )
    for k, out in enumerate(outs):
        out[...] = partial[rows_at(me ^ k, cs), :].astype(BF16)


def last_back(area, small, idx, *refs):
    pieces, weights = refs[:PEERS], refs[PEERS]
    cot, shifted = refs[PEERS + 1 : PEERS + 3]
    outs = refs[PEERS + 3 : 2 * PEERS + 3]
    partial = refs[2 * PEERS + 3]
    me = idx[0]
    cs, width = cot.shape
    image = lax.broadcasted_iota(jnp.int32, (1, width), 1) // area
    grad = jnp.zeros((cs, width), F32)
    for k, ref in enumerate(pieces):
        tiled = jnp.concatenate([ref[...].astype(F32)] * (width // 128), axis=1)
        grad = jnp.where(image == (me ^ k), tiled, grad)
    cot[...] = grad
    spread_grad(grad, shifted, area, small, offsets(1))
    push_back(me, weights, shifted, partial, outs)


def gelu_back(idx, *refs):
    pieces = refs[:PEERS]
    normed, params, grad_pre, sums = refs[PEERS:]
    grad = pieces[0][...].astype(F32)
    for ref in pieces[1:]:
        grad += ref[...].astype(F32)
    norm = normed[...]
    g = gelu_slope(params[:, 0:1] * norm + params[:, 1:2]) * grad
    grad_pre[...] = g
    sums[...] = columns(
        (jnp.sum(g * norm, axis=1, keepdims=True), jnp.sum(g, axis=1, keepdims=True)),
        g.shape[0],
    )


def norm_back(nt, added, last, area, small, idx, *refs):
    grad_pre, normed, scales, params, narrow = refs[:5]
    sums = refs[5 : 5 + nt]
    rest = refs[5 + nt :]
    base, rest = (rest[0], rest[1:]) if added else (None, rest)
    me = idx[0]
    cs, width = grad_pre.shape
    order = rest[-1]
    got = in_order(sums, idx[1], order)
    total = got[0]
    for g in got[1:]:
        total = total + g
    gain_grad, shift_grad = total[:, 0:1], total[:, 1:2]
    norm = normed[...]
    back = params[:, 0:1] * scales[:, 0:1] * (
        grad_pre[...]
        - narrow[0:1, :] * (shift_grad + norm * gain_grad) / scales[:, 1:2]
    )
    if added:
        back = base[...] + back
    grad = back.astype(BF16).astype(F32)
    if not last:
        weights, sums_out, shifted = rest[:3]
        outs, partial = rest[3 : 3 + PEERS], rest[3 + PEERS]
        if added:
            grad_out, outs, partial = rest[3], rest[4 : 4 + PEERS], rest[4 + PEERS]
            grad_out[...] = grad.astype(BF16)
        sums_out[...] = total
        spread_grad(grad, shifted, area, small, offsets(1))
        push_back(me, weights, shifted, partial, outs)
    else:
        weights, grad_skip, sums_out, shifted = rest[:4]
        outs, partial = rest[4 : 4 + PEERS], rest[4 + PEERS]
        sums_out[...] = total
        offs = offsets(2)
        spread_grad(grad, shifted, area, small, offs)
        shifted[9 * cs :, :] = grad_skip[...]
        for phase in range(4):
            acc = None
            for k, (p, _, _) in enumerate(offs + [(0, 0, 0)]):
                if p != phase:
                    continue
                y = lax.dot_general(
                    shifted[k * cs : (k + 1) * cs, :],
                    weights[k * cs : (k + 1) * cs, :],
                    (((0,), (0,)), ((), ())),
                    preferred_element_type=F32,
                )
                acc = y if acc is None else acc + y
            partial[phase] = acc
        for k, out in enumerate(outs):
            for phase in range(4):
                out[phase * area : (phase + 1) * area, :] = partial[
                    phase, rows_at(me ^ k, area), :
                ].astype(BF16)


def weight_grad(idx, shifted, act, out):
    out[...] = lax.dot_general(
        shifted[...], act[...], (((1,), (1,)), ((), ())), preferred_element_type=F32
    ).astype(BF16)


def weight_grad_first(idx, shifted, act, out):
    cs = shifted.shape[0] // 10
    for k, (phase, _, _) in enumerate(offsets(2) + [(0, 0, 0)]):
        out[k * cs : (k + 1) * cs, :] = jnp.dot(
            shifted[k * cs : (k + 1) * cs, :], act[phase], preferred_element_type=F32
        ).astype(BF16)


def entry_back(idx, *refs):
    pieces = refs[:PEERS]
    image, norm, gain, shift, grad_pre, sums = refs[PEERS:]
    c_in = gain.shape[1]
    grad = pieces[0][...].astype(F32)
    for ref in pieces[1:]:
        grad += ref[...].astype(F32)
    normed = (image[:, :c_in].astype(F32) - norm[0:1, :c_in]) * norm[1:2, :c_in]
    g = gelu_slope(gain[...] * normed + shift[...]) * grad
    grad_pre[...] = g
    sums[...] = jnp.zeros_like(sums)
    sums[0:1, :] = jnp.sum(g * normed, axis=0, keepdims=True)
    sums[1:2, :] = jnp.sum(g, axis=0, keepdims=True)


def add_sums(which, idx, *refs):
    out, order = refs[-2:]
    got = in_order(refs[:-2], idx[which], order)
    total = got[0]
    for g in got[1:]:
        total = total + g
    out[...] = total


def entry_grad(idx, grad_pre, image, norm, gain, total, out):
    c_in = gain.shape[1]
    weight = image[:, c_in : c_in + 1].astype(F32)
    scale = norm[1:2, :c_in]
    normed = (image[:, :c_in].astype(F32) - norm[0:1, :c_in]) * scale
    out[...] = gain[...] * scale * (
        grad_pre[...]
        - weight * (total[1:2, :] + normed * total[0:1, :]) / norm[2:3, :c_in]
    )


def program(
    nx,
    ny,
    images,
    valid_count,
    pixel_mask,
    gain_entry,
    shift_entry,
    conv_first,
    gain_middle,
    shift_middle,
    conv_second,
    projection,
    gain_inner,
    shift_inner,
    conv_third,
    gain_last,
    shift_last,
    conv_fourth,
    cotangent,
):
    fy = PEERS // nx
    nt = ny // fy
    side, c_in = images.shape[1], images.shape[3]
    small = side // 2
    area = small * small
    c_out = conv_first.shape[1]
    cs = c_out // PEERS
    width = PEERS * area
    lanes = c_in + 64
    gx, gy = lax.axis_index("gx"), lax.axis_index("gy")
    me = gx * fy + gy % fy
    mine = gy // fy
    idx = jnp.stack([me, mine]).astype(jnp.int32)

    def device(s, t):
        return (s // fy) * ny + t * fy + s % fy

    def share(pieces):
        out = [pieces[0]]
        for k in range(1, PEERS):
            perm = [(device(s, t), device(s ^ k, t)) for s in range(PEERS) for t in range(nt)]
            out.append(lax.ppermute(pieces[k], ("gx", "gy"), perm))
        return out

    def pool(piece):
        out = [piece]
        for k in range(1, nt):
            perm = [(device(s, t), device(s, t ^ k)) for s in range(PEERS) for t in range(nt)]
            out.append(lax.ppermute(piece, ("gx", "gy"), perm))
        return out

    live = (jnp.arange(1) < valid_count[0]).astype(F32)
    wide = pixel_mask.astype(F32) * live[:, None, None]
    image = jnp.concatenate(
        [images[0], wide[0][:, :, None].astype(BF16), jnp.zeros((side, side, 63), BF16)], axis=2
    )
    image = image.reshape(small, 2, small, 2, lanes).transpose(1, 3, 0, 2, 4)
    image = image.reshape(4 * area, lanes)
    group = share([image] * PEERS)

    def columns_of(weight):
        part = lax.dynamic_slice_in_dim(weight, gx * (fy * cs), fy * cs, axis=1)
        part = part.T.reshape(1, fy, cs, weight.shape[0])
        return jnp.broadcast_to(part, (nt, fy, cs, weight.shape[0])).reshape(
            ny, cs, weight.shape[0]
        )

    def turn(block):
        return lax.all_to_all(block, "gy", 0, 0, tiled=True)

    def by_offset(got, chans):
        flat = got.transpose(1, 0, 2).reshape(cs, -1)
        return flat.reshape(cs, -1, chans).transpose(1, 0, 2).reshape(-1, chans)

    rows_first = conv_first.shape[0]
    got_first = turn(
        jnp.concatenate([columns_of(conv_first), columns_of(projection)], axis=2)
    )
    w_first = jnp.concatenate(
        [by_offset(got_first[:, :, :rows_first], c_in), by_offset(got_first[:, :, rows_first:], c_in)]
    )
    w_second = by_offset(turn(columns_of(conv_second)), c_out)
    w_third = by_offset(turn(columns_of(conv_third)), c_out)
    w_fourth = by_offset(turn(columns_of(conv_fourth)), c_out)

    def own(gain, shift):
        pair = jnp.stack([gain, shift], axis=1)
        return lax.dynamic_slice_in_dim(pair, me * cs, cs, axis=0)

    p_middle = own(gain_middle, shift_middle)
    p_inner = own(gain_inner, shift_inner)
    p_last = own(gain_last, shift_last)
    g_entry, s_entry = gain_entry[None], shift_entry[None]

    tile = shape((cs, width))
    tile16 = shape((cs, width), BF16)
    stat = shape((cs, 128))
    stat_order = pltpu.VMEM((nt, cs, 128), F32)
    full16 = shape((c_out, width), BF16)
    conv_flops = 2 * 9 * cs * c_out * width

    cot_parts = call(
        split_cotangent,
        [shape((cs, 128), BF16)] * PEERS,
        [idx, cotangent.reshape(area, c_out)],
        [pltpu.VMEM((c_out, 2 * area), F32)],
    )
    cot_parts = share(cot_parts)

    stats = call(functools.partial(entry_stats, area), shape((8, lanes)), [idx, *group])
    first, skipped, stats, norm_one, narrow, act_one = call(
        functools.partial(entry_block, nt, area, small),
        [tile, tile, stat, shape((8, lanes)), shape((8, width)), shape((4, width, c_in), BF16)],
        [idx, *group, *pool(stats), g_entry, s_entry, w_first],
        [pltpu.VMEM((nt, 8, lanes), F32), pltpu.VMEM((width, lanes), BF16)],
        flops=conv_flops // 2,
    )

    def activate(value, params, stats):
        return call(
            functools.partial(act_block, nt),
            [tile16, tile, stat],
            [idx, value, params, *pool(stats)],
            [stat_order],
        )

    def convolve(act, weights, base, last=False):
        more = [] if base is None else [base]
        outs = [tile16, full16] if last else [tile, stat, full16]
        return call(
            functools.partial(conv_block, base is not None, not last, area, small),
            outs,
            [idx, *share([act] * PEERS), weights, narrow, *more],
            [pltpu.VMEM((9 * cs, width), F32)],
            flops=conv_flops,
        )

    act, normed_two, scale_two = activate(first, p_middle, stats)
    hidden, stats, act_two = convolve(act, w_second, skipped)
    act, normed_three, scale_three = activate(hidden, p_inner, stats)
    third, stats, act_three = convolve(act, w_third, None)
    act, normed_four, scale_four = activate(third, p_last, stats)

    cot, shifted_four, *parts = call(
        functools.partial(last_back, area, small),
        [tile, shape((9 * cs, width), BF16)] + [tile16] * PEERS,
        [idx, *cot_parts, w_fourth],
        [pltpu.VMEM((c_out, width), F32)],
        flops=conv_flops,
    )

    def slope(parts, normed, params):
        return call(gelu_back, [tile, stat], [idx, *share(parts), normed, params])

    grad_pre, sums = slope(parts, normed_four, p_last)
    pooled = pool(sums)
    result, act_four = convolve(act, w_fourth, hidden, last=True)

    def back(grad_pre, normed, scales, params, pooled, weights, base):
        more = [] if base is None else [base]
        outs = [stat, shape((9 * cs, width), BF16)] + ([] if base is None else [tile16])
        return call(
            functools.partial(norm_back, nt, base is not None, False, area, small),
            outs + [tile16] * PEERS,
            [idx, grad_pre, normed, scales, params, narrow, *pooled, *more, weights],
            [pltpu.VMEM((c_out, width), F32), stat_order],
            flops=conv_flops,
        )

    last_sums, shifted_three, *parts = back(
        grad_pre, normed_four, scale_four, p_last, pooled, w_third, None
    )
    grad_pre, sums = slope(parts, normed_three, p_inner)
    inner_sums, shifted_two, grad_hidden, *parts = back(
        grad_pre, normed_three, scale_three, p_inner, pool(sums), w_second, cot
    )
    grad_pre, sums = slope(parts, normed_two, p_middle)
    middle_sums, shifted_one, *parts = call(
        functools.partial(norm_back, nt, False, True, area, small),
        [stat, shape((10 * cs, width), BF16)] + [shape((4 * area, c_in), BF16)] * PEERS,
        [idx, grad_pre, normed_two, scale_two, p_middle, narrow, *pool(sums), w_first, grad_hidden],
        [pltpu.VMEM((4, width, c_in), F32), stat_order],
        flops=conv_flops // 2,
    )
    grad_pre, sums = call(
        entry_back,
        [shape((4 * area, c_in)), shape((8, c_in))],
        [idx, *share(parts), image, norm_one, g_entry, s_entry],
    )
    sums = call(
        functools.partial(add_sums, 0),
        shape((8, c_in)),
        [idx, *share([sums] * PEERS)],
        [pltpu.VMEM((PEERS, 8, c_in), F32)],
    )
    sums = call(
        functools.partial(add_sums, 1),
        shape((8, c_in)),
        [idx, *pool(sums)],
        [pltpu.VMEM((nt, 8, c_in), F32)],
    )
    image_grad = call(
        entry_grad,
        shape((4 * area, c_in)),
        [idx, grad_pre, image, norm_one, g_entry, sums],
    )
    image_grad = image_grad.reshape(2, 2, small, small, c_in).transpose(2, 0, 3, 1, 4)
    image_grad = image_grad.reshape(1, side, side, c_in)

    def grad_rows(flat):
        got = turn(flat.reshape(cs, ny, -1).transpose(1, 0, 2))
        got = got.reshape(nt, fy * cs, -1).astype(F32).sum(axis=0).astype(BF16)
        pieces = [got]
        for k in range(1, nx):
            pieces.append(lax.ppermute(got, "gx", [(i, i ^ k) for i in range(nx)]))
        whole = jnp.take(jnp.stack(pieces), gx ^ jnp.arange(nx), axis=0).reshape(c_out, -1)
        return whole.T.astype(F32)

    def conv_grad(shifted, act):
        grad = call(
            weight_grad, shape((9 * cs, c_out), BF16), [idx, shifted, act], flops=conv_flops
        )
        return grad_rows(grad.reshape(9, cs, c_out).transpose(1, 0, 2).reshape(cs, -1))

    fourth_grad = conv_grad(shifted_four, act_four)
    third_grad = conv_grad(shifted_three, act_three)
    second_grad = conv_grad(shifted_two, act_two)
    grad = call(
        weight_grad_first,
        shape((10 * cs, c_in), BF16),
        [idx, shifted_one, act_one],
        flops=conv_flops // 2,
    )
    first_grad = grad[: 9 * cs].reshape(9, cs, c_in).transpose(1, 0, 2).reshape(cs, ny, -1)
    skip_grad = grad[9 * cs :].reshape(cs, ny, -1)
    both = grad_rows(jnp.concatenate([first_grad, skip_grad], axis=2).reshape(cs, -1))

    out_parts = call(
        functools.partial(split_images, area),
        [shape((cs, 128), BF16)] * PEERS,
        [idx, result],
    )
    out = call(
        join_result,
        shape((area, c_out), BF16),
        [idx, *share(out_parts)],
        [pltpu.VMEM((c_out, 128), F32)],
    )
    small_sums = jnp.concatenate(
        [middle_sums[:, :2], inner_sums[:, :2], last_sums[:, :2]], axis=1
    )
    pieces = jnp.stack(share([small_sums] * PEERS))
    six = jnp.take(pieces, me ^ jnp.arange(PEERS), axis=0).reshape(c_out, 6)
    return (
        out.reshape(1, small, small, c_out),
        image_grad,
        sums[0],
        sums[1],
        both[:rows_first],
        six[:, 0],
        six[:, 1],
        second_grad,
        both[rows_first:],
        six[:, 2],
        six[:, 3],
        third_grad,
        six[:, 4],
        six[:, 5],
        fourth_grad,
    )


def solution(mesh):
    whole = P(("gx", "gy"), None, None, None)
    rows = P("gy", None)
    return jax.shard_map(
        functools.partial(program, mesh.shape["gx"], mesh.shape["gy"]),
        mesh=mesh,
        in_specs=(
            whole,
            P(("gx", "gy")),
            P(("gx", "gy"), None, None),
            P(),
            P(),
            rows,
            P(),
            P(),
            rows,
            rows,
            P(),
            P(),
            rows,
            P(),
            P(),
            rows,
            whole,
        ),
        out_specs=(
            whole, whole, P(), P(), rows, P(), P(), rows, rows, P(), P(), rows, P(), P(), rows,
        ),
        check_vma=False,
    )
```

```python
import functools

import jax
import jax.numpy as jnp
from jax import lax
from jax.experimental import pallas as pl
from jax.experimental.pallas import tpu as pltpu
from jax.sharding import PartitionSpec as P

EPS = 1e-05
F32 = jnp.float32
BF16 = jnp.bfloat16
PEERS = 8
C0 = 0.7978845608028654
C1 = 0.044715
VMEM = pl.BlockSpec(memory_space=pltpu.VMEM)
SMEM = pl.BlockSpec(memory_space=pltpu.SMEM)


def gelu(v):
    return 0.5 * v * (1.0 + jnp.tanh(C0 * (v + C1 * (v * v * v))))


def gelu_slope(v):
    t = jnp.tanh(C0 * (v + C1 * (v * v * v)))
    return 0.5 * (1.0 + t) + 0.5 * v * (1.0 - t * t) * (C0 * (1.0 + 3.0 * C1 * (v * v)))


def call(kernel, outs, args, scratch=(), flops=1 << 20):
    size = sum(a.size * a.dtype.itemsize for a in args)
    return pl.pallas_call(
        kernel,
        out_shape=outs,
        in_specs=[SMEM] + [VMEM] * (len(args) - 1),
        out_specs=jax.tree.map(lambda _: VMEM, outs),
        scratch_shapes=list(scratch),
        compiler_params=pltpu.CompilerParams(vmem_limit_bytes=24 * 1024 * 1024),
        cost_estimate=pl.CostEstimate(flops=flops, bytes_accessed=size, transcendentals=0),
    )(*args)


def shape(dims, dtype=F32):
    return jax.ShapeDtypeStruct(dims, dtype)


def rows_at(index, count):
    return pl.ds(pl.multiple_of(index * count, count), count)


def columns(parts, height):
    lane = lax.broadcasted_iota(jnp.int32, (height, 128), 1)
    out = jnp.zeros((height, 128), F32)
    for k, part in enumerate(parts):
        out = jnp.where(lane == k, part, out)
    return out


def in_order(refs, me, scratch):
    for k, ref in enumerate(refs):
        scratch[me ^ k] = ref[...]
    return [scratch[k] for k in range(len(refs))]


def merge_moments(stats):
    total = sum(n for _, _, n in stats)
    mean = sum(n * m for m, _, n in stats) / total
    squares = sum(q + n * (m - mean) * (m - mean) for m, q, n in stats)
    return mean, lax.rsqrt(squares / total + EPS), total


def pixel(width, area, small):
    lane = lax.broadcasted_iota(jnp.int32, (1, width), 1) % area
    return lane // small, lane % small


def inside(row, col, drow, dcol, small):
    return (row + drow >= 0) & (row + drow < small) & (col + dcol >= 0) & (col + dcol < small)


def moved(value, step):
    shift = (-step) % value.shape[1]
    return pltpu.roll(value, shift, 1) if shift else value


def offsets(stride):
    out = []
    for krow in range(3):
        for kcol in range(3):
            if stride == 1:
                out.append((0, krow - 1, kcol - 1))
            else:
                phase = (krow != 1) * 2 + (kcol != 1)
                out.append((phase, -(krow == 0), -(kcol == 0)))
    return out


def masked_stats(value, weight, n):
    mean = jnp.sum(value * weight, axis=1, keepdims=True) / n
    centred = value - mean
    return mean, jnp.sum(weight * centred * centred, axis=1, keepdims=True)


def spans(heads, rows, ny):
    reach = max((heads * j) % 128 for j in range(ny)) + rows
    return -(-reach // 128) * 128


def one_hot(height, width, shift):
    row = lax.broadcasted_iota(jnp.int32, (height, width), 0)
    col = lax.broadcasted_iota(jnp.int32, (height, width), 1)
    return (col == row + shift).astype(BF16)


def pick(left, right, dims=((1,), (0,))):
    return lax.dot_general(left, right, (dims, ((), ())), preferred_element_type=F32).astype(BF16)


def tile_sources(tile, rows, ny, lanes):
    out = []
    for j in range(ny):
        base = (rows * j) // 128
        last = (rows * (j + 1) - 1) // 128
        if base <= tile <= last:
            out.append((j, (tile - base) * 128))
    return out


def lane_tile(got, tile, rows, ny):
    out = None
    for j, lane in tile_sources(tile, rows, ny, got.shape[2]):
        part = got[j, :, lane : lane + 128]
        out = part if out is None else out + part
    return out


def pixel_order(small, width, of):
    area = small * small
    row = lax.broadcasted_iota(jnp.int32, (4 * area, width), 0)
    col = lax.broadcasted_iota(jnp.int32, (4 * area, width), 1)
    phase, pix = row // area, row % area
    y = 2 * (pix // small) + phase // 2
    x = 2 * (pix % small) + phase % 2
    return (col == of(y, x)).astype(BF16)


def entry_image(small, idx, image, mask, valid, out, weight):
    side = 2 * small
    c_in = image.shape[1]
    count = side * side
    order = pixel_order(small, count, lambda y, x: y * side + x)
    out[:, :c_in] = pick(order, image[...])
    live = (valid[0] > 0).astype(F32)
    row = lax.broadcasted_iota(jnp.int32, (count, side), 0)
    col = lax.broadcasted_iota(jnp.int32, (count, side), 1)
    by_row = jnp.dot(
        (row // side == col).astype(BF16),
        mask[...].astype(F32).astype(BF16),
        preferred_element_type=F32,
    )
    column = jnp.sum(jnp.where(row % side == col, by_row, 0.0), axis=1, keepdims=True) * live
    lane = lax.broadcasted_iota(jnp.int32, (count, 128), 1)
    spread = jnp.where(lane == 0, column, 0.0)
    weight[...] = spread
    out[:, c_in:] = pick(order, spread.astype(BF16))[:, : out.shape[1] - c_in]


def entry_weights(cs, fy, heads, idx, *refs):
    weights, out = refs[:-1], refs[-1]
    ny, _, lanes = out.shape
    gx, gy = idx[2], idx[3]
    c_out = weights[0].shape[1]
    shift = (heads * gy) % 128
    total = None
    for weight in weights:
        rows = weight.shape[0]
        mine = pick(one_hot(fy * cs, c_out, gx * (fy * cs)), weight[...], ((1,), (1,)))
        part = pick(mine, one_hot(rows, lanes, shift))
        total = part if total is None else total + part
        shift = shift + rows
    for j in range(ny):
        out[j] = total[(j % fy) * cs : (j % fy + 1) * cs]


def assemble(got, out, rows, ny):
    cs = got.shape[1]
    tiles = out.shape[1] // 128
    for k in range(9):
        for q in range(tiles):
            out[k * cs : (k + 1) * cs, q * 128 : (q + 1) * 128] = lane_tile(
                got, tiles * k + q, rows, ny
            )


def assemble_first(got, out, flat, rows, extra, ny):
    cs = got.shape[1]
    lanes = got.shape[2]
    c_in = out.shape[1]
    keep = lax.broadcasted_iota(jnp.int32, (1, 128), 1)
    tiles = flat.shape[1] // 128
    for tile in range(tiles):
        total = jnp.zeros((cs, 128), BF16)
        for j, lane in tile_sources(tile, rows, ny, lanes):
            begin = rows * j - tile * 128
            held = (keep >= begin) & (keep < begin + rows)
            part = got[j, :, lane : lane + 128]
            total = total + jnp.where(held, part.astype(F32), 0.0).astype(BF16)
        flat[:, tile * 128 : (tile + 1) * 128] = total
    for k in range(9):
        begin = k * c_in
        base = begin // 128 * 128
        reach = min(-(-(begin + c_in) // 128) * 128, flat.shape[1])
        move = one_hot(c_in, reach - base, begin - base)
        out[k * cs : (k + 1) * cs, :] = pick(flat[:, base:reach], move, ((1,), (1,)))
    total = None
    for j in range(ny):
        row = lax.broadcasted_iota(jnp.int32, (lanes, c_in), 0)
        col = lax.broadcasted_iota(jnp.int32, (lanes, c_in), 1)
        begin = (rows * j) % 128 + rows
        held = (col >= extra * j) & (col < extra * (j + 1)) & (row == col - extra * j + begin)
        part = jnp.dot(got[j], held.astype(BF16), preferred_element_type=F32)
        total = part if total is None else total + part
    out[9 * cs :, :] = total.astype(BF16)


def entry_stats(area, idx, *refs):
    images, out = refs[:PEERS], refs[PEERS]
    lanes = out.shape[1]
    first = jnp.zeros((1, lanes), F32)
    wide = jnp.zeros((1, 1), F32)
    narrow = jnp.zeros((1, 1), F32)
    c_in = lanes - 64
    for ref in images:
        x = ref[...].astype(F32)
        w = x[:, c_in : c_in + 1]
        first += jnp.sum(x * w, axis=0, keepdims=True)
        wide += jnp.sum(w, axis=0, keepdims=True)
        narrow += jnp.sum(w[:area], axis=0, keepdims=True)
    mean = first / wide
    squares = jnp.zeros((1, lanes), F32)
    for ref in images:
        x = ref[...].astype(F32)
        w = x[:, c_in : c_in + 1]
        d = x - mean
        squares += jnp.sum(d * d * w, axis=0, keepdims=True)
    out[...] = jnp.zeros_like(out)
    out[0:1, :] = mean
    out[1:2, :] = squares
    out[2:3, :] = jnp.broadcast_to(wide, (1, lanes))
    out[3:4, :] = jnp.broadcast_to(narrow, (1, lanes))


def entry_block(nt, ny, heads, extra, area, small, idx, *refs):
    images = refs[:PEERS]
    stats = refs[PEERS : PEERS + nt]
    gain, shift, got_first = refs[PEERS + nt : PEERS + nt + 3]
    first, skipped, out_stats, norm, narrow, act, w_first = refs[PEERS + nt + 3 : PEERS + nt + 10]
    order, masks, flat = refs[PEERS + nt + 10 :]
    me, mine = idx[0], idx[1]
    c_in = gain.shape[1]
    lanes = norm.shape[1]
    cs = first.shape[0]
    width = first.shape[1]
    assemble_first(got_first, w_first, flat, heads, extra, ny)
    got = in_order(stats, mine, order)
    mean, scale, total = merge_moments([(g[0:1], g[1:2], g[2:3]) for g in got])
    norm[...] = jnp.zeros_like(norm)
    norm[0:1, :] = mean
    norm[1:2, :] = scale
    norm[2:3, :] = total
    norm[3:4, :] = sum(g[3:4] for g in got)
    for k, ref in enumerate(images):
        x = ref[...]
        v = x[:, :c_in].astype(F32)
        pre = gain[...] * ((v - mean[:, :c_in]) * scale[:, :c_in]) + shift[...]
        a = gelu(pre).astype(BF16)
        for phase in range(4):
            act[phase, rows_at(me ^ k, area), :] = a[phase * area : (phase + 1) * area]
        masks[rows_at(me ^ k, area), :] = x[:area]
    ones = (lax.broadcasted_iota(jnp.int32, (8, lanes), 1) == c_in).astype(BF16)
    weight8 = lax.dot_general(
        ones, masks[...], (((1,), (1,)), ((), ())), preferred_element_type=F32
    )
    narrow[...] = weight8
    weight = weight8[0:1]
    row, col = pixel(width, area, small)
    total_first = jnp.zeros((cs, width), F32)
    for k, (phase, drow, dcol) in enumerate(offsets(2)):
        y = lax.dot_general(
            w_first[k * cs : (k + 1) * cs, :],
            act[phase],
            (((1,), (1,)), ((), ())),
            preferred_element_type=F32,
        )
        y = moved(y, drow * small + dcol)
        total_first += jnp.where(inside(row, col, drow, dcol, small), y, 0.0)
    first[...] = total_first
    skipped[...] = lax.dot_general(
        w_first[9 * cs :, :], act[0], (((1,), (1,)), ((), ())), preferred_element_type=F32
    )
    n = jnp.sum(weight, axis=1, keepdims=True)
    mean2, squares = masked_stats(total_first, weight, n)
    out_stats[...] = columns((mean2, squares, n), cs)


def act_block(nt, idx, *refs):
    value, params = refs[:2]
    stats = refs[2 : 2 + nt]
    act, normed, scales, order = refs[2 + nt :]
    got = in_order(stats, idx[1], order)
    mean, scale, total = merge_moments([(g[:, 0:1], g[:, 1:2], g[:, 2:3]) for g in got])
    norm = (value[...] - mean) * scale
    normed[...] = norm
    act[...] = gelu(params[:, 0:1] * norm + params[:, 1:2]).astype(BF16)
    scales[...] = columns((scale, total), norm.shape[0])


def conv_block(added, last, rows, ny, area, small, idx, *refs):
    pieces = refs[:PEERS]
    weights, narrow = refs[PEERS : PEERS + 2]
    rest = refs[PEERS + 2 :]
    base, rest = (rest[0], rest[1:]) if added else (None, rest)
    me = idx[0]
    cs, width = pieces[0].shape
    if last:
        outs, act, spread = rest[:PEERS], rest[PEERS], rest[PEERS + 1]
    else:
        value, out_stats, act, whole, spread = rest
        assemble(weights, whole, rows, ny)
        weights = whole
    for k, ref in enumerate(pieces):
        act[rows_at(me ^ k, cs), :] = ref[...]
    spread[...] = jnp.dot(weights[...], act[...], preferred_element_type=F32)
    row, col = pixel(width, area, small)
    total = base[...] if added else jnp.zeros((cs, width), F32)
    for k, (_, drow, dcol) in enumerate(offsets(1)):
        y = moved(spread[k * cs : (k + 1) * cs, :], drow * small + dcol)
        total += jnp.where(inside(row, col, drow, dcol, small), y, 0.0)
    if last:
        result = total.astype(BF16)
        lane = lax.broadcasted_iota(jnp.int32, (width, 128), 0)
        slot = lax.broadcasted_iota(jnp.int32, (width, 128), 1)
        for k, out in enumerate(outs):
            out[...] = pick(result, (lane == (me ^ k) * area + slot).astype(BF16))
    else:
        value[...] = total
        weight = narrow[0:1, :]
        n = jnp.sum(weight, axis=1, keepdims=True)
        mean, squares = masked_stats(total, weight, n)
        out_stats[...] = columns((mean, squares, n), cs)


def join_result(idx, *refs):
    pieces, (out, stack) = refs[:PEERS], refs[PEERS:]
    cs = pieces[0].shape[0]
    for k, ref in enumerate(pieces):
        stack[rows_at(idx[0] ^ k, cs), :] = ref[...].astype(F32)
    out[...] = stack[...].T[: out.shape[0]].astype(BF16)


def split_cotangent(idx, *refs):
    cot, outs, stack = refs[0], refs[1 : 1 + PEERS], refs[1 + PEERS]
    c = cot[...].astype(F32)
    stack[...] = jnp.concatenate([c, c], axis=0).T
    cs = outs[0].shape[0]
    for k, out in enumerate(outs):
        out[...] = stack[rows_at(idx[0] ^ k, cs), :].astype(BF16)


def spread_grad(grad, shifted, area, small, offs):
    cs, width = grad.shape
    row, col = pixel(width, area, small)
    for k, (_, drow, dcol) in enumerate(offs):
        g = moved(grad, -(drow * small + dcol))
        g = jnp.where(inside(row, col, -drow, -dcol, small), g, 0.0)
        shifted[k * cs : (k + 1) * cs, :] = g.astype(BF16)


def push_back(me, weights, shifted, partial, outs):
    cs = outs[0].shape[0]
    partial[...] = lax.dot_general(
        weights[...], shifted[...], (((0,), (0,)), ((), ())), preferred_element_type=F32
    )
    for k, out in enumerate(outs):
        out[...] = partial[rows_at(me ^ k, cs), :].astype(BF16)


def last_back(rows, ny, area, small, idx, *refs):
    pieces, got = refs[:PEERS], refs[PEERS]
    cot, shifted, weights = refs[PEERS + 1 : PEERS + 4]
    outs = refs[PEERS + 4 : 2 * PEERS + 4]
    partial = refs[2 * PEERS + 4]
    assemble(got, weights, rows, ny)
    me = idx[0]
    cs, width = cot.shape
    image = lax.broadcasted_iota(jnp.int32, (1, width), 1) // area
    grad = jnp.zeros((cs, width), F32)
    for k, ref in enumerate(pieces):
        tiled = jnp.concatenate([ref[...].astype(F32)] * (width // 128), axis=1)
        grad = jnp.where(image == (me ^ k), tiled, grad)
    cot[...] = grad
    spread_grad(grad, shifted, area, small, offsets(1))
    push_back(me, weights, shifted, partial, outs)


def gelu_back(idx, *refs):
    pieces = refs[:PEERS]
    normed, params, grad_pre, sums = refs[PEERS:]
    grad = pieces[0][...].astype(F32)
    for ref in pieces[1:]:
        grad += ref[...].astype(F32)
    norm = normed[...]
    g = gelu_slope(params[:, 0:1] * norm + params[:, 1:2]) * grad
    grad_pre[...] = g
    sums[...] = columns(
        (jnp.sum(g * norm, axis=1, keepdims=True), jnp.sum(g, axis=1, keepdims=True)),
        g.shape[0],
    )


def norm_back(nt, added, last, area, small, idx, *refs):
    grad_pre, normed, scales, params, narrow = refs[:5]
    sums = refs[5 : 5 + nt]
    rest = refs[5 + nt :]
    base, rest = (rest[0], rest[1:]) if added else (None, rest)
    me = idx[0]
    cs, width = grad_pre.shape
    order = rest[-1]
    got = in_order(sums, idx[1], order)
    total = got[0]
    for g in got[1:]:
        total = total + g
    gain_grad, shift_grad = total[:, 0:1], total[:, 1:2]
    norm = normed[...]
    back = params[:, 0:1] * scales[:, 0:1] * (
        grad_pre[...]
        - narrow[0:1, :] * (shift_grad + norm * gain_grad) / scales[:, 1:2]
    )
    if added:
        back = base[...] + back
    grad = back.astype(BF16).astype(F32)
    if not last:
        weights, sums_out, shifted = rest[:3]
        outs, partial = rest[3 : 3 + PEERS], rest[3 + PEERS]
        if added:
            grad_out, outs, partial = rest[3], rest[4 : 4 + PEERS], rest[4 + PEERS]
            grad_out[...] = grad.astype(BF16)
        sums_out[...] = total
        spread_grad(grad, shifted, area, small, offsets(1))
        push_back(me, weights, shifted, partial, outs)
    else:
        weights, grad_skip, sums_out, shifted = rest[:4]
        outs, partial = rest[4 : 4 + PEERS], rest[4 + PEERS]
        sums_out[...] = total
        offs = offsets(2)
        spread_grad(grad, shifted, area, small, offs)
        shifted[9 * cs :, :] = grad_skip[...]
        for phase in range(4):
            acc = None
            for k, (p, _, _) in enumerate(offs + [(0, 0, 0)]):
                if p != phase:
                    continue
                y = lax.dot_general(
                    shifted[k * cs : (k + 1) * cs, :],
                    weights[k * cs : (k + 1) * cs, :],
                    (((0,), (0,)), ((), ())),
                    preferred_element_type=F32,
                )
                acc = y if acc is None else acc + y
            partial[phase] = acc
        for k, out in enumerate(outs):
            for phase in range(4):
                out[phase * area : (phase + 1) * area, :] = partial[
                    phase, rows_at(me ^ k, area), :
                ].astype(BF16)


def weight_grad(rows, idx, shifted, act, out, full):
    full[...] = lax.dot_general(
        shifted[...], act[...], (((1,), (1,)), ((), ())), preferred_element_type=F32
    )
    ny, cs, lanes = out.shape
    tiles = full.shape[1] // 128
    for j in range(ny):
        base = (rows * j) // 128
        for q in range(lanes // 128):
            tile = base + q
            if tile < 9 * tiles:
                k, p = tile // tiles, tile % tiles
                part = full[k * cs : (k + 1) * cs, p * 128 : (p + 1) * 128]
                out[j, :, q * 128 : (q + 1) * 128] = part.astype(BF16)
            else:
                out[j, :, q * 128 : (q + 1) * 128] = jnp.zeros((cs, 128), BF16)


def weight_grad_first(rows, extra, idx, shifted, act, out, flat):
    ny, cs, lanes = out.shape
    c_in = act.shape[2]
    flat[...] = jnp.zeros_like(flat)
    for k, (phase, _, _) in enumerate(offsets(2)):
        grad = jnp.dot(
            shifted[k * cs : (k + 1) * cs, :], act[phase], preferred_element_type=F32
        ).astype(BF16)
        begin = k * c_in
        base = begin // 128 * 128
        reach = -(-(begin + c_in) // 128) * 128
        move = one_hot(c_in, reach - base, begin - base)
        flat[:, base:reach] += jnp.dot(grad, move, preferred_element_type=F32)
    skip = jnp.dot(shifted[9 * cs :, :], act[0], preferred_element_type=F32).astype(BF16)
    lane = lax.broadcasted_iota(jnp.int32, (1, lanes), 1)
    for j in range(ny):
        base = (rows * j) // 128 * 128
        begin = (rows * j) % 128
        row = lax.broadcasted_iota(jnp.int32, (c_in, lanes), 0)
        col = lax.broadcasted_iota(jnp.int32, (c_in, lanes), 1)
        held = (row >= extra * j) & (row < extra * (j + 1)) & (
            col == row - extra * j + begin + rows
        )
        tail = jnp.dot(skip, held.astype(BF16), preferred_element_type=F32)
        own = (lane >= begin) & (lane < begin + rows)
        out[j] = (jnp.where(own, flat[:, base : base + lanes], 0.0) + tail).astype(BF16)


def fold(nt, fy, idx, got, out):
    cs = got.shape[1]
    for y in range(fy):
        total = got[y].astype(F32)
        for t in range(1, nt):
            total += got[t * fy + y].astype(F32)
        out[y * cs : (y + 1) * cs, :] = total.astype(BF16)


def own_rows(heads, idx, *refs):
    count = sum(1 for ref in refs if ref.dtype == BF16) - 1
    pieces, outs, stack = refs[:count], refs[count:-1], refs[-1]
    height = pieces[0].shape[0]
    for k, ref in enumerate(pieces):
        stack[rows_at(idx[2] ^ k, height), :] = ref[...]
    shift = (heads * idx[3]) % 128
    for out in outs:
        rows = out.shape[0]
        out[...] = lax.dot_general(
            one_hot(rows, stack.shape[1], shift),
            stack[...],
            (((1,), (1,)), ((), ())),
            preferred_element_type=F32,
        )
        shift = shift + rows


def entry_back(small, idx, *refs):
    pieces = refs[:PEERS]
    image, norm, gain, shift, grad_pre, sums = refs[PEERS:]
    c_in = gain.shape[1]
    side = 2 * small
    grad = pieces[0][...].astype(F32)
    for ref in pieces[1:]:
        grad += ref[...].astype(F32)
    order = pixel_order(small, side * side, lambda y, x: y * side + x)
    high = grad.astype(BF16)
    low = (grad - high.astype(F32)).astype(BF16)
    grad = sum(
        lax.dot_general(order, part, (((0,), (0,)), ((), ())), preferred_element_type=F32)
        for part in (high, low)
    )
    normed = (image[...].astype(F32) - norm[0:1, :c_in]) * norm[1:2, :c_in]
    g = gelu_slope(gain[...] * normed + shift[...]) * grad
    grad_pre[...] = g
    sums[...] = jnp.zeros_like(sums)
    sums[0:1, :c_in] = jnp.sum(g * normed, axis=0, keepdims=True)
    sums[1:2, :c_in] = jnp.sum(g, axis=0, keepdims=True)


def bundle(idx, first, second, third, sums, out):
    cs = first.shape[0]
    tiles = sums.shape[1] // 128
    out[0:8, :] = jnp.zeros((8, 128), F32)
    for r in range(2):
        for q in range(tiles):
            k = r * tiles + q
            out[k : k + 1, :] = sums[r : r + 1, q * 128 : (q + 1) * 128]
    out[8:, :] = columns(
        [v for ref in (first, second, third) for v in (ref[:, 0:1], ref[:, 1:2])], cs
    )


def unbundle(idx, *refs):
    pieces = refs[:PEERS]
    out, six, order, stack = refs[PEERS:]
    got = in_order(pieces, idx[0], order)
    cs = stack.shape[0] // PEERS
    total = got[0][0:8]
    for g in got[1:]:
        total = total + g[0:8]
    out[...] = total
    for k, g in enumerate(got):
        stack[k * cs : (k + 1) * cs, :] = g[8:]
    six[...] = stack[...].T[0:8]


def entry_grad(nt, idx, *refs):
    sums = refs[:nt]
    grad_pre, image, weight, norm, gain, gain_grad, shift_grad, out, order = refs[nt:]
    got = in_order(sums, idx[1], order)
    total = got[0]
    for g in got[1:]:
        total = total + g
    lanes = gain_grad.shape[1]
    tiles = lanes // 128
    for q in range(tiles):
        gain_grad[0:1, q * 128 : (q + 1) * 128] = total[q : q + 1]
        shift_grad[0:1, q * 128 : (q + 1) * 128] = total[tiles + q : tiles + q + 1]
    c_in = gain.shape[1]
    scale = norm[1:2, :c_in]
    normed = (image[...].astype(F32) - norm[0:1, :c_in]) * scale
    out[...] = gain[...] * scale * (
        grad_pre[...]
        - weight[:, 0:1]
        * (shift_grad[0:1, :c_in] + normed * gain_grad[0:1, :c_in])
        / norm[2:3, :c_in]
    )


def program(
    nx,
    ny,
    images,
    valid_count,
    pixel_mask,
    gain_entry,
    shift_entry,
    conv_first,
    gain_middle,
    shift_middle,
    conv_second,
    projection,
    gain_inner,
    shift_inner,
    conv_third,
    gain_last,
    shift_last,
    conv_fourth,
    cotangent,
):
    fy = PEERS // nx
    nt = ny // fy
    side, c_in = images.shape[1], images.shape[3]
    small = side // 2
    area = small * small
    c_out = conv_first.shape[1]
    cs = c_out // PEERS
    width = PEERS * area
    lanes = c_in + 64
    gx, gy = lax.axis_index("gx"), lax.axis_index("gy")
    me = gx * fy + gy % fy
    mine = gy // fy
    idx = jnp.stack([me, mine, gx, gy]).astype(jnp.int32)

    def device(s, t):
        return (s // fy) * ny + t * fy + s % fy

    def to_slice(piece, k):
        perm = [(device(s, t), device(s ^ k, t)) for s in range(PEERS) for t in range(nt)]
        return lax.ppermute(piece, ("gx", "gy"), perm)

    def share(pieces):
        return [pieces[0]] + [to_slice(pieces[k], k) for k in range(1, PEERS)]

    near = 2 if fy == 2 else 1
    far = [bit for bit in (4, 2, 1) if bit != near]

    def spread_out(piece):
        held = {0: piece}
        held[far[0]] = to_slice(piece, far[0])
        held[far[1]] = to_slice(piece, far[1])
        held[far[0] + far[1]] = to_slice(held[far[1]], far[0])
        for k in (0, *far, far[0] + far[1]):
            held[k + near] = to_slice(held[k], near)
        return [held[k] for k in range(PEERS)]

    def pool(piece):
        out = [piece]
        for k in range(1, nt):
            perm = [(device(s, t), device(s, t ^ k)) for s in range(PEERS) for t in range(nt)]
            out.append(lax.ppermute(piece, ("gx", "gy"), perm))
        return out

    def after(value, *others):
        return lax.optimization_barrier((value, *others))[0]

    def turn(block):
        return lax.all_to_all(block, "gy", 0, 0, tiled=True)

    rows_first, rows_skip = conv_first.shape[0], projection.shape[0]
    rows_mid = conv_second.shape[0]
    span_first = spans(rows_first, rows_first + rows_skip, ny)
    span_mid = spans(rows_mid, rows_mid, ny)

    def outgoing(heads, span, *weights):
        return call(
            functools.partial(entry_weights, cs, fy, heads),
            shape((ny, cs, span), BF16),
            [idx, *weights],
        )

    pixels = images.reshape(side * side, c_in)
    image, wide = pl.pallas_call(
        functools.partial(entry_image, small),
        out_shape=[shape((4 * area, lanes), BF16), shape((4 * area, 128))],
        in_specs=[SMEM, VMEM, VMEM, SMEM],
        out_specs=[VMEM, VMEM],
        cost_estimate=pl.CostEstimate(flops=1 << 20, bytes_accessed=1 << 20, transcendentals=0),
    )(idx, pixels, pixel_mask.reshape(side, side), valid_count)
    group = spread_out(image)
    out_first = outgoing(rows_first, span_first, after(conv_first, image), projection)
    got_first = turn(out_first)

    def own(gain, shift):
        pair = jnp.stack([gain, shift], axis=1)
        return lax.dynamic_slice_in_dim(pair, me * cs, cs, axis=0)

    p_middle = own(gain_middle, shift_middle)
    p_inner = own(gain_inner, shift_inner)
    p_last = own(gain_last, shift_last)
    g_entry, s_entry = gain_entry[None], shift_entry[None]

    tile = shape((cs, width))
    tile16 = shape((cs, width), BF16)
    stat = shape((cs, 128))
    stat_order = pltpu.VMEM((nt, cs, 128), F32)
    full16 = shape((c_out, width), BF16)
    whole16 = shape((9 * cs, c_out), BF16)
    conv_flops = 2 * 9 * cs * c_out * width

    stats = call(functools.partial(entry_stats, area), shape((8, lanes)), [idx, *group])
    got_second = turn(outgoing(rows_mid, span_mid, after(conv_second, stats)))
    first, skipped, stats, norm_one, narrow, act_one, w_first = call(
        functools.partial(entry_block, nt, ny, rows_first, rows_skip, area, small),
        [
            tile,
            tile,
            stat,
            shape((8, lanes)),
            shape((8, width)),
            shape((4, width, c_in), BF16),
            shape((10 * cs, c_in), BF16),
        ],
        [idx, *group, *pool(stats), g_entry, s_entry, got_first],
        [
            pltpu.VMEM((nt, 8, lanes), F32),
            pltpu.VMEM((width, lanes), BF16),
            pltpu.VMEM((cs, -(-9 * c_in // 128) * 128), BF16),
        ],
        flops=conv_flops // 2,
    )
    got_third = turn(outgoing(rows_mid, span_mid, after(conv_third, stats)))

    cot_parts = call(
        split_cotangent,
        [shape((cs, 128), BF16)] * PEERS,
        [idx, after(cotangent, stats).reshape(area, c_out)],
        [pltpu.VMEM((c_out, 2 * area), F32)],
    )
    cot_parts = share(cot_parts)

    def activate(value, params, stats):
        return call(
            functools.partial(act_block, nt),
            [tile16, tile, stat],
            [idx, value, params, *pool(stats)],
            [stat_order],
        )

    def convolve(act, weights, base, last=False):
        more = [] if base is None else [base]
        if last:
            outs = [shape((cs, 128), BF16)] * PEERS + [full16]
        else:
            outs = [tile, stat, full16, whole16]
        return call(
            functools.partial(conv_block, base is not None, last, rows_mid, ny, area, small),
            outs,
            [idx, *spread_out(act), weights, narrow, *more],
            [pltpu.VMEM((9 * cs, width), F32)],
            flops=conv_flops,
        )

    act, normed_two, scale_two = activate(first, p_middle, stats)
    hidden, stats, act_two, w_second = convolve(act, got_second, skipped)
    got_fourth = turn(outgoing(rows_mid, span_mid, after(conv_fourth, stats)))
    act, normed_three, scale_three = activate(hidden, p_inner, stats)
    third, stats, act_three, w_third = convolve(act, got_third, None)
    act, normed_four, scale_four = activate(third, p_last, stats)

    cot, shifted_four, w_fourth, *parts = call(
        functools.partial(last_back, rows_mid, ny, area, small),
        [tile, shape((9 * cs, width), BF16), whole16] + [tile16] * PEERS,
        [idx, *cot_parts, got_fourth],
        [pltpu.VMEM((c_out, width), F32)],
        flops=conv_flops,
    )

    def slope(parts, normed, params):
        return call(gelu_back, [tile, stat], [idx, *share(parts), normed, params])

    def back(grad_pre, normed, scales, params, pooled, weights, base):
        more = [] if base is None else [base]
        outs = [stat, shape((9 * cs, width), BF16)] + ([] if base is None else [tile16])
        return call(
            functools.partial(norm_back, nt, base is not None, False, area, small),
            outs + [tile16] * PEERS,
            [idx, grad_pre, normed, scales, params, narrow, *pooled, *more, weights],
            [pltpu.VMEM((c_out, width), F32), stat_order],
            flops=conv_flops,
        )

    def send_grad(shifted, act):
        grad = call(
            functools.partial(weight_grad, rows_mid),
            shape((ny, cs, span_mid), BF16),
            [idx, shifted, act],
            [pltpu.VMEM((9 * cs, c_out), F32)],
            flops=conv_flops,
        )
        return turn(grad)

    def land_grad(got, heads, *rows):
        span = got.shape[2]
        got = call(functools.partial(fold, nt, fy), shape((fy * cs, span), BF16), [idx, got])
        pieces = [got]
        for k in range(1, nx):
            pieces.append(lax.ppermute(got, "gx", [(i, i ^ k) for i in range(nx)]))
        return call(
            functools.partial(own_rows, heads),
            [shape((r, c_out)) for r in rows],
            [idx, *pieces],
            [pltpu.VMEM((c_out, span), BF16)],
        )

    grad_pre, sums = slope(parts, normed_four, p_last)
    pooled = pool(sums)
    *out_parts, act_four = convolve(act, w_fourth, hidden, last=True)

    last_sums, shifted_three, *parts = back(
        grad_pre, normed_four, scale_four, p_last, pooled, w_third, None
    )
    sent_fourth = send_grad(shifted_four, act_four)
    grad_pre, sums = slope(parts, normed_three, p_inner)
    inner_sums, shifted_two, grad_hidden, *parts = back(
        grad_pre, normed_three, scale_three, p_inner, pool(sums), w_second, cot
    )
    sent_third = send_grad(shifted_three, act_three)
    grad_pre, sums = slope(parts, normed_two, p_middle)
    middle_sums, shifted_one, *parts = call(
        functools.partial(norm_back, nt, False, True, area, small),
        [stat, shape((10 * cs, width), BF16)] + [shape((4 * area, c_in), BF16)] * PEERS,
        [idx, grad_pre, normed_two, scale_two, p_middle, narrow, *pool(sums), w_first, grad_hidden],
        [pltpu.VMEM((4, width, c_in), F32), stat_order],
        flops=conv_flops // 2,
    )
    sent_second = send_grad(shifted_two, act_two)
    parts = share(parts)
    grad = call(
        functools.partial(weight_grad_first, rows_first, rows_skip),
        shape((ny, cs, span_first), BF16),
        [idx, shifted_one, act_one],
        [pltpu.VMEM((cs, 9 * c_in + span_first), F32)],
        flops=conv_flops // 2,
    )
    sent_first = turn(grad)
    (fourth_grad,) = land_grad(sent_fourth, rows_mid, rows_mid)
    (third_grad,) = land_grad(sent_third, rows_mid, rows_mid)
    (second_grad,) = land_grad(sent_second, rows_mid, rows_mid)
    first_grad, skip_grad = land_grad(sent_first, rows_first, rows_first, rows_skip)

    padded = -(-c_in // 128) * 128
    grad_pre, sums = call(
        functools.partial(entry_back, small),
        [shape((4 * area, c_in)), shape((8, padded))],
        [idx, *parts, pixels, norm_one, g_entry, s_entry],
    )
    message = call(
        bundle, shape((8 + cs, 128)), [idx, middle_sums, inner_sums, last_sums, sums]
    )
    sums, six = call(
        unbundle,
        [shape((8, 128)), shape((8, c_out))],
        [idx, *spread_out(message)],
        [pltpu.VMEM((PEERS, 8 + cs, 128), F32), pltpu.VMEM((c_out, 128), F32)],
    )
    gain_entry_grad, shift_entry_grad, image_grad = call(
        functools.partial(entry_grad, nt),
        [shape((1, padded)), shape((1, padded)), shape((4 * area, c_in))],
        [idx, *pool(sums), grad_pre, pixels, wide, norm_one, g_entry],
        [pltpu.VMEM((nt, 8, 128), F32)],
    )

    out = call(
        join_result,
        shape((area, c_out), BF16),
        [idx, *share(out_parts)],
        [pltpu.VMEM((c_out, 128), F32)],
    )
    return (
        out.reshape(1, small, small, c_out),
        image_grad.reshape(1, side, side, c_in),
        gain_entry_grad[0, :c_in],
        shift_entry_grad[0, :c_in],
        first_grad,
        six[0],
        six[1],
        second_grad,
        skip_grad,
        six[2],
        six[3],
        third_grad,
        six[4],
        six[5],
        fourth_grad,
    )


def solution(mesh):
    whole = P(("gx", "gy"), None, None, None)
    rows = P("gy", None)
    return jax.shard_map(
        functools.partial(program, mesh.shape["gx"], mesh.shape["gy"]),
        mesh=mesh,
        in_specs=(
            whole,
            P(("gx", "gy")),
            P(("gx", "gy"), None, None),
            P(),
            P(),
            rows,
            P(),
            P(),
            rows,
            rows,
            P(),
            P(),
            rows,
            P(),
            P(),
            rows,
            whole,
        ),
        out_specs=(
            whole, whole, P(), P(), rows, P(), P(), rows, rows, P(), P(), rows, P(), P(), rows,
        ),
        check_vma=False,
    )
```

```python
import functools

import jax
import jax.numpy as jnp
from jax import lax
from jax.experimental import pallas as pl
from jax.experimental.pallas import tpu as pltpu
from jax.sharding import PartitionSpec as P

EPS = 1e-05
F32 = jnp.float32
BF16 = jnp.bfloat16
PEERS = 8
C0 = 0.7978845608028654
C1 = 0.044715
VMEM = pl.BlockSpec(memory_space=pltpu.VMEM)
SMEM = pl.BlockSpec(memory_space=pltpu.SMEM)


def gelu(v):
    return 0.5 * v * (1.0 + jnp.tanh(C0 * (v + C1 * (v * v * v))))


def gelu_slope(v):
    t = jnp.tanh(C0 * (v + C1 * (v * v * v)))
    return 0.5 * (1.0 + t) + 0.5 * v * (1.0 - t * t) * (C0 * (1.0 + 3.0 * C1 * (v * v)))


def call(kernel, outs, args, scratch=(), flops=1 << 20):
    size = sum(a.size * a.dtype.itemsize for a in args)
    return pl.pallas_call(
        kernel,
        out_shape=outs,
        in_specs=[SMEM] + [VMEM] * (len(args) - 1),
        out_specs=jax.tree.map(lambda _: VMEM, outs),
        scratch_shapes=list(scratch),
        compiler_params=pltpu.CompilerParams(vmem_limit_bytes=12 * 1024 * 1024),
        cost_estimate=pl.CostEstimate(flops=flops, bytes_accessed=size, transcendentals=0),
    )(*args)


def shape(dims, dtype=F32):
    return jax.ShapeDtypeStruct(dims, dtype)


def rows_at(index, count):
    return pl.ds(pl.multiple_of(index * count, count), count)


def columns(parts, height):
    lane = lax.broadcasted_iota(jnp.int32, (height, 128), 1)
    out = jnp.zeros((height, 128), F32)
    for k, part in enumerate(parts):
        out = jnp.where(lane == k, part, out)
    return out


def in_order(refs, me, scratch):
    for k, ref in enumerate(refs):
        scratch[me ^ k] = ref[...]
    return [scratch[k] for k in range(len(refs))]


def merge_moments(stats):
    total = sum(n for _, _, n in stats)
    mean = sum(n * m for m, _, n in stats) / total
    squares = sum(q + n * (m - mean) * (m - mean) for m, q, n in stats)
    return mean, lax.rsqrt(squares / total + EPS), total


def pixel(width, area, small):
    lane = lax.broadcasted_iota(jnp.int32, (1, width), 1) % area
    return lane // small, lane % small


def inside(row, col, drow, dcol, small):
    return (row + drow >= 0) & (row + drow < small) & (col + dcol >= 0) & (col + dcol < small)


def moved(value, step):
    shift = (-step) % value.shape[1]
    return pltpu.roll(value, shift, 1) if shift else value


OFFSETS = [(0, krow - 1, kcol - 1) for krow in range(3) for kcol in range(3)]

STRIDED = [
    ((krow != 1) * 2 + (kcol != 1), -(krow == 0), -(kcol == 0))
    for krow in range(3)
    for kcol in range(3)
] + [(0, 0, 0)]
PLACED = sorted(range(10), key=lambda k: (STRIDED[k][0], k))
PHASES = [[k for k in PLACED if STRIDED[k][0] == phase] for phase in range(4)]


def row_of(k, cs):
    at = PLACED.index(k)
    return slice(at * cs, (at + 1) * cs)


def phase_rows(phase, cs):
    first, last = PHASES[phase][0], PHASES[phase][-1]
    return slice(PLACED.index(first) * cs, (PLACED.index(last) + 1) * cs)


def masked_stats(value, weight, n):
    mean = jnp.sum(value * weight, axis=1, keepdims=True) / n
    centred = value - mean
    return mean, jnp.sum(weight * centred * centred, axis=1, keepdims=True)


def span_of(rows):
    return -(-rows // 128) * 128


def one_hot(height, width, shift):
    row = lax.broadcasted_iota(jnp.int32, (height, width), 0)
    col = lax.broadcasted_iota(jnp.int32, (height, width), 1)
    return (col == row + shift).astype(BF16)


def pick32(left, right, dims=((1,), (0,))):
    return lax.dot_general(left, right, (dims, ((), ())), preferred_element_type=F32)


def pick(left, right, dims=((1,), (0,))):
    return pick32(left, right, dims).astype(BF16)


def lane_tile(held, tile, rows, span):
    units = 2 * held.shape[1]
    lane = lax.broadcasted_iota(jnp.int32, (1, 128), 1)
    out = None
    for v in range(units):
        begin = rows * v - tile * 128
        if begin >= 128 or begin + rows <= 0:
            continue
        base = rows * v // 128
        at = (tile - base) * 128 % span
        part = held[v % 2, v // 2, :, at : at + 128]
        if begin > 0 or begin + rows < 128:
            own = (lane >= begin) & (lane < begin + rows)
            part = jnp.where(own, part.astype(F32), 0.0).astype(BF16)
        out = part if out is None else out + part
    return out


def pixel_order(small, width, of):
    area = small * small
    row = lax.broadcasted_iota(jnp.int32, (4 * area, width), 0)
    col = lax.broadcasted_iota(jnp.int32, (4 * area, width), 1)
    phase, pix = row // area, row % area
    y = 2 * (pix // small) + phase // 2
    x = 2 * (pix % small) + phase % 2
    return (col == of(y, x)).astype(BF16)


def entry_image(small, idx, image, mask, valid, out, weight):
    side = 2 * small
    c_in = image.shape[1]
    count = side * side
    order = pixel_order(small, count, lambda y, x: y * side + x)
    out[:, :c_in] = pick(order, image[...])
    live = (valid[0] > 0).astype(F32)
    row = lax.broadcasted_iota(jnp.int32, (count, side), 0)
    col = lax.broadcasted_iota(jnp.int32, (count, side), 1)
    by_row = jnp.dot(
        (row // side == col).astype(BF16),
        mask[...].astype(F32).astype(BF16),
        preferred_element_type=F32,
    )
    column = jnp.sum(jnp.where(row % side == col, by_row, 0.0), axis=1, keepdims=True) * live
    lane = lax.broadcasted_iota(jnp.int32, (count, 128), 1)
    spread = jnp.where(lane == 0, column, 0.0)
    weight[...] = spread
    out[:, c_in:] = pick(order, spread.astype(BF16))[:, : out.shape[1] - c_in]


def entry_weights(cs, fy, idx, *refs):
    weights, out = refs[:-1], refs[-1]
    ny, _, span = out.shape
    gx, gy = idx[2], idx[3]
    core = gx % 2
    c_out = weights[0].shape[1]
    unit = weights[0].shape[0] // 2
    begin = unit * (2 * gy + core) % 128
    total = None
    for weight in weights:
        rows = weight.shape[0]
        half = rows // 2
        mine = pick(one_hot(fy * cs, c_out, gx // 2 * (fy * cs)), weight[...], ((1,), (1,)))
        row = lax.broadcasted_iota(jnp.int32, (rows, span), 0) - core * half
        col = lax.broadcasted_iota(jnp.int32, (rows, span), 1)
        place = (row >= 0) & (row < half) & (
            (col == row + begin) | (col == row + begin - span)
        )
        part = pick(mine, place.astype(BF16))
        total = part if total is None else total + part
        begin = begin + half
    for j in range(ny):
        out[j] = total[(j % fy) * cs : (j % fy + 1) * cs]


def both_halves(core, got, other, held):
    held[core] = got[...]
    held[1 - core] = other[...]


def assemble(held, out, rows):
    cs, span = held.shape[2], held.shape[3]
    tiles = out.shape[1] // 128
    for k in range(9):
        for q in range(tiles):
            out[k * cs : (k + 1) * cs, q * 128 : (q + 1) * 128] = lane_tile(
                held, tiles * k + q, rows, span
            )


def assemble_first(held, out, flat, rows, extra):
    cs, span = held.shape[2], held.shape[3]
    c_in = out.shape[1]
    tiles = flat.shape[1] // 128
    for tile in range(tiles):
        flat[:, tile * 128 : (tile + 1) * 128] = lane_tile(held, tile, rows, span)
    for k in range(9):
        begin = k * c_in
        base = begin // 128 * 128
        reach = min(-(-(begin + c_in) // 128) * 128, flat.shape[1])
        move = one_hot(c_in, reach - base, begin - base)
        out[row_of(k, cs), :] = pick(flat[:, base:reach], move, ((1,), (1,)))
    total = None
    for v in range(2 * held.shape[1]):
        row = lax.broadcasted_iota(jnp.int32, (span, c_in), 0)
        col = lax.broadcasted_iota(jnp.int32, (span, c_in), 1)
        at = col - extra * v
        begin = rows * v % 128 + rows
        place = (at >= 0) & (at < extra) & ((row == at + begin) | (row == at + begin - span))
        part = pick32(held[v % 2, v // 2], place.astype(BF16))
        total = part if total is None else total + part
    out[row_of(9, cs), :] = total.astype(BF16)


def entry_stats(area, idx, *refs):
    images, out = refs[:PEERS], refs[PEERS]
    lanes = out.shape[1]
    first = jnp.zeros((1, lanes), F32)
    wide = jnp.zeros((1, 1), F32)
    narrow = jnp.zeros((1, 1), F32)
    c_in = lanes - 64
    for ref in images:
        x = ref[...].astype(F32)
        w = x[:, c_in : c_in + 1]
        first += jnp.sum(x * w, axis=0, keepdims=True)
        wide += jnp.sum(w, axis=0, keepdims=True)
        narrow += jnp.sum(w[:area], axis=0, keepdims=True)
    mean = first / wide
    squares = jnp.zeros((1, lanes), F32)
    for ref in images:
        x = ref[...].astype(F32)
        w = x[:, c_in : c_in + 1]
        d = x - mean
        squares += jnp.sum(d * d * w, axis=0, keepdims=True)
    out[...] = jnp.zeros_like(out)
    out[0:1, :] = mean
    out[1:2, :] = squares
    out[2:3, :] = jnp.broadcast_to(wide, (1, lanes))
    out[3:4, :] = jnp.broadcast_to(narrow, (1, lanes))


def entry_block(nt, rows, extra, area, small, idx, *refs):
    images = refs[:PEERS]
    stats = refs[PEERS : PEERS + nt]
    gain, shift, got, other = refs[PEERS + nt : PEERS + nt + 4]
    first, skipped, out_stats, norm, narrow, act, w_first = refs[PEERS + nt + 4 : PEERS + nt + 11]
    order, masks, flat, held = refs[PEERS + nt + 11 :]
    me, mine = idx[0], idx[1]
    c_in = gain.shape[1]
    lanes = norm.shape[1]
    cs = first.shape[0]
    width = first.shape[1]
    both_halves(idx[2] % 2, got, other, held)
    assemble_first(held, w_first, flat, rows, extra)
    got = in_order(stats, mine, order)
    mean, scale, total = merge_moments([(g[0:1], g[1:2], g[2:3]) for g in got])
    norm[...] = jnp.zeros_like(norm)
    norm[0:1, :] = mean
    norm[1:2, :] = scale
    norm[2:3, :] = total
    norm[3:4, :] = sum(g[3:4] for g in got)
    for k, ref in enumerate(images):
        x = ref[...]
        v = x[:, :c_in].astype(F32)
        pre = gain[...] * ((v - mean[:, :c_in]) * scale[:, :c_in]) + shift[...]
        a = gelu(pre).astype(BF16)
        for phase in range(4):
            act[phase, rows_at(me ^ k, area), :] = a[phase * area : (phase + 1) * area]
        masks[rows_at(me ^ k, area), :] = x[:area]
    ones = (lax.broadcasted_iota(jnp.int32, (8, lanes), 1) == c_in).astype(BF16)
    weight8 = lax.dot_general(
        ones, masks[...], (((1,), (1,)), ((), ())), preferred_element_type=F32
    )
    narrow[...] = weight8
    weight = weight8[0:1]
    row, col = pixel(width, area, small)
    total_first = jnp.zeros((cs, width), F32)
    for phase in range(4):
        group = lax.dot_general(
            w_first[phase_rows(phase, cs), :],
            act[phase],
            (((1,), (1,)), ((), ())),
            preferred_element_type=F32,
        )
        for at, k in enumerate(PHASES[phase]):
            y = group[at * cs : (at + 1) * cs]
            if k == 9:
                skipped[...] = y
                continue
            _, drow, dcol = STRIDED[k]
            y = moved(y, drow * small + dcol)
            total_first += jnp.where(inside(row, col, drow, dcol, small), y, 0.0)
    first[...] = total_first
    n = jnp.sum(weight, axis=1, keepdims=True)
    mean2, squares = masked_stats(total_first, weight, n)
    out_stats[...] = columns((mean2, squares, n), cs)


def act_block(nt, idx, *refs):
    value, params = refs[:2]
    stats = refs[2 : 2 + nt]
    act, normed, scales, order = refs[2 + nt :]
    got = in_order(stats, idx[1], order)
    mean, scale, total = merge_moments([(g[:, 0:1], g[:, 1:2], g[:, 2:3]) for g in got])
    norm = (value[...] - mean) * scale
    normed[...] = norm
    act[...] = gelu(params[:, 0:1] * norm + params[:, 1:2]).astype(BF16)
    scales[...] = columns((scale, total), norm.shape[0])


def conv_block(added, last, rows, area, small, idx, *refs):
    pieces = refs[:PEERS]
    narrow, weights = refs[PEERS : PEERS + 2]
    rest = refs[PEERS + 2 :]
    if not last:
        other, rest = rest[0], rest[1:]
    base, rest = (rest[0], rest[1:]) if added else (None, rest)
    me = idx[0]
    cs, width = pieces[0].shape
    if last:
        outs, act, spread = rest[:PEERS], rest[PEERS], rest[PEERS + 1]
    else:
        value, out_stats, act, whole, spread, held = rest
        both_halves(idx[2] % 2, weights, other, held)
        assemble(held, whole, rows)
        weights = whole
    for k, ref in enumerate(pieces):
        act[rows_at(me ^ k, cs), :] = ref[...]
    spread[...] = jnp.dot(weights[...], act[...], preferred_element_type=F32)
    row, col = pixel(width, area, small)
    total = base[...] if added else jnp.zeros((cs, width), F32)
    for k, (_, drow, dcol) in enumerate(OFFSETS):
        y = moved(spread[k * cs : (k + 1) * cs, :], drow * small + dcol)
        total += jnp.where(inside(row, col, drow, dcol, small), y, 0.0)
    if last:
        result = total.astype(BF16)
        lane = lax.broadcasted_iota(jnp.int32, (width, 128), 0)
        slot = lax.broadcasted_iota(jnp.int32, (width, 128), 1)
        for k, out in enumerate(outs):
            out[...] = pick(result, (lane == (me ^ k) * area + slot).astype(BF16))
    else:
        value[...] = total
        weight = narrow[0:1, :]
        n = jnp.sum(weight, axis=1, keepdims=True)
        mean, squares = masked_stats(total, weight, n)
        out_stats[...] = columns((mean, squares, n), cs)


def join_result(idx, *refs):
    pieces, (out, stack) = refs[:PEERS], refs[PEERS:]
    cs = pieces[0].shape[0]
    for k, ref in enumerate(pieces):
        stack[rows_at(idx[0] ^ k, cs), :] = ref[...].astype(F32)
    out[...] = stack[...].T[: out.shape[0]].astype(BF16)


def split_cotangent(idx, *refs):
    cot, outs, stack = refs[0], refs[1 : 1 + PEERS], refs[1 + PEERS]
    c = cot[...].astype(F32)
    stack[...] = jnp.concatenate([c, c], axis=0).T
    cs = outs[0].shape[0]
    for k, out in enumerate(outs):
        out[...] = stack[rows_at(idx[0] ^ k, cs), :].astype(BF16)


def spread_grad(grad, shifted, area, small, offs, row_at):
    cs, width = grad.shape
    row, col = pixel(width, area, small)
    for k, (_, drow, dcol) in enumerate(offs):
        g = moved(grad, -(drow * small + dcol))
        g = jnp.where(inside(row, col, -drow, -dcol, small), g, 0.0)
        shifted[row_at(k, cs), :] = g.astype(BF16)


def plain_rows(k, cs):
    return slice(k * cs, (k + 1) * cs)


def push_back(me, weights, shifted, partial, outs):
    cs = outs[0].shape[0]
    partial[...] = lax.dot_general(
        weights[...], shifted[...], (((0,), (0,)), ((), ())), preferred_element_type=F32
    )
    for k, out in enumerate(outs):
        out[...] = partial[rows_at(me ^ k, cs), :].astype(BF16)


def last_back(rows, area, small, idx, *refs):
    pieces, (got, other) = refs[:PEERS], refs[PEERS : PEERS + 2]
    cot, shifted, weights = refs[PEERS + 2 : PEERS + 5]
    outs = refs[PEERS + 5 : 2 * PEERS + 5]
    partial, held = refs[2 * PEERS + 5 :]
    both_halves(idx[2] % 2, got, other, held)
    assemble(held, weights, rows)
    me = idx[0]
    cs, width = cot.shape
    image = lax.broadcasted_iota(jnp.int32, (1, width), 1) // area
    grad = jnp.zeros((cs, width), F32)
    for k, ref in enumerate(pieces):
        tiled = jnp.concatenate([ref[...].astype(F32)] * (width // 128), axis=1)
        grad = jnp.where(image == (me ^ k), tiled, grad)
    cot[...] = grad
    spread_grad(grad, shifted, area, small, OFFSETS, plain_rows)
    push_back(me, weights, shifted, partial, outs)


def gelu_back(idx, *refs):
    pieces = refs[:PEERS]
    normed, params, grad_pre, sums = refs[PEERS:]
    grad = pieces[0][...].astype(F32)
    for ref in pieces[1:]:
        grad += ref[...].astype(F32)
    norm = normed[...]
    g = gelu_slope(params[:, 0:1] * norm + params[:, 1:2]) * grad
    grad_pre[...] = g
    sums[...] = columns(
        (jnp.sum(g * norm, axis=1, keepdims=True), jnp.sum(g, axis=1, keepdims=True)),
        g.shape[0],
    )


def norm_back(nt, added, last, area, small, idx, *refs):
    grad_pre, normed, scales, params, narrow = refs[:5]
    sums = refs[5 : 5 + nt]
    rest = refs[5 + nt :]
    base, rest = (rest[0], rest[1:]) if added else (None, rest)
    me = idx[0]
    cs, width = grad_pre.shape
    order = rest[-1]
    got = in_order(sums, idx[1], order)
    total = got[0]
    for g in got[1:]:
        total = total + g
    gain_grad, shift_grad = total[:, 0:1], total[:, 1:2]
    norm = normed[...]
    back = params[:, 0:1] * scales[:, 0:1] * (
        grad_pre[...]
        - narrow[0:1, :] * (shift_grad + norm * gain_grad) / scales[:, 1:2]
    )
    if added:
        back = base[...] + back
    grad = back.astype(BF16).astype(F32)
    if not last:
        weights, sums_out, shifted = rest[:3]
        outs, partial = rest[3 : 3 + PEERS], rest[3 + PEERS]
        if added:
            grad_out, outs, partial = rest[3], rest[4 : 4 + PEERS], rest[4 + PEERS]
            grad_out[...] = grad.astype(BF16)
        sums_out[...] = total
        spread_grad(grad, shifted, area, small, OFFSETS, plain_rows)
        push_back(me, weights, shifted, partial, outs)
    else:
        weights, grad_skip, sums_out, shifted = rest[:4]
        outs, partial = rest[4 : 4 + PEERS], rest[4 + PEERS]
        sums_out[...] = total
        spread_grad(grad, shifted, area, small, STRIDED[:9], row_of)
        shifted[row_of(9, cs), :] = grad_skip[...]
        for phase in range(4):
            partial[phase] = lax.dot_general(
                shifted[phase_rows(phase, cs), :],
                weights[phase_rows(phase, cs), :],
                (((0,), (0,)), ((), ())),
                preferred_element_type=F32,
            )
        for k, out in enumerate(outs):
            for phase in range(4):
                out[phase * area : (phase + 1) * area, :] = partial[
                    phase, rows_at(me ^ k, area), :
                ].astype(BF16)


def part_halves(core, units, own, other):
    own[...] = units[core]
    other[...] = units[1 - core].astype(BF16)


def weight_grad(rows, idx, shifted, act, own, other, full, units):
    full[...] = lax.dot_general(
        shifted[...], act[...], (((1,), (1,)), ((), ())), preferred_element_type=F32
    )
    ny, cs, span = own.shape
    tiles = full.shape[1] // 128
    for v in range(2 * ny):
        begin = rows * v % 128
        parts = []
        for q in range((begin + rows + 127) // 128):
            k, p = divmod(rows * v // 128 + q, tiles)
            parts.append(full[k * cs : (k + 1) * cs, p * 128 : (p + 1) * 128])
        window = jnp.concatenate(parts, axis=1)
        units[v % 2, v // 2] = moved(window, begin)[:, :span]
    part_halves(idx[2] % 2, units, own, other)


def weight_grad_first(rows, extra, idx, shifted, act, own, other, flat, units):
    ny, cs, span = own.shape
    c_in = act.shape[2]
    flat[...] = jnp.zeros_like(flat)
    skip = None
    for phase in range(4):
        group = jnp.dot(
            shifted[phase_rows(phase, cs), :], act[phase], preferred_element_type=F32
        ).astype(BF16)
        for at, k in enumerate(PHASES[phase]):
            grad = group[at * cs : (at + 1) * cs]
            if k == 9:
                skip = grad
                continue
            begin = k * c_in
            base = begin // 128 * 128
            reach = -(-(begin + c_in) // 128) * 128
            move = one_hot(c_in, reach - base, begin - base)
            flat[:, base:reach] += jnp.dot(grad, move, preferred_element_type=F32)
    lane = lax.broadcasted_iota(jnp.int32, (1, span), 1)
    for v in range(2 * ny):
        begin = rows * v % 128
        base = rows * v - begin
        window = moved(flat[:, base : base + span + 128], begin)[:, :span]
        row = lax.broadcasted_iota(jnp.int32, (c_in, span), 0)
        col = lax.broadcasted_iota(jnp.int32, (c_in, span), 1)
        place = (row >= extra * v) & (row < extra * (v + 1)) & (col == row - extra * v + rows)
        tail = pick32(skip, place.astype(BF16))
        units[v % 2, v // 2] = jnp.where(lane < rows, window, 0.0) + tail
    part_halves(idx[2] % 2, units, own, other)


def add_half(idx, own, other, out):
    out[...] = (own[...] + other[...].astype(F32)).astype(BF16)


def fold(nz, fy, idx, got, out):
    cs = got.shape[1]
    for f in range(fy):
        total = got[f].astype(F32)
        for z in range(1, nz):
            total += got[z * fy + f].astype(F32)
        out[f * cs : (f + 1) * cs, :] = total.astype(BF16)


def own_rows(count, idx, *refs):
    pieces, outs, stack = refs[:count], refs[count:-1], refs[-1]
    for k, ref in enumerate(pieces):
        at = idx[2] ^ k
        stack[at % 2, at // 2] = ref[...]
    sides = stack.shape[1]
    for half in range(2):
        whole = jnp.concatenate([stack[half, x].astype(F32) for x in range(sides)], axis=0).T
        begin = 0
        for out in outs:
            rows = out.shape[0] // 2
            out[half * rows : (half + 1) * rows, :] = whole[begin : begin + rows]
            begin += rows


def entry_back(small, idx, *refs):
    pieces = refs[:PEERS]
    image, norm, gain, shift, grad_pre, sums = refs[PEERS:]
    c_in = gain.shape[1]
    side = 2 * small
    grad = pieces[0][...].astype(F32)
    for ref in pieces[1:]:
        grad += ref[...].astype(F32)
    order = pixel_order(small, side * side, lambda y, x: y * side + x)
    high = grad.astype(BF16)
    low = (grad - high.astype(F32)).astype(BF16)
    grad = sum(
        lax.dot_general(order, part, (((0,), (0,)), ((), ())), preferred_element_type=F32)
        for part in (high, low)
    )
    normed = (image[...].astype(F32) - norm[0:1, :c_in]) * norm[1:2, :c_in]
    g = gelu_slope(gain[...] * normed + shift[...]) * grad
    grad_pre[...] = g
    sums[...] = jnp.zeros_like(sums)
    sums[0:1, :c_in] = jnp.sum(g * normed, axis=0, keepdims=True)
    sums[1:2, :c_in] = jnp.sum(g, axis=0, keepdims=True)


def bundle(idx, first, second, third, sums, out):
    cs = first.shape[0]
    tiles = sums.shape[1] // 128
    out[0:8, :] = jnp.zeros((8, 128), F32)
    for r in range(2):
        for q in range(tiles):
            k = r * tiles + q
            out[k : k + 1, :] = sums[r : r + 1, q * 128 : (q + 1) * 128]
    out[8:, :] = columns(
        [v for ref in (first, second, third) for v in (ref[:, 0:1], ref[:, 1:2])], cs
    )


def unbundle(idx, *refs):
    pieces = refs[:PEERS]
    out, six, order, stack = refs[PEERS:]
    got = in_order(pieces, idx[0], order)
    cs = stack.shape[0] // PEERS
    total = got[0][0:8]
    for g in got[1:]:
        total = total + g[0:8]
    out[...] = total
    for k, g in enumerate(got):
        stack[k * cs : (k + 1) * cs, :] = g[8:]
    six[...] = stack[...].T[0:8]


def entry_grad(nt, idx, *refs):
    sums = refs[:nt]
    grad_pre, image, weight, norm, gain, gain_grad, shift_grad, out, order = refs[nt:]
    got = in_order(sums, idx[1], order)
    total = got[0]
    for g in got[1:]:
        total = total + g
    lanes = gain_grad.shape[1]
    tiles = lanes // 128
    for q in range(tiles):
        gain_grad[0:1, q * 128 : (q + 1) * 128] = total[q : q + 1]
        shift_grad[0:1, q * 128 : (q + 1) * 128] = total[tiles + q : tiles + q + 1]
    c_in = gain.shape[1]
    scale = norm[1:2, :c_in]
    normed = (image[...].astype(F32) - norm[0:1, :c_in]) * scale
    out[...] = gain[...] * scale * (
        grad_pre[...]
        - weight[:, 0:1]
        * (shift_grad[0:1, :c_in] + normed * gain_grad[0:1, :c_in])
        / norm[2:3, :c_in]
    )


def program(
    nx,
    ny,
    images,
    valid_count,
    pixel_mask,
    gain_entry,
    shift_entry,
    conv_first,
    gain_middle,
    shift_middle,
    conv_second,
    projection,
    gain_inner,
    shift_inner,
    conv_third,
    gain_last,
    shift_last,
    conv_fourth,
    cotangent,
):
    fy = PEERS // (nx // 2)
    nz = ny // fy
    nt = 2 * nz
    side, c_in = images.shape[1], images.shape[3]
    small = side // 2
    area = small * small
    c_out = conv_first.shape[1]
    cs = c_out // PEERS
    width = PEERS * area
    lanes = c_in + 64
    gx, gy = lax.axis_index("gx"), lax.axis_index("gy")
    me = gx // 2 * fy + gy % fy
    mine = gy // fy * 2 + gx % 2
    idx = jnp.stack([me, mine, gx, gy]).astype(jnp.int32)

    def device(s, t):
        return (s // fy * 2 + t % 2) * ny + t // 2 * fy + s % fy

    def to_slice(piece, k):
        perm = [(device(s, t), device(s ^ k, t)) for s in range(PEERS) for t in range(nt)]
        return lax.ppermute(piece, ("gx", "gy"), perm)

    def share(pieces):
        return [pieces[0]] + [to_slice(pieces[k], k) for k in range(1, PEERS)]

    def spread_out(piece):
        held = {0: piece}
        for k in (4, 2, 1):
            held[k] = to_slice(piece, k)
        held[6] = to_slice(held[2], 4)
        held[3] = to_slice(held[1], 2)
        held[5] = to_slice(held[4], 1)
        held[7] = to_slice(held[3], 4)
        return [held[k] for k in range(PEERS)]

    def pool(piece):
        out = [piece]
        for k in range(1, nt):
            perm = [(device(s, t), device(s, t ^ k)) for s in range(PEERS) for t in range(nt)]
            out.append(lax.ppermute(piece, ("gx", "gy"), perm))
        return out

    def after(value, *others):
        return lax.optimization_barrier((value, *others))[0]

    def turn(block):
        return lax.all_to_all(block, "gy", 0, 0, tiled=True)

    def across(block):
        return lax.ppermute(block, "gx", [(i, i ^ 1) for i in range(nx)])

    unit_first, unit_skip = conv_first.shape[0] // 2, projection.shape[0] // 2
    unit_mid = conv_second.shape[0] // 2
    span_first, span_mid = span_of(unit_first + unit_skip), span_of(unit_mid)

    def fetch(span, *weights):
        out = call(
            functools.partial(entry_weights, cs, fy),
            shape((ny, cs, span), BF16),
            [idx, *weights],
        )
        got = turn(out)
        return [got, across(got)]

    def halves(span):
        return pltpu.VMEM((2, ny, cs, span), BF16)

    pixels = images.reshape(side * side, c_in)
    image, wide = pl.pallas_call(
        functools.partial(entry_image, small),
        out_shape=[shape((4 * area, lanes), BF16), shape((4 * area, 128))],
        in_specs=[SMEM, VMEM, VMEM, SMEM],
        out_specs=[VMEM, VMEM],
        compiler_params=pltpu.CompilerParams(vmem_limit_bytes=12 * 1024 * 1024),
        cost_estimate=pl.CostEstimate(flops=1 << 20, bytes_accessed=1 << 20, transcendentals=0),
    )(idx, pixels, pixel_mask.reshape(side, side), valid_count)
    group = spread_out(image)
    got_first = fetch(span_first, after(conv_first, image), projection)

    def own(gain, shift):
        pair = jnp.stack([gain, shift], axis=1)
        return lax.dynamic_slice_in_dim(pair, me * cs, cs, axis=0)

    p_middle = own(gain_middle, shift_middle)
    p_inner = own(gain_inner, shift_inner)
    p_last = own(gain_last, shift_last)
    g_entry, s_entry = gain_entry[None], shift_entry[None]

    tile = shape((cs, width))
    tile16 = shape((cs, width), BF16)
    stat = shape((cs, 128))
    stat_order = pltpu.VMEM((nt, cs, 128), F32)
    full16 = shape((c_out, width), BF16)
    whole16 = shape((9 * cs, c_out), BF16)
    conv_flops = 2 * 9 * cs * c_out * width

    stats = call(functools.partial(entry_stats, area), shape((8, lanes)), [idx, *group])
    got_second = fetch(span_mid, after(conv_second, stats))
    first, skipped, stats, norm_one, narrow, act_one, w_first = call(
        functools.partial(entry_block, nt, unit_first, unit_skip, area, small),
        [
            tile,
            tile,
            stat,
            shape((8, lanes)),
            shape((8, width)),
            shape((4, width, c_in), BF16),
            shape((10 * cs, c_in), BF16),
        ],
        [idx, *group, *pool(stats), g_entry, s_entry, *got_first],
        [
            pltpu.VMEM((nt, 8, lanes), F32),
            pltpu.VMEM((width, lanes), BF16),
            pltpu.VMEM((cs, span_of(9 * c_in)), BF16),
            halves(span_first),
        ],
        flops=conv_flops // 2,
    )
    got_third = fetch(span_mid, after(conv_third, stats))

    cot_parts = call(
        split_cotangent,
        [shape((cs, 128), BF16)] * PEERS,
        [idx, after(cotangent, stats).reshape(area, c_out)],
        [pltpu.VMEM((c_out, 2 * area), F32)],
    )
    cot_parts = share(cot_parts)

    def activate(value, params, stats):
        return call(
            functools.partial(act_block, nt),
            [tile16, tile, stat],
            [idx, value, params, *pool(stats)],
            [stat_order],
        )

    def convolve(act, weights, base, last=False):
        more = [] if base is None else [base]
        if last:
            outs = [shape((cs, 128), BF16)] * PEERS + [full16]
        else:
            outs = [tile, stat, full16, whole16]
        return call(
            functools.partial(conv_block, base is not None, last, unit_mid, area, small),
            outs,
            [idx, *spread_out(act), narrow, *weights, *more],
            [pltpu.VMEM((9 * cs, width), F32)] + ([] if last else [halves(span_mid)]),
            flops=conv_flops,
        )

    act, normed_two, scale_two = activate(first, p_middle, stats)
    hidden, stats, act_two, w_second = convolve(act, got_second, skipped)
    got_fourth = fetch(span_mid, after(conv_fourth, stats))
    act, normed_three, scale_three = activate(hidden, p_inner, stats)
    third, stats, act_three, w_third = convolve(act, got_third, None)
    act, normed_four, scale_four = activate(third, p_last, stats)

    cot, shifted_four, w_fourth, *parts = call(
        functools.partial(last_back, unit_mid, area, small),
        [tile, shape((9 * cs, width), BF16), whole16] + [tile16] * PEERS,
        [idx, *cot_parts, *got_fourth],
        [pltpu.VMEM((c_out, width), F32), halves(span_mid)],
        flops=conv_flops,
    )

    def slope(parts, normed, params):
        return call(gelu_back, [tile, stat], [idx, *share(parts), normed, params])

    def back(grad_pre, normed, scales, params, pooled, weights, base):
        more = [] if base is None else [base]
        outs = [stat, shape((9 * cs, width), BF16)] + ([] if base is None else [tile16])
        return call(
            functools.partial(norm_back, nt, base is not None, False, area, small),
            outs + [tile16] * PEERS,
            [idx, grad_pre, normed, scales, params, narrow, *pooled, *more, weights],
            [pltpu.VMEM((c_out, width), F32), stat_order],
            flops=conv_flops,
        )

    def send_grad(kernel, span, shifted, act, scratch):
        own, other = call(
            kernel,
            [shape((ny, cs, span)), shape((ny, cs, span), BF16)],
            [idx, shifted, act],
            [scratch, pltpu.VMEM((2, ny, cs, span), F32)],
            flops=conv_flops,
        )
        both = call(add_half, shape((ny, cs, span), BF16), [idx, own, across(other)])
        return turn(both)

    def send_mid(shifted, act):
        kernel = functools.partial(weight_grad, unit_mid)
        return send_grad(kernel, span_mid, shifted, act, pltpu.VMEM((9 * cs, c_out), F32))

    def land_grad(got, *rows):
        span = got.shape[2]
        got = call(functools.partial(fold, nz, fy), shape((fy * cs, span), BF16), [idx, got])
        pieces = {0: got}
        for k in range(2, nx, 2):
            pieces[k] = lax.ppermute(got, "gx", [(i, i ^ k) for i in range(nx)])
        for k in range(0, nx, 2):
            pieces[k + 1] = across(pieces[k])
        return call(
            functools.partial(own_rows, nx),
            [shape((r, c_out)) for r in rows],
            [idx, *[pieces[k] for k in range(nx)]],
            [pltpu.VMEM((2, nx // 2, fy * cs, span), BF16)],
        )

    grad_pre, sums = slope(parts, normed_four, p_last)
    pooled = pool(sums)
    *out_parts, act_four = convolve(act, [w_fourth], hidden, last=True)

    last_sums, shifted_three, *parts = back(
        grad_pre, normed_four, scale_four, p_last, pooled, w_third, None
    )
    sent_fourth = send_mid(shifted_four, act_four)
    grad_pre, sums = slope(parts, normed_three, p_inner)
    inner_sums, shifted_two, grad_hidden, *parts = back(
        grad_pre, normed_three, scale_three, p_inner, pool(sums), w_second, cot
    )
    sent_third = send_mid(shifted_three, act_three)
    grad_pre, sums = slope(parts, normed_two, p_middle)
    middle_sums, shifted_one, *parts = call(
        functools.partial(norm_back, nt, False, True, area, small),
        [stat, shape((10 * cs, width), BF16)] + [shape((4 * area, c_in), BF16)] * PEERS,
        [idx, grad_pre, normed_two, scale_two, p_middle, narrow, *pool(sums), w_first, grad_hidden],
        [pltpu.VMEM((4, width, c_in), F32), stat_order],
        flops=conv_flops // 2,
    )
    sent_second = send_mid(shifted_two, act_two)
    parts = share(parts)
    sent_first = send_grad(
        functools.partial(weight_grad_first, unit_first, unit_skip),
        span_first,
        shifted_one,
        act_one,
        pltpu.VMEM((cs, span_of(9 * c_in + span_first + 128)), F32),
    )
    (fourth_grad,) = land_grad(sent_fourth, 2 * unit_mid)
    (third_grad,) = land_grad(sent_third, 2 * unit_mid)
    (second_grad,) = land_grad(sent_second, 2 * unit_mid)
    first_grad, skip_grad = land_grad(sent_first, 2 * unit_first, 2 * unit_skip)

    padded = -(-c_in // 128) * 128
    grad_pre, sums = call(
        functools.partial(entry_back, small),
        [shape((4 * area, c_in)), shape((8, padded))],
        [idx, *parts, pixels, norm_one, g_entry, s_entry],
    )
    message = call(
        bundle, shape((8 + cs, 128)), [idx, middle_sums, inner_sums, last_sums, sums]
    )
    sums, six = call(
        unbundle,
        [shape((8, 128)), shape((8, c_out))],
        [idx, *spread_out(message)],
        [pltpu.VMEM((PEERS, 8 + cs, 128), F32), pltpu.VMEM((c_out, 128), F32)],
    )
    gain_entry_grad, shift_entry_grad, image_grad = call(
        functools.partial(entry_grad, nt),
        [shape((1, padded)), shape((1, padded)), shape((4 * area, c_in))],
        [idx, *pool(sums), grad_pre, pixels, wide, norm_one, g_entry],
        [pltpu.VMEM((nt, 8, 128), F32)],
    )

    out = call(
        join_result,
        shape((area, c_out), BF16),
        [idx, *share(out_parts)],
        [pltpu.VMEM((c_out, 128), F32)],
    )
    return (
        out.reshape(1, small, small, c_out),
        image_grad.reshape(1, side, side, c_in),
        gain_entry_grad[0, :c_in],
        shift_entry_grad[0, :c_in],
        first_grad,
        six[0],
        six[1],
        second_grad,
        skip_grad,
        six[2],
        six[3],
        third_grad,
        six[4],
        six[5],
        fourth_grad,
    )


def solution(mesh):
    whole = P(("gx", "gy"), None, None, None)
    rows = P("gy", None)
    return jax.shard_map(
        functools.partial(program, mesh.shape["gx"], mesh.shape["gy"]),
        mesh=mesh,
        in_specs=(
            whole,
            P(("gx", "gy")),
            P(("gx", "gy"), None, None),
            P(),
            P(),
            rows,
            P(),
            P(),
            rows,
            rows,
            P(),
            P(),
            rows,
            P(),
            P(),
            rows,
            whole,
        ),
        out_specs=(
            whole, whole, P(), P(), rows, P(), P(), rows, rows, P(), P(), rows, P(), P(), rows,
        ),
        check_vma=False,
    )
```

```python
import functools

import jax
import jax.numpy as jnp
from jax import lax
from jax.experimental import pallas as pl
from jax.experimental.pallas import tpu as pltpu
from jax.sharding import PartitionSpec as P

EPS = 1e-05
F32 = jnp.float32
BF16 = jnp.bfloat16
PEERS = 4
C0 = 0.7978845608028654
C1 = 0.044715
VMEM = pl.BlockSpec(memory_space=pltpu.VMEM)
SMEM = pl.BlockSpec(memory_space=pltpu.SMEM)


def gelu(v):
    return 0.5 * v * (1.0 + jnp.tanh(C0 * (v + C1 * (v * v * v))))


def gelu_slope(v):
    t = jnp.tanh(C0 * (v + C1 * (v * v * v)))
    return 0.5 * (1.0 + t) + 0.5 * v * (1.0 - t * t) * (C0 * (1.0 + 3.0 * C1 * (v * v)))


def call(kernel, outs, args, scratch=(), flops=1 << 20):
    size = sum(a.size * a.dtype.itemsize for a in args)
    return pl.pallas_call(
        kernel,
        out_shape=outs,
        in_specs=[SMEM] + [VMEM] * (len(args) - 1),
        out_specs=jax.tree.map(lambda _: VMEM, outs),
        scratch_shapes=list(scratch),
        compiler_params=pltpu.CompilerParams(vmem_limit_bytes=16 * 1024 * 1024),
        cost_estimate=pl.CostEstimate(flops=flops, bytes_accessed=size, transcendentals=0),
    )(*args)


def shape(dims, dtype=F32):
    return jax.ShapeDtypeStruct(dims, dtype)


def rows_at(index, count):
    return pl.ds(pl.multiple_of(index * count, count), count)


def as_rows(parts):
    height = parts[0].shape[0]
    lane = lax.broadcasted_iota(jnp.int32, (height, 128), 1)
    out = jnp.zeros((height, 128), F32)
    for k, part in enumerate(parts):
        out = jnp.where(lane == k, part, out)
    return out.T[0:8]


def as_columns(rows):
    return jnp.concatenate([rows, jnp.zeros((120, rows.shape[1]), F32)], axis=0).T


def in_order(refs, me, scratch):
    for k, ref in enumerate(refs):
        scratch[me ^ k] = ref[...]
    return [scratch[k] for k in range(len(refs))]


def merge_moments(stats):
    total = sum(n for _, _, n in stats)
    mean = sum(n * m for m, _, n in stats) / total
    squares = sum(q + n * (m - mean) * (m - mean) for m, q, n in stats)
    return mean, squares, total


def merge_rows(refs):
    mean, squares, total = merge_moments([(g[0:1], g[1:2], g[2:3]) for g in refs])
    return mean, squares, total, sum(g[3:4] for g in refs)


def pixel(width, area, small):
    lane = lax.broadcasted_iota(jnp.int32, (1, width), 1) % area
    return lane // small, lane % small


def inside(row, col, drow, dcol, small):
    return (row + drow >= 0) & (row + drow < small) & (col + dcol >= 0) & (col + dcol < small)


def moved(value, step):
    shift = (-step) % value.shape[1]
    return pltpu.roll(value, shift, 1) if shift else value


OFFSETS = [(0, krow - 1, kcol - 1) for krow in range(3) for kcol in range(3)]

STRIDED = [
    ((krow != 1) * 2 + (kcol != 1), -(krow == 0), -(kcol == 0))
    for krow in range(3)
    for kcol in range(3)
] + [(0, 0, 0)]
PLACED = sorted(range(10), key=lambda k: (STRIDED[k][0], k))
PHASES = [[k for k in PLACED if STRIDED[k][0] == phase] for phase in range(4)]


def row_of(k, cs):
    at = PLACED.index(k)
    return slice(at * cs, (at + 1) * cs)


def phase_rows(phase, cs):
    first, last = PHASES[phase][0], PHASES[phase][-1]
    return slice(PLACED.index(first) * cs, (PLACED.index(last) + 1) * cs)


def masked_stats(value, weight, n):
    mean = jnp.sum(value * weight, axis=1, keepdims=True) / n
    centred = value - mean
    return mean, jnp.sum(weight * centred * centred, axis=1, keepdims=True)


def span_of(rows):
    return -(-rows // 128) * 128


def one_hot(height, width, shift):
    row = lax.broadcasted_iota(jnp.int32, (height, width), 0)
    col = lax.broadcasted_iota(jnp.int32, (height, width), 1)
    return (col == row + shift).astype(BF16)


def pick32(left, right, dims=((1,), (0,))):
    return lax.dot_general(left, right, (dims, ((), ())), preferred_element_type=F32)


def pick(left, right, dims=((1,), (0,))):
    return pick32(left, right, dims).astype(BF16)


def lane_tile(held, tile, rows, span):
    sides, ny = held.shape[1], held.shape[2]
    lane = lax.broadcasted_iota(jnp.int32, (1, 128), 1)
    out = None
    for v in range(2 * ny):
        begin = rows * v - tile * 128
        if begin >= 128 or begin + rows <= 0:
            continue
        at = (tile - rows * v // 128) * 128 % span
        part = jnp.concatenate(
            [held[v % 2, x, v // 2, :, at : at + 128].astype(F32) for x in range(sides)], axis=0
        )
        if begin > 0 or begin + rows < 128:
            own = (lane >= begin) & (lane < begin + rows)
            part = jnp.where(own, part, 0.0)
        out = part if out is None else out + part
    return out.astype(BF16)


def pixel_order(small, width, of):
    area = small * small
    row = lax.broadcasted_iota(jnp.int32, (4 * area, width), 0)
    col = lax.broadcasted_iota(jnp.int32, (4 * area, width), 1)
    phase, pix = row // area, row % area
    y = 2 * (pix // small) + phase // 2
    x = 2 * (pix % small) + phase % 2
    return (col == of(y, x)).astype(BF16)


def entry_image(small, idx, image, mask, valid, out, weight):
    side = 2 * small
    c_in = image.shape[1]
    count = side * side
    order = pixel_order(small, count, lambda y, x: y * side + x)
    out[:, :c_in] = pick(order, image[...])
    live = (valid[0] > 0).astype(F32)
    row = lax.broadcasted_iota(jnp.int32, (count, side), 0)
    col = lax.broadcasted_iota(jnp.int32, (count, side), 1)
    by_row = jnp.dot(
        (row // side == col).astype(BF16),
        mask[...].astype(F32).astype(BF16),
        preferred_element_type=F32,
    )
    column = jnp.sum(jnp.where(row % side == col, by_row, 0.0), axis=1, keepdims=True) * live
    lane = lax.broadcasted_iota(jnp.int32, (count, 128), 1)
    spread = jnp.where(lane == 0, column, 0.0)
    weight[...] = spread
    out[:, c_in:] = pick(order, spread.astype(BF16))[:, : out.shape[1] - c_in]


def entry_weights(cs, fy, idx, *refs):
    weights, out = refs[:-1], refs[-1]
    ny, cb, span = out.shape
    gx, gy = idx[2], idx[3]
    core, side = gx % 2, gx // 2
    c_out = weights[0].shape[1]
    unit = weights[0].shape[0] // 2
    begin = unit * (2 * gy + core) % 128
    row = lax.broadcasted_iota(jnp.int32, (fy * cb, c_out), 0)
    col = lax.broadcasted_iota(jnp.int32, (fy * cb, c_out), 1)
    chosen = (col == row // cb * cs + side * cb + row % cb).astype(BF16)
    total = None
    for weight in weights:
        rows = weight.shape[0]
        half = rows // 2
        mine = pick(chosen, weight[...], ((1,), (1,)))
        row = lax.broadcasted_iota(jnp.int32, (rows, span), 0) - core * half
        col = lax.broadcasted_iota(jnp.int32, (rows, span), 1)
        place = (row >= 0) & (row < half) & (
            (col == row + begin) | (col == row + begin - span)
        )
        part = pick32(mine, place.astype(BF16))
        total = part if total is None else total + part
        begin = begin + half
    for j in range(ny):
        out[j] = total[(j % fy) * cb : (j % fy + 1) * cb].astype(BF16)


def hold(gx, messages, held):
    for k, ref in enumerate(messages):
        at = gx ^ k
        held[at % 2, at // 2] = ref[...]


def assemble(held, out, rows):
    cs, span = held.shape[1] * held.shape[3], held.shape[4]
    tiles = out.shape[1] // 128
    for k in range(9):
        for q in range(tiles):
            out[k * cs : (k + 1) * cs, q * 128 : (q + 1) * 128] = lane_tile(
                held, tiles * k + q, rows, span
            )


def assemble_first(held, out, flat, rows, extra):
    cs, span = held.shape[1] * held.shape[3], held.shape[4]
    c_in = out.shape[1]
    tiles = flat.shape[1] // 128
    for tile in range(tiles):
        flat[:, tile * 128 : (tile + 1) * 128] = lane_tile(held, tile, rows, span)
    for k in range(9):
        begin = k * c_in
        base = begin // 128 * 128
        reach = min(-(-(begin + c_in) // 128) * 128, flat.shape[1])
        move = one_hot(c_in, reach - base, begin - base)
        out[row_of(k, cs), :] = pick(flat[:, base:reach], move, ((1,), (1,)))
    total = None
    for v in range(2 * held.shape[2]):
        row = lax.broadcasted_iota(jnp.int32, (span, c_in), 0)
        col = lax.broadcasted_iota(jnp.int32, (span, c_in), 1)
        at = col - extra * v
        begin = rows * v % 128 + rows
        place = (at >= 0) & (at < extra) & ((row == at + begin) | (row == at + begin - span))
        part = jnp.concatenate(
            [
                pick32(held[v % 2, x, v // 2], place.astype(BF16))
                for x in range(held.shape[1])
            ],
            axis=0,
        )
        total = part if total is None else total + part
    out[row_of(9, cs), :] = total.astype(BF16)


def entry_stats(area, idx, *refs):
    images, out = refs[:PEERS], refs[PEERS]
    lanes = out.shape[1]
    first = jnp.zeros((1, lanes), F32)
    wide = jnp.zeros((1, 1), F32)
    narrow = jnp.zeros((1, 1), F32)
    c_in = lanes - 64
    for ref in images:
        x = ref[...].astype(F32)
        w = x[:, c_in : c_in + 1]
        first += jnp.sum(x * w, axis=0, keepdims=True)
        wide += jnp.sum(w, axis=0, keepdims=True)
        narrow += jnp.sum(w[:area], axis=0, keepdims=True)
    mean = first / wide
    squares = jnp.zeros((1, lanes), F32)
    for ref in images:
        x = ref[...].astype(F32)
        w = x[:, c_in : c_in + 1]
        d = x - mean
        squares += jnp.sum(d * d * w, axis=0, keepdims=True)
    out[...] = jnp.zeros_like(out)
    out[0:1, :] = mean
    out[1:2, :] = squares
    out[2:3, :] = jnp.broadcast_to(wide, (1, lanes))
    out[3:4, :] = jnp.broadcast_to(narrow, (1, lanes))


def entry_block(nz, nx, rows, extra, area, small, idx, *refs):
    images = refs[:PEERS]
    stats, rest = refs[PEERS : PEERS + nz], refs[PEERS + nz :]
    gain, shift, messages, rest = rest[0], rest[1], rest[2 : 2 + nx], rest[2 + nx :]
    first, skipped, out_stats, norm, narrow, act, w_first = rest[:7]
    order, masks, flat, held = rest[7:]
    me, mine = idx[0], idx[1]
    c_in = gain.shape[1]
    lanes = norm.shape[1]
    cs = first.shape[0]
    width = first.shape[1]
    hold(idx[2], messages, held)
    assemble_first(held, w_first, flat, rows, extra)
    mean, squares, total, count = merge_rows(in_order(stats, mine, order))
    scale = lax.rsqrt(squares / total + EPS)
    norm[...] = jnp.zeros_like(norm)
    norm[0:1, :] = mean
    norm[1:2, :] = scale
    norm[2:3, :] = total
    norm[3:4, :] = count
    for k, ref in enumerate(images):
        x = ref[...]
        v = x[:, :c_in].astype(F32)
        pre = gain[...] * ((v - mean[:, :c_in]) * scale[:, :c_in]) + shift[...]
        a = gelu(pre).astype(BF16)
        for phase in range(4):
            act[phase, rows_at(me ^ k, area), :] = a[phase * area : (phase + 1) * area]
        masks[rows_at(me ^ k, area), :] = x[:area]
    ones = (lax.broadcasted_iota(jnp.int32, (8, lanes), 1) == c_in).astype(BF16)
    weight8 = lax.dot_general(
        ones, masks[...], (((1,), (1,)), ((), ())), preferred_element_type=F32
    )
    narrow[...] = weight8
    weight = weight8[0:1]
    row, col = pixel(width, area, small)
    total_first = jnp.zeros((cs, width), F32)
    for phase in range(4):
        group = lax.dot_general(
            w_first[phase_rows(phase, cs), :],
            act[phase],
            (((1,), (1,)), ((), ())),
            preferred_element_type=F32,
        )
        for at, k in enumerate(PHASES[phase]):
            y = group[at * cs : (at + 1) * cs]
            if k == 9:
                skipped[...] = y
                continue
            _, drow, dcol = STRIDED[k]
            y = moved(y, drow * small + dcol)
            total_first += jnp.where(inside(row, col, drow, dcol, small), y, 0.0)
    first[...] = total_first
    n = jnp.sum(weight, axis=1, keepdims=True)
    mean2, squares = masked_stats(total_first, weight, n)
    out_stats[...] = as_rows((mean2, squares, n))


def merge_stats(idx, *refs):
    out, order = refs[-2:]
    mean, squares, total, count = merge_rows(in_order(refs[:-2], idx[2], order))
    out[...] = jnp.zeros_like(out)
    out[0:1] = mean
    out[1:2] = squares
    out[2:3] = total
    out[3:4] = count


def add_rows(which, idx, *refs):
    out, order = refs[-2:]
    got = in_order(refs[:-2], idx[which], order)
    total = got[0]
    for g in got[1:]:
        total = total + g
    out[...] = total


def act_block(nz, idx, *refs):
    value, params = refs[:2]
    stats = refs[2 : 2 + nz]
    act, normed, scales, order = refs[2 + nz :]
    mean, squares, total, _ = merge_rows(in_order(stats, idx[1], order))
    rows = jnp.concatenate(
        [mean, lax.rsqrt(squares / total + EPS), total, jnp.zeros((5, mean.shape[1]), F32)], axis=0
    )
    cols = as_columns(rows)
    norm = (value[...] - cols[:, 0:1]) * cols[:, 1:2]
    normed[...] = norm
    act[...] = gelu(params[:, 0:1] * norm + params[:, 1:2]).astype(BF16)
    scales[...] = cols


def conv_block(nx, added, last, rows, area, small, idx, *refs):
    pieces = refs[:PEERS]
    narrow, rest = refs[PEERS], refs[PEERS + 1 :]
    if last:
        weights, rest = rest[0], rest[1:]
    else:
        messages, rest = rest[:nx], rest[nx:]
    base, rest = (rest[0], rest[1:]) if added else (None, rest)
    me = idx[0]
    cs, width = pieces[0].shape
    if last:
        outs, act, spread = rest[:PEERS], rest[PEERS], rest[PEERS + 1]
    else:
        value, out_stats, act, whole, spread, held = rest
        hold(idx[2], messages, held)
        assemble(held, whole, rows)
        weights = whole
    for k, ref in enumerate(pieces):
        act[rows_at(me ^ k, cs), :] = ref[...]
    spread[...] = jnp.dot(weights[...], act[...], preferred_element_type=F32)
    row, col = pixel(width, area, small)
    total = base[...] if added else jnp.zeros((cs, width), F32)
    for k, (_, drow, dcol) in enumerate(OFFSETS):
        y = moved(spread[k * cs : (k + 1) * cs, :], drow * small + dcol)
        total += jnp.where(inside(row, col, drow, dcol, small), y, 0.0)
    if last:
        result = total.astype(BF16)
        lane = lax.broadcasted_iota(jnp.int32, (width, 128), 0)
        slot = lax.broadcasted_iota(jnp.int32, (width, 128), 1)
        for k, out in enumerate(outs):
            out[...] = pick(result, (lane == (me ^ k) * area + slot).astype(BF16))
    else:
        value[...] = total
        weight = narrow[0:1, :]
        n = jnp.sum(weight, axis=1, keepdims=True)
        mean, squares = masked_stats(total, weight, n)
        out_stats[...] = as_rows((mean, squares, n))


def join_result(idx, *refs):
    pieces, (out, stack) = refs[:PEERS], refs[PEERS:]
    cs = pieces[0].shape[0]
    for k, ref in enumerate(pieces):
        stack[rows_at(idx[0] ^ k, cs), :] = ref[...].astype(F32)
    out[...] = stack[...].T[: out.shape[0]].astype(BF16)


def split_cotangent(idx, *refs):
    cot, outs, stack = refs[0], refs[1 : 1 + PEERS], refs[1 + PEERS]
    c = cot[...].astype(F32)
    stack[...] = jnp.concatenate([c, c], axis=0).T
    cs = outs[0].shape[0]
    for k, out in enumerate(outs):
        out[...] = stack[rows_at(idx[0] ^ k, cs), :].astype(BF16)


def spread_grad(grad, shifted, area, small, offs, row_at):
    cs, width = grad.shape
    row, col = pixel(width, area, small)
    for k, (_, drow, dcol) in enumerate(offs):
        g = moved(grad, -(drow * small + dcol))
        g = jnp.where(inside(row, col, -drow, -dcol, small), g, 0.0)
        shifted[row_at(k, cs), :] = g.astype(BF16)


def plain_rows(k, cs):
    return slice(k * cs, (k + 1) * cs)


def push_back(me, weights, shifted, partial, outs):
    cs = outs[0].shape[0]
    partial[...] = lax.dot_general(
        weights[...], shifted[...], (((0,), (0,)), ((), ())), preferred_element_type=F32
    )
    for k, out in enumerate(outs):
        out[...] = partial[rows_at(me ^ k, cs), :].astype(BF16)


def last_back(nx, rows, area, small, idx, *refs):
    pieces, messages, rest = refs[:PEERS], refs[PEERS : PEERS + nx], refs[PEERS + nx :]
    cot, shifted, weights = rest[:3]
    outs = rest[3 : PEERS + 3]
    partial, held = rest[PEERS + 3 :]
    hold(idx[2], messages, held)
    assemble(held, weights, rows)
    me = idx[0]
    cs, width = cot.shape
    image = lax.broadcasted_iota(jnp.int32, (1, width), 1) // area
    grad = jnp.zeros((cs, width), F32)
    for k, ref in enumerate(pieces):
        tiled = jnp.concatenate([ref[...].astype(F32)] * (width // 128), axis=1)
        grad = jnp.where(image == (me ^ k), tiled, grad)
    cot[...] = grad
    spread_grad(grad, shifted, area, small, OFFSETS, plain_rows)
    push_back(me, weights, shifted, partial, outs)


def gelu_back(idx, *refs):
    pieces = refs[:PEERS]
    normed, params, grad_pre, sums = refs[PEERS:]
    grad = pieces[0][...].astype(F32)
    for ref in pieces[1:]:
        grad += ref[...].astype(F32)
    norm = normed[...]
    g = gelu_slope(params[:, 0:1] * norm + params[:, 1:2]) * grad
    grad_pre[...] = g
    sums[...] = as_rows(
        (jnp.sum(g * norm, axis=1, keepdims=True), jnp.sum(g, axis=1, keepdims=True))
    )


def norm_back(nz, added, last, area, small, idx, *refs):
    grad_pre, normed, scales, params, narrow = refs[:5]
    sums = refs[5 : 5 + nz]
    rest = refs[5 + nz :]
    base, rest = (rest[0], rest[1:]) if added else (None, rest)
    me = idx[0]
    cs, width = grad_pre.shape
    order = rest[-1]
    got = in_order(sums, idx[1], order)
    total = got[0]
    for g in got[1:]:
        total = total + g
    cols = as_columns(total)
    gain_grad, shift_grad = cols[:, 0:1], cols[:, 1:2]
    norm = normed[...]
    back = params[:, 0:1] * scales[:, 1:2] * (
        grad_pre[...]
        - narrow[0:1, :] * (shift_grad + norm * gain_grad) / scales[:, 2:3]
    )
    if added:
        back = base[...] + back
    grad = back.astype(BF16).astype(F32)
    if not last:
        weights, sums_out, shifted = rest[:3]
        outs, partial = rest[3 : 3 + PEERS], rest[3 + PEERS]
        if added:
            grad_out, outs, partial = rest[3], rest[4 : 4 + PEERS], rest[4 + PEERS]
            grad_out[...] = grad.astype(BF16)
        sums_out[...] = total
        spread_grad(grad, shifted, area, small, OFFSETS, plain_rows)
        push_back(me, weights, shifted, partial, outs)
    else:
        weights, grad_skip, sums_out, shifted = rest[:4]
        outs, partial = rest[4 : 4 + PEERS], rest[4 + PEERS]
        sums_out[...] = total
        spread_grad(grad, shifted, area, small, STRIDED[:9], row_of)
        shifted[row_of(9, cs), :] = grad_skip[...]
        for phase in range(4):
            partial[phase] = lax.dot_general(
                shifted[phase_rows(phase, cs), :],
                weights[phase_rows(phase, cs), :],
                (((0,), (0,)), ((), ())),
                preferred_element_type=F32,
            )
        for k, out in enumerate(outs):
            for phase in range(4):
                out[phase * area : (phase + 1) * area, :] = partial[
                    phase, rows_at(me ^ k, area), :
                ].astype(BF16)


def part_halves(core, units, own, other):
    own[...] = units[core]
    other[...] = units[1 - core].astype(BF16)


def weight_grad(rows, idx, shifted, act, own, other, full, units):
    full[...] = lax.dot_general(
        shifted[...], act[...], (((1,), (1,)), ((), ())), preferred_element_type=F32
    )
    ny, cs, span = own.shape
    tiles = full.shape[1] // 128
    for v in range(2 * ny):
        begin = rows * v % 128
        parts = []
        for q in range((begin + rows + 127) // 128):
            k, p = divmod(rows * v // 128 + q, tiles)
            parts.append(full[k * cs : (k + 1) * cs, p * 128 : (p + 1) * 128])
        window = jnp.concatenate(parts, axis=1)
        units[v % 2, v // 2] = moved(window, begin)[:, :span]
    part_halves(idx[2] % 2, units, own, other)


def weight_grad_first(rows, extra, idx, shifted, act, own, other, flat, units):
    ny, cs, span = own.shape
    c_in = act.shape[2]
    flat[...] = jnp.zeros_like(flat)
    skip = None
    for phase in range(4):
        group = jnp.dot(
            shifted[phase_rows(phase, cs), :], act[phase], preferred_element_type=F32
        ).astype(BF16)
        for at, k in enumerate(PHASES[phase]):
            grad = group[at * cs : (at + 1) * cs]
            if k == 9:
                skip = grad
                continue
            begin = k * c_in
            base = begin // 128 * 128
            reach = -(-(begin + c_in) // 128) * 128
            move = one_hot(c_in, reach - base, begin - base)
            flat[:, base:reach] += jnp.dot(grad, move, preferred_element_type=F32)
    lane = lax.broadcasted_iota(jnp.int32, (1, span), 1)
    for v in range(2 * ny):
        begin = rows * v % 128
        base = rows * v - begin
        window = moved(flat[:, base : base + span + 128], begin)[:, :span]
        row = lax.broadcasted_iota(jnp.int32, (c_in, span), 0)
        col = lax.broadcasted_iota(jnp.int32, (c_in, span), 1)
        place = (row >= extra * v) & (row < extra * (v + 1)) & (col == row - extra * v + rows)
        tail = pick32(skip, place.astype(BF16))
        units[v % 2, v // 2] = jnp.where(lane < rows, window, 0.0) + tail
    part_halves(idx[2] % 2, units, own, other)


def reduce_core(count, idx, *refs):
    own, other, outs, total = refs[:count], refs[count : 2 * count], refs[2 * count : -1], refs[-1]
    cb = outs[0].shape[1]
    at = 0
    for a, b in zip(own, other):
        span = a.shape[2]
        total[:, :, at : at + span] = a[...] + b[...].astype(F32)
        at += span
    for k, out in enumerate(outs):
        for j in range(total.shape[0]):
            out[j] = total[j, rows_at(idx[2] // 2 ^ k, cb), :].astype(out.dtype)


def reduce_side(idx, *refs):
    total = refs[0][...]
    for ref in refs[1:-1]:
        total += ref[...].astype(F32)
    refs[-1][...] = total.astype(BF16)


def fold(nz, fy, idx, got, out):
    cs = got.shape[1]
    for f in range(fy):
        total = got[f].astype(F32)
        for z in range(1, nz):
            total += got[z * fy + f].astype(F32)
        out[f * cs : (f + 1) * cs, :] = total.astype(BF16)


def own_rows(count, spans, idx, *refs):
    pieces, outs, stack = refs[:count], refs[count:-1], refs[-1]
    for k, ref in enumerate(pieces):
        at = idx[2] ^ k
        stack[at % 2, at // 2] = ref[...]
    sides, height = stack.shape[1], stack.shape[2]
    fy_cb = [(f, x) for f in range(PEERS) for x in range(sides)]
    cb = height // PEERS
    for half in range(2):
        whole = jnp.concatenate(
            [stack[half, x, f * cb : (f + 1) * cb, :].astype(F32) for f, x in fy_cb], axis=0
        ).T
        at = 0
        for span, group in spans:
            begin = at
            for n in group:
                out = outs[n]
                rows = out.shape[0] // 2
                out[half * rows : (half + 1) * rows, :] = whole[begin : begin + rows]
                begin += rows
            at += span


def entry_back(small, idx, *refs):
    pieces = refs[:PEERS]
    image, norm, gain, shift, grad_pre, sums = refs[PEERS:]
    c_in = gain.shape[1]
    side = 2 * small
    grad = pieces[0][...].astype(F32)
    for ref in pieces[1:]:
        grad += ref[...].astype(F32)
    order = pixel_order(small, side * side, lambda y, x: y * side + x)
    high = grad.astype(BF16)
    low = (grad - high.astype(F32)).astype(BF16)
    grad = sum(
        lax.dot_general(order, part, (((0,), (0,)), ((), ())), preferred_element_type=F32)
        for part in (high, low)
    )
    normed = (image[...].astype(F32) - norm[0:1, :c_in]) * norm[1:2, :c_in]
    g = gelu_slope(gain[...] * normed + shift[...]) * grad
    grad_pre[...] = g
    sums[...] = jnp.zeros_like(sums)
    sums[0:1, :c_in] = jnp.sum(g * normed, axis=0, keepdims=True)
    sums[1:2, :c_in] = jnp.sum(g, axis=0, keepdims=True)


def bundle(idx, first, second, third, sums, out):
    out[...] = jnp.zeros_like(out)
    out[0:8, :] = sums[...]
    for k, ref in enumerate((first, second, third)):
        out[8 + 2 * k : 10 + 2 * k, : ref.shape[1]] = ref[0:2]


def unbundle(idx, *refs):
    out, six, order = refs[-3:]
    got = in_order(refs[:-3], idx[0], order)
    total = got[0][0:8]
    for g in got[1:]:
        total = total + g[0:8]
    out[...] = total
    cs = six.shape[1] // PEERS
    six[...] = jnp.concatenate([g[8:16, :cs] for g in got], axis=1)


def entry_grad(nz, idx, *refs):
    sums = refs[:nz]
    grad_pre, image, weight, norm, gain, gain_grad, shift_grad, out, order = refs[nz:]
    got = in_order(sums, idx[1], order)
    total = got[0]
    for g in got[1:]:
        total = total + g
    gain_grad[...] = total[0:1]
    shift_grad[...] = total[1:2]
    c_in = gain.shape[1]
    scale = norm[1:2, :c_in]
    normed = (image[...].astype(F32) - norm[0:1, :c_in]) * scale
    out[...] = gain[...] * scale * (
        grad_pre[...]
        - weight[:, 0:1]
        * (shift_grad[0:1, :c_in] + normed * gain_grad[0:1, :c_in])
        / norm[2:3, :c_in]
    )


def program(
    nx,
    ny,
    images,
    valid_count,
    pixel_mask,
    gain_entry,
    shift_entry,
    conv_first,
    gain_middle,
    shift_middle,
    conv_second,
    projection,
    gain_inner,
    shift_inner,
    conv_third,
    gain_last,
    shift_last,
    conv_fourth,
    cotangent,
):
    fy = PEERS
    nz = ny // fy
    side, c_in = images.shape[1], images.shape[3]
    small = side // 2
    area = small * small
    c_out = conv_first.shape[1]
    cs = c_out // PEERS
    width = PEERS * area
    lanes = c_in + 64
    gx, gy = lax.axis_index("gx"), lax.axis_index("gy")
    me = gy % fy
    mine = gy // fy
    idx = jnp.stack([me, mine, gx, gy]).astype(jnp.int32)

    def to_slice(piece, k):
        return lax.ppermute(piece, "gy", [(j, j // fy * fy + (j % fy ^ k)) for j in range(ny)])

    def share(pieces):
        return [pieces[0]] + [to_slice(pieces[k], k) for k in range(1, PEERS)]

    def spread_out(piece):
        return share([piece] * PEERS)

    def to_gx(piece, k):
        return lax.ppermute(piece, "gx", [(i, i ^ k) for i in range(nx)])

    def pool(piece, kernel):
        pieces = [piece] + [to_gx(piece, k) for k in range(1, nx)]
        piece = call(
            kernel,
            shape(piece.shape),
            [idx, *pieces],
            [pltpu.VMEM((nx, *piece.shape), F32)],
        )
        out = [piece]
        for k in range(1, nz):
            perm = [(j, (j // fy ^ k) * fy + j % fy) for j in range(ny)]
            out.append(lax.ppermute(piece, "gy", perm))
        return out

    add_gx = functools.partial(add_rows, 2)

    def after(value, *others):
        return lax.optimization_barrier((value, *others))[0]

    def turn(block):
        return lax.all_to_all(block, "gy", 0, 0, tiled=True)

    def along_gx(block):
        held = {0: block}
        for k in range(2, nx, 2):
            held[k] = to_gx(block, k)
        for k in range(0, nx, 2):
            held[k + 1] = to_gx(held[k], 1)
        return [held[k] for k in range(nx)]

    unit_first, unit_skip = conv_first.shape[0] // 2, projection.shape[0] // 2
    unit_mid = conv_second.shape[0] // 2
    span_first, span_mid = span_of(unit_first + unit_skip), span_of(unit_mid)

    cb = cs // (nx // 2)

    def fetch(span, *weights):
        out = call(
            functools.partial(entry_weights, cs, fy),
            shape((ny, cb, span), BF16),
            [idx, *weights],
        )
        return along_gx(turn(out))

    def halves(span):
        return pltpu.VMEM((2, nx // 2, ny, cb, span), BF16)

    pixels = images.reshape(side * side, c_in)
    image, wide = pl.pallas_call(
        functools.partial(entry_image, small),
        out_shape=[shape((4 * area, lanes), BF16), shape((4 * area, 128))],
        in_specs=[SMEM, VMEM, VMEM, SMEM],
        out_specs=[VMEM, VMEM],
        compiler_params=pltpu.CompilerParams(vmem_limit_bytes=16 * 1024 * 1024),
        cost_estimate=pl.CostEstimate(flops=1 << 20, bytes_accessed=1 << 20, transcendentals=0),
    )(idx, pixels, pixel_mask.reshape(side, side), valid_count)
    group = spread_out(image)
    got_first = fetch(span_first, after(conv_first, image), projection)

    def own(gain, shift):
        pair = jnp.stack([gain, shift], axis=1)
        return lax.dynamic_slice_in_dim(pair, me * cs, cs, axis=0)

    p_middle = own(gain_middle, shift_middle)
    p_inner = own(gain_inner, shift_inner)
    p_last = own(gain_last, shift_last)
    g_entry, s_entry = gain_entry[None], shift_entry[None]

    tile = shape((cs, width))
    tile16 = shape((cs, width), BF16)
    cols = shape((cs, 128))
    stat = shape((8, cs))
    stat_order = pltpu.VMEM((nz, 8, cs), F32)
    full16 = shape((c_out, width), BF16)
    whole16 = shape((9 * cs, c_out), BF16)
    conv_flops = 2 * 9 * cs * c_out * width

    stats = call(functools.partial(entry_stats, area), shape((8, lanes)), [idx, *group])
    got_second = fetch(span_mid, after(conv_second, image))
    pooled = pool(stats, merge_stats)
    got_third = fetch(span_mid, after(conv_third, pooled[0]))
    first, skipped, stats, norm_one, narrow, act_one, w_first = call(
        functools.partial(entry_block, nz, nx, unit_first, unit_skip, area, small),
        [
            tile,
            tile,
            stat,
            shape((8, lanes)),
            shape((8, width)),
            shape((4, width, c_in), BF16),
            shape((10 * cs, c_in), BF16),
        ],
        [idx, *group, *pooled, g_entry, s_entry, *got_first],
        [
            pltpu.VMEM((nz, 8, lanes), F32),
            pltpu.VMEM((width, lanes), BF16),
            pltpu.VMEM((cs, span_of(9 * c_in)), BF16),
            halves(span_first),
        ],
        flops=conv_flops // 2,
    )

    cot_parts = call(
        split_cotangent,
        [shape((cs, 128), BF16)] * PEERS,
        [idx, after(cotangent, stats).reshape(area, c_out)],
        [pltpu.VMEM((c_out, 2 * area), F32)],
    )
    cot_parts = share(cot_parts)

    def activate(value, params, pooled):
        return call(
            functools.partial(act_block, nz),
            [tile16, tile, cols],
            [idx, value, params, *pooled],
            [stat_order],
        )

    def convolve(act, weights, base, last=False):
        more = [] if base is None else [base]
        if last:
            outs = [shape((cs, 128), BF16)] * PEERS + [full16]
        else:
            outs = [tile, stat, full16, whole16]
        return call(
            functools.partial(conv_block, nx, base is not None, last, unit_mid, area, small),
            outs,
            [idx, *spread_out(act), narrow, *weights, *more],
            [pltpu.VMEM((9 * cs, width), F32)] + ([] if last else [halves(span_mid)]),
            flops=conv_flops,
        )

    pooled = pool(stats, merge_stats)
    got_fourth = fetch(span_mid, after(conv_fourth, pooled[0]))
    act, normed_two, scale_two = activate(first, p_middle, pooled)
    hidden, stats, act_two, w_second = convolve(act, got_second, skipped)
    act, normed_three, scale_three = activate(hidden, p_inner, pool(stats, merge_stats))
    third, stats, act_three, w_third = convolve(act, got_third, None)
    act, normed_four, scale_four = activate(third, p_last, pool(stats, merge_stats))

    cot, shifted_four, w_fourth, *parts = call(
        functools.partial(last_back, nx, unit_mid, area, small),
        [tile, shape((9 * cs, width), BF16), whole16] + [tile16] * PEERS,
        [idx, *cot_parts, *got_fourth],
        [pltpu.VMEM((c_out, width), F32), halves(span_mid)],
        flops=conv_flops,
    )

    def slope(parts, normed, params):
        return call(gelu_back, [tile, stat], [idx, *share(parts), normed, params])

    def back(grad_pre, normed, scales, params, pooled, weights, base):
        more = [] if base is None else [base]
        outs = [stat, shape((9 * cs, width), BF16)] + ([] if base is None else [tile16])
        return call(
            functools.partial(norm_back, nz, base is not None, False, area, small),
            outs + [tile16] * PEERS,
            [idx, grad_pre, normed, scales, params, narrow, *pooled, *more, weights],
            [pltpu.VMEM((c_out, width), F32), stat_order],
            flops=conv_flops,
        )

    def grad_of(kernel, span, shifted, act, scratch):
        return call(
            kernel,
            [shape((ny, cs, span)), shape((ny, cs, span), BF16)],
            [idx, shifted, act],
            [scratch, pltpu.VMEM((2, ny, cs, span), F32)],
            flops=conv_flops,
        )

    def grad_mid(shifted, act):
        kernel = functools.partial(weight_grad, unit_mid)
        return grad_of(kernel, span_mid, shifted, act, pltpu.VMEM((9 * cs, c_out), F32))

    def send_grads(*grads):
        own = [a for a, _ in grads]
        other = [to_gx(b, 1) for _, b in grads]
        span = sum(a.shape[2] for a in own)
        sides = nx // 2
        parts = call(
            functools.partial(reduce_core, len(own)),
            [shape((ny, cb, span))] + [shape((ny, cb, span), BF16)] * (sides - 1),
            [idx, *own, *other],
            [pltpu.VMEM((ny, cs, span), F32)],
        )
        parts = [parts[0]] + [to_gx(parts[k], 2 * k) for k in range(1, sides)]
        return turn(call(reduce_side, shape((ny, cb, span), BF16), [idx, *parts]))

    def land_grads(got, spans, *rows):
        span = got.shape[2]
        got = call(functools.partial(fold, nz, fy), shape((fy * cb, span), BF16), [idx, got])
        return call(
            functools.partial(own_rows, nx, spans),
            [shape((r, c_out)) for r in rows],
            [idx, *along_gx(got)],
            [pltpu.VMEM((2, nx // 2, fy * cb, span), BF16)],
        )

    grad_pre, sums = slope(parts, normed_four, p_last)
    pooled = pool(sums, add_gx)
    *out_parts, act_four = convolve(act, [w_fourth], hidden, last=True)

    last_sums, shifted_three, *parts = back(
        grad_pre, normed_four, scale_four, p_last, pooled, w_third, None
    )
    grad_pre, sums = slope(parts, normed_three, p_inner)
    inner_sums, shifted_two, grad_hidden, *parts = back(
        grad_pre, normed_three, scale_three, p_inner, pool(sums, add_gx), w_second, cot
    )
    sent_late = send_grads(grad_mid(shifted_four, act_four), grad_mid(shifted_three, act_three))
    grad_pre, sums = slope(parts, normed_two, p_middle)
    middle_sums, shifted_one, *parts = call(
        functools.partial(norm_back, nz, False, True, area, small),
        [stat, shape((10 * cs, width), BF16)] + [shape((4 * area, c_in), BF16)] * PEERS,
        [idx, grad_pre, normed_two, scale_two, p_middle, narrow, *pool(sums, add_gx), w_first, grad_hidden],
        [pltpu.VMEM((4, width, c_in), F32), stat_order],
        flops=conv_flops // 2,
    )
    parts = share(parts)
    grad_first = grad_of(
        functools.partial(weight_grad_first, unit_first, unit_skip),
        span_first,
        shifted_one,
        act_one,
        pltpu.VMEM((cs, span_of(9 * c_in + span_first + 128)), F32),
    )
    sent_early = send_grads(grad_mid(shifted_two, act_two), grad_first)
    fourth_grad, third_grad = land_grads(
        sent_late, ((span_mid, (0,)), (span_mid, (1,))), 2 * unit_mid, 2 * unit_mid
    )
    second_grad, first_grad, skip_grad = land_grads(
        sent_early,
        ((span_mid, (0,)), (span_first, (1, 2))),
        2 * unit_mid,
        2 * unit_first,
        2 * unit_skip,
    )

    padded = -(-c_in // 128) * 128
    grad_pre, sums = call(
        functools.partial(entry_back, small),
        [shape((4 * area, c_in)), shape((8, padded))],
        [idx, *parts, pixels, norm_one, g_entry, s_entry],
    )
    message = call(
        bundle, shape((16, padded)), [idx, middle_sums, inner_sums, last_sums, sums]
    )
    sums, six = call(
        unbundle,
        [shape((8, padded)), shape((8, c_out))],
        [idx, *spread_out(message)],
        [pltpu.VMEM((PEERS, 16, padded), F32)],
    )
    gain_entry_grad, shift_entry_grad, image_grad = call(
        functools.partial(entry_grad, nz),
        [shape((1, padded)), shape((1, padded)), shape((4 * area, c_in))],
        [idx, *pool(sums, add_gx), grad_pre, pixels, wide, norm_one, g_entry],
        [pltpu.VMEM((nz, 8, padded), F32)],
    )

    out = call(
        join_result,
        shape((area, c_out), BF16),
        [idx, *share(out_parts)],
        [pltpu.VMEM((c_out, 128), F32)],
    )
    return (
        out.reshape(1, small, small, c_out),
        image_grad.reshape(1, side, side, c_in),
        gain_entry_grad[0, :c_in],
        shift_entry_grad[0, :c_in],
        first_grad,
        six[0],
        six[1],
        second_grad,
        skip_grad,
        six[2],
        six[3],
        third_grad,
        six[4],
        six[5],
        fourth_grad,
    )


def solution(mesh):
    whole = P(("gx", "gy"), None, None, None)
    rows = P("gy", None)
    return jax.shard_map(
        functools.partial(program, mesh.shape["gx"], mesh.shape["gy"]),
        mesh=mesh,
        in_specs=(
            whole,
            P(("gx", "gy")),
            P(("gx", "gy"), None, None),
            P(),
            P(),
            rows,
            P(),
            P(),
            rows,
            rows,
            P(),
            P(),
            rows,
            P(),
            P(),
            rows,
            whole,
        ),
        out_specs=(
            whole, whole, P(), P(), rows, P(), P(), rows, rows, P(), P(), rows, P(), P(), rows,
        ),
        check_vma=False,
    )
```

```python
import functools

import jax
import jax.numpy as jnp
from jax import lax
from jax.experimental import pallas as pl
from jax.experimental.pallas import tpu as pltpu
from jax.sharding import PartitionSpec as P

EPS = 1e-05
F32 = jnp.float32
BF16 = jnp.bfloat16
PEERS = 4
C0 = 0.7978845608028654
C1 = 0.044715
VMEM = pl.BlockSpec(memory_space=pltpu.VMEM)
SMEM = pl.BlockSpec(memory_space=pltpu.SMEM)


def gelu(v):
    return 0.5 * v * (1.0 + jnp.tanh(C0 * (v + C1 * (v * v * v))))


def gelu_slope(v):
    t = jnp.tanh(C0 * (v + C1 * (v * v * v)))
    return 0.5 * (1.0 + t) + 0.5 * v * (1.0 - t * t) * (C0 * (1.0 + 3.0 * C1 * (v * v)))


def call(kernel, outs, args, scratch=(), flops=8 * 10**8):
    size = sum(a.size * a.dtype.itemsize for a in args)
    return pl.pallas_call(
        kernel,
        out_shape=outs,
        in_specs=[SMEM] + [VMEM] * (len(args) - 1),
        out_specs=jax.tree.map(lambda _: VMEM, outs),
        scratch_shapes=list(scratch),
        compiler_params=pltpu.CompilerParams(vmem_limit_bytes=16 * 1024 * 1024),
        cost_estimate=pl.CostEstimate(flops=flops, bytes_accessed=size, transcendentals=0),
    )(*args)


def shape(dims, dtype=F32):
    return jax.ShapeDtypeStruct(dims, dtype)


def rows_at(index, count):
    return pl.ds(pl.multiple_of(index * count, count), count)


def as_rows(parts):
    height = parts[0].shape[0]
    lane = lax.broadcasted_iota(jnp.int32, (height, 128), 1)
    out = jnp.zeros((height, 128), F32)
    for k, part in enumerate(parts):
        out = jnp.where(lane == k, part, out)
    return out.T[0:8]


def as_columns(rows):
    return jnp.concatenate([rows, jnp.zeros((120, rows.shape[1]), F32)], axis=0).T


def in_order(refs, me, scratch):
    for k, ref in enumerate(refs):
        scratch[me ^ k] = ref[...]
    return [scratch[k] for k in range(len(refs))]


def merge_moments(stats):
    total = sum(n for _, _, n in stats)
    mean = sum(n * m for m, _, n in stats) / total
    squares = sum(q + n * (m - mean) * (m - mean) for m, q, n in stats)
    return mean, squares, total


def merge_rows(refs):
    mean, squares, total = merge_moments([(g[0:1], g[1:2], g[2:3]) for g in refs])
    return mean, squares, total, sum(g[3:4] for g in refs)


def pixel(width, area, small):
    lane = lax.broadcasted_iota(jnp.int32, (1, width), 1) % area
    return lane // small, lane % small


def inside(row, col, drow, dcol, small):
    return (row + drow >= 0) & (row + drow < small) & (col + dcol >= 0) & (col + dcol < small)


def moved(value, step):
    shift = (-step) % value.shape[1]
    return pltpu.roll(value, shift, 1) if shift else value


OFFSETS = [(0, krow - 1, kcol - 1) for krow in range(3) for kcol in range(3)]

STRIDED = [
    ((krow != 1) * 2 + (kcol != 1), -(krow == 0), -(kcol == 0))
    for krow in range(3)
    for kcol in range(3)
] + [(0, 0, 0)]
PLACED = sorted(range(10), key=lambda k: (STRIDED[k][0], k))
PHASES = [[k for k in PLACED if STRIDED[k][0] == phase] for phase in range(4)]


def row_of(k, cs):
    at = PLACED.index(k)
    return slice(at * cs, (at + 1) * cs)


def phase_rows(phase, cs):
    first, last = PHASES[phase][0], PHASES[phase][-1]
    return slice(PLACED.index(first) * cs, (PLACED.index(last) + 1) * cs)


def masked_stats(value, weight, n):
    mean = jnp.sum(value * weight, axis=1, keepdims=True) / n
    centred = value - mean
    return mean, jnp.sum(weight * centred * centred, axis=1, keepdims=True)


def span_of(rows):
    return -(-rows // 128) * 128


def one_hot(height, width, shift):
    row = lax.broadcasted_iota(jnp.int32, (height, width), 0)
    col = lax.broadcasted_iota(jnp.int32, (height, width), 1)
    return (col == row + shift).astype(BF16)


def pick32(left, right, dims=((1,), (0,))):
    return lax.dot_general(left, right, (dims, ((), ())), preferred_element_type=F32)


def pick(left, right, dims=((1,), (0,))):
    return pick32(left, right, dims).astype(BF16)


def lane_tile(held, tile, rows, span):
    sides, ny = held.shape[1], held.shape[2]
    lane = lax.broadcasted_iota(jnp.int32, (1, 128), 1)
    out = None
    for v in range(2 * ny):
        begin = rows * v - tile * 128
        if begin >= 128 or begin + rows <= 0:
            continue
        at = (tile - rows * v // 128) * 128 % span
        part = jnp.concatenate(
            [held[v % 2, x, v // 2, :, at : at + 128].astype(F32) for x in range(sides)], axis=0
        )
        if begin > 0 or begin + rows < 128:
            own = (lane >= begin) & (lane < begin + rows)
            part = jnp.where(own, part, 0.0)
        out = part if out is None else out + part
    return out.astype(BF16)


def pixel_order(small, width, of):
    area = small * small
    row = lax.broadcasted_iota(jnp.int32, (4 * area, width), 0)
    col = lax.broadcasted_iota(jnp.int32, (4 * area, width), 1)
    phase, pix = row // area, row % area
    y = 2 * (pix // small) + phase // 2
    x = 2 * (pix % small) + phase % 2
    return (col == of(y, x)).astype(BF16)


def entry_image(small, idx, image, mask, valid, out, weight):
    side = 2 * small
    c_in = image.shape[1]
    count = side * side
    order = pixel_order(small, count, lambda y, x: y * side + x)
    out[:, :c_in] = pick(order, image[...])
    live = (valid[0] > 0).astype(F32)
    row = lax.broadcasted_iota(jnp.int32, (count, side), 0)
    col = lax.broadcasted_iota(jnp.int32, (count, side), 1)
    by_row = jnp.dot(
        (row // side == col).astype(BF16),
        mask[...].astype(F32).astype(BF16),
        preferred_element_type=F32,
    )
    column = jnp.sum(jnp.where(row % side == col, by_row, 0.0), axis=1, keepdims=True) * live
    lane = lax.broadcasted_iota(jnp.int32, (count, 128), 1)
    spread = jnp.where(lane == 0, column, 0.0)
    weight[...] = spread
    out[:, c_in:] = pick(order, spread.astype(BF16))[:, : out.shape[1] - c_in]


def entry_weights(cs, fy, idx, *refs):
    weights, out = refs[:-1], refs[-1]
    ny, cb, span = out.shape
    gx, gy = idx[2], idx[3]
    core, side = gx % 2, gx // 2
    c_out = weights[0].shape[1]
    unit = weights[0].shape[0] // 2
    begin = unit * (2 * gy + core) % 128
    row = lax.broadcasted_iota(jnp.int32, (fy * cb, c_out), 0)
    col = lax.broadcasted_iota(jnp.int32, (fy * cb, c_out), 1)
    chosen = (col == row // cb * cs + side * cb + row % cb).astype(BF16)
    total = None
    for weight in weights:
        rows = weight.shape[0]
        half = rows // 2
        mine = pick(chosen, weight[...], ((1,), (1,)))
        row = lax.broadcasted_iota(jnp.int32, (rows, span), 0) - core * half
        col = lax.broadcasted_iota(jnp.int32, (rows, span), 1)
        place = (row >= 0) & (row < half) & (
            (col == row + begin) | (col == row + begin - span)
        )
        part = pick32(mine, place.astype(BF16))
        total = part if total is None else total + part
        begin = begin + half
    for j in range(ny):
        out[j] = total[(j % fy) * cb : (j % fy + 1) * cb].astype(BF16)


def hold(gx, messages, held):
    for k, ref in enumerate(messages):
        at = gx ^ k
        held[at % 2, at // 2] = ref[...]


def assemble(held, out, rows):
    cs, span = held.shape[1] * held.shape[3], held.shape[4]
    tiles = out.shape[1] // 128
    for k in range(9):
        for q in range(tiles):
            out[k * cs : (k + 1) * cs, q * 128 : (q + 1) * 128] = lane_tile(
                held, tiles * k + q, rows, span
            )


def assemble_first(held, out, flat, rows, extra):
    cs, span = held.shape[1] * held.shape[3], held.shape[4]
    c_in = out.shape[1]
    tiles = flat.shape[1] // 128
    for tile in range(tiles):
        flat[:, tile * 128 : (tile + 1) * 128] = lane_tile(held, tile, rows, span)
    for k in range(9):
        begin = k * c_in
        base = begin // 128 * 128
        reach = min(-(-(begin + c_in) // 128) * 128, flat.shape[1])
        move = one_hot(c_in, reach - base, begin - base)
        out[row_of(k, cs), :] = pick(flat[:, base:reach], move, ((1,), (1,)))
    total = None
    for v in range(2 * held.shape[2]):
        row = lax.broadcasted_iota(jnp.int32, (span, c_in), 0)
        col = lax.broadcasted_iota(jnp.int32, (span, c_in), 1)
        at = col - extra * v
        begin = rows * v % 128 + rows
        place = (at >= 0) & (at < extra) & ((row == at + begin) | (row == at + begin - span))
        part = jnp.concatenate(
            [
                pick32(held[v % 2, x, v // 2], place.astype(BF16))
                for x in range(held.shape[1])
            ],
            axis=0,
        )
        total = part if total is None else total + part
    out[row_of(9, cs), :] = total.astype(BF16)


def entry_stats(area, idx, *refs):
    images, out = refs[:PEERS], refs[PEERS]
    lanes = out.shape[1]
    first = jnp.zeros((1, lanes), F32)
    wide = jnp.zeros((1, 1), F32)
    narrow = jnp.zeros((1, 1), F32)
    c_in = lanes - 64
    for ref in images:
        x = ref[...].astype(F32)
        w = x[:, c_in : c_in + 1]
        first += jnp.sum(x * w, axis=0, keepdims=True)
        wide += jnp.sum(w, axis=0, keepdims=True)
        narrow += jnp.sum(w[:area], axis=0, keepdims=True)
    mean = first / wide
    squares = jnp.zeros((1, lanes), F32)
    for ref in images:
        x = ref[...].astype(F32)
        w = x[:, c_in : c_in + 1]
        d = x - mean
        squares += jnp.sum(d * d * w, axis=0, keepdims=True)
    out[...] = jnp.zeros_like(out)
    out[0:1, :] = mean
    out[1:2, :] = squares
    out[2:3, :] = jnp.broadcast_to(wide, (1, lanes))
    out[3:4, :] = jnp.broadcast_to(narrow, (1, lanes))


def entry_block(nz, nx, rows, extra, area, small, idx, *refs):
    images = refs[:PEERS]
    stats, rest = refs[PEERS : PEERS + nz], refs[PEERS + nz :]
    gain, shift, messages, rest = rest[0], rest[1], rest[2 : 2 + nx], rest[2 + nx :]
    first, skipped, out_stats, norm, narrow, act, w_first = rest[:7]
    order, masks, flat, held = rest[7:]
    me, mine = idx[0], idx[1]
    c_in = gain.shape[1]
    lanes = norm.shape[1]
    cs = first.shape[0]
    width = first.shape[1]
    hold(idx[2], messages, held)
    assemble_first(held, w_first, flat, rows, extra)
    mean, squares, total, count = merge_rows(in_order(stats, mine, order))
    scale = lax.rsqrt(squares / total + EPS)
    norm[...] = jnp.zeros_like(norm)
    norm[0:1, :] = mean
    norm[1:2, :] = scale
    norm[2:3, :] = total
    norm[3:4, :] = count
    for k, ref in enumerate(images):
        x = ref[...]
        v = x[:, :c_in].astype(F32)
        pre = gain[...] * ((v - mean[:, :c_in]) * scale[:, :c_in]) + shift[...]
        a = gelu(pre).astype(BF16)
        for phase in range(4):
            act[phase, rows_at(me ^ k, area), :] = a[phase * area : (phase + 1) * area]
        masks[rows_at(me ^ k, area), :] = x[:area]
    ones = (lax.broadcasted_iota(jnp.int32, (8, lanes), 1) == c_in).astype(BF16)
    weight8 = lax.dot_general(
        ones, masks[...], (((1,), (1,)), ((), ())), preferred_element_type=F32
    )
    narrow[...] = weight8
    weight = weight8[0:1]
    row, col = pixel(width, area, small)
    total_first = jnp.zeros((cs, width), F32)
    for phase in range(4):
        group = lax.dot_general(
            w_first[phase_rows(phase, cs), :],
            act[phase],
            (((1,), (1,)), ((), ())),
            preferred_element_type=F32,
        )
        for at, k in enumerate(PHASES[phase]):
            y = group[at * cs : (at + 1) * cs]
            if k == 9:
                skipped[...] = y
                continue
            _, drow, dcol = STRIDED[k]
            y = moved(y, drow * small + dcol)
            total_first += jnp.where(inside(row, col, drow, dcol, small), y, 0.0)
    first[...] = total_first
    n = jnp.sum(weight, axis=1, keepdims=True)
    mean2, squares = masked_stats(total_first, weight, n)
    out_stats[...] = as_rows((mean2, squares, n))


def merge_stats(idx, *refs):
    out, order = refs[-2:]
    mean, squares, total, count = merge_rows(in_order(refs[:-2], idx[2], order))
    out[...] = jnp.zeros_like(out)
    out[0:1] = mean
    out[1:2] = squares
    out[2:3] = total
    out[3:4] = count


def add_rows(which, idx, *refs):
    out, order = refs[-2:]
    got = in_order(refs[:-2], idx[which], order)
    total = got[0]
    for g in got[1:]:
        total = total + g
    out[...] = total


def act_block(nz, idx, *refs):
    value, params = refs[:2]
    stats = refs[2 : 2 + nz]
    act, normed, scales, order = refs[2 + nz :]
    mean, squares, total, _ = merge_rows(in_order(stats, idx[1], order))
    rows = jnp.concatenate(
        [mean, lax.rsqrt(squares / total + EPS), total, jnp.zeros((5, mean.shape[1]), F32)], axis=0
    )
    cols = as_columns(rows)
    norm = (value[...] - cols[:, 0:1]) * cols[:, 1:2]
    normed[...] = norm
    act[...] = gelu(params[:, 0:1] * norm + params[:, 1:2]).astype(BF16)
    scales[...] = cols


def conv_block(nx, added, last, rows, area, small, idx, *refs):
    pieces = refs[:PEERS]
    narrow, rest = refs[PEERS], refs[PEERS + 1 :]
    if last:
        weights, rest = rest[0], rest[1:]
    else:
        messages, rest = rest[:nx], rest[nx:]
    base, rest = (rest[0], rest[1:]) if added else (None, rest)
    me = idx[0]
    cs, width = pieces[0].shape
    if last:
        outs, act, spread = rest[:PEERS], rest[PEERS], rest[PEERS + 1]
    else:
        value, out_stats, act, whole, spread, held = rest
        hold(idx[2], messages, held)
        assemble(held, whole, rows)
        weights = whole
    for k, ref in enumerate(pieces):
        act[rows_at(me ^ k, cs), :] = ref[...]
    spread[...] = jnp.dot(weights[...], act[...], preferred_element_type=F32)
    row, col = pixel(width, area, small)
    total = base[...] if added else jnp.zeros((cs, width), F32)
    for k, (_, drow, dcol) in enumerate(OFFSETS):
        y = moved(spread[k * cs : (k + 1) * cs, :], drow * small + dcol)
        total += jnp.where(inside(row, col, drow, dcol, small), y, 0.0)
    if last:
        result = total.astype(BF16)
        lane = lax.broadcasted_iota(jnp.int32, (width, 128), 0)
        slot = lax.broadcasted_iota(jnp.int32, (width, 128), 1)
        for k, out in enumerate(outs):
            out[...] = pick(result, (lane == (me ^ k) * area + slot).astype(BF16))
    else:
        value[...] = total
        weight = narrow[0:1, :]
        n = jnp.sum(weight, axis=1, keepdims=True)
        mean, squares = masked_stats(total, weight, n)
        out_stats[...] = as_rows((mean, squares, n))


def join_result(idx, *refs):
    pieces, (out, stack) = refs[:PEERS], refs[PEERS:]
    cs = pieces[0].shape[0]
    for k, ref in enumerate(pieces):
        stack[rows_at(idx[0] ^ k, cs), :] = ref[...].astype(F32)
    out[...] = stack[...].T[: out.shape[0]].astype(BF16)


def split_cotangent(idx, *refs):
    cot, outs, stack = refs[0], refs[1 : 1 + PEERS], refs[1 + PEERS]
    c = cot[...].astype(F32)
    stack[...] = jnp.concatenate([c, c], axis=0).T
    cs = outs[0].shape[0]
    for k, out in enumerate(outs):
        out[...] = stack[rows_at(idx[0] ^ k, cs), :].astype(BF16)


def spread_grad(grad, shifted, area, small, offs, row_at):
    cs, width = grad.shape
    row, col = pixel(width, area, small)
    for k, (_, drow, dcol) in enumerate(offs):
        g = moved(grad, -(drow * small + dcol))
        g = jnp.where(inside(row, col, -drow, -dcol, small), g, 0.0)
        shifted[row_at(k, cs), :] = g.astype(BF16)


def plain_rows(k, cs):
    return slice(k * cs, (k + 1) * cs)


def push_back(me, weights, shifted, partial, outs):
    cs = outs[0].shape[0]
    partial[...] = lax.dot_general(
        weights[...], shifted[...], (((0,), (0,)), ((), ())), preferred_element_type=F32
    )
    for k, out in enumerate(outs):
        out[...] = partial[rows_at(me ^ k, cs), :].astype(BF16)


def last_back(nx, rows, area, small, idx, *refs):
    pieces, messages, rest = refs[:PEERS], refs[PEERS : PEERS + nx], refs[PEERS + nx :]
    cot, shifted, weights = rest[:3]
    outs = rest[3 : PEERS + 3]
    partial, held = rest[PEERS + 3 :]
    hold(idx[2], messages, held)
    assemble(held, weights, rows)
    me = idx[0]
    cs, width = cot.shape
    image = lax.broadcasted_iota(jnp.int32, (1, width), 1) // area
    grad = jnp.zeros((cs, width), F32)
    for k, ref in enumerate(pieces):
        tiled = jnp.concatenate([ref[...].astype(F32)] * (width // 128), axis=1)
        grad = jnp.where(image == (me ^ k), tiled, grad)
    cot[...] = grad
    spread_grad(grad, shifted, area, small, OFFSETS, plain_rows)
    push_back(me, weights, shifted, partial, outs)


def gelu_back(idx, *refs):
    pieces = refs[:PEERS]
    normed, params, grad_pre, sums = refs[PEERS:]
    grad = pieces[0][...].astype(F32)
    for ref in pieces[1:]:
        grad += ref[...].astype(F32)
    norm = normed[...]
    g = gelu_slope(params[:, 0:1] * norm + params[:, 1:2]) * grad
    grad_pre[...] = g
    sums[...] = as_rows(
        (jnp.sum(g * norm, axis=1, keepdims=True), jnp.sum(g, axis=1, keepdims=True))
    )


def norm_back(nz, added, last, area, small, idx, *refs):
    grad_pre, normed, scales, params, narrow = refs[:5]
    sums = refs[5 : 5 + nz]
    rest = refs[5 + nz :]
    base, rest = (rest[0], rest[1:]) if added else (None, rest)
    me = idx[0]
    cs, width = grad_pre.shape
    order = rest[-1]
    got = in_order(sums, idx[1], order)
    total = got[0]
    for g in got[1:]:
        total = total + g
    cols = as_columns(total)
    gain_grad, shift_grad = cols[:, 0:1], cols[:, 1:2]
    norm = normed[...]
    back = params[:, 0:1] * scales[:, 1:2] * (
        grad_pre[...]
        - narrow[0:1, :] * (shift_grad + norm * gain_grad) / scales[:, 2:3]
    )
    if added:
        back = base[...] + back
    grad = back.astype(BF16).astype(F32)
    if not last:
        weights, sums_out, shifted = rest[:3]
        outs, partial = rest[3 : 3 + PEERS], rest[3 + PEERS]
        if added:
            grad_out, outs, partial = rest[3], rest[4 : 4 + PEERS], rest[4 + PEERS]
            grad_out[...] = grad.astype(BF16)
        sums_out[...] = total
        spread_grad(grad, shifted, area, small, OFFSETS, plain_rows)
        push_back(me, weights, shifted, partial, outs)
    else:
        weights, grad_skip, sums_out, shifted = rest[:4]
        outs, partial = rest[4 : 4 + PEERS], rest[4 + PEERS]
        sums_out[...] = total
        spread_grad(grad, shifted, area, small, STRIDED[:9], row_of)
        shifted[row_of(9, cs), :] = grad_skip[...]
        for phase in range(4):
            partial[phase] = lax.dot_general(
                shifted[phase_rows(phase, cs), :],
                weights[phase_rows(phase, cs), :],
                (((0,), (0,)), ((), ())),
                preferred_element_type=F32,
            )
        for k, out in enumerate(outs):
            for phase in range(4):
                out[phase * area : (phase + 1) * area, :] = partial[
                    phase, rows_at(me ^ k, area), :
                ].astype(BF16)


def part_halves(core, units, own, other):
    own[...] = units[core]
    other[...] = units[1 - core].astype(BF16)


def weight_grad(rows, idx, shifted, act, own, other, full, units):
    full[...] = lax.dot_general(
        shifted[...], act[...], (((1,), (1,)), ((), ())), preferred_element_type=F32
    )
    ny, cs, span = own.shape
    tiles = full.shape[1] // 128
    for v in range(2 * ny):
        begin = rows * v % 128
        parts = []
        for q in range((begin + rows + 127) // 128):
            k, p = divmod(rows * v // 128 + q, tiles)
            parts.append(full[k * cs : (k + 1) * cs, p * 128 : (p + 1) * 128])
        window = jnp.concatenate(parts, axis=1)
        units[v % 2, v // 2] = moved(window, begin)[:, :span]
    part_halves(idx[2] % 2, units, own, other)


def weight_grad_first(rows, extra, idx, shifted, act, own, other, flat, units):
    ny, cs, span = own.shape
    c_in = act.shape[2]
    flat[...] = jnp.zeros_like(flat)
    skip = None
    for phase in range(4):
        group = jnp.dot(
            shifted[phase_rows(phase, cs), :], act[phase], preferred_element_type=F32
        ).astype(BF16)
        for at, k in enumerate(PHASES[phase]):
            grad = group[at * cs : (at + 1) * cs]
            if k == 9:
                skip = grad
                continue
            begin = k * c_in
            base = begin // 128 * 128
            reach = -(-(begin + c_in) // 128) * 128
            move = one_hot(c_in, reach - base, begin - base)
            flat[:, base:reach] += jnp.dot(grad, move, preferred_element_type=F32)
    lane = lax.broadcasted_iota(jnp.int32, (1, span), 1)
    for v in range(2 * ny):
        begin = rows * v % 128
        base = rows * v - begin
        window = moved(flat[:, base : base + span + 128], begin)[:, :span]
        row = lax.broadcasted_iota(jnp.int32, (c_in, span), 0)
        col = lax.broadcasted_iota(jnp.int32, (c_in, span), 1)
        place = (row >= extra * v) & (row < extra * (v + 1)) & (col == row - extra * v + rows)
        tail = pick32(skip, place.astype(BF16))
        units[v % 2, v // 2] = jnp.where(lane < rows, window, 0.0) + tail
    part_halves(idx[2] % 2, units, own, other)


def reduce_core(count, idx, *refs):
    own, other, outs, total = refs[:count], refs[count : 2 * count], refs[2 * count : -1], refs[-1]
    cb = outs[0].shape[1]
    at = 0
    for a, b in zip(own, other):
        span = a.shape[2]
        total[:, :, at : at + span] = a[...] + b[...].astype(F32)
        at += span
    for k, out in enumerate(outs):
        for j in range(total.shape[0]):
            out[j] = total[j, rows_at(idx[2] // 2 ^ k, cb), :].astype(out.dtype)


def reduce_side(idx, *refs):
    total = refs[0][...]
    for ref in refs[1:-1]:
        total += ref[...].astype(F32)
    refs[-1][...] = total.astype(BF16)


def fold(nz, fy, idx, got, out):
    cs = got.shape[1]
    for f in range(fy):
        total = got[f].astype(F32)
        for z in range(1, nz):
            total += got[z * fy + f].astype(F32)
        out[f * cs : (f + 1) * cs, :] = total.astype(BF16)


def own_rows(count, spans, idx, *refs):
    pieces, outs, stack = refs[:count], refs[count:-1], refs[-1]
    for k, ref in enumerate(pieces):
        at = idx[2] ^ k
        stack[at % 2, at // 2] = ref[...]
    sides, height = stack.shape[1], stack.shape[2]
    fy_cb = [(f, x) for f in range(PEERS) for x in range(sides)]
    cb = height // PEERS
    for half in range(2):
        whole = jnp.concatenate(
            [stack[half, x, f * cb : (f + 1) * cb, :].astype(F32) for f, x in fy_cb], axis=0
        ).T
        at = 0
        for span, group in spans:
            begin = at
            for n in group:
                out = outs[n]
                rows = out.shape[0] // 2
                out[half * rows : (half + 1) * rows, :] = whole[begin : begin + rows]
                begin += rows
            at += span


def entry_back(small, idx, *refs):
    pieces = refs[:PEERS]
    image, norm, gain, shift, grad_pre, sums = refs[PEERS:]
    c_in = gain.shape[1]
    side = 2 * small
    grad = pieces[0][...].astype(F32)
    for ref in pieces[1:]:
        grad += ref[...].astype(F32)
    order = pixel_order(small, side * side, lambda y, x: y * side + x)
    high = grad.astype(BF16)
    low = (grad - high.astype(F32)).astype(BF16)
    grad = sum(
        lax.dot_general(order, part, (((0,), (0,)), ((), ())), preferred_element_type=F32)
        for part in (high, low)
    )
    normed = (image[...].astype(F32) - norm[0:1, :c_in]) * norm[1:2, :c_in]
    g = gelu_slope(gain[...] * normed + shift[...]) * grad
    grad_pre[...] = g
    sums[...] = jnp.zeros_like(sums)
    sums[0:1, :c_in] = jnp.sum(g * normed, axis=0, keepdims=True)
    sums[1:2, :c_in] = jnp.sum(g, axis=0, keepdims=True)


def bundle(idx, first, second, third, sums, out):
    out[...] = jnp.zeros_like(out)
    out[0:8, :] = sums[...]
    for k, ref in enumerate((first, second, third)):
        out[8 + 2 * k : 10 + 2 * k, : ref.shape[1]] = ref[0:2]


def unbundle(idx, *refs):
    out, six, order = refs[-3:]
    got = in_order(refs[:-3], idx[0], order)
    total = got[0][0:8]
    for g in got[1:]:
        total = total + g[0:8]
    out[...] = total
    cs = six.shape[1] // PEERS
    six[...] = jnp.concatenate([g[8:16, :cs] for g in got], axis=1)


def entry_grad(nz, idx, *refs):
    sums = refs[:nz]
    grad_pre, image, weight, norm, gain, gain_grad, shift_grad, out, order = refs[nz:]
    got = in_order(sums, idx[1], order)
    total = got[0]
    for g in got[1:]:
        total = total + g
    gain_grad[...] = total[0:1]
    shift_grad[...] = total[1:2]
    c_in = gain.shape[1]
    scale = norm[1:2, :c_in]
    normed = (image[...].astype(F32) - norm[0:1, :c_in]) * scale
    out[...] = gain[...] * scale * (
        grad_pre[...]
        - weight[:, 0:1]
        * (shift_grad[0:1, :c_in] + normed * gain_grad[0:1, :c_in])
        / norm[2:3, :c_in]
    )


def program(
    nx,
    ny,
    images,
    valid_count,
    pixel_mask,
    gain_entry,
    shift_entry,
    conv_first,
    gain_middle,
    shift_middle,
    conv_second,
    projection,
    gain_inner,
    shift_inner,
    conv_third,
    gain_last,
    shift_last,
    conv_fourth,
    cotangent,
):
    fy = PEERS
    nz = ny // fy
    side, c_in = images.shape[1], images.shape[3]
    small = side // 2
    area = small * small
    c_out = conv_first.shape[1]
    cs = c_out // PEERS
    width = PEERS * area
    lanes = c_in + 64
    gx, gy = lax.axis_index("gx"), lax.axis_index("gy")
    me = gy % fy
    mine = gy // fy
    idx = jnp.stack([me, mine, gx, gy]).astype(jnp.int32)

    def to_slice(piece, k):
        return lax.ppermute(piece, "gy", [(j, j // fy * fy + (j % fy ^ k)) for j in range(ny)])

    def share(pieces):
        return [pieces[0]] + [to_slice(pieces[k], k) for k in range(1, PEERS)]

    def spread_out(piece):
        return share([piece] * PEERS)

    def to_gx(piece, k):
        return lax.ppermute(piece, "gx", [(i, i ^ k) for i in range(nx)])

    def pool(piece, kernel):
        pieces = [piece] + [to_gx(piece, k) for k in range(1, nx)]
        piece = call(
            kernel,
            shape(piece.shape),
            [idx, *pieces],
            [pltpu.VMEM((nx, *piece.shape), F32)],
        )
        out = [piece]
        for k in range(1, nz):
            perm = [(j, (j // fy ^ k) * fy + j % fy) for j in range(ny)]
            out.append(lax.ppermute(piece, "gy", perm))
        return out

    add_gx = functools.partial(add_rows, 2)

    def after(value, *others):
        return lax.optimization_barrier((value, *others))[0]

    def turn(block):
        return lax.all_to_all(block, "gy", 0, 0, tiled=True)

    def along_gx(block):
        held = {0: block}
        for k in range(2, nx, 2):
            held[k] = to_gx(block, k)
        for k in range(0, nx, 2):
            held[k + 1] = to_gx(held[k], 1)
        return [held[k] for k in range(nx)]

    unit_first, unit_skip = conv_first.shape[0] // 2, projection.shape[0] // 2
    unit_mid = conv_second.shape[0] // 2
    span_first, span_mid = span_of(unit_first + unit_skip), span_of(unit_mid)

    cb = cs // (nx // 2)

    def fetch(span, *weights, then=()):
        out = call(
            functools.partial(entry_weights, cs, fy),
            shape((ny, cb, span), BF16),
            [idx, *weights],
        )
        return along_gx(turn(after(out, *then)))

    def halves(span):
        return pltpu.VMEM((2, nx // 2, ny, cb, span), BF16)

    pixels = images.reshape(side * side, c_in)
    image, wide = pl.pallas_call(
        functools.partial(entry_image, small),
        out_shape=[shape((4 * area, lanes), BF16), shape((4 * area, 128))],
        in_specs=[SMEM, VMEM, VMEM, SMEM],
        out_specs=[VMEM, VMEM],
        compiler_params=pltpu.CompilerParams(vmem_limit_bytes=16 * 1024 * 1024),
        cost_estimate=pl.CostEstimate(flops=1 << 20, bytes_accessed=1 << 20, transcendentals=0),
    )(idx, pixels, pixel_mask.reshape(side, side), valid_count)
    group = spread_out(image)
    got_first = fetch(span_first, conv_first, projection, then=group[1:])

    def own(gain, shift):
        pair = jnp.stack([gain, shift], axis=1)
        return lax.dynamic_slice_in_dim(pair, me * cs, cs, axis=0)

    p_middle = own(gain_middle, shift_middle)
    p_inner = own(gain_inner, shift_inner)
    p_last = own(gain_last, shift_last)
    g_entry, s_entry = gain_entry[None], shift_entry[None]

    tile = shape((cs, width))
    tile16 = shape((cs, width), BF16)
    cols = shape((cs, 128))
    stat = shape((8, cs))
    stat_order = pltpu.VMEM((nz, 8, cs), F32)
    full16 = shape((c_out, width), BF16)
    whole16 = shape((9 * cs, c_out), BF16)
    conv_flops = 25 * 10**8

    stats = call(functools.partial(entry_stats, area), shape((8, lanes)), [idx, *group])
    got_second = fetch(span_mid, conv_second, then=got_first[:1])
    pooled = pool(stats, merge_stats)
    got_third = fetch(span_mid, conv_third, then=got_second[:1])
    first, skipped, stats, norm_one, narrow, act_one, w_first = call(
        functools.partial(entry_block, nz, nx, unit_first, unit_skip, area, small),
        [
            tile,
            tile,
            stat,
            shape((8, lanes)),
            shape((8, width)),
            shape((4, width, c_in), BF16),
            shape((10 * cs, c_in), BF16),
        ],
        [idx, *group, *pooled, g_entry, s_entry, *got_first],
        [
            pltpu.VMEM((nz, 8, lanes), F32),
            pltpu.VMEM((width, lanes), BF16),
            pltpu.VMEM((cs, span_of(9 * c_in)), BF16),
            halves(span_first),
        ],
        flops=conv_flops // 2,
    )

    cot_parts = call(
        split_cotangent,
        [shape((cs, 128), BF16)] * PEERS,
        [idx, after(cotangent, stats).reshape(area, c_out)],
        [pltpu.VMEM((c_out, 2 * area), F32)],
    )
    cot_parts = share(cot_parts)

    def activate(value, params, pooled):
        return call(
            functools.partial(act_block, nz),
            [tile16, tile, cols],
            [idx, value, params, *pooled],
            [stat_order],
        )

    def convolve(act, weights, base, last=False):
        more = [] if base is None else [base]
        if last:
            outs = [shape((cs, 128), BF16)] * PEERS + [full16]
        else:
            outs = [tile, stat, full16, whole16]
        return call(
            functools.partial(conv_block, nx, base is not None, last, unit_mid, area, small),
            outs,
            [idx, *spread_out(act), narrow, *weights, *more],
            [pltpu.VMEM((9 * cs, width), F32)] + ([] if last else [halves(span_mid)]),
            flops=conv_flops,
        )

    pooled = pool(stats, merge_stats)
    got_fourth = fetch(span_mid, conv_fourth, then=got_third[:1])
    act, normed_two, scale_two = activate(first, p_middle, pooled)
    hidden, stats, act_two, w_second = convolve(act, got_second, skipped)
    act, normed_three, scale_three = activate(hidden, p_inner, pool(stats, merge_stats))
    third, stats, act_three, w_third = convolve(act, got_third, None)
    act, normed_four, scale_four = activate(third, p_last, pool(stats, merge_stats))

    cot, shifted_four, w_fourth, *parts = call(
        functools.partial(last_back, nx, unit_mid, area, small),
        [tile, shape((9 * cs, width), BF16), whole16] + [tile16] * PEERS,
        [idx, *cot_parts, *got_fourth],
        [pltpu.VMEM((c_out, width), F32), halves(span_mid)],
        flops=conv_flops,
    )

    def slope(parts, normed, params, *done):
        parts = share(parts)
        return call(gelu_back, [tile, stat], [idx, *parts, after(normed, *done), params])

    def back(grad_pre, normed, scales, params, pooled, weights, base):
        more = [] if base is None else [base]
        outs = [stat, shape((9 * cs, width), BF16)] + ([] if base is None else [tile16])
        return call(
            functools.partial(norm_back, nz, base is not None, False, area, small),
            outs + [tile16] * PEERS,
            [idx, grad_pre, normed, scales, params, narrow, *pooled, *more, weights],
            [pltpu.VMEM((c_out, width), F32), stat_order],
            flops=conv_flops,
        )

    def grad_of(kernel, span, shifted, act, scratch):
        return call(
            kernel,
            [shape((ny, cs, span)), shape((ny, cs, span), BF16)],
            [idx, shifted, act],
            [scratch, pltpu.VMEM((2, ny, cs, span), F32)],
            flops=conv_flops,
        )

    def grad_mid(shifted, act):
        kernel = functools.partial(weight_grad, unit_mid)
        return grad_of(kernel, span_mid, shifted, act, pltpu.VMEM((9 * cs, c_out), F32))

    def reduce_grads(*grads):
        own = [a for a, _ in grads]
        other = [to_gx(b, 1) for _, b in grads]
        span = sum(a.shape[2] for a in own)
        sides = nx // 2
        return call(
            functools.partial(reduce_core, len(own)),
            [shape((ny, cb, span))] + [shape((ny, cb, span), BF16)] * (sides - 1),
            [idx, *own, *other],
            [pltpu.VMEM((ny, cs, span), F32)],
        )

    def merge_sides(parts):
        parts = [parts[0]] + [to_gx(parts[k], 2 * k) for k in range(1, nx // 2)]
        return call(reduce_side, shape(parts[0].shape, BF16), [idx, *parts])

    def land_grads(got, spans, *rows):
        span = got.shape[2]
        got = call(functools.partial(fold, nz, fy), shape((fy * cb, span), BF16), [idx, got])
        return call(
            functools.partial(own_rows, nx, spans),
            [shape((r, c_out)) for r in rows],
            [idx, *along_gx(got)],
            [pltpu.VMEM((2, nx // 2, fy * cb, span), BF16)],
        )

    grad_pre, sums = slope(parts, normed_four, p_last)
    pooled = pool(sums, add_gx)
    *out_parts, act_four = convolve(act, [w_fourth], hidden, last=True)

    grad_fourth = grad_mid(shifted_four, act_four)
    last_sums, shifted_three, *parts = back(
        grad_pre, normed_four, scale_four, p_last, pooled, w_third, None
    )
    grad_pre, sums = slope(parts, normed_three, p_inner, *grad_fourth)
    inner_sums, shifted_two, grad_hidden, *parts = back(
        grad_pre, normed_three, scale_three, p_inner, pool(sums, add_gx), w_second, cot
    )
    late = reduce_grads(grad_fourth, grad_mid(shifted_three, act_three))
    grad_pre, sums = slope(parts, normed_two, p_middle, late[0])
    grad_second = grad_mid(shifted_two, act_two)
    late = merge_sides(late)
    middle_sums, shifted_one, *parts = call(
        functools.partial(norm_back, nz, False, True, area, small),
        [stat, shape((10 * cs, width), BF16)] + [shape((4 * area, c_in), BF16)] * PEERS,
        [
            idx,
            grad_pre,
            normed_two,
            scale_two,
            p_middle,
            after(narrow, late),
            *pool(sums, add_gx),
            w_first,
            grad_hidden,
        ],
        [pltpu.VMEM((4, width, c_in), F32), stat_order],
        flops=conv_flops // 2,
    )
    parts = share(parts)
    sent_late = turn(late)
    grad_first = grad_of(
        functools.partial(weight_grad_first, unit_first, unit_skip),
        span_first,
        shifted_one,
        act_one,
        pltpu.VMEM((cs, span_of(9 * c_in + span_first + 128)), F32),
    )
    second = turn(merge_sides(reduce_grads(grad_second)))
    first = turn(merge_sides(reduce_grads(grad_first)))
    fourth_grad, third_grad = land_grads(
        sent_late, ((span_mid, (0,)), (span_mid, (1,))), 2 * unit_mid, 2 * unit_mid
    )
    (second_grad,) = land_grads(second, ((span_mid, (0,)),), 2 * unit_mid)
    first_grad, skip_grad = land_grads(
        first, ((span_first, (0, 1)),), 2 * unit_first, 2 * unit_skip
    )

    padded = -(-c_in // 128) * 128
    grad_pre, sums = call(
        functools.partial(entry_back, small),
        [shape((4 * area, c_in)), shape((8, padded))],
        [idx, *parts, pixels, norm_one, g_entry, s_entry],
    )
    message = call(
        bundle, shape((16, padded)), [idx, middle_sums, inner_sums, last_sums, sums]
    )
    sums, six = call(
        unbundle,
        [shape((8, padded)), shape((8, c_out))],
        [idx, *spread_out(message)],
        [pltpu.VMEM((PEERS, 16, padded), F32)],
    )
    gain_entry_grad, shift_entry_grad, image_grad = call(
        functools.partial(entry_grad, nz),
        [shape((1, padded)), shape((1, padded)), shape((4 * area, c_in))],
        [idx, *pool(sums, add_gx), grad_pre, pixels, wide, norm_one, g_entry],
        [pltpu.VMEM((nz, 8, padded), F32)],
    )

    out = call(
        join_result,
        shape((area, c_out), BF16),
        [idx, *share(out_parts)],
        [pltpu.VMEM((c_out, 128), F32)],
    )
    return (
        out.reshape(1, small, small, c_out),
        image_grad.reshape(1, side, side, c_in),
        gain_entry_grad[0, :c_in],
        shift_entry_grad[0, :c_in],
        first_grad,
        six[0],
        six[1],
        second_grad,
        skip_grad,
        six[2],
        six[3],
        third_grad,
        six[4],
        six[5],
        fourth_grad,
    )


def solution(mesh):
    whole = P(("gx", "gy"), None, None, None)
    rows = P("gy", None)
    return jax.shard_map(
        functools.partial(program, mesh.shape["gx"], mesh.shape["gy"]),
        mesh=mesh,
        in_specs=(
            whole,
            P(("gx", "gy")),
            P(("gx", "gy"), None, None),
            P(),
            P(),
            rows,
            P(),
            P(),
            rows,
            rows,
            P(),
            P(),
            rows,
            P(),
            P(),
            rows,
            whole,
        ),
        out_specs=(
            whole, whole, P(), P(), rows, P(), P(), rows, rows, P(), P(), rows, P(), P(), rows,
        ),
        check_vma=False,
    )
```

```python
import functools

import jax
import jax.numpy as jnp
from jax import lax
from jax.experimental import pallas as pl
from jax.experimental.pallas import tpu as pltpu
from jax.sharding import PartitionSpec as P

EPS = 1e-05
F32 = jnp.float32
BF16 = jnp.bfloat16
PEERS = 4
C0 = 0.7978845608028654
C1 = 0.044715
VMEM = pl.BlockSpec(memory_space=pltpu.VMEM)
SMEM = pl.BlockSpec(memory_space=pltpu.SMEM)


def gelu(v):
    return 0.5 * v * (1.0 + jnp.tanh(C0 * (v + C1 * (v * v * v))))


def gelu_slope(v):
    t = jnp.tanh(C0 * (v + C1 * (v * v * v)))
    return 0.5 * (1.0 + t) + 0.5 * v * (1.0 - t * t) * (C0 * (1.0 + 3.0 * C1 * (v * v)))


def call(kernel, outs, args, scratch=(), flops=8 * 10**8):
    size = sum(a.size * a.dtype.itemsize for a in args)
    return pl.pallas_call(
        kernel,
        out_shape=outs,
        in_specs=[SMEM] + [VMEM] * (len(args) - 1),
        out_specs=jax.tree.map(lambda _: VMEM, outs),
        scratch_shapes=list(scratch),
        compiler_params=pltpu.CompilerParams(vmem_limit_bytes=16 * 1024 * 1024),
        cost_estimate=pl.CostEstimate(flops=flops, bytes_accessed=size, transcendentals=0),
    )(*args)


def shape(dims, dtype=F32):
    return jax.ShapeDtypeStruct(dims, dtype)


def rows_at(index, count):
    return pl.ds(pl.multiple_of(index * count, count), count)


def as_rows(parts):
    height = parts[0].shape[0]
    lane = lax.broadcasted_iota(jnp.int32, (height, 128), 1)
    out = jnp.zeros((height, 128), F32)
    for k, part in enumerate(parts):
        out = jnp.where(lane == k, part, out)
    return out.T[0:8]


def as_columns(rows):
    return jnp.concatenate([rows, jnp.zeros((120, rows.shape[1]), F32)], axis=0).T


def in_order(refs, me, scratch):
    for k, ref in enumerate(refs):
        scratch[me ^ k] = ref[...]
    return [scratch[k] for k in range(len(refs))]


def merge_moments(stats):
    total = sum(n for _, _, n in stats)
    mean = sum(n * m for m, _, n in stats) / total
    squares = sum(q + n * (m - mean) * (m - mean) for m, q, n in stats)
    return mean, squares, total


def merge_rows(refs):
    mean, squares, total = merge_moments([(g[0:1], g[1:2], g[2:3]) for g in refs])
    return mean, squares, total, sum(g[3:4] for g in refs)


def pixel(width, area, small):
    lane = lax.broadcasted_iota(jnp.int32, (1, width), 1) % area
    return lane // small, lane % small


def inside(row, col, drow, dcol, small):
    return (row + drow >= 0) & (row + drow < small) & (col + dcol >= 0) & (col + dcol < small)


def moved(value, step):
    shift = (-step) % value.shape[1]
    return pltpu.roll(value, shift, 1) if shift else value


OFFSETS = [(0, krow - 1, kcol - 1) for krow in range(3) for kcol in range(3)]

STRIDED = [
    ((krow != 1) * 2 + (kcol != 1), -(krow == 0), -(kcol == 0))
    for krow in range(3)
    for kcol in range(3)
] + [(0, 0, 0)]
PLACED = sorted(range(10), key=lambda k: (STRIDED[k][0], k))
PHASES = [[k for k in PLACED if STRIDED[k][0] == phase] for phase in range(4)]


def row_of(k, cs):
    at = PLACED.index(k)
    return slice(at * cs, (at + 1) * cs)


def phase_rows(phase, cs):
    first, last = PHASES[phase][0], PHASES[phase][-1]
    return slice(PLACED.index(first) * cs, (PLACED.index(last) + 1) * cs)


def masked_stats(value, weight, n):
    mean = jnp.sum(value * weight, axis=1, keepdims=True) / n
    centred = value - mean
    return mean, jnp.sum(weight * centred * centred, axis=1, keepdims=True)


def span_of(rows):
    return -(-rows // 128) * 128


def one_hot(height, width, shift):
    row = lax.broadcasted_iota(jnp.int32, (height, width), 0)
    col = lax.broadcasted_iota(jnp.int32, (height, width), 1)
    return (col == row + shift).astype(BF16)


def pick32(left, right, dims=((1,), (0,))):
    return lax.dot_general(left, right, (dims, ((), ())), preferred_element_type=F32)


def pick(left, right, dims=((1,), (0,))):
    return pick32(left, right, dims).astype(BF16)


def lane_tile(held, tile, rows, span):
    sides, ny = held.shape[1], held.shape[2]
    lane = lax.broadcasted_iota(jnp.int32, (1, 128), 1)
    out = None
    for v in range(2 * ny):
        begin = rows * v - tile * 128
        if begin >= 128 or begin + rows <= 0:
            continue
        at = (tile - rows * v // 128) * 128 % span
        part = jnp.concatenate(
            [held[v % 2, x, v // 2, :, at : at + 128].astype(F32) for x in range(sides)], axis=0
        )
        if begin > 0 or begin + rows < 128:
            own = (lane >= begin) & (lane < begin + rows)
            part = jnp.where(own, part, 0.0)
        out = part if out is None else out + part
    return out.astype(BF16)


def pixel_order(small, width, of):
    area = small * small
    row = lax.broadcasted_iota(jnp.int32, (4 * area, width), 0)
    col = lax.broadcasted_iota(jnp.int32, (4 * area, width), 1)
    phase, pix = row // area, row % area
    y = 2 * (pix // small) + phase // 2
    x = 2 * (pix % small) + phase % 2
    return (col == of(y, x)).astype(BF16)


def entry_image(small, idx, image, mask, valid, out, weight):
    side = 2 * small
    c_in = image.shape[1]
    count = side * side
    order = pixel_order(small, count, lambda y, x: y * side + x)
    out[:, :c_in] = pick(order, image[...])
    live = (valid[0] > 0).astype(F32)
    row = lax.broadcasted_iota(jnp.int32, (count, side), 0)
    col = lax.broadcasted_iota(jnp.int32, (count, side), 1)
    by_row = jnp.dot(
        (row // side == col).astype(BF16),
        mask[...].astype(F32).astype(BF16),
        preferred_element_type=F32,
    )
    column = jnp.sum(jnp.where(row % side == col, by_row, 0.0), axis=1, keepdims=True) * live
    lane = lax.broadcasted_iota(jnp.int32, (count, 128), 1)
    spread = jnp.where(lane == 0, column, 0.0)
    weight[...] = spread
    out[:, c_in:] = pick(order, spread.astype(BF16))[:, : out.shape[1] - c_in]


def entry_weights(cs, fy, idx, *refs):
    weights, out = refs[:-1], refs[-1]
    ny, cb, span = out.shape
    gx, gy = idx[2], idx[3]
    core, side = gx % 2, gx // 2
    c_out = weights[0].shape[1]
    unit = weights[0].shape[0] // 2
    begin = unit * (2 * gy + core) % 128
    row = lax.broadcasted_iota(jnp.int32, (fy * cb, c_out), 0)
    col = lax.broadcasted_iota(jnp.int32, (fy * cb, c_out), 1)
    chosen = (col == row // cb * cs + side * cb + row % cb).astype(BF16)
    total = None
    for weight in weights:
        rows = weight.shape[0]
        half = rows // 2
        mine = pick(chosen, weight[...], ((1,), (1,)))
        row = lax.broadcasted_iota(jnp.int32, (rows, span), 0) - core * half
        col = lax.broadcasted_iota(jnp.int32, (rows, span), 1)
        place = (row >= 0) & (row < half) & (
            (col == row + begin) | (col == row + begin - span)
        )
        part = pick32(mine, place.astype(BF16))
        total = part if total is None else total + part
        begin = begin + half
    for j in range(ny):
        out[j] = total[(j % fy) * cb : (j % fy + 1) * cb].astype(BF16)


def hold(gx, messages, held):
    for k, ref in enumerate(messages):
        at = gx ^ k
        held[at % 2, at // 2] = ref[...]


def assemble(held, out, rows):
    cs, span = held.shape[1] * held.shape[3], held.shape[4]
    tiles = out.shape[1] // 128
    for k in range(9):
        for q in range(tiles):
            out[k * cs : (k + 1) * cs, q * 128 : (q + 1) * 128] = lane_tile(
                held, tiles * k + q, rows, span
            )


def assemble_first(held, out, flat, rows, extra):
    cs, span = held.shape[1] * held.shape[3], held.shape[4]
    c_in = out.shape[1]
    tiles = flat.shape[1] // 128
    for tile in range(tiles):
        flat[:, tile * 128 : (tile + 1) * 128] = lane_tile(held, tile, rows, span)
    for k in range(9):
        begin = k * c_in
        base = begin // 128 * 128
        reach = min(-(-(begin + c_in) // 128) * 128, flat.shape[1])
        move = one_hot(c_in, reach - base, begin - base)
        out[row_of(k, cs), :] = pick(flat[:, base:reach], move, ((1,), (1,)))
    total = None
    for v in range(2 * held.shape[2]):
        row = lax.broadcasted_iota(jnp.int32, (span, c_in), 0)
        col = lax.broadcasted_iota(jnp.int32, (span, c_in), 1)
        at = col - extra * v
        begin = rows * v % 128 + rows
        place = (at >= 0) & (at < extra) & ((row == at + begin) | (row == at + begin - span))
        part = jnp.concatenate(
            [
                pick32(held[v % 2, x, v // 2], place.astype(BF16))
                for x in range(held.shape[1])
            ],
            axis=0,
        )
        total = part if total is None else total + part
    out[row_of(9, cs), :] = total.astype(BF16)


def entry_stats(area, idx, *refs):
    images, out = refs[:PEERS], refs[PEERS]
    lanes = out.shape[1]
    first = jnp.zeros((1, lanes), F32)
    wide = jnp.zeros((1, 1), F32)
    narrow = jnp.zeros((1, 1), F32)
    c_in = lanes - 64
    for ref in images:
        x = ref[...].astype(F32)
        w = x[:, c_in : c_in + 1]
        first += jnp.sum(x * w, axis=0, keepdims=True)
        wide += jnp.sum(w, axis=0, keepdims=True)
        narrow += jnp.sum(w[:area], axis=0, keepdims=True)
    mean = first / wide
    squares = jnp.zeros((1, lanes), F32)
    for ref in images:
        x = ref[...].astype(F32)
        w = x[:, c_in : c_in + 1]
        d = x - mean
        squares += jnp.sum(d * d * w, axis=0, keepdims=True)
    out[...] = jnp.zeros_like(out)
    out[0:1, :] = mean
    out[1:2, :] = squares
    out[2:3, :] = jnp.broadcast_to(wide, (1, lanes))
    out[3:4, :] = jnp.broadcast_to(narrow, (1, lanes))


def entry_block(nz, nx, rows, extra, area, small, idx, *refs):
    images = refs[:PEERS]
    stats, rest = refs[PEERS : PEERS + nz], refs[PEERS + nz :]
    gain, shift, messages, rest = rest[0], rest[1], rest[2 : 2 + nx], rest[2 + nx :]
    first, skipped, out_stats, norm, narrow, act, w_first = rest[:7]
    order, masks, flat, held = rest[7:]
    me, mine = idx[0], idx[1]
    c_in = gain.shape[1]
    lanes = norm.shape[1]
    cs = first.shape[0]
    width = first.shape[1]
    hold(idx[2], messages, held)
    assemble_first(held, w_first, flat, rows, extra)
    mean, squares, total, count = merge_rows(in_order(stats, mine, order))
    scale = lax.rsqrt(squares / total + EPS)
    norm[...] = jnp.zeros_like(norm)
    norm[0:1, :] = mean
    norm[1:2, :] = scale
    norm[2:3, :] = total
    norm[3:4, :] = count
    for k, ref in enumerate(images):
        x = ref[...]
        v = x[:, :c_in].astype(F32)
        pre = gain[...] * ((v - mean[:, :c_in]) * scale[:, :c_in]) + shift[...]
        a = gelu(pre).astype(BF16)
        for phase in range(4):
            act[phase, rows_at(me ^ k, area), :] = a[phase * area : (phase + 1) * area]
        masks[rows_at(me ^ k, area), :] = x[:area]
    ones = (lax.broadcasted_iota(jnp.int32, (8, lanes), 1) == c_in).astype(BF16)
    weight8 = lax.dot_general(
        ones, masks[...], (((1,), (1,)), ((), ())), preferred_element_type=F32
    )
    narrow[...] = weight8
    weight = weight8[0:1]
    row, col = pixel(width, area, small)
    total_first = jnp.zeros((cs, width), F32)
    for phase in range(4):
        group = lax.dot_general(
            w_first[phase_rows(phase, cs), :],
            act[phase],
            (((1,), (1,)), ((), ())),
            preferred_element_type=F32,
        )
        for at, k in enumerate(PHASES[phase]):
            y = group[at * cs : (at + 1) * cs]
            if k == 9:
                skipped[...] = y
                continue
            _, drow, dcol = STRIDED[k]
            y = moved(y, drow * small + dcol)
            total_first += jnp.where(inside(row, col, drow, dcol, small), y, 0.0)
    first[...] = total_first
    n = jnp.sum(weight, axis=1, keepdims=True)
    mean2, squares = masked_stats(total_first, weight, n)
    out_stats[...] = as_rows((mean2, squares, n))


def merge_stats(idx, *refs):
    out, order = refs[-2:]
    mean, squares, total, count = merge_rows(in_order(refs[:-2], idx[2], order))
    out[...] = jnp.zeros_like(out)
    out[0:1] = mean
    out[1:2] = squares
    out[2:3] = total
    out[3:4] = count


def add_rows(which, idx, *refs):
    out, order = refs[-2:]
    got = in_order(refs[:-2], idx[which], order)
    total = got[0]
    for g in got[1:]:
        total = total + g
    out[...] = total


def act_block(nz, idx, *refs):
    value, params = refs[:2]
    stats, rest = refs[2 : 2 + nz], refs[2 + nz :]
    if rest[-1].shape[1] == 128:
        cot, normed, scales, outs, order, stack = (*rest[:3], rest[3:-2], *rest[-2:])
    else:
        cot, normed, scales, outs, order = (None, *rest[:2], rest[2:-1], rest[-1])
    mean, squares, total, _ = merge_rows(in_order(stats, idx[1], order))
    rows = jnp.concatenate(
        [mean, lax.rsqrt(squares / total + EPS), total, jnp.zeros((5, mean.shape[1]), F32)], axis=0
    )
    cols = as_columns(rows)
    norm = (value[...] - cols[:, 0:1]) * cols[:, 1:2]
    normed[...] = norm
    act = gelu(params[:, 0:1] * norm + params[:, 1:2]).astype(BF16)
    cs, width = norm.shape
    if cot is not None:
        c = cot[...].astype(F32)
        stack[...] = jnp.concatenate([c, c], axis=0).T
    for k, out in enumerate(outs):
        out[:, :width] = act
        if cot is not None:
            out[:, width:] = stack[rows_at(idx[0] ^ k, cs), :].astype(BF16)
    scales[...] = cols


def conv_block(nx, added, last, rows, area, small, idx, *refs):
    pieces = refs[:PEERS]
    narrow, rest = refs[PEERS], refs[PEERS + 1 :]
    if last:
        weights, rest = rest[0], rest[1:]
    else:
        messages, rest = rest[:nx], rest[nx:]
    base, rest = (rest[0], rest[1:]) if added else (None, rest)
    me = idx[0]
    cs, width = pieces[0].shape[0], narrow.shape[1]
    if last:
        outs, act, spread = rest[:PEERS], rest[PEERS], rest[PEERS + 1]
    else:
        value, out_stats, act, whole, spread, held = rest
        hold(idx[2], messages, held)
        assemble(held, whole, rows)
        weights = whole
    for k, ref in enumerate(pieces):
        act[rows_at(me ^ k, cs), :] = ref[:, :width]
    spread[...] = jnp.dot(weights[...], act[...], preferred_element_type=F32)
    row, col = pixel(width, area, small)
    total = base[...] if added else jnp.zeros((cs, width), F32)
    for k, (_, drow, dcol) in enumerate(OFFSETS):
        y = moved(spread[k * cs : (k + 1) * cs, :], drow * small + dcol)
        total += jnp.where(inside(row, col, drow, dcol, small), y, 0.0)
    if last:
        result = total.astype(BF16)
        lane = lax.broadcasted_iota(jnp.int32, (width, 128), 0)
        slot = lax.broadcasted_iota(jnp.int32, (width, 128), 1)
        for k, out in enumerate(outs):
            out[...] = pick(result, (lane == (me ^ k) * area + slot).astype(BF16))
    else:
        value[...] = total
        weight = narrow[0:1, :]
        n = jnp.sum(weight, axis=1, keepdims=True)
        mean, squares = masked_stats(total, weight, n)
        out_stats[...] = as_rows((mean, squares, n))


def join_result(idx, *refs):
    pieces, (out, stack) = refs[:PEERS], refs[PEERS:]
    cs = pieces[0].shape[0]
    for k, ref in enumerate(pieces):
        stack[rows_at(idx[0] ^ k, cs), :] = ref[:, -128:].astype(F32)
    out[...] = stack[...].T[: out.shape[0]].astype(BF16)


def spread_grad(grad, shifted, area, small, offs, row_at):
    cs, width = grad.shape
    row, col = pixel(width, area, small)
    for k, (_, drow, dcol) in enumerate(offs):
        g = moved(grad, -(drow * small + dcol))
        g = jnp.where(inside(row, col, -drow, -dcol, small), g, 0.0)
        shifted[row_at(k, cs), :] = g.astype(BF16)


def plain_rows(k, cs):
    return slice(k * cs, (k + 1) * cs)


def push_back(me, weights, shifted, partial, outs):
    cs, width = outs[0].shape[0], shifted.shape[1]
    partial[...] = lax.dot_general(
        weights[...], shifted[...], (((0,), (0,)), ((), ())), preferred_element_type=F32
    )
    for k, out in enumerate(outs):
        out[:, :width] = partial[rows_at(me ^ k, cs), :].astype(BF16)


def last_back(nx, rows, area, small, idx, *refs):
    pieces, messages, rest = refs[:PEERS], refs[PEERS : PEERS + nx], refs[PEERS + nx :]
    cot, shifted, weights = rest[:3]
    outs = rest[3 : PEERS + 3]
    partial, held = rest[PEERS + 3 :]
    hold(idx[2], messages, held)
    assemble(held, weights, rows)
    me = idx[0]
    cs, width = cot.shape
    image = lax.broadcasted_iota(jnp.int32, (1, width), 1) // area
    grad = jnp.zeros((cs, width), F32)
    for k, ref in enumerate(pieces):
        tiled = jnp.concatenate([ref[:, width:].astype(F32)] * (width // 128), axis=1)
        grad = jnp.where(image == (me ^ k), tiled, grad)
    cot[...] = grad
    spread_grad(grad, shifted, area, small, OFFSETS, plain_rows)
    push_back(me, weights, shifted, partial, outs)


def gelu_back(idx, *refs):
    pieces = refs[:PEERS]
    normed, params, grad_pre, sums = refs[PEERS:]
    width = normed.shape[1]
    grad = pieces[0][:, :width].astype(F32)
    for ref in pieces[1:]:
        grad += ref[:, :width].astype(F32)
    norm = normed[...]
    g = gelu_slope(params[:, 0:1] * norm + params[:, 1:2]) * grad
    grad_pre[...] = g
    sums[...] = as_rows(
        (jnp.sum(g * norm, axis=1, keepdims=True), jnp.sum(g, axis=1, keepdims=True))
    )


def norm_back(nz, added, last, area, small, idx, *refs):
    grad_pre, normed, scales, params, narrow = refs[:5]
    sums = refs[5 : 5 + nz]
    rest = refs[5 + nz :]
    base, rest = (rest[0], rest[1:]) if added else (None, rest)
    me = idx[0]
    cs, width = grad_pre.shape
    order = rest[-1]
    got = in_order(sums, idx[1], order)
    total = got[0]
    for g in got[1:]:
        total = total + g
    cols = as_columns(total)
    gain_grad, shift_grad = cols[:, 0:1], cols[:, 1:2]
    norm = normed[...]
    back = params[:, 0:1] * scales[:, 1:2] * (
        grad_pre[...]
        - narrow[0:1, :] * (shift_grad + norm * gain_grad) / scales[:, 2:3]
    )
    if added:
        back = base[...] + back
    grad = back.astype(BF16).astype(F32)
    if not last:
        riders = ()
        if not added:
            riders, rest = rest[:PEERS], rest[PEERS:]
        weights, sums_out, shifted = rest[:3]
        outs, partial = rest[3 : 3 + PEERS], rest[3 + PEERS]
        for rider, out in zip(riders, outs):
            out[:, width:] = rider[...]
        if added:
            grad_out, outs, partial = rest[3], rest[4 : 4 + PEERS], rest[4 + PEERS]
            grad_out[...] = grad.astype(BF16)
        sums_out[...] = total
        spread_grad(grad, shifted, area, small, OFFSETS, plain_rows)
        push_back(me, weights, shifted, partial, outs)
    else:
        weights, grad_skip, sums_out, shifted = rest[:4]
        outs, partial = rest[4 : 4 + PEERS], rest[4 + PEERS]
        sums_out[...] = total
        spread_grad(grad, shifted, area, small, STRIDED[:9], row_of)
        shifted[row_of(9, cs), :] = grad_skip[...]
        for phase in range(4):
            partial[phase] = lax.dot_general(
                shifted[phase_rows(phase, cs), :],
                weights[phase_rows(phase, cs), :],
                (((0,), (0,)), ((), ())),
                preferred_element_type=F32,
            )
        for k, out in enumerate(outs):
            for phase in range(4):
                out[phase * area : (phase + 1) * area, :] = partial[
                    phase, rows_at(me ^ k, area), :
                ].astype(BF16)


def part_halves(core, units, own, other):
    own[...] = units[core]
    other[...] = units[1 - core].astype(BF16)


def weight_grad(rows, idx, shifted, act, own, other, full, units):
    full[...] = lax.dot_general(
        shifted[...], act[...], (((1,), (1,)), ((), ())), preferred_element_type=F32
    )
    ny, cs, span = own.shape
    tiles = full.shape[1] // 128
    for v in range(2 * ny):
        begin = rows * v % 128
        parts = []
        for q in range((begin + rows + 127) // 128):
            k, p = divmod(rows * v // 128 + q, tiles)
            parts.append(full[k * cs : (k + 1) * cs, p * 128 : (p + 1) * 128])
        window = jnp.concatenate(parts, axis=1)
        units[v % 2, v // 2] = moved(window, begin)[:, :span]
    part_halves(idx[2] % 2, units, own, other)


def weight_grad_first(rows, extra, idx, shifted, act, own, other, flat, units):
    ny, cs, span = own.shape
    c_in = act.shape[2]
    flat[...] = jnp.zeros_like(flat)
    skip = None
    for phase in range(4):
        group = jnp.dot(
            shifted[phase_rows(phase, cs), :], act[phase], preferred_element_type=F32
        ).astype(BF16)
        for at, k in enumerate(PHASES[phase]):
            grad = group[at * cs : (at + 1) * cs]
            if k == 9:
                skip = grad
                continue
            begin = k * c_in
            base = begin // 128 * 128
            reach = -(-(begin + c_in) // 128) * 128
            move = one_hot(c_in, reach - base, begin - base)
            flat[:, base:reach] += jnp.dot(grad, move, preferred_element_type=F32)
    lane = lax.broadcasted_iota(jnp.int32, (1, span), 1)
    for v in range(2 * ny):
        begin = rows * v % 128
        base = rows * v - begin
        window = moved(flat[:, base : base + span + 128], begin)[:, :span]
        row = lax.broadcasted_iota(jnp.int32, (c_in, span), 0)
        col = lax.broadcasted_iota(jnp.int32, (c_in, span), 1)
        place = (row >= extra * v) & (row < extra * (v + 1)) & (col == row - extra * v + rows)
        tail = pick32(skip, place.astype(BF16))
        units[v % 2, v // 2] = jnp.where(lane < rows, window, 0.0) + tail
    part_halves(idx[2] % 2, units, own, other)


def reduce_core(count, idx, *refs):
    own, other, outs, total = refs[:count], refs[count : 2 * count], refs[2 * count : -1], refs[-1]
    cb = outs[0].shape[1]
    at = 0
    for a, b in zip(own, other):
        span = a.shape[2]
        total[:, :, at : at + span] = a[...] + b[...].astype(F32)
        at += span
    for k, out in enumerate(outs):
        for j in range(total.shape[0]):
            out[j] = total[j, rows_at(idx[2] // 2 ^ k, cb), :].astype(out.dtype)


def reduce_side(sides, idx, *refs):
    out = refs[-1]
    at = 0
    for n in range(0, len(refs) - 1, sides):
        total = refs[n][...]
        for ref in refs[n + 1 : n + sides]:
            total += ref[...].astype(F32)
        out[:, :, at : at + total.shape[2]] = total.astype(BF16)
        at += total.shape[2]


def fold(nz, fy, idx, got, out):
    cs = got.shape[1]
    for f in range(fy):
        total = got[f].astype(F32)
        for z in range(1, nz):
            total += got[z * fy + f].astype(F32)
        out[f * cs : (f + 1) * cs, :] = total.astype(BF16)


def own_rows(count, spans, idx, *refs):
    pieces, outs, stack = refs[:count], refs[count:-1], refs[-1]
    for k, ref in enumerate(pieces):
        at = idx[2] ^ k
        stack[at % 2, at // 2] = ref[...]
    sides, height = stack.shape[1], stack.shape[2]
    fy_cb = [(f, x) for f in range(PEERS) for x in range(sides)]
    cb = height // PEERS
    for half in range(2):
        whole = jnp.concatenate(
            [stack[half, x, f * cb : (f + 1) * cb, :].astype(F32) for f, x in fy_cb], axis=0
        ).T
        at = 0
        for span, group in spans:
            begin = at
            for n in group:
                out = outs[n]
                rows = out.shape[0] // 2
                out[half * rows : (half + 1) * rows, :] = whole[begin : begin + rows]
                begin += rows
            at += span


def entry_back(small, idx, *refs):
    pieces = refs[:PEERS]
    image, norm, gain, shift, grad_pre, sums = refs[PEERS:]
    c_in = gain.shape[1]
    side = 2 * small
    grad = pieces[0][...].astype(F32)
    for ref in pieces[1:]:
        grad += ref[...].astype(F32)
    order = pixel_order(small, side * side, lambda y, x: y * side + x)
    high = grad.astype(BF16)
    low = (grad - high.astype(F32)).astype(BF16)
    grad = sum(
        lax.dot_general(order, part, (((0,), (0,)), ((), ())), preferred_element_type=F32)
        for part in (high, low)
    )
    normed = (image[...].astype(F32) - norm[0:1, :c_in]) * norm[1:2, :c_in]
    g = gelu_slope(gain[...] * normed + shift[...]) * grad
    grad_pre[...] = g
    sums[...] = jnp.zeros_like(sums)
    sums[0:1, :c_in] = jnp.sum(g * normed, axis=0, keepdims=True)
    sums[1:2, :c_in] = jnp.sum(g, axis=0, keepdims=True)


def bundle(idx, first, second, third, sums, out):
    out[...] = jnp.zeros_like(out)
    out[0:8, :] = sums[...]
    for k, ref in enumerate((first, second, third)):
        out[8 + 2 * k : 10 + 2 * k, : ref.shape[1]] = ref[0:2]


def unbundle(idx, *refs):
    out, six, order = refs[-3:]
    got = in_order(refs[:-3], idx[0], order)
    total = got[0][0:8]
    for g in got[1:]:
        total = total + g[0:8]
    out[...] = total
    cs = six.shape[1] // PEERS
    six[...] = jnp.concatenate([g[8:16, :cs] for g in got], axis=1)


def entry_grad(nz, idx, *refs):
    sums = refs[:nz]
    grad_pre, image, weight, norm, gain, gain_grad, shift_grad, out, order = refs[nz:]
    got = in_order(sums, idx[1], order)
    total = got[0]
    for g in got[1:]:
        total = total + g
    gain_grad[...] = total[0:1]
    shift_grad[...] = total[1:2]
    c_in = gain.shape[1]
    scale = norm[1:2, :c_in]
    normed = (image[...].astype(F32) - norm[0:1, :c_in]) * scale
    out[...] = gain[...] * scale * (
        grad_pre[...]
        - weight[:, 0:1]
        * (shift_grad[0:1, :c_in] + normed * gain_grad[0:1, :c_in])
        / norm[2:3, :c_in]
    )


def program(
    nx,
    ny,
    images,
    valid_count,
    pixel_mask,
    gain_entry,
    shift_entry,
    conv_first,
    gain_middle,
    shift_middle,
    conv_second,
    projection,
    gain_inner,
    shift_inner,
    conv_third,
    gain_last,
    shift_last,
    conv_fourth,
    cotangent,
):
    fy = PEERS
    nz = ny // fy
    side, c_in = images.shape[1], images.shape[3]
    small = side // 2
    area = small * small
    c_out = conv_first.shape[1]
    cs = c_out // PEERS
    width = PEERS * area
    lanes = c_in + 64
    gx, gy = lax.axis_index("gx"), lax.axis_index("gy")
    me = gy % fy
    mine = gy // fy
    idx = jnp.stack([me, mine, gx, gy]).astype(jnp.int32)

    def to_slice(piece, k):
        return lax.ppermute(piece, "gy", [(j, j // fy * fy + (j % fy ^ k)) for j in range(ny)])

    def share(pieces):
        return [pieces[0]] + [to_slice(pieces[k], k) for k in range(1, PEERS)]

    def spread_out(piece):
        return share([piece] * PEERS)

    def to_gx(piece, k):
        return lax.ppermute(piece, "gx", [(i, i ^ k) for i in range(nx)])

    def pool(piece, kernel):
        pieces = [piece] + [to_gx(piece, k) for k in range(1, nx)]
        piece = call(
            kernel,
            shape(piece.shape),
            [idx, *pieces],
            [pltpu.VMEM((nx, *piece.shape), F32)],
        )
        out = [piece]
        for k in range(1, nz):
            perm = [(j, (j // fy ^ k) * fy + j % fy) for j in range(ny)]
            out.append(lax.ppermute(piece, "gy", perm))
        return out

    add_gx = functools.partial(add_rows, 2)

    def after(value, *others):
        return lax.optimization_barrier((value, *others))[0]

    def turn(block):
        return lax.all_to_all(block, "gy", 0, 0, tiled=True)

    def along_gx(block):
        held = {0: block}
        for k in range(2, nx, 2):
            held[k] = to_gx(block, k)
        for k in range(0, nx, 2):
            held[k + 1] = to_gx(held[k], 1)
        return [held[k] for k in range(nx)]

    unit_first, unit_skip = conv_first.shape[0] // 2, projection.shape[0] // 2
    unit_mid = conv_second.shape[0] // 2
    span_first, span_mid = span_of(unit_first + unit_skip), span_of(unit_mid)

    cb = cs // (nx // 2)

    def fetch(span, *weights, then=()):
        out = call(
            functools.partial(entry_weights, cs, fy),
            shape((ny, cb, span), BF16),
            [idx, *weights],
        )
        return turn(after(out, *then))

    def halves(span):
        return pltpu.VMEM((2, nx // 2, ny, cb, span), BF16)

    pixels = images.reshape(side * side, c_in)
    image, wide = pl.pallas_call(
        functools.partial(entry_image, small),
        out_shape=[shape((4 * area, lanes), BF16), shape((4 * area, 128))],
        in_specs=[SMEM, VMEM, VMEM, SMEM],
        out_specs=[VMEM, VMEM],
        compiler_params=pltpu.CompilerParams(vmem_limit_bytes=16 * 1024 * 1024),
        cost_estimate=pl.CostEstimate(flops=1 << 20, bytes_accessed=1 << 20, transcendentals=0),
    )(idx, pixels, pixel_mask.reshape(side, side), valid_count)
    group = spread_out(image)
    got_first = along_gx(fetch(span_first, conv_first, projection, then=group[1:]))

    def own(gain, shift):
        pair = jnp.stack([gain, shift], axis=1)
        return lax.dynamic_slice_in_dim(pair, me * cs, cs, axis=0)

    p_middle = own(gain_middle, shift_middle)
    p_inner = own(gain_inner, shift_inner)
    p_last = own(gain_last, shift_last)
    g_entry, s_entry = gain_entry[None], shift_entry[None]

    tile = shape((cs, width))
    tile16 = shape((cs, width), BF16)
    cols = shape((cs, 128))
    stat = shape((8, cs))
    stat_order = pltpu.VMEM((nz, 8, cs), F32)
    full16 = shape((c_out, width), BF16)
    whole16 = shape((9 * cs, c_out), BF16)
    conv_flops = 25 * 10**8

    stats = call(functools.partial(entry_stats, area), shape((8, lanes)), [idx, *group])
    pooled = pool(stats, merge_stats)
    got_second = fetch(span_mid, conv_second, then=pooled[-1:])
    first, skipped, stats, norm_one, narrow, act_one, w_first = call(
        functools.partial(entry_block, nz, nx, unit_first, unit_skip, area, small),
        [
            tile,
            tile,
            stat,
            shape((8, lanes)),
            shape((8, width)),
            shape((4, width, c_in), BF16),
            shape((10 * cs, c_in), BF16),
        ],
        [idx, *group, *pooled, g_entry, s_entry, *got_first],
        [
            pltpu.VMEM((nz, 8, lanes), F32),
            pltpu.VMEM((width, lanes), BF16),
            pltpu.VMEM((cs, span_of(9 * c_in)), BF16),
            halves(span_first),
        ],
        flops=conv_flops // 2,
    )

    def activate(value, params, pooled, cot=None):
        more = [] if cot is None else [cot]
        count = 1 if cot is None else PEERS
        out = tile16 if cot is None else shape((cs, width + 128), BF16)
        return call(
            functools.partial(act_block, nz),
            [tile, cols] + [out] * count,
            [idx, value, params, *pooled, *more],
            [stat_order] + ([] if cot is None else [pltpu.VMEM((c_out, 128), F32)]),
        )

    def convolve(pieces, weights, base, last=False):
        more = [] if base is None else [base]
        if last:
            outs = [shape((cs, 128), BF16)] * PEERS + [full16]
        else:
            outs = [tile, stat, full16, whole16]
        return call(
            functools.partial(conv_block, nx, base is not None, last, unit_mid, area, small),
            outs,
            [idx, *pieces, narrow, *weights, *more],
            [pltpu.VMEM((9 * cs, width), F32)] + ([] if last else [halves(span_mid)]),
            flops=conv_flops,
        )

    pooled = pool(stats, merge_stats)
    got_second = along_gx(after(got_second, pooled[0]))
    got_third = fetch(span_mid, conv_third, then=pooled[-1:])
    normed_two, scale_two, *messages = activate(
        first, p_middle, pooled, cotangent.reshape(area, c_out)
    )
    pieces = share(messages)
    hidden, stats, act_two, w_second = convolve(pieces, got_second, skipped)
    got_fourth = fetch(span_mid, conv_fourth, then=[stats])
    pooled = pool(stats, merge_stats)
    got_third = along_gx(after(got_third, pooled[0]))
    got_fourth = along_gx(after(got_fourth, pooled[0]))
    normed_three, scale_three, act = activate(hidden, p_inner, pooled)
    third, stats, act_three, w_third = convolve(spread_out(act), got_third, None)
    normed_four, scale_four, act = activate(third, p_last, pool(stats, merge_stats))

    cot, shifted_four, w_fourth, *parts = call(
        functools.partial(last_back, nx, unit_mid, area, small),
        [tile, shape((9 * cs, width), BF16), whole16] + [tile16] * PEERS,
        [idx, *pieces, *got_fourth],
        [pltpu.VMEM((c_out, width), F32), halves(span_mid)],
        flops=conv_flops,
    )

    def slope(parts, normed, params, *done):
        return call(gelu_back, [tile, stat], [idx, *parts, after(normed, *done), params])

    def back(grad_pre, normed, scales, params, pooled, weights, base, riders=()):
        more = list(riders) if base is None else [base]
        part = tile16 if base is not None else shape((cs, width + 128), BF16)
        outs = [stat, shape((9 * cs, width), BF16)] + ([] if base is None else [tile16])
        return call(
            functools.partial(norm_back, nz, base is not None, False, area, small),
            outs + [part] * PEERS,
            [idx, grad_pre, normed, scales, params, narrow, *pooled, *more, weights],
            [pltpu.VMEM((c_out, width), F32), stat_order],
            flops=conv_flops,
        )

    def grad_of(kernel, span, shifted, act, scratch):
        return call(
            kernel,
            [shape((ny, cs, span)), shape((ny, cs, span), BF16)],
            [idx, shifted, act],
            [scratch, pltpu.VMEM((2, ny, cs, span), F32)],
            flops=conv_flops,
        )

    def grad_mid(shifted, act):
        kernel = functools.partial(weight_grad, unit_mid)
        return grad_of(kernel, span_mid, shifted, act, pltpu.VMEM((9 * cs, c_out), F32))

    def reduce_grads(*grads):
        own = [a for a, _ in grads]
        other = [to_gx(b, 1) for _, b in grads]
        span = sum(a.shape[2] for a in own)
        sides = nx // 2
        return call(
            functools.partial(reduce_core, len(own)),
            [shape((ny, cb, span))] + [shape((ny, cb, span), BF16)] * (sides - 1),
            [idx, *own, *other],
            [pltpu.VMEM((ny, cs, span), F32)],
        )

    def move_sides(parts):
        return [parts[0]] + [to_gx(parts[k], 2 * k) for k in range(1, nx // 2)]

    def add_sides(*groups):
        span = sum(parts[0].shape[2] for parts in groups)
        return call(
            functools.partial(reduce_side, nx // 2),
            shape((ny, cb, span), BF16),
            [idx, *[p for parts in groups for p in parts]],
        )

    def merge_sides(parts):
        return add_sides(move_sides(parts))

    def land_grads(got, spans, *rows):
        span = got.shape[2]
        got = call(functools.partial(fold, nz, fy), shape((fy * cb, span), BF16), [idx, got])
        return call(
            functools.partial(own_rows, nx, spans),
            [shape((r, c_out)) for r in rows],
            [idx, *along_gx(got)],
            [pltpu.VMEM((2, nx // 2, fy * cb, span), BF16)],
        )

    grad_pre, sums = slope(share(parts), normed_four, p_last)
    pooled = pool(sums, add_gx)
    *out_parts, act_four = convolve(spread_out(act), [w_fourth], hidden, last=True)

    grad_fourth = grad_mid(shifted_four, act_four)
    last_sums, shifted_three, *parts = back(
        grad_pre, normed_four, scale_four, p_last, pooled, w_third, None, out_parts
    )
    parts = share(parts)
    out = call(
        join_result,
        shape((area, c_out), BF16),
        [idx, *parts],
        [pltpu.VMEM((c_out, 128), F32)],
    )
    grad_pre, sums = slope(parts, normed_three, p_inner, *grad_fourth)
    grad_third = grad_mid(after(shifted_three, parts[1]), act_three)
    late = reduce_grads(grad_fourth, grad_third)
    pooled = pool(sums, add_gx)
    inner_sums, shifted_two, grad_hidden, *parts = back(
        grad_pre, normed_three, scale_three, p_inner, [after(pooled[0], late[0])] + pooled[1:], w_second, cot
    )
    late = merge_sides(late)
    parts = share(parts)
    grad_second = grad_mid(after(shifted_two, parts[1]), act_two)
    grad_pre, sums = slope(parts, normed_two, p_middle, *grad_second)
    second = reduce_grads(grad_second)
    pooled = pool(sums, add_gx)
    moved_second = move_sides([after(p, pooled[0]) for p in second])
    middle_sums, shifted_one, *parts = call(
        functools.partial(norm_back, nz, False, True, area, small),
        [stat, shape((10 * cs, width), BF16)] + [shape((4 * area, c_in), BF16)] * PEERS,
        [
            idx,
            grad_pre,
            normed_two,
            scale_two,
            p_middle,
            after(narrow, late),
            *pooled,
            w_first,
            grad_hidden,
        ],
        [pltpu.VMEM((4, width, c_in), F32), stat_order],
        flops=conv_flops // 2,
    )
    parts = share(parts)
    sent_late = turn(after(late, parts[1]))
    grad_first = grad_of(
        functools.partial(weight_grad_first, unit_first, unit_skip),
        span_first,
        after(shifted_one, parts[1]),
        act_one,
        pltpu.VMEM((cs, span_of(9 * c_in + span_first + 128)), F32),
    )
    sent_early = turn(add_sides(moved_second, move_sides(reduce_grads(grad_first))))
    fourth_grad, third_grad = land_grads(
        sent_late, ((span_mid, (0,)), (span_mid, (1,))), 2 * unit_mid, 2 * unit_mid
    )
    second_grad, first_grad, skip_grad = land_grads(
        sent_early,
        ((span_mid, (0,)), (span_first, (1, 2))),
        2 * unit_mid,
        2 * unit_first,
        2 * unit_skip,
    )

    padded = -(-c_in // 128) * 128
    grad_pre, sums = call(
        functools.partial(entry_back, small),
        [shape((4 * area, c_in)), shape((8, padded))],
        [idx, *parts, pixels, norm_one, g_entry, s_entry],
    )
    message = call(
        bundle, shape((16, padded)), [idx, middle_sums, inner_sums, last_sums, sums]
    )
    sums, six = call(
        unbundle,
        [shape((8, padded)), shape((8, c_out))],
        [idx, *spread_out(message)],
        [pltpu.VMEM((PEERS, 16, padded), F32)],
    )
    gain_entry_grad, shift_entry_grad, image_grad = call(
        functools.partial(entry_grad, nz),
        [shape((1, padded)), shape((1, padded)), shape((4 * area, c_in))],
        [idx, *pool(sums, add_gx), grad_pre, pixels, wide, norm_one, g_entry],
        [pltpu.VMEM((nz, 8, padded), F32)],
    )

    return (
        out.reshape(1, small, small, c_out),
        image_grad.reshape(1, side, side, c_in),
        gain_entry_grad[0, :c_in],
        shift_entry_grad[0, :c_in],
        first_grad,
        six[0],
        six[1],
        second_grad,
        skip_grad,
        six[2],
        six[3],
        third_grad,
        six[4],
        six[5],
        fourth_grad,
    )


def solution(mesh):
    whole = P(("gx", "gy"), None, None, None)
    rows = P("gy", None)
    return jax.shard_map(
        functools.partial(program, mesh.shape["gx"], mesh.shape["gy"]),
        mesh=mesh,
        in_specs=(
            whole,
            P(("gx", "gy")),
            P(("gx", "gy"), None, None),
            P(),
            P(),
            rows,
            P(),
            P(),
            rows,
            rows,
            P(),
            P(),
            rows,
            P(),
            P(),
            rows,
            whole,
        ),
        out_specs=(
            whole, whole, P(), P(), rows, P(), P(), rows, rows, P(), P(), rows, P(), P(), rows,
        ),
        check_vma=False,
    )
```

```python
import functools

import jax
import jax.numpy as jnp
from jax import lax
from jax.experimental import pallas as pl
from jax.experimental.pallas import tpu as pltpu
from jax.sharding import PartitionSpec as P

EPS = 1e-05
F32 = jnp.float32
BF16 = jnp.bfloat16
PEERS = 4
C0 = 0.7978845608028654
C1 = 0.044715
VMEM = pl.BlockSpec(memory_space=pltpu.VMEM)
SMEM = pl.BlockSpec(memory_space=pltpu.SMEM)


def gelu(v):
    return 0.5 * v * (1.0 + jnp.tanh(C0 * (v + C1 * (v * v * v))))


def gelu_slope(v):
    t = jnp.tanh(C0 * (v + C1 * (v * v * v)))
    return 0.5 * (1.0 + t) + 0.5 * v * (1.0 - t * t) * (C0 * (1.0 + 3.0 * C1 * (v * v)))


def call(kernel, outs, args, scratch=(), flops=8 * 10**8):
    size = sum(a.size * a.dtype.itemsize for a in args)
    return pl.pallas_call(
        kernel,
        out_shape=outs,
        in_specs=[SMEM] + [VMEM] * (len(args) - 1),
        out_specs=jax.tree.map(lambda _: VMEM, outs),
        scratch_shapes=list(scratch),
        compiler_params=pltpu.CompilerParams(vmem_limit_bytes=16 * 1024 * 1024),
        cost_estimate=pl.CostEstimate(flops=flops, bytes_accessed=size, transcendentals=0),
    )(*args)


def shape(dims, dtype=F32):
    return jax.ShapeDtypeStruct(dims, dtype)


def rows_at(index, count):
    return pl.ds(pl.multiple_of(index * count, count), count)


def as_rows(parts):
    height = parts[0].shape[0]
    lane = lax.broadcasted_iota(jnp.int32, (height, 128), 1)
    out = jnp.zeros((height, 128), F32)
    for k, part in enumerate(parts):
        out = jnp.where(lane == k, part, out)
    return out.T[0:8]


def as_columns(rows):
    return jnp.concatenate([rows, jnp.zeros((120, rows.shape[1]), F32)], axis=0).T


def in_order(refs, me, scratch):
    for k, ref in enumerate(refs):
        scratch[me ^ k] = ref[...]
    return [scratch[k] for k in range(len(refs))]


def merge_moments(stats):
    total = sum(n for _, _, n in stats)
    mean = sum(n * m for m, _, n in stats) / total
    squares = sum(q + n * (m - mean) * (m - mean) for m, q, n in stats)
    return mean, squares, total


def merge_rows(refs):
    mean, squares, total = merge_moments([(g[0:1], g[1:2], g[2:3]) for g in refs])
    return mean, squares, total, sum(g[3:4] for g in refs)


def pixel(width, area, small):
    lane = lax.broadcasted_iota(jnp.int32, (1, width), 1) % area
    return lane // small, lane % small


def inside(row, col, drow, dcol, small):
    return (row + drow >= 0) & (row + drow < small) & (col + dcol >= 0) & (col + dcol < small)


def moved(value, step):
    shift = (-step) % value.shape[1]
    return pltpu.roll(value, shift, 1) if shift else value


OFFSETS = [(0, krow - 1, kcol - 1) for krow in range(3) for kcol in range(3)]

STRIDED = [
    ((krow != 1) * 2 + (kcol != 1), -(krow == 0), -(kcol == 0))
    for krow in range(3)
    for kcol in range(3)
] + [(0, 0, 0)]
PLACED = sorted(range(10), key=lambda k: (STRIDED[k][0], k))
PHASES = [[k for k in PLACED if STRIDED[k][0] == phase] for phase in range(4)]


def row_of(k, cs):
    at = PLACED.index(k)
    return slice(at * cs, (at + 1) * cs)


def phase_rows(phase, cs):
    first, last = PHASES[phase][0], PHASES[phase][-1]
    return slice(PLACED.index(first) * cs, (PLACED.index(last) + 1) * cs)


def masked_stats(value, weight, n):
    mean = jnp.sum(value * weight, axis=1, keepdims=True) / n
    centred = value - mean
    return mean, jnp.sum(weight * centred * centred, axis=1, keepdims=True)


def span_of(rows):
    return -(-rows // 128) * 128


def one_hot(height, width, shift):
    row = lax.broadcasted_iota(jnp.int32, (height, width), 0)
    col = lax.broadcasted_iota(jnp.int32, (height, width), 1)
    return (col == row + shift).astype(BF16)


def pick32(left, right, dims=((1,), (0,))):
    return lax.dot_general(left, right, (dims, ((), ())), preferred_element_type=F32)


def pick(left, right, dims=((1,), (0,))):
    return pick32(left, right, dims).astype(BF16)


def lane_tile(held, tile, rows, span):
    sides, ny = held.shape[1], held.shape[2]
    lane = lax.broadcasted_iota(jnp.int32, (1, 128), 1)
    out = None
    for v in range(2 * ny):
        begin = rows * v - tile * 128
        if begin >= 128 or begin + rows <= 0:
            continue
        at = (tile - rows * v // 128) * 128 % span
        part = jnp.concatenate(
            [held[v % 2, x, v // 2, :, at : at + 128].astype(F32) for x in range(sides)], axis=0
        )
        if begin > 0 or begin + rows < 128:
            own = (lane >= begin) & (lane < begin + rows)
            part = jnp.where(own, part, 0.0)
        out = part if out is None else out + part
    return out.astype(BF16)


def pixel_order(small, width, of):
    area = small * small
    row = lax.broadcasted_iota(jnp.int32, (4 * area, width), 0)
    col = lax.broadcasted_iota(jnp.int32, (4 * area, width), 1)
    phase, pix = row // area, row % area
    y = 2 * (pix // small) + phase // 2
    x = 2 * (pix % small) + phase % 2
    return (col == of(y, x)).astype(BF16)


def entry_image(small, idx, image, mask, valid, out, weight):
    side = 2 * small
    c_in = image.shape[1]
    count = side * side
    order = pixel_order(small, count, lambda y, x: y * side + x)
    out[:, :c_in] = pick(order, image[...])
    live = (valid[0] > 0).astype(F32)
    row = lax.broadcasted_iota(jnp.int32, (count, side), 0)
    col = lax.broadcasted_iota(jnp.int32, (count, side), 1)
    by_row = jnp.dot(
        (row // side == col).astype(BF16),
        mask[...].astype(F32).astype(BF16),
        preferred_element_type=F32,
    )
    column = jnp.sum(jnp.where(row % side == col, by_row, 0.0), axis=1, keepdims=True) * live
    lane = lax.broadcasted_iota(jnp.int32, (count, 128), 1)
    spread = jnp.where(lane == 0, column, 0.0)
    weight[...] = spread
    out[:, c_in:] = pick(order, spread.astype(BF16))[:, : out.shape[1] - c_in]


def entry_weights(cs, fy, idx, *refs):
    weights, out = refs[:-1], refs[-1]
    ny, cb, span = out.shape
    gx, gy = idx[2], idx[3]
    core, side = gx % 2, gx // 2
    c_out = weights[0].shape[1]
    unit = weights[0].shape[0] // 2
    begin = unit * (2 * gy + core) % 128
    row = lax.broadcasted_iota(jnp.int32, (fy * cb, c_out), 0)
    col = lax.broadcasted_iota(jnp.int32, (fy * cb, c_out), 1)
    chosen = (col == row // cb * cs + side * cb + row % cb).astype(BF16)
    total = None
    for weight in weights:
        rows = weight.shape[0]
        half = rows // 2
        mine = pick(chosen, weight[...], ((1,), (1,)))
        row = lax.broadcasted_iota(jnp.int32, (rows, span), 0) - core * half
        col = lax.broadcasted_iota(jnp.int32, (rows, span), 1)
        place = (row >= 0) & (row < half) & (
            (col == row + begin) | (col == row + begin - span)
        )
        part = pick32(mine, place.astype(BF16))
        total = part if total is None else total + part
        begin = begin + half
    for j in range(ny):
        out[j] = total[(j % fy) * cb : (j % fy + 1) * cb].astype(BF16)


def hold(gx, messages, held):
    for k, ref in enumerate(messages):
        at = gx ^ k
        held[at % 2, at // 2] = ref[...]


def assemble(held, out, rows):
    cs, span = held.shape[1] * held.shape[3], held.shape[4]
    tiles = out.shape[1] // 128
    for k in range(9):
        for q in range(tiles):
            out[k * cs : (k + 1) * cs, q * 128 : (q + 1) * 128] = lane_tile(
                held, tiles * k + q, rows, span
            )


def assemble_first(held, out, flat, rows, extra):
    cs, span = held.shape[1] * held.shape[3], held.shape[4]
    c_in = out.shape[1]
    tiles = flat.shape[1] // 128
    for tile in range(tiles):
        flat[:, tile * 128 : (tile + 1) * 128] = lane_tile(held, tile, rows, span)
    for k in range(9):
        begin = k * c_in
        base = begin // 128 * 128
        reach = min(-(-(begin + c_in) // 128) * 128, flat.shape[1])
        move = one_hot(c_in, reach - base, begin - base)
        out[row_of(k, cs), :] = pick(flat[:, base:reach], move, ((1,), (1,)))
    total = None
    for v in range(2 * held.shape[2]):
        row = lax.broadcasted_iota(jnp.int32, (span, c_in), 0)
        col = lax.broadcasted_iota(jnp.int32, (span, c_in), 1)
        at = col - extra * v
        begin = rows * v % 128 + rows
        place = (at >= 0) & (at < extra) & ((row == at + begin) | (row == at + begin - span))
        part = jnp.concatenate(
            [
                pick32(held[v % 2, x, v // 2], place.astype(BF16))
                for x in range(held.shape[1])
            ],
            axis=0,
        )
        total = part if total is None else total + part
    out[row_of(9, cs), :] = total.astype(BF16)


def entry_stats(area, idx, *refs):
    images, out = refs[:PEERS], refs[PEERS]
    lanes = out.shape[1]
    first = jnp.zeros((1, lanes), F32)
    wide = jnp.zeros((1, 1), F32)
    narrow = jnp.zeros((1, 1), F32)
    c_in = lanes - 64
    for ref in images:
        x = ref[...].astype(F32)
        w = x[:, c_in : c_in + 1]
        first += jnp.sum(x * w, axis=0, keepdims=True)
        wide += jnp.sum(w, axis=0, keepdims=True)
        narrow += jnp.sum(w[:area], axis=0, keepdims=True)
    mean = first / wide
    squares = jnp.zeros((1, lanes), F32)
    for ref in images:
        x = ref[...].astype(F32)
        w = x[:, c_in : c_in + 1]
        d = x - mean
        squares += jnp.sum(d * d * w, axis=0, keepdims=True)
    out[...] = jnp.zeros_like(out)
    out[0:1, :] = mean
    out[1:2, :] = squares
    out[2:3, :] = jnp.broadcast_to(wide, (1, lanes))
    out[3:4, :] = jnp.broadcast_to(narrow, (1, lanes))


def entry_block(nz, nx, rows, extra, area, small, idx, *refs):
    images = refs[:PEERS]
    stats, rest = refs[PEERS : PEERS + nz], refs[PEERS + nz :]
    gain, shift, messages, rest = rest[0], rest[1], rest[2 : 2 + nx], rest[2 + nx :]
    first, skipped, out_stats, norm, narrow, act, w_first = rest[:7]
    order, masks, flat, held = rest[7:]
    me, mine = idx[0], idx[1]
    c_in = gain.shape[1]
    lanes = norm.shape[1]
    cs = first.shape[0]
    width = first.shape[1]
    hold(idx[2], messages, held)
    assemble_first(held, w_first, flat, rows, extra)
    mean, squares, total, count = merge_rows(in_order(stats, mine, order))
    scale = lax.rsqrt(squares / total + EPS)
    norm[...] = jnp.zeros_like(norm)
    norm[0:1, :] = mean
    norm[1:2, :] = scale
    norm[2:3, :] = total
    norm[3:4, :] = count
    for k, ref in enumerate(images):
        x = ref[...]
        v = x[:, :c_in].astype(F32)
        pre = gain[...] * ((v - mean[:, :c_in]) * scale[:, :c_in]) + shift[...]
        a = gelu(pre).astype(BF16)
        for phase in range(4):
            act[phase, rows_at(me ^ k, area), :] = a[phase * area : (phase + 1) * area]
        masks[rows_at(me ^ k, area), :] = x[:area]
    ones = (lax.broadcasted_iota(jnp.int32, (8, lanes), 1) == c_in).astype(BF16)
    weight8 = lax.dot_general(
        ones, masks[...], (((1,), (1,)), ((), ())), preferred_element_type=F32
    )
    narrow[...] = weight8
    weight = weight8[0:1]
    row, col = pixel(width, area, small)
    total_first = jnp.zeros((cs, width), F32)
    for phase in range(4):
        group = lax.dot_general(
            w_first[phase_rows(phase, cs), :],
            act[phase],
            (((1,), (1,)), ((), ())),
            preferred_element_type=F32,
        )
        for at, k in enumerate(PHASES[phase]):
            y = group[at * cs : (at + 1) * cs]
            if k == 9:
                skipped[...] = y
                continue
            _, drow, dcol = STRIDED[k]
            y = moved(y, drow * small + dcol)
            total_first += jnp.where(inside(row, col, drow, dcol, small), y, 0.0)
    first[...] = total_first
    n = jnp.sum(weight, axis=1, keepdims=True)
    mean2, squares = masked_stats(total_first, weight, n)
    out_stats[...] = as_rows((mean2, squares, n))


def merge_stats(idx, *refs):
    out, order = refs[-2:]
    mean, squares, total, count = merge_rows(in_order(refs[:-2], idx[2], order))
    out[...] = jnp.zeros_like(out)
    out[0:1] = mean
    out[1:2] = squares
    out[2:3] = total
    out[3:4] = count


def add_rows(which, idx, *refs):
    out, order = refs[-2:]
    got = in_order(refs[:-2], idx[which], order)
    total = got[0]
    for g in got[1:]:
        total = total + g
    out[...] = total


def act_block(nz, idx, *refs):
    value, params = refs[:2]
    stats, rest = refs[2 : 2 + nz], refs[2 + nz :]
    if rest[-1].shape[1] == 128:
        cot, normed, scales, outs, order, stack = (*rest[:3], rest[3:-2], *rest[-2:])
    else:
        cot, normed, scales, outs, order = (None, *rest[:2], rest[2:-1], rest[-1])
    mean, squares, total, _ = merge_rows(in_order(stats, idx[1], order))
    rows = jnp.concatenate(
        [mean, lax.rsqrt(squares / total + EPS), total, jnp.zeros((5, mean.shape[1]), F32)], axis=0
    )
    cols = as_columns(rows)
    norm = (value[...] - cols[:, 0:1]) * cols[:, 1:2]
    normed[...] = norm
    act = gelu(params[:, 0:1] * norm + params[:, 1:2]).astype(BF16)
    cs, width = norm.shape
    if cot is not None:
        c = cot[...].astype(F32)
        stack[...] = jnp.concatenate([c, c], axis=0).T
    for k, out in enumerate(outs):
        out[:, :width] = act
        if cot is not None:
            out[:, width:] = stack[rows_at(idx[0] ^ k, cs), :].astype(BF16)
    scales[...] = cols


def conv_block(nx, added, last, rows, area, small, idx, *refs):
    pieces = refs[:PEERS]
    narrow, rest = refs[PEERS], refs[PEERS + 1 :]
    if last:
        weights, rest = rest[0], rest[1:]
    else:
        messages, rest = rest[:nx], rest[nx:]
    base, rest = (rest[0], rest[1:]) if added else (None, rest)
    me = idx[0]
    cs, width = pieces[0].shape[0], narrow.shape[1]
    if last:
        outs, act, spread = rest[:PEERS], rest[PEERS], rest[PEERS + 1]
    else:
        value, out_stats, act, whole, spread, held = rest
        hold(idx[2], messages, held)
        assemble(held, whole, rows)
        weights = whole
    for k, ref in enumerate(pieces):
        act[rows_at(me ^ k, cs), :] = ref[:, :width]
    spread[...] = jnp.dot(weights[...], act[...], preferred_element_type=F32)
    row, col = pixel(width, area, small)
    total = base[...] if added else jnp.zeros((cs, width), F32)
    for k, (_, drow, dcol) in enumerate(OFFSETS):
        y = moved(spread[k * cs : (k + 1) * cs, :], drow * small + dcol)
        total += jnp.where(inside(row, col, drow, dcol, small), y, 0.0)
    if last:
        result = total.astype(BF16)
        lane = lax.broadcasted_iota(jnp.int32, (width, 128), 0)
        slot = lax.broadcasted_iota(jnp.int32, (width, 128), 1)
        for k, out in enumerate(outs):
            out[...] = pick(result, (lane == (me ^ k) * area + slot).astype(BF16))
    else:
        value[...] = total
        weight = narrow[0:1, :]
        n = jnp.sum(weight, axis=1, keepdims=True)
        mean, squares = masked_stats(total, weight, n)
        out_stats[...] = as_rows((mean, squares, n))


def join_result(idx, *refs):
    pieces, (out, stack) = refs[:PEERS], refs[PEERS:]
    cs = pieces[0].shape[0]
    for k, ref in enumerate(pieces):
        stack[rows_at(idx[0] ^ k, cs), :] = ref[:, -128:].astype(F32)
    out[...] = stack[...].T[: out.shape[0]].astype(BF16)


def spread_grad(grad, shifted, area, small, offs, row_at):
    cs, width = grad.shape
    row, col = pixel(width, area, small)
    for k, (_, drow, dcol) in enumerate(offs):
        g = moved(grad, -(drow * small + dcol))
        g = jnp.where(inside(row, col, -drow, -dcol, small), g, 0.0)
        shifted[row_at(k, cs), :] = g.astype(BF16)


def plain_rows(k, cs):
    return slice(k * cs, (k + 1) * cs)


def push_back(me, weights, shifted, partial, outs):
    cs, width = outs[0].shape[0], shifted.shape[1]
    partial[...] = lax.dot_general(
        weights[...], shifted[...], (((0,), (0,)), ((), ())), preferred_element_type=F32
    )
    for k, out in enumerate(outs):
        out[:, :width] = partial[rows_at(me ^ k, cs), :].astype(BF16)


def last_back(nx, rows, area, small, idx, *refs):
    pieces, messages, rest = refs[:PEERS], refs[PEERS : PEERS + nx], refs[PEERS + nx :]
    cot, shifted, weights = rest[:3]
    outs = rest[3 : PEERS + 3]
    partial, held = rest[PEERS + 3 :]
    hold(idx[2], messages, held)
    assemble(held, weights, rows)
    me = idx[0]
    cs, width = cot.shape
    image = lax.broadcasted_iota(jnp.int32, (1, width), 1) // area
    grad = jnp.zeros((cs, width), F32)
    for k, ref in enumerate(pieces):
        tiled = jnp.concatenate([ref[:, width:].astype(F32)] * (width // 128), axis=1)
        grad = jnp.where(image == (me ^ k), tiled, grad)
    cot[...] = grad
    spread_grad(grad, shifted, area, small, OFFSETS, plain_rows)
    push_back(me, weights, shifted, partial, outs)


def gelu_back(idx, *refs):
    pieces = refs[:PEERS]
    normed, params, grad_pre, sums = refs[PEERS:]
    width = normed.shape[1]
    grad = pieces[0][:, :width].astype(F32)
    for ref in pieces[1:]:
        grad += ref[:, :width].astype(F32)
    norm = normed[...]
    g = gelu_slope(params[:, 0:1] * norm + params[:, 1:2]) * grad
    grad_pre[...] = g
    sums[...] = as_rows(
        (jnp.sum(g * norm, axis=1, keepdims=True), jnp.sum(g, axis=1, keepdims=True))
    )


def norm_back(nz, added, last, area, small, idx, *refs):
    grad_pre, normed, scales, params, narrow = refs[:5]
    sums = refs[5 : 5 + nz]
    rest = refs[5 + nz :]
    base, rest = (rest[0], rest[1:]) if added else (None, rest)
    me = idx[0]
    cs, width = grad_pre.shape
    order = rest[-1]
    got = in_order(sums, idx[1], order)
    total = got[0]
    for g in got[1:]:
        total = total + g
    cols = as_columns(total)
    gain_grad, shift_grad = cols[:, 0:1], cols[:, 1:2]
    norm = normed[...]
    back = params[:, 0:1] * scales[:, 1:2] * (
        grad_pre[...]
        - narrow[0:1, :] * (shift_grad + norm * gain_grad) / scales[:, 2:3]
    )
    if added:
        back = base[...] + back
    grad = back.astype(BF16).astype(F32)
    if not last:
        riders = ()
        if not added:
            riders, rest = rest[:PEERS], rest[PEERS:]
        weights, sums_out, shifted = rest[:3]
        outs, partial = rest[3 : 3 + PEERS], rest[3 + PEERS]
        for rider, out in zip(riders, outs):
            out[:, width:] = rider[...]
        if added:
            grad_out, outs, partial = rest[3], rest[4 : 4 + PEERS], rest[4 + PEERS]
            grad_out[...] = grad.astype(BF16)
        sums_out[...] = total
        spread_grad(grad, shifted, area, small, OFFSETS, plain_rows)
        push_back(me, weights, shifted, partial, outs)
    else:
        weights, grad_skip, sums_out, shifted = rest[:4]
        outs, partial = rest[4 : 4 + PEERS], rest[4 + PEERS]
        sums_out[...] = total
        spread_grad(grad, shifted, area, small, STRIDED[:9], row_of)
        shifted[row_of(9, cs), :] = grad_skip[...]
        for phase in range(4):
            partial[phase] = lax.dot_general(
                shifted[phase_rows(phase, cs), :],
                weights[phase_rows(phase, cs), :],
                (((0,), (0,)), ((), ())),
                preferred_element_type=F32,
            )
        for k, out in enumerate(outs):
            for phase in range(4):
                out[phase * area : (phase + 1) * area, :] = partial[
                    phase, rows_at(me ^ k, area), :
                ].astype(BF16)


def part_halves(core, units, own, other):
    own[...] = units[core]
    other[...] = units[1 - core].astype(BF16)


def weight_grad(rows, idx, shifted, act, own, other, full, units):
    full[...] = lax.dot_general(
        shifted[...], act[...], (((1,), (1,)), ((), ())), preferred_element_type=F32
    )
    ny, cs, span = own.shape
    tiles = full.shape[1] // 128
    for v in range(2 * ny):
        begin = rows * v % 128
        parts = []
        for q in range((begin + rows + 127) // 128):
            k, p = divmod(rows * v // 128 + q, tiles)
            parts.append(full[k * cs : (k + 1) * cs, p * 128 : (p + 1) * 128])
        window = jnp.concatenate(parts, axis=1)
        units[v % 2, v // 2] = moved(window, begin)[:, :span]
    part_halves(idx[2] % 2, units, own, other)


def weight_grad_first(rows, extra, idx, shifted, act, own, other, flat, units):
    ny, cs, span = own.shape
    c_in = act.shape[2]
    flat[...] = jnp.zeros_like(flat)
    skip = None
    for phase in range(4):
        group = jnp.dot(
            shifted[phase_rows(phase, cs), :], act[phase], preferred_element_type=F32
        ).astype(BF16)
        for at, k in enumerate(PHASES[phase]):
            grad = group[at * cs : (at + 1) * cs]
            if k == 9:
                skip = grad
                continue
            begin = k * c_in
            base = begin // 128 * 128
            reach = -(-(begin + c_in) // 128) * 128
            move = one_hot(c_in, reach - base, begin - base)
            flat[:, base:reach] += jnp.dot(grad, move, preferred_element_type=F32)
    lane = lax.broadcasted_iota(jnp.int32, (1, span), 1)
    for v in range(2 * ny):
        begin = rows * v % 128
        base = rows * v - begin
        window = moved(flat[:, base : base + span + 128], begin)[:, :span]
        row = lax.broadcasted_iota(jnp.int32, (c_in, span), 0)
        col = lax.broadcasted_iota(jnp.int32, (c_in, span), 1)
        place = (row >= extra * v) & (row < extra * (v + 1)) & (col == row - extra * v + rows)
        tail = pick32(skip, place.astype(BF16))
        units[v % 2, v // 2] = jnp.where(lane < rows, window, 0.0) + tail
    part_halves(idx[2] % 2, units, own, other)


def reduce_core(count, idx, *refs):
    own, other, outs, total = refs[:count], refs[count : 2 * count], refs[2 * count : -1], refs[-1]
    cb = outs[0].shape[1]
    at = 0
    for a, b in zip(own, other):
        span = a.shape[2]
        total[:, :, at : at + span] = a[...] + b[...].astype(F32)
        at += span
    for k, out in enumerate(outs):
        for j in range(total.shape[0]):
            out[j] = total[j, rows_at(idx[2] // 2 ^ k, cb), :].astype(out.dtype)


def reduce_side(sides, idx, *refs):
    out = refs[-1]
    at = 0
    for n in range(0, len(refs) - 1, sides):
        total = refs[n][...]
        for ref in refs[n + 1 : n + sides]:
            total += ref[...].astype(F32)
        out[:, :, at : at + total.shape[2]] = total.astype(BF16)
        at += total.shape[2]


def fold(nz, fy, idx, got, out):
    cs = got.shape[1]
    for f in range(fy):
        total = got[f].astype(F32)
        for z in range(1, nz):
            total += got[z * fy + f].astype(F32)
        out[f * cs : (f + 1) * cs, :] = total.astype(BF16)


def own_rows(count, spans, idx, *refs):
    pieces, outs, stack = refs[:count], refs[count:-1], refs[-1]
    for k, ref in enumerate(pieces):
        at = idx[2] ^ k
        stack[at % 2, at // 2] = ref[...]
    sides, height = stack.shape[1], stack.shape[2]
    fy_cb = [(f, x) for f in range(PEERS) for x in range(sides)]
    cb = height // PEERS
    for half in range(2):
        whole = jnp.concatenate(
            [stack[half, x, f * cb : (f + 1) * cb, :].astype(F32) for f, x in fy_cb], axis=0
        ).T
        at = 0
        for span, group in spans:
            begin = at
            for n in group:
                out = outs[n]
                rows = out.shape[0] // 2
                out[half * rows : (half + 1) * rows, :] = whole[begin : begin + rows]
                begin += rows
            at += span


def entry_back(small, idx, *refs):
    pieces = refs[:PEERS]
    image, norm, gain, shift, grad_pre, sums = refs[PEERS:]
    c_in = gain.shape[1]
    side = 2 * small
    grad = pieces[0][...].astype(F32)
    for ref in pieces[1:]:
        grad += ref[...].astype(F32)
    order = pixel_order(small, side * side, lambda y, x: y * side + x)
    high = grad.astype(BF16)
    low = (grad - high.astype(F32)).astype(BF16)
    grad = sum(
        lax.dot_general(order, part, (((0,), (0,)), ((), ())), preferred_element_type=F32)
        for part in (high, low)
    )
    normed = (image[...].astype(F32) - norm[0:1, :c_in]) * norm[1:2, :c_in]
    g = gelu_slope(gain[...] * normed + shift[...]) * grad
    grad_pre[...] = g
    sums[...] = jnp.zeros_like(sums)
    sums[0:1, :c_in] = jnp.sum(g * normed, axis=0, keepdims=True)
    sums[1:2, :c_in] = jnp.sum(g, axis=0, keepdims=True)


def bundle(idx, first, second, third, sums, out):
    out[...] = jnp.zeros_like(out)
    out[0:8, :] = sums[...]
    for k, ref in enumerate((first, second, third)):
        out[8 + 2 * k : 10 + 2 * k, : ref.shape[1]] = ref[0:2]


def unbundle(idx, *refs):
    out, six, order = refs[-3:]
    got = in_order(refs[:-3], idx[0], order)
    total = got[0][0:8]
    for g in got[1:]:
        total = total + g[0:8]
    out[...] = total
    cs = six.shape[1] // PEERS
    six[...] = jnp.concatenate([g[8:16, :cs] for g in got], axis=1)


def entry_grad(nz, idx, *refs):
    sums = refs[:nz]
    grad_pre, image, weight, norm, gain, gain_grad, shift_grad, out, order = refs[nz:]
    got = in_order(sums, idx[1], order)
    total = got[0]
    for g in got[1:]:
        total = total + g
    gain_grad[...] = total[0:1]
    shift_grad[...] = total[1:2]
    c_in = gain.shape[1]
    scale = norm[1:2, :c_in]
    normed = (image[...].astype(F32) - norm[0:1, :c_in]) * scale
    out[...] = gain[...] * scale * (
        grad_pre[...]
        - weight[:, 0:1]
        * (shift_grad[0:1, :c_in] + normed * gain_grad[0:1, :c_in])
        / norm[2:3, :c_in]
    )


def program(
    nx,
    ny,
    images,
    valid_count,
    pixel_mask,
    gain_entry,
    shift_entry,
    conv_first,
    gain_middle,
    shift_middle,
    conv_second,
    projection,
    gain_inner,
    shift_inner,
    conv_third,
    gain_last,
    shift_last,
    conv_fourth,
    cotangent,
):
    fy = PEERS
    nz = ny // fy
    side, c_in = images.shape[1], images.shape[3]
    small = side // 2
    area = small * small
    c_out = conv_first.shape[1]
    cs = c_out // PEERS
    width = PEERS * area
    lanes = c_in + 64
    gx, gy = lax.axis_index("gx"), lax.axis_index("gy")
    me = gy % fy
    mine = gy // fy
    idx = jnp.stack([me, mine, gx, gy]).astype(jnp.int32)

    def to_slice(piece, k):
        return lax.ppermute(piece, "gy", [(j, j // fy * fy + (j % fy ^ k)) for j in range(ny)])

    def share(pieces):
        return [pieces[0]] + [to_slice(pieces[k], k) for k in range(1, PEERS)]

    def spread_out(piece):
        return share([piece] * PEERS)

    def to_gx(piece, k):
        return lax.ppermute(piece, "gx", [(i, i ^ k) for i in range(nx)])

    def pool(piece, kernel):
        pieces = [piece] + [to_gx(piece, k) for k in range(1, nx)]
        piece = call(
            kernel,
            shape(piece.shape),
            [idx, *pieces],
            [pltpu.VMEM((nx, *piece.shape), F32)],
        )
        out = [piece]
        for k in range(1, nz):
            perm = [(j, (j // fy ^ k) * fy + j % fy) for j in range(ny)]
            out.append(lax.ppermute(piece, "gy", perm))
        return out

    add_gx = functools.partial(add_rows, 2)

    def after(value, *others):
        return lax.optimization_barrier((value, *others))[0]

    def turn(block):
        return lax.all_to_all(block, "gy", 0, 0, tiled=True)

    def along_gx(block):
        held = {0: block}
        for k in range(2, nx, 2):
            held[k] = to_gx(block, k)
        for k in range(0, nx, 2):
            held[k + 1] = to_gx(held[k], 1)
        return [held[k] for k in range(nx)]

    unit_first, unit_skip = conv_first.shape[0] // 2, projection.shape[0] // 2
    unit_mid = conv_second.shape[0] // 2
    span_first, span_mid = span_of(unit_first + unit_skip), span_of(unit_mid)

    cb = cs // (nx // 2)

    def ready(span, *weights):
        return call(
            functools.partial(entry_weights, cs, fy),
            shape((ny, cb, span), BF16),
            [idx, *weights],
            flops=20 * 10**8,
        )

    def halves(span):
        return pltpu.VMEM((2, nx // 2, ny, cb, span), BF16)

    pixels = images.reshape(side * side, c_in)
    image, wide = pl.pallas_call(
        functools.partial(entry_image, small),
        out_shape=[shape((4 * area, lanes), BF16), shape((4 * area, 128))],
        in_specs=[SMEM, VMEM, VMEM, SMEM],
        out_specs=[VMEM, VMEM],
        compiler_params=pltpu.CompilerParams(vmem_limit_bytes=16 * 1024 * 1024),
        cost_estimate=pl.CostEstimate(flops=1 << 20, bytes_accessed=1 << 20, transcendentals=0),
    )(idx, pixels, pixel_mask.reshape(side, side), valid_count)
    group = spread_out(image)
    got_first = along_gx(turn(after(ready(span_first, conv_first, projection), *group[1:])))

    def own(gain, shift):
        pair = jnp.stack([gain, shift], axis=1)
        return lax.dynamic_slice_in_dim(pair, me * cs, cs, axis=0)

    p_middle = own(gain_middle, shift_middle)
    p_inner = own(gain_inner, shift_inner)
    p_last = own(gain_last, shift_last)
    g_entry, s_entry = gain_entry[None], shift_entry[None]

    tile = shape((cs, width))
    tile16 = shape((cs, width), BF16)
    cols = shape((cs, 128))
    stat = shape((8, cs))
    stat_order = pltpu.VMEM((nz, 8, cs), F32)
    full16 = shape((c_out, width), BF16)
    whole16 = shape((9 * cs, c_out), BF16)
    conv_flops = 25 * 10**8

    stats = call(functools.partial(entry_stats, area), shape((8, lanes)), [idx, *group])
    pooled = pool(stats, merge_stats)
    out_second = ready(span_mid, conv_second)
    out_third = ready(span_mid, conv_third)
    out_fourth = ready(span_mid, conv_fourth)
    got_second = turn(after(out_second, pooled[-1]))
    first, skipped, stats, norm_one, narrow, act_one, w_first = call(
        functools.partial(entry_block, nz, nx, unit_first, unit_skip, area, small),
        [
            tile,
            tile,
            stat,
            shape((8, lanes)),
            shape((8, width)),
            shape((4, width, c_in), BF16),
            shape((10 * cs, c_in), BF16),
        ],
        [
            idx,
            *group,
            *pooled,
            after(g_entry, out_second, out_third, out_fourth),
            s_entry,
            *got_first,
        ],
        [
            pltpu.VMEM((nz, 8, lanes), F32),
            pltpu.VMEM((width, lanes), BF16),
            pltpu.VMEM((cs, span_of(9 * c_in)), BF16),
            halves(span_first),
        ],
        flops=conv_flops // 2,
    )

    def activate(value, params, pooled, cot=None):
        more = [] if cot is None else [cot]
        count = 1 if cot is None else PEERS
        out = tile16 if cot is None else shape((cs, width + 128), BF16)
        return call(
            functools.partial(act_block, nz),
            [tile, cols] + [out] * count,
            [idx, value, params, *pooled, *more],
            [stat_order] + ([] if cot is None else [pltpu.VMEM((c_out, 128), F32)]),
        )

    def convolve(pieces, weights, base, last=False):
        more = [] if base is None else [base]
        if last:
            outs = [shape((cs, 128), BF16)] * PEERS + [full16]
        else:
            outs = [tile, stat, full16, whole16]
        return call(
            functools.partial(conv_block, nx, base is not None, last, unit_mid, area, small),
            outs,
            [idx, *pieces, narrow, *weights, *more],
            [pltpu.VMEM((9 * cs, width), F32)] + ([] if last else [halves(span_mid)]),
            flops=conv_flops,
        )

    pooled = pool(stats, merge_stats)
    got_second = along_gx(after(got_second, pooled[0]))
    got_third = turn(after(out_third, pooled[-1]))
    normed_two, scale_two, *messages = activate(
        first, p_middle, pooled, cotangent.reshape(area, c_out)
    )
    pieces = share(messages)
    hidden, stats, act_two, w_second = convolve(pieces, got_second, skipped)
    got_fourth = turn(after(out_fourth, stats))
    pooled = pool(stats, merge_stats)
    got_third = along_gx(after(got_third, pooled[0]))
    got_fourth = along_gx(after(got_fourth, pooled[-1]))
    normed_three, scale_three, act = activate(hidden, p_inner, pooled)
    third, stats, act_three, w_third = convolve(spread_out(act), got_third, None)
    normed_four, scale_four, act = activate(third, p_last, pool(stats, merge_stats))

    cot, shifted_four, w_fourth, *parts = call(
        functools.partial(last_back, nx, unit_mid, area, small),
        [tile, shape((9 * cs, width), BF16), whole16] + [tile16] * PEERS,
        [idx, *pieces, *got_fourth],
        [pltpu.VMEM((c_out, width), F32), halves(span_mid)],
        flops=conv_flops,
    )

    def slope(parts, normed, params, *done):
        return call(gelu_back, [tile, stat], [idx, *parts, after(normed, *done), params])

    def back(grad_pre, normed, scales, params, pooled, weights, base, riders=()):
        more = list(riders) if base is None else [base]
        part = tile16 if base is not None else shape((cs, width + 128), BF16)
        outs = [stat, shape((9 * cs, width), BF16)] + ([] if base is None else [tile16])
        return call(
            functools.partial(norm_back, nz, base is not None, False, area, small),
            outs + [part] * PEERS,
            [idx, grad_pre, normed, scales, params, narrow, *pooled, *more, weights],
            [pltpu.VMEM((c_out, width), F32), stat_order],
            flops=conv_flops,
        )

    def grad_of(kernel, span, shifted, act, scratch):
        return call(
            kernel,
            [shape((ny, cs, span)), shape((ny, cs, span), BF16)],
            [idx, shifted, act],
            [scratch, pltpu.VMEM((2, ny, cs, span), F32)],
            flops=conv_flops,
        )

    def grad_mid(shifted, act):
        kernel = functools.partial(weight_grad, unit_mid)
        return grad_of(kernel, span_mid, shifted, act, pltpu.VMEM((9 * cs, c_out), F32))

    def reduce_grads(*grads):
        own = [a for a, _ in grads]
        other = [to_gx(b, 1) for _, b in grads]
        span = sum(a.shape[2] for a in own)
        sides = nx // 2
        return call(
            functools.partial(reduce_core, len(own)),
            [shape((ny, cb, span))] + [shape((ny, cb, span), BF16)] * (sides - 1),
            [idx, *own, *other],
            [pltpu.VMEM((ny, cs, span), F32)],
        )

    def move_sides(parts):
        return [parts[0]] + [to_gx(parts[k], 2 * k) for k in range(1, nx // 2)]

    def add_sides(*groups):
        span = sum(parts[0].shape[2] for parts in groups)
        return call(
            functools.partial(reduce_side, nx // 2),
            shape((ny, cb, span), BF16),
            [idx, *[p for parts in groups for p in parts]],
        )

    def merge_sides(parts):
        return add_sides(move_sides(parts))

    def land_grads(got, spans, *rows):
        span = got.shape[2]
        got = call(functools.partial(fold, nz, fy), shape((fy * cb, span), BF16), [idx, got])
        return call(
            functools.partial(own_rows, nx, spans),
            [shape((r, c_out)) for r in rows],
            [idx, *along_gx(got)],
            [pltpu.VMEM((2, nx // 2, fy * cb, span), BF16)],
        )

    grad_pre, sums = slope(share(parts), normed_four, p_last)
    pooled = pool(sums, add_gx)
    *out_parts, act_four = convolve(spread_out(act), [w_fourth], hidden, last=True)

    grad_fourth = grad_mid(shifted_four, act_four)
    last_sums, shifted_three, *parts = back(
        grad_pre,
        normed_four,
        scale_four,
        after(p_last, *grad_fourth),
        pooled,
        w_third,
        None,
        out_parts,
    )
    parts = share(parts)
    out = call(
        join_result,
        shape((area, c_out), BF16),
        [idx, *parts],
        [pltpu.VMEM((c_out, 128), F32)],
    )
    grad_pre, sums = slope(parts, normed_three, p_inner)
    grad_third = grad_mid(after(shifted_three, sums), act_three)
    inner_sums, shifted_two, grad_hidden, *parts = back(
        grad_pre,
        normed_three,
        scale_three,
        after(p_inner, *grad_third),
        pool(sums, add_gx),
        w_second,
        cot,
    )
    late = reduce_grads(grad_fourth, grad_third)
    grad_pre, sums = slope(share(parts), normed_two, p_middle, late[0])
    grad_second = grad_mid(after(shifted_two, sums), act_two)
    pooled = pool(sums, add_gx)
    late = move_sides([after(p, pooled[0]) for p in late])
    middle_sums, shifted_one, *parts = call(
        functools.partial(norm_back, nz, False, True, area, small),
        [stat, shape((10 * cs, width), BF16)] + [shape((4 * area, c_in), BF16)] * PEERS,
        [
            idx,
            grad_pre,
            normed_two,
            scale_two,
            p_middle,
            after(narrow, *grad_second),
            *pooled,
            w_first,
            grad_hidden,
        ],
        [pltpu.VMEM((4, width, c_in), F32), stat_order],
        flops=conv_flops // 2,
    )
    parts = share(parts)
    sent_late = turn(add_sides([after(late[0], *parts[1:])] + late[1:]))
    grad_first = grad_of(
        functools.partial(weight_grad_first, unit_first, unit_skip),
        span_first,
        after(shifted_one, *parts[1:]),
        act_one,
        pltpu.VMEM((cs, span_of(9 * c_in + span_first + 128)), F32),
    )
    sent_early = turn(
        add_sides(move_sides(reduce_grads(grad_second)), move_sides(reduce_grads(grad_first)))
    )
    fourth_grad, third_grad = land_grads(
        sent_late, ((span_mid, (0,)), (span_mid, (1,))), 2 * unit_mid, 2 * unit_mid
    )
    second_grad, first_grad, skip_grad = land_grads(
        sent_early,
        ((span_mid, (0,)), (span_first, (1, 2))),
        2 * unit_mid,
        2 * unit_first,
        2 * unit_skip,
    )

    padded = -(-c_in // 128) * 128
    grad_pre, sums = call(
        functools.partial(entry_back, small),
        [shape((4 * area, c_in)), shape((8, padded))],
        [idx, *parts, pixels, norm_one, g_entry, s_entry],
    )
    message = call(
        bundle, shape((16, padded)), [idx, middle_sums, inner_sums, last_sums, sums]
    )
    sums, six = call(
        unbundle,
        [shape((8, padded)), shape((8, c_out))],
        [idx, *spread_out(message)],
        [pltpu.VMEM((PEERS, 16, padded), F32)],
    )
    gain_entry_grad, shift_entry_grad, image_grad = call(
        functools.partial(entry_grad, nz),
        [shape((1, padded)), shape((1, padded)), shape((4 * area, c_in))],
        [idx, *pool(sums, add_gx), grad_pre, pixels, wide, norm_one, g_entry],
        [pltpu.VMEM((nz, 8, padded), F32)],
    )

    return (
        out.reshape(1, small, small, c_out),
        image_grad.reshape(1, side, side, c_in),
        gain_entry_grad[0, :c_in],
        shift_entry_grad[0, :c_in],
        first_grad,
        six[0],
        six[1],
        second_grad,
        skip_grad,
        six[2],
        six[3],
        third_grad,
        six[4],
        six[5],
        fourth_grad,
    )


def solution(mesh):
    whole = P(("gx", "gy"), None, None, None)
    rows = P("gy", None)
    return jax.shard_map(
        functools.partial(program, mesh.shape["gx"], mesh.shape["gy"]),
        mesh=mesh,
        in_specs=(
            whole,
            P(("gx", "gy")),
            P(("gx", "gy"), None, None),
            P(),
            P(),
            rows,
            P(),
            P(),
            rows,
            rows,
            P(),
            P(),
            rows,
            P(),
            P(),
            rows,
            whole,
        ),
        out_specs=(
            whole, whole, P(), P(), rows, P(), P(), rows, rows, P(), P(), rows, P(), P(), rows,
        ),
        check_vma=False,
    )
```

```python
import functools

import jax
import jax.numpy as jnp
from jax import lax
from jax.experimental import pallas as pl
from jax.experimental.pallas import tpu as pltpu
from jax.sharding import PartitionSpec as P

EPS = 1e-05
F32 = jnp.float32
BF16 = jnp.bfloat16
PEERS = 4
C0 = 0.7978845608028654
C1 = 0.044715
VMEM = pl.BlockSpec(memory_space=pltpu.VMEM)
SMEM = pl.BlockSpec(memory_space=pltpu.SMEM)


def gelu(v):
    return 0.5 * v * (1.0 + jnp.tanh(C0 * (v + C1 * (v * v * v))))


def gelu_slope(v):
    t = jnp.tanh(C0 * (v + C1 * (v * v * v)))
    return 0.5 * (1.0 + t) + 0.5 * v * (1.0 - t * t) * (C0 * (1.0 + 3.0 * C1 * (v * v)))


def call(kernel, outs, args, scratch=(), flops=8 * 10**8):
    size = sum(a.size * a.dtype.itemsize for a in args)
    return pl.pallas_call(
        kernel,
        out_shape=outs,
        in_specs=[SMEM] + [VMEM] * (len(args) - 1),
        out_specs=jax.tree.map(lambda _: VMEM, outs),
        scratch_shapes=list(scratch),
        compiler_params=pltpu.CompilerParams(vmem_limit_bytes=16 * 1024 * 1024),
        cost_estimate=pl.CostEstimate(flops=flops, bytes_accessed=size, transcendentals=0),
    )(*args)


def shape(dims, dtype=F32):
    return jax.ShapeDtypeStruct(dims, dtype)


def rows_at(index, count):
    return pl.ds(pl.multiple_of(index * count, count), count)


def as_rows(parts):
    height = parts[0].shape[0]
    lane = lax.broadcasted_iota(jnp.int32, (height, 128), 1)
    out = jnp.zeros((height, 128), F32)
    for k, part in enumerate(parts):
        out = jnp.where(lane == k, part, out)
    return out.T[0:8]


def as_columns(rows):
    return jnp.concatenate([rows, jnp.zeros((120, rows.shape[1]), F32)], axis=0).T


def in_order(refs, me, scratch):
    for k, ref in enumerate(refs):
        scratch[me ^ k] = ref[...]
    return [scratch[k] for k in range(len(refs))]


def merge_moments(stats):
    total = sum(n for _, _, n in stats)
    mean = sum(n * m for m, _, n in stats) / total
    squares = sum(q + n * (m - mean) * (m - mean) for m, q, n in stats)
    return mean, squares, total


def merge_rows(refs):
    mean, squares, total = merge_moments([(g[0:1], g[1:2], g[2:3]) for g in refs])
    return mean, squares, total, sum(g[3:4] for g in refs)


def pixel(width, area, small):
    lane = lax.broadcasted_iota(jnp.int32, (1, width), 1) % area
    return lane // small, lane % small


def inside(row, col, drow, dcol, small):
    return (row + drow >= 0) & (row + drow < small) & (col + dcol >= 0) & (col + dcol < small)


def moved(value, step):
    shift = (-step) % value.shape[1]
    return pltpu.roll(value, shift, 1) if shift else value


OFFSETS = [(0, krow - 1, kcol - 1) for krow in range(3) for kcol in range(3)]

STRIDED = [
    ((krow != 1) * 2 + (kcol != 1), -(krow == 0), -(kcol == 0))
    for krow in range(3)
    for kcol in range(3)
] + [(0, 0, 0)]
PLACED = sorted(range(10), key=lambda k: (STRIDED[k][0], k))
PHASES = [[k for k in PLACED if STRIDED[k][0] == phase] for phase in range(4)]


def row_of(k, cs):
    at = PLACED.index(k)
    return slice(at * cs, (at + 1) * cs)


def phase_rows(phase, cs):
    first, last = PHASES[phase][0], PHASES[phase][-1]
    return slice(PLACED.index(first) * cs, (PLACED.index(last) + 1) * cs)


def masked_stats(value, weight, n):
    mean = jnp.sum(value * weight, axis=1, keepdims=True) / n
    centred = value - mean
    return mean, jnp.sum(weight * centred * centred, axis=1, keepdims=True)


def span_of(rows):
    return -(-rows // 128) * 128


def one_hot(height, width, shift):
    row = lax.broadcasted_iota(jnp.int32, (height, width), 0)
    col = lax.broadcasted_iota(jnp.int32, (height, width), 1)
    return (col == row + shift).astype(BF16)


def pick32(left, right, dims=((1,), (0,))):
    return lax.dot_general(left, right, (dims, ((), ())), preferred_element_type=F32)


def pick(left, right, dims=((1,), (0,))):
    return pick32(left, right, dims).astype(BF16)


def lane_tile(held, tile, rows, span):
    sides, ny = held.shape[1], held.shape[2]
    lane = lax.broadcasted_iota(jnp.int32, (1, 128), 1)
    out = None
    for v in range(2 * ny):
        begin = rows * v - tile * 128
        if begin >= 128 or begin + rows <= 0:
            continue
        at = (tile - rows * v // 128) * 128 % span
        part = jnp.concatenate(
            [held[v % 2, x, v // 2, :, at : at + 128].astype(F32) for x in range(sides)], axis=0
        )
        if begin > 0 or begin + rows < 128:
            own = (lane >= begin) & (lane < begin + rows)
            part = jnp.where(own, part, 0.0)
        out = part if out is None else out + part
    return out.astype(BF16)


def pixel_order(small, width, of):
    area = small * small
    row = lax.broadcasted_iota(jnp.int32, (4 * area, width), 0)
    col = lax.broadcasted_iota(jnp.int32, (4 * area, width), 1)
    phase, pix = row // area, row % area
    y = 2 * (pix // small) + phase // 2
    x = 2 * (pix % small) + phase % 2
    return (col == of(y, x)).astype(BF16)


def entry_image(small, idx, image, mask, valid, out, weight):
    side = 2 * small
    c_in = image.shape[1]
    count = side * side
    order = pixel_order(small, count, lambda y, x: y * side + x)
    out[:, :c_in] = pick(order, image[...])
    live = (valid[0] > 0).astype(F32)
    row = lax.broadcasted_iota(jnp.int32, (count, side), 0)
    col = lax.broadcasted_iota(jnp.int32, (count, side), 1)
    by_row = jnp.dot(
        (row // side == col).astype(BF16),
        mask[...].astype(F32).astype(BF16),
        preferred_element_type=F32,
    )
    column = jnp.sum(jnp.where(row % side == col, by_row, 0.0), axis=1, keepdims=True) * live
    lane = lax.broadcasted_iota(jnp.int32, (count, 128), 1)
    spread = jnp.where(lane == 0, column, 0.0)
    weight[...] = spread
    out[:, c_in:] = pick(order, spread.astype(BF16))[:, : out.shape[1] - c_in]


def entry_weights(cs, fy, sections, idx, *refs):
    weights, out = list(refs[:-1]), refs[-1]
    ny, cb, lanes = out.shape
    span = lanes // len(sections)
    gx, gy = idx[2], idx[3]
    core, side = gx % 2, (gx // 2 if cb < cs else 0)
    c_out = weights[0].shape[1]
    row = lax.broadcasted_iota(jnp.int32, (fy * cb, c_out), 0)
    col = lax.broadcasted_iota(jnp.int32, (fy * cb, c_out), 1)
    chosen = (col == row // cb * cs + side * cb + row % cb).astype(BF16)
    for n, count in enumerate(sections):
        begin = weights[0].shape[0] // 2 * (2 * gy + core) % 128
        total = None
        for _ in range(count):
            weight = weights.pop(0)
            rows = weight.shape[0]
            half = rows // 2
            mine = pick(chosen, weight[...], ((1,), (1,)))
            row = lax.broadcasted_iota(jnp.int32, (rows, span), 0) - core * half
            col = lax.broadcasted_iota(jnp.int32, (rows, span), 1)
            place = (row >= 0) & (row < half) & (
                (col == row + begin) | (col == row + begin - span)
            )
            part = pick32(mine, place.astype(BF16))
            total = part if total is None else total + part
            begin = begin + half
        for j in range(ny):
            out[j, :, n * span : (n + 1) * span] = total[
                (j % fy) * cb : (j % fy + 1) * cb
            ].astype(BF16)


def hold(gx, messages, held, section=0):
    span = held.shape[4]
    for k, ref in enumerate(messages):
        at = gx ^ k
        side = at // 2 if held.shape[1] > 1 else 0
        held[at % 2, side] = ref[:, :, section * span : (section + 1) * span]


def assemble(held, out, rows):
    cs, span = held.shape[1] * held.shape[3], held.shape[4]
    tiles = out.shape[1] // 128
    for k in range(9):
        for q in range(tiles):
            out[k * cs : (k + 1) * cs, q * 128 : (q + 1) * 128] = lane_tile(
                held, tiles * k + q, rows, span
            )


def assemble_first(held, out, flat, rows, extra):
    cs, span = held.shape[1] * held.shape[3], held.shape[4]
    c_in = out.shape[1]
    tiles = flat.shape[1] // 128
    for tile in range(tiles):
        flat[:, tile * 128 : (tile + 1) * 128] = lane_tile(held, tile, rows, span)
    for k in range(9):
        begin = k * c_in
        base = begin // 128 * 128
        reach = min(-(-(begin + c_in) // 128) * 128, flat.shape[1])
        move = one_hot(c_in, reach - base, begin - base)
        out[row_of(k, cs), :] = pick(flat[:, base:reach], move, ((1,), (1,)))
    total = None
    for v in range(2 * held.shape[2]):
        row = lax.broadcasted_iota(jnp.int32, (span, c_in), 0)
        col = lax.broadcasted_iota(jnp.int32, (span, c_in), 1)
        at = col - extra * v
        begin = rows * v % 128 + rows
        place = (at >= 0) & (at < extra) & ((row == at + begin) | (row == at + begin - span))
        part = jnp.concatenate(
            [
                pick32(held[v % 2, x, v // 2], place.astype(BF16))
                for x in range(held.shape[1])
            ],
            axis=0,
        )
        total = part if total is None else total + part
    out[row_of(9, cs), :] = total.astype(BF16)


def entry_stats(area, idx, *refs):
    images, out = refs[:PEERS], refs[PEERS]
    lanes = out.shape[1]
    first = jnp.zeros((1, lanes), F32)
    wide = jnp.zeros((1, 1), F32)
    narrow = jnp.zeros((1, 1), F32)
    c_in = lanes - 64
    for ref in images:
        x = ref[...].astype(F32)
        w = x[:, c_in : c_in + 1]
        first += jnp.sum(x * w, axis=0, keepdims=True)
        wide += jnp.sum(w, axis=0, keepdims=True)
        narrow += jnp.sum(w[:area], axis=0, keepdims=True)
    mean = first / wide
    squares = jnp.zeros((1, lanes), F32)
    for ref in images:
        x = ref[...].astype(F32)
        w = x[:, c_in : c_in + 1]
        d = x - mean
        squares += jnp.sum(d * d * w, axis=0, keepdims=True)
    out[...] = jnp.zeros_like(out)
    out[0:1, :] = mean
    out[1:2, :] = squares
    out[2:3, :] = jnp.broadcast_to(wide, (1, lanes))
    out[3:4, :] = jnp.broadcast_to(narrow, (1, lanes))


def entry_block(nz, rows, extra, area, small, idx, *refs):
    images = refs[:PEERS]
    stats, rest = refs[PEERS : PEERS + nz], refs[PEERS + nz :]
    gain, shift, messages, rest = rest[0], rest[1], rest[2:4], rest[4:]
    first, skipped, out_stats, norm, narrow, act, w_first = rest[:7]
    order, masks, flat, held = rest[7:]
    me, mine = idx[0], idx[1]
    c_in = gain.shape[1]
    lanes = norm.shape[1]
    cs = first.shape[0]
    width = first.shape[1]
    hold(idx[2], messages, held)
    assemble_first(held, w_first, flat, rows, extra)
    mean, squares, total, count = merge_rows(in_order(stats, mine, order))
    scale = lax.rsqrt(squares / total + EPS)
    norm[...] = jnp.zeros_like(norm)
    norm[0:1, :] = mean
    norm[1:2, :] = scale
    norm[2:3, :] = total
    norm[3:4, :] = count
    for k, ref in enumerate(images):
        x = ref[...]
        v = x[:, :c_in].astype(F32)
        pre = gain[...] * ((v - mean[:, :c_in]) * scale[:, :c_in]) + shift[...]
        a = gelu(pre).astype(BF16)
        for phase in range(4):
            act[phase, rows_at(me ^ k, area), :] = a[phase * area : (phase + 1) * area]
        masks[rows_at(me ^ k, area), :] = x[:area]
    ones = (lax.broadcasted_iota(jnp.int32, (8, lanes), 1) == c_in).astype(BF16)
    weight8 = lax.dot_general(
        ones, masks[...], (((1,), (1,)), ((), ())), preferred_element_type=F32
    )
    narrow[...] = weight8
    weight = weight8[0:1]
    row, col = pixel(width, area, small)
    total_first = jnp.zeros((cs, width), F32)
    for phase in range(4):
        group = lax.dot_general(
            w_first[phase_rows(phase, cs), :],
            act[phase],
            (((1,), (1,)), ((), ())),
            preferred_element_type=F32,
        )
        for at, k in enumerate(PHASES[phase]):
            y = group[at * cs : (at + 1) * cs]
            if k == 9:
                skipped[...] = y
                continue
            _, drow, dcol = STRIDED[k]
            y = moved(y, drow * small + dcol)
            total_first += jnp.where(inside(row, col, drow, dcol, small), y, 0.0)
    first[...] = total_first
    n = jnp.sum(weight, axis=1, keepdims=True)
    mean2, squares = masked_stats(total_first, weight, n)
    out_stats[...] = as_rows((mean2, squares, n))


def merge_stats(idx, *refs):
    out, order = refs[-2:]
    mean, squares, total, count = merge_rows(in_order(refs[:-2], idx[2], order))
    out[...] = jnp.zeros_like(out)
    out[0:1] = mean
    out[1:2] = squares
    out[2:3] = total
    out[3:4] = count


def add_rows(which, idx, *refs):
    out, order = refs[-2:]
    got = in_order(refs[:-2], idx[which], order)
    total = got[0]
    for g in got[1:]:
        total = total + g
    out[...] = total


def act_block(nz, idx, *refs):
    value, params = refs[:2]
    stats, rest = refs[2 : 2 + nz], refs[2 + nz :]
    if rest[-1].shape[1] == 128:
        cot, normed, scales, outs, order, stack = (*rest[:3], rest[3:-2], *rest[-2:])
    else:
        cot, normed, scales, outs, order = (None, *rest[:2], rest[2:-1], rest[-1])
    mean, squares, total, _ = merge_rows(in_order(stats, idx[1], order))
    rows = jnp.concatenate(
        [mean, lax.rsqrt(squares / total + EPS), total, jnp.zeros((5, mean.shape[1]), F32)], axis=0
    )
    cols = as_columns(rows)
    norm = (value[...] - cols[:, 0:1]) * cols[:, 1:2]
    normed[...] = norm
    act = gelu(params[:, 0:1] * norm + params[:, 1:2]).astype(BF16)
    cs, width = norm.shape
    if cot is not None:
        c = cot[...].astype(F32)
        stack[...] = jnp.concatenate([c, c], axis=0).T
    for k, out in enumerate(outs):
        out[:, :width] = act
        if cot is not None:
            out[:, width:] = stack[rows_at(idx[0] ^ k, cs), :].astype(BF16)
    scales[...] = cols


def conv_block(nx, added, last, rows, section, area, small, idx, *refs):
    pieces = refs[:PEERS]
    narrow, rest = refs[PEERS], refs[PEERS + 1 :]
    if last:
        weights, rest = rest[0], rest[1:]
    else:
        messages, rest = rest[:nx], rest[nx:]
    base, rest = (rest[0], rest[1:]) if added else (None, rest)
    me = idx[0]
    cs, width = pieces[0].shape[0], narrow.shape[1]
    if last:
        outs, act, spread = rest[:PEERS], rest[PEERS], rest[PEERS + 1]
    else:
        value, out_stats, act, whole, spread, held = rest
        hold(idx[2], messages, held, section)
        assemble(held, whole, rows)
        weights = whole
    for k, ref in enumerate(pieces):
        act[rows_at(me ^ k, cs), :] = ref[:, :width]
    spread[...] = jnp.dot(weights[...], act[...], preferred_element_type=F32)
    row, col = pixel(width, area, small)
    total = base[...] if added else jnp.zeros((cs, width), F32)
    for k, (_, drow, dcol) in enumerate(OFFSETS):
        y = moved(spread[k * cs : (k + 1) * cs, :], drow * small + dcol)
        total += jnp.where(inside(row, col, drow, dcol, small), y, 0.0)
    if last:
        result = total.astype(BF16)
        lane = lax.broadcasted_iota(jnp.int32, (width, 128), 0)
        slot = lax.broadcasted_iota(jnp.int32, (width, 128), 1)
        for k, out in enumerate(outs):
            out[...] = pick(result, (lane == (me ^ k) * area + slot).astype(BF16))
    else:
        value[...] = total
        weight = narrow[0:1, :]
        n = jnp.sum(weight, axis=1, keepdims=True)
        mean, squares = masked_stats(total, weight, n)
        out_stats[...] = as_rows((mean, squares, n))


def join_result(idx, *refs):
    pieces, (out, stack) = refs[:PEERS], refs[PEERS:]
    cs = pieces[0].shape[0]
    for k, ref in enumerate(pieces):
        stack[rows_at(idx[0] ^ k, cs), :] = ref[:, -128:].astype(F32)
    out[...] = stack[...].T[: out.shape[0]].astype(BF16)


def spread_grad(grad, shifted, area, small, offs, row_at):
    cs, width = grad.shape
    row, col = pixel(width, area, small)
    for k, (_, drow, dcol) in enumerate(offs):
        g = moved(grad, -(drow * small + dcol))
        g = jnp.where(inside(row, col, -drow, -dcol, small), g, 0.0)
        shifted[row_at(k, cs), :] = g.astype(BF16)


def plain_rows(k, cs):
    return slice(k * cs, (k + 1) * cs)


def push_back(me, weights, shifted, partial, outs):
    cs, width = outs[0].shape[0], shifted.shape[1]
    partial[...] = lax.dot_general(
        weights[...], shifted[...], (((0,), (0,)), ((), ())), preferred_element_type=F32
    )
    for k, out in enumerate(outs):
        out[:, :width] = partial[rows_at(me ^ k, cs), :].astype(BF16)


def last_back(nx, rows, area, small, idx, *refs):
    pieces, messages, rest = refs[:PEERS], refs[PEERS : PEERS + nx], refs[PEERS + nx :]
    cot, shifted, weights = rest[:3]
    outs = rest[3 : PEERS + 3]
    partial, held = rest[PEERS + 3 :]
    hold(idx[2], messages, held)
    assemble(held, weights, rows)
    me = idx[0]
    cs, width = cot.shape
    image = lax.broadcasted_iota(jnp.int32, (1, width), 1) // area
    grad = jnp.zeros((cs, width), F32)
    for k, ref in enumerate(pieces):
        tiled = jnp.concatenate([ref[:, width:].astype(F32)] * (width // 128), axis=1)
        grad = jnp.where(image == (me ^ k), tiled, grad)
    cot[...] = grad
    spread_grad(grad, shifted, area, small, OFFSETS, plain_rows)
    push_back(me, weights, shifted, partial, outs)


def gelu_back(idx, *refs):
    pieces = refs[:PEERS]
    normed, params, grad_pre, sums = refs[PEERS:]
    width = normed.shape[1]
    grad = pieces[0][:, :width].astype(F32)
    for ref in pieces[1:]:
        grad += ref[:, :width].astype(F32)
    norm = normed[...]
    g = gelu_slope(params[:, 0:1] * norm + params[:, 1:2]) * grad
    grad_pre[...] = g
    sums[...] = as_rows(
        (jnp.sum(g * norm, axis=1, keepdims=True), jnp.sum(g, axis=1, keepdims=True))
    )


def norm_back(nz, added, last, area, small, idx, *refs):
    grad_pre, normed, scales, params, narrow = refs[:5]
    sums = refs[5 : 5 + nz]
    rest = refs[5 + nz :]
    base, rest = (rest[0], rest[1:]) if added else (None, rest)
    me = idx[0]
    cs, width = grad_pre.shape
    order = rest[-1]
    got = in_order(sums, idx[1], order)
    total = got[0]
    for g in got[1:]:
        total = total + g
    cols = as_columns(total)
    gain_grad, shift_grad = cols[:, 0:1], cols[:, 1:2]
    norm = normed[...]
    back = params[:, 0:1] * scales[:, 1:2] * (
        grad_pre[...]
        - narrow[0:1, :] * (shift_grad + norm * gain_grad) / scales[:, 2:3]
    )
    if added:
        back = base[...] + back
    grad = back.astype(BF16).astype(F32)
    if not last:
        riders = ()
        if not added:
            riders, rest = rest[:PEERS], rest[PEERS:]
        weights, sums_out, shifted = rest[:3]
        outs, partial = rest[3 : 3 + PEERS], rest[3 + PEERS]
        for rider, out in zip(riders, outs):
            out[:, width:] = rider[...]
        if added:
            grad_out, outs, partial = rest[3], rest[4 : 4 + PEERS], rest[4 + PEERS]
            grad_out[...] = grad.astype(BF16)
        sums_out[...] = total
        spread_grad(grad, shifted, area, small, OFFSETS, plain_rows)
        push_back(me, weights, shifted, partial, outs)
    else:
        weights, grad_skip, sums_out, shifted = rest[:4]
        outs, partial = rest[4 : 4 + PEERS], rest[4 + PEERS]
        sums_out[...] = total
        spread_grad(grad, shifted, area, small, STRIDED[:9], row_of)
        shifted[row_of(9, cs), :] = grad_skip[...]
        for phase in range(4):
            partial[phase] = lax.dot_general(
                shifted[phase_rows(phase, cs), :],
                weights[phase_rows(phase, cs), :],
                (((0,), (0,)), ((), ())),
                preferred_element_type=F32,
            )
        for k, out in enumerate(outs):
            for phase in range(4):
                out[phase * area : (phase + 1) * area, :] = partial[
                    phase, rows_at(me ^ k, area), :
                ].astype(BF16)


def part_halves(core, units, own, other):
    own[...] = units[core]
    other[...] = units[1 - core].astype(BF16)


def weight_grad(rows, idx, shifted, act, own, other, full, units):
    full[...] = lax.dot_general(
        shifted[...], act[...], (((1,), (1,)), ((), ())), preferred_element_type=F32
    )
    ny, cs, span = own.shape
    tiles = full.shape[1] // 128
    for v in range(2 * ny):
        begin = rows * v % 128
        parts = []
        for q in range((begin + rows + 127) // 128):
            k, p = divmod(rows * v // 128 + q, tiles)
            parts.append(full[k * cs : (k + 1) * cs, p * 128 : (p + 1) * 128])
        window = jnp.concatenate(parts, axis=1)
        units[v % 2, v // 2] = moved(window, begin)[:, :span]
    part_halves(idx[2] % 2, units, own, other)


def weight_grad_first(rows, extra, idx, shifted, act, own, other, flat, units):
    ny, cs, span = own.shape
    c_in = act.shape[2]
    flat[...] = jnp.zeros_like(flat)
    skip = None
    for phase in range(4):
        group = jnp.dot(
            shifted[phase_rows(phase, cs), :], act[phase], preferred_element_type=F32
        ).astype(BF16)
        for at, k in enumerate(PHASES[phase]):
            grad = group[at * cs : (at + 1) * cs]
            if k == 9:
                skip = grad
                continue
            begin = k * c_in
            base = begin // 128 * 128
            reach = -(-(begin + c_in) // 128) * 128
            move = one_hot(c_in, reach - base, begin - base)
            flat[:, base:reach] += jnp.dot(grad, move, preferred_element_type=F32)
    lane = lax.broadcasted_iota(jnp.int32, (1, span), 1)
    for v in range(2 * ny):
        begin = rows * v % 128
        base = rows * v - begin
        window = moved(flat[:, base : base + span + 128], begin)[:, :span]
        row = lax.broadcasted_iota(jnp.int32, (c_in, span), 0)
        col = lax.broadcasted_iota(jnp.int32, (c_in, span), 1)
        place = (row >= extra * v) & (row < extra * (v + 1)) & (col == row - extra * v + rows)
        tail = pick32(skip, place.astype(BF16))
        units[v % 2, v // 2] = jnp.where(lane < rows, window, 0.0) + tail
    part_halves(idx[2] % 2, units, own, other)


def reduce_core(count, idx, *refs):
    own, other, outs, total = refs[:count], refs[count : 2 * count], refs[2 * count : -1], refs[-1]
    cb = outs[0].shape[1]
    at = 0
    for a, b in zip(own, other):
        span = a.shape[2]
        total[:, :, at : at + span] = a[...] + b[...].astype(F32)
        at += span
    for k, out in enumerate(outs):
        for j in range(total.shape[0]):
            out[j] = total[j, rows_at(idx[2] // 2 ^ k, cb), :].astype(out.dtype)


def reduce_side(sides, idx, *refs):
    out = refs[-1]
    at = 0
    for n in range(0, len(refs) - 1, sides):
        total = refs[n][...]
        for ref in refs[n + 1 : n + sides]:
            total += ref[...].astype(F32)
        out[:, :, at : at + total.shape[2]] = total.astype(BF16)
        at += total.shape[2]


def fold(nz, fy, idx, got, out):
    cs = got.shape[1]
    for f in range(fy):
        total = got[f].astype(F32)
        for z in range(1, nz):
            total += got[z * fy + f].astype(F32)
        out[f * cs : (f + 1) * cs, :] = total.astype(BF16)


def own_rows(count, spans, idx, *refs):
    pieces, outs, stack = refs[:count], refs[count:-1], refs[-1]
    for k, ref in enumerate(pieces):
        at = idx[2] ^ k
        stack[at % 2, at // 2] = ref[...]
    sides, height = stack.shape[1], stack.shape[2]
    fy_cb = [(f, x) for f in range(PEERS) for x in range(sides)]
    cb = height // PEERS
    for half in range(2):
        whole = jnp.concatenate(
            [stack[half, x, f * cb : (f + 1) * cb, :].astype(F32) for f, x in fy_cb], axis=0
        ).T
        at = 0
        for span, group in spans:
            begin = at
            for n in group:
                out = outs[n]
                rows = out.shape[0] // 2
                out[half * rows : (half + 1) * rows, :] = whole[begin : begin + rows]
                begin += rows
            at += span


def entry_back(small, idx, *refs):
    pieces = refs[:PEERS]
    image, norm, gain, shift, grad_pre, sums = refs[PEERS:]
    c_in = gain.shape[1]
    side = 2 * small
    grad = pieces[0][...].astype(F32)
    for ref in pieces[1:]:
        grad += ref[...].astype(F32)
    order = pixel_order(small, side * side, lambda y, x: y * side + x)
    high = grad.astype(BF16)
    low = (grad - high.astype(F32)).astype(BF16)
    grad = sum(
        lax.dot_general(order, part, (((0,), (0,)), ((), ())), preferred_element_type=F32)
        for part in (high, low)
    )
    normed = (image[...].astype(F32) - norm[0:1, :c_in]) * norm[1:2, :c_in]
    g = gelu_slope(gain[...] * normed + shift[...]) * grad
    grad_pre[...] = g
    sums[...] = jnp.zeros_like(sums)
    sums[0:1, :c_in] = jnp.sum(g * normed, axis=0, keepdims=True)
    sums[1:2, :c_in] = jnp.sum(g, axis=0, keepdims=True)


def bundle(idx, first, second, third, sums, out):
    out[...] = jnp.zeros_like(out)
    out[0:8, :] = sums[...]
    for k, ref in enumerate((first, second, third)):
        out[8 + 2 * k : 10 + 2 * k, : ref.shape[1]] = ref[0:2]


def unbundle(idx, *refs):
    out, six, order = refs[-3:]
    got = in_order(refs[:-3], idx[0], order)
    total = got[0][0:8]
    for g in got[1:]:
        total = total + g[0:8]
    out[...] = total
    cs = six.shape[1] // PEERS
    six[...] = jnp.concatenate([g[8:16, :cs] for g in got], axis=1)


def entry_grad(nz, idx, *refs):
    sums = refs[:nz]
    grad_pre, image, weight, norm, gain, gain_grad, shift_grad, out, order = refs[nz:]
    got = in_order(sums, idx[1], order)
    total = got[0]
    for g in got[1:]:
        total = total + g
    gain_grad[...] = total[0:1]
    shift_grad[...] = total[1:2]
    c_in = gain.shape[1]
    scale = norm[1:2, :c_in]
    normed = (image[...].astype(F32) - norm[0:1, :c_in]) * scale
    out[...] = gain[...] * scale * (
        grad_pre[...]
        - weight[:, 0:1]
        * (shift_grad[0:1, :c_in] + normed * gain_grad[0:1, :c_in])
        / norm[2:3, :c_in]
    )


def program(
    nx,
    ny,
    images,
    valid_count,
    pixel_mask,
    gain_entry,
    shift_entry,
    conv_first,
    gain_middle,
    shift_middle,
    conv_second,
    projection,
    gain_inner,
    shift_inner,
    conv_third,
    gain_last,
    shift_last,
    conv_fourth,
    cotangent,
):
    fy = PEERS
    nz = ny // fy
    side, c_in = images.shape[1], images.shape[3]
    small = side // 2
    area = small * small
    c_out = conv_first.shape[1]
    cs = c_out // PEERS
    width = PEERS * area
    lanes = c_in + 64
    gx, gy = lax.axis_index("gx"), lax.axis_index("gy")
    me = gy % fy
    mine = gy // fy
    idx = jnp.stack([me, mine, gx, gy]).astype(jnp.int32)

    def to_slice(piece, k):
        return lax.ppermute(piece, "gy", [(j, j // fy * fy + (j % fy ^ k)) for j in range(ny)])

    def share(pieces):
        return [pieces[0]] + [to_slice(pieces[k], k) for k in range(1, PEERS)]

    def spread_out(piece):
        return share([piece] * PEERS)

    def to_gx(piece, k):
        return lax.ppermute(piece, "gx", [(i, i ^ k) for i in range(nx)])

    def pool(piece, kernel):
        pieces = [piece] + [to_gx(piece, k) for k in range(1, nx)]
        piece = call(
            kernel,
            shape(piece.shape),
            [idx, *pieces],
            [pltpu.VMEM((nx, *piece.shape), F32)],
        )
        out = [piece]
        for k in range(1, nz):
            perm = [(j, (j // fy ^ k) * fy + j % fy) for j in range(ny)]
            out.append(lax.ppermute(piece, "gy", perm))
        return out

    add_gx = functools.partial(add_rows, 2)

    def after(value, *others):
        return lax.optimization_barrier((value, *others))[0]

    def turn(block):
        return lax.all_to_all(block, "gy", 0, 0, tiled=True)

    def over_x(block):
        return {0: block, **{k: to_gx(block, k) for k in range(2, nx, 2)}}

    def over_core(held):
        held = dict(held)
        for k in list(held):
            held[k + 1] = to_gx(held[k], 1)
        return [held[k] for k in sorted(held)]

    def along_gx(block):
        return over_core(over_x(block))

    unit_first, unit_skip = conv_first.shape[0] // 2, projection.shape[0] // 2
    unit_mid = conv_second.shape[0] // 2
    span_first, span_mid = span_of(unit_first + unit_skip), span_of(unit_mid)

    cb = cs // (nx // 2)

    def ready(span, channels, sections, *weights):
        return call(
            functools.partial(entry_weights, cs, fy, sections),
            shape((ny, channels, span * len(sections)), BF16),
            [idx, *weights],
            flops=20 * 10**8 * len(sections),
        )

    def halves(span, channels=None):
        channels = channels or cb
        return pltpu.VMEM((2, cs // channels, ny, channels, span), BF16)

    pixels = images.reshape(side * side, c_in)
    image, wide = pl.pallas_call(
        functools.partial(entry_image, small),
        out_shape=[shape((4 * area, lanes), BF16), shape((4 * area, 128))],
        in_specs=[SMEM, VMEM, VMEM, SMEM],
        out_specs=[VMEM, VMEM],
        compiler_params=pltpu.CompilerParams(vmem_limit_bytes=16 * 1024 * 1024),
        cost_estimate=pl.CostEstimate(flops=1 << 20, bytes_accessed=1 << 20, transcendentals=0),
    )(idx, pixels, pixel_mask.reshape(side, side), valid_count)
    group = spread_out(image)
    out_first = ready(span_first, cs, (2,), conv_first, projection)
    got_first = over_core({0: turn(after(out_first, group[1]))})

    def own(gain, shift):
        pair = jnp.stack([gain, shift], axis=1)
        return lax.dynamic_slice_in_dim(pair, me * cs, cs, axis=0)

    p_middle = own(gain_middle, shift_middle)
    p_inner = own(gain_inner, shift_inner)
    p_last = own(gain_last, shift_last)
    g_entry, s_entry = gain_entry[None], shift_entry[None]

    tile = shape((cs, width))
    tile16 = shape((cs, width), BF16)
    cols = shape((cs, 128))
    stat = shape((8, cs))
    stat_order = pltpu.VMEM((nz, 8, cs), F32)
    full16 = shape((c_out, width), BF16)
    whole16 = shape((9 * cs, c_out), BF16)
    conv_flops = 25 * 10**8

    stats = call(functools.partial(entry_stats, area), shape((8, lanes)), [idx, *group])
    pooled = pool(stats, merge_stats)
    out_middle = ready(span_mid, cb, (1, 1), conv_second, conv_third)
    out_fourth = ready(span_mid, cb, (1,), conv_fourth)
    got_middle = turn(after(out_middle, pooled[-1]))
    first, skipped, stats, norm_one, narrow, act_one, w_first = call(
        functools.partial(entry_block, nz, unit_first, unit_skip, area, small),
        [
            tile,
            tile,
            stat,
            shape((8, lanes)),
            shape((8, width)),
            shape((4, width, c_in), BF16),
            shape((10 * cs, c_in), BF16),
        ],
        [
            idx,
            *group,
            *pooled,
            after(g_entry, out_middle, out_fourth),
            s_entry,
            *got_first,
        ],
        [
            pltpu.VMEM((nz, 8, lanes), F32),
            pltpu.VMEM((width, lanes), BF16),
            pltpu.VMEM((cs, span_of(9 * c_in)), BF16),
            halves(span_first, cs),
        ],
        flops=conv_flops // 2,
    )

    def activate(value, params, pooled, cot=None):
        more = [] if cot is None else [cot]
        count = 1 if cot is None else PEERS
        out = tile16 if cot is None else shape((cs, width + 128), BF16)
        return call(
            functools.partial(act_block, nz),
            [tile, cols] + [out] * count,
            [idx, value, params, *pooled, *more],
            [stat_order] + ([] if cot is None else [pltpu.VMEM((c_out, 128), F32)]),
        )

    def convolve(pieces, weights, base, section=0, last=False):
        more = [] if base is None else [base]
        if last:
            outs = [shape((cs, 128), BF16)] * PEERS + [full16]
        else:
            outs = [tile, stat, full16, whole16]
        return call(
            functools.partial(
                conv_block, nx, base is not None, last, unit_mid, section, area, small
            ),
            outs,
            [idx, *pieces, narrow, *weights, *more],
            [pltpu.VMEM((9 * cs, width), F32)] + ([] if last else [halves(span_mid)]),
            flops=conv_flops,
        )

    pooled = pool(stats, merge_stats)
    got_middle = over_x(after(got_middle, pooled[0]))
    normed_two, scale_two, *messages = activate(
        first, p_middle, pooled, cotangent.reshape(area, c_out)
    )
    got_middle = over_core({k: after(v, messages[0]) for k, v in got_middle.items()})
    pieces = share(messages)
    got_fourth = turn(after(out_fourth, pieces[1]))
    hidden, stats, act_two, w_second = convolve(pieces, got_middle, skipped, section=0)
    pooled = pool(stats, merge_stats)
    got_fourth = over_x(after(got_fourth, pooled[0]))
    normed_three, scale_three, act = activate(hidden, p_inner, pooled)
    got_fourth = over_core({k: after(v, act) for k, v in got_fourth.items()})
    third, stats, act_three, w_third = convolve(spread_out(act), got_middle, None, section=1)
    normed_four, scale_four, act = activate(third, p_last, pool(stats, merge_stats))

    cot, shifted_four, w_fourth, *parts = call(
        functools.partial(last_back, nx, unit_mid, area, small),
        [tile, shape((9 * cs, width), BF16), whole16] + [tile16] * PEERS,
        [idx, *pieces, *got_fourth],
        [pltpu.VMEM((c_out, width), F32), halves(span_mid)],
        flops=conv_flops,
    )

    def slope(parts, normed, params, *done):
        return call(gelu_back, [tile, stat], [idx, *parts, after(normed, *done), params])

    def back(grad_pre, normed, scales, params, pooled, weights, base, riders=()):
        more = list(riders) if base is None else [base]
        part = tile16 if base is not None else shape((cs, width + 128), BF16)
        outs = [stat, shape((9 * cs, width), BF16)] + ([] if base is None else [tile16])
        return call(
            functools.partial(norm_back, nz, base is not None, False, area, small),
            outs + [part] * PEERS,
            [idx, grad_pre, normed, scales, params, narrow, *pooled, *more, weights],
            [pltpu.VMEM((c_out, width), F32), stat_order],
            flops=conv_flops,
        )

    def grad_of(kernel, span, shifted, act, scratch):
        return call(
            kernel,
            [shape((ny, cs, span)), shape((ny, cs, span), BF16)],
            [idx, shifted, act],
            [scratch, pltpu.VMEM((2, ny, cs, span), F32)],
            flops=conv_flops,
        )

    def grad_mid(shifted, act):
        kernel = functools.partial(weight_grad, unit_mid)
        return grad_of(kernel, span_mid, shifted, act, pltpu.VMEM((9 * cs, c_out), F32))

    def reduce_grads(*grads):
        own = [a for a, _ in grads]
        other = [to_gx(b, 1) for _, b in grads]
        span = sum(a.shape[2] for a in own)
        sides = nx // 2
        return call(
            functools.partial(reduce_core, len(own)),
            [shape((ny, cb, span))] + [shape((ny, cb, span), BF16)] * (sides - 1),
            [idx, *own, *other],
            [pltpu.VMEM((ny, cs, span), F32)],
        )

    def move_sides(parts):
        return [parts[0]] + [to_gx(parts[k], 2 * k) for k in range(1, nx // 2)]

    def add_sides(*groups):
        span = sum(parts[0].shape[2] for parts in groups)
        return call(
            functools.partial(reduce_side, nx // 2),
            shape((ny, cb, span), BF16),
            [idx, *[p for parts in groups for p in parts]],
        )

    def merge_sides(parts):
        return add_sides(move_sides(parts))

    def land_grads(got, spans, *rows):
        span = got.shape[2]
        got = call(functools.partial(fold, nz, fy), shape((fy * cb, span), BF16), [idx, got])
        return call(
            functools.partial(own_rows, nx, spans),
            [shape((r, c_out)) for r in rows],
            [idx, *along_gx(got)],
            [pltpu.VMEM((2, nx // 2, fy * cb, span), BF16)],
        )

    grad_pre, sums = slope(share(parts), normed_four, p_last)
    pooled = pool(sums, add_gx)
    *out_parts, act_four = convolve(spread_out(act), [w_fourth], hidden, last=True)

    grad_fourth = grad_mid(shifted_four, act_four)
    last_sums, shifted_three, *parts = back(
        grad_pre,
        normed_four,
        scale_four,
        after(p_last, *grad_fourth),
        pooled,
        w_third,
        None,
        out_parts,
    )
    parts = share(parts)
    out = call(
        join_result,
        shape((area, c_out), BF16),
        [idx, *parts],
        [pltpu.VMEM((c_out, 128), F32)],
    )
    grad_pre, sums = slope(parts, normed_three, p_inner)
    grad_third = grad_mid(after(shifted_three, sums), act_three)
    inner_sums, shifted_two, grad_hidden, *parts = back(
        grad_pre,
        normed_three,
        scale_three,
        after(p_inner, *grad_third),
        pool(sums, add_gx),
        w_second,
        cot,
    )
    late = reduce_grads(grad_fourth, grad_third)
    grad_pre, sums = slope(share(parts), normed_two, p_middle, late[0])
    grad_second = grad_mid(after(shifted_two, sums), act_two)
    pooled = pool(sums, add_gx)
    late = move_sides([after(p, pooled[0]) for p in late])
    middle_sums, shifted_one, *parts = call(
        functools.partial(norm_back, nz, False, True, area, small),
        [stat, shape((10 * cs, width), BF16)] + [shape((4 * area, c_in), BF16)] * PEERS,
        [
            idx,
            grad_pre,
            normed_two,
            scale_two,
            p_middle,
            after(narrow, *grad_second),
            *pooled,
            w_first,
            grad_hidden,
        ],
        [pltpu.VMEM((4, width, c_in), F32), stat_order],
        flops=conv_flops // 2,
    )
    parts = share(parts)
    second = reduce_grads(grad_second)
    late[0] = after(late[0], second[0], *parts[1:])
    sent_late = turn(add_sides(late))
    grad_first = grad_of(
        functools.partial(weight_grad_first, unit_first, unit_skip),
        span_first,
        after(shifted_one, *parts[1:]),
        act_one,
        pltpu.VMEM((cs, span_of(9 * c_in + span_first + 128)), F32),
    )
    padded = -(-c_in // 128) * 128
    grad_pre, sums = call(
        functools.partial(entry_back, small),
        [shape((4 * area, c_in)), shape((8, padded))],
        [idx, *parts, pixels, norm_one, g_entry, s_entry],
    )
    first = reduce_grads(grad_first)
    message = call(
        bundle, shape((16, padded)), [idx, middle_sums, inner_sums, last_sums, sums]
    )
    sums, six = call(
        unbundle,
        [shape((8, padded)), shape((8, c_out))],
        [idx, *spread_out(message)],
        [pltpu.VMEM((PEERS, 16, padded), F32)],
    )
    second = move_sides(second)
    second[0] = after(second[0], message)
    sent_early = turn(add_sides(second, move_sides(first)))
    fourth_grad, third_grad = land_grads(
        sent_late, ((span_mid, (0,)), (span_mid, (1,))), 2 * unit_mid, 2 * unit_mid
    )
    pooled = pool(sums, add_gx)
    second_grad, first_grad, skip_grad = land_grads(
        after(sent_early, fourth_grad, pooled[0]),
        ((span_mid, (0,)), (span_first, (1, 2))),
        2 * unit_mid,
        2 * unit_first,
        2 * unit_skip,
    )
    gain_entry_grad, shift_entry_grad, image_grad = call(
        functools.partial(entry_grad, nz),
        [shape((1, padded)), shape((1, padded)), shape((4 * area, c_in))],
        [idx, *pooled, grad_pre, pixels, wide, norm_one, g_entry],
        [pltpu.VMEM((nz, 8, padded), F32)],
    )

    return (
        out.reshape(1, small, small, c_out),
        image_grad.reshape(1, side, side, c_in),
        gain_entry_grad[0, :c_in],
        shift_entry_grad[0, :c_in],
        first_grad,
        six[0],
        six[1],
        second_grad,
        skip_grad,
        six[2],
        six[3],
        third_grad,
        six[4],
        six[5],
        fourth_grad,
    )


def solution(mesh):
    whole = P(("gx", "gy"), None, None, None)
    rows = P("gy", None)
    return jax.shard_map(
        functools.partial(program, mesh.shape["gx"], mesh.shape["gy"]),
        mesh=mesh,
        in_specs=(
            whole,
            P(("gx", "gy")),
            P(("gx", "gy"), None, None),
            P(),
            P(),
            rows,
            P(),
            P(),
            rows,
            rows,
            P(),
            P(),
            rows,
            P(),
            P(),
            rows,
            whole,
        ),
        out_specs=(
            whole, whole, P(), P(), rows, P(), P(), rows, rows, P(), P(), rows, P(), P(), rows,
        ),
        check_vma=False,
    )
```

```python
import functools

import jax
import jax.numpy as jnp
from jax import lax
from jax.experimental import pallas as pl
from jax.experimental.pallas import tpu as pltpu
from jax.sharding import PartitionSpec as P

EPS = 1e-05
COST = 6 * 10**7
F32 = jnp.float32
BF16 = jnp.bfloat16
PEERS = 4
C0 = 0.7978845608028654
C1 = 0.044715
VMEM = pl.BlockSpec(memory_space=pltpu.VMEM)
SMEM = pl.BlockSpec(memory_space=pltpu.SMEM)


def gelu(v):
    return 0.5 * v * (1.0 + jnp.tanh(C0 * (v + C1 * (v * v * v))))


def gelu_slope(v):
    t = jnp.tanh(C0 * (v + C1 * (v * v * v)))
    return 0.5 * (1.0 + t) + 0.5 * v * (1.0 - t * t) * (C0 * (1.0 + 3.0 * C1 * (v * v)))


def after(value, *others):
    return lax.optimization_barrier((value, *others))[0]


class Order:
    def __init__(self, idx):
        self.idx = idx
        self.last = ()

    def __call__(self, kernel, outs, args, scratch=(), scalars=0, cost=7):
        idx = after(self.idx, *self.last)
        got = pl.pallas_call(
            kernel,
            out_shape=outs,
            in_specs=[SMEM] + [VMEM] * (len(args) - scalars) + [SMEM] * scalars,
            out_specs=jax.tree.map(lambda _: VMEM, outs),
            scratch_shapes=list(scratch),
            compiler_params=pltpu.CompilerParams(vmem_limit_bytes=16 * 1024 * 1024),
            cost_estimate=pl.CostEstimate(
                flops=cost * COST, bytes_accessed=1024, transcendentals=0
            ),
        )(idx, *args)
        self.last = (jax.tree.leaves(got)[0],)
        return got


def shape(dims, dtype=F32):
    return jax.ShapeDtypeStruct(dims, dtype)


def rows_at(index, count):
    return pl.ds(pl.multiple_of(index * count, count), count)


def as_rows(parts):
    height = parts[0].shape[0]
    lane = lax.broadcasted_iota(jnp.int32, (height, 128), 1)
    out = jnp.zeros((height, 128), F32)
    for k, part in enumerate(parts):
        out = jnp.where(lane == k, part, out)
    return out.T[0:8]


def as_columns(rows):
    return jnp.concatenate([rows, jnp.zeros((120, rows.shape[1]), F32)], axis=0).T


def in_order(refs, me, scratch):
    for k, ref in enumerate(refs):
        scratch[me ^ k] = ref[...]
    return [scratch[k] for k in range(len(refs))]


def merge_moments(stats):
    total = sum(n for _, _, n in stats)
    mean = sum(n * m for m, _, n in stats) / total
    squares = sum(q + n * (m - mean) * (m - mean) for m, q, n in stats)
    return mean, squares, total


def merge_rows(refs):
    mean, squares, total = merge_moments([(g[0:1], g[1:2], g[2:3]) for g in refs])
    return mean, squares, total, sum(g[3:4] for g in refs)


def pixel(width, area, small):
    lane = lax.broadcasted_iota(jnp.int32, (1, width), 1) % area
    return lane // small, lane % small


def inside(row, col, drow, dcol, small):
    return (row + drow >= 0) & (row + drow < small) & (col + dcol >= 0) & (col + dcol < small)


def moved(value, step):
    shift = (-step) % value.shape[1]
    return pltpu.roll(value, shift, 1) if shift else value


OFFSETS = [(0, krow - 1, kcol - 1) for krow in range(3) for kcol in range(3)]

STRIDED = [
    ((krow != 1) * 2 + (kcol != 1), -(krow == 0), -(kcol == 0))
    for krow in range(3)
    for kcol in range(3)
] + [(0, 0, 0)]
PLACED = sorted(range(10), key=lambda k: (STRIDED[k][0], k))
PHASES = [[k for k in PLACED if STRIDED[k][0] == phase] for phase in range(4)]


def row_of(k, cs):
    at = PLACED.index(k)
    return slice(at * cs, (at + 1) * cs)


def phase_rows(phase, cs):
    first, last = PHASES[phase][0], PHASES[phase][-1]
    return slice(PLACED.index(first) * cs, (PLACED.index(last) + 1) * cs)


def masked_stats(value, weight, n):
    mean = jnp.sum(value * weight, axis=1, keepdims=True) / n
    centred = value - mean
    return mean, jnp.sum(weight * centred * centred, axis=1, keepdims=True)


def span_of(rows):
    return -(-rows // 128) * 128


def one_hot(height, width, shift):
    row = lax.broadcasted_iota(jnp.int32, (height, width), 0)
    col = lax.broadcasted_iota(jnp.int32, (height, width), 1)
    return (col == row + shift).astype(BF16)


def pick32(left, right, dims=((1,), (0,))):
    return lax.dot_general(left, right, (dims, ((), ())), preferred_element_type=F32)


def pick(left, right, dims=((1,), (0,))):
    return pick32(left, right, dims).astype(BF16)


def lane_tile(held, tile, rows, span):
    sides, ny = held.shape[1], held.shape[2]
    lane = lax.broadcasted_iota(jnp.int32, (1, 128), 1)
    out = None
    for v in range(2 * ny):
        begin = rows * v - tile * 128
        if begin >= 128 or begin + rows <= 0:
            continue
        at = (tile - rows * v // 128) * 128 % span
        part = jnp.concatenate(
            [held[v % 2, x, v // 2, :, at : at + 128].astype(F32) for x in range(sides)], axis=0
        )
        if begin > 0 or begin + rows < 128:
            own = (lane >= begin) & (lane < begin + rows)
            part = jnp.where(own, part, 0.0)
        out = part if out is None else out + part
    return out.astype(BF16)


def pixel_order(small, width, of):
    area = small * small
    row = lax.broadcasted_iota(jnp.int32, (4 * area, width), 0)
    col = lax.broadcasted_iota(jnp.int32, (4 * area, width), 1)
    phase, pix = row // area, row % area
    y = 2 * (pix // small) + phase // 2
    x = 2 * (pix % small) + phase % 2
    return (col == of(y, x)).astype(BF16)


def entry_image(small, idx, image, mask, valid, out, weight):
    side = 2 * small
    c_in = image.shape[1]
    count = side * side
    order = pixel_order(small, count, lambda y, x: y * side + x)
    out[:, :c_in] = pick(order, image[...])
    live = (valid[0] > 0).astype(F32)
    row = lax.broadcasted_iota(jnp.int32, (count, side), 0)
    col = lax.broadcasted_iota(jnp.int32, (count, side), 1)
    by_row = jnp.dot(
        (row // side == col).astype(BF16),
        mask[...].astype(F32).astype(BF16),
        preferred_element_type=F32,
    )
    column = jnp.sum(jnp.where(row % side == col, by_row, 0.0), axis=1, keepdims=True) * live
    lane = lax.broadcasted_iota(jnp.int32, (count, 128), 1)
    spread = jnp.where(lane == 0, column, 0.0)
    weight[...] = spread
    out[:, c_in:] = pick(order, spread.astype(BF16))[:, : out.shape[1] - c_in]


def entry_weights(cs, fy, sections, idx, *refs):
    weights, out = list(refs[:-1]), refs[-1]
    ny, cb, lanes = out.shape
    span = lanes // len(sections)
    gx, gy = idx[2], idx[3]
    core, side = gx % 2, (gx // 2 if cb < cs else 0)
    c_out = weights[0].shape[1]
    row = lax.broadcasted_iota(jnp.int32, (fy * cb, c_out), 0)
    col = lax.broadcasted_iota(jnp.int32, (fy * cb, c_out), 1)
    chosen = (col == row // cb * cs + side * cb + row % cb).astype(BF16)
    for n, count in enumerate(sections):
        begin = weights[0].shape[0] // 2 * (2 * gy + core) % 128
        total = None
        for _ in range(count):
            weight = weights.pop(0)
            rows = weight.shape[0]
            half = rows // 2
            mine = pick(chosen, weight[...], ((1,), (1,)))
            row = lax.broadcasted_iota(jnp.int32, (rows, span), 0) - core * half
            col = lax.broadcasted_iota(jnp.int32, (rows, span), 1)
            place = (row >= 0) & (row < half) & (
                (col == row + begin) | (col == row + begin - span)
            )
            part = pick32(mine, place.astype(BF16))
            total = part if total is None else total + part
            begin = begin + half
        for j in range(ny):
            out[j, :, n * span : (n + 1) * span] = total[
                (j % fy) * cb : (j % fy + 1) * cb
            ].astype(BF16)


def hold(gx, messages, held, section=0):
    span = held.shape[4]
    for k, ref in enumerate(messages):
        at = gx ^ k
        side = at // 2 if held.shape[1] > 1 else 0
        held[at % 2, side] = ref[:, :, section * span : (section + 1) * span]


def assemble(held, out, rows):
    cs, span = held.shape[1] * held.shape[3], held.shape[4]
    tiles = out.shape[1] // 128
    for k in range(9):
        for q in range(tiles):
            out[k * cs : (k + 1) * cs, q * 128 : (q + 1) * 128] = lane_tile(
                held, tiles * k + q, rows, span
            )


def assemble_first(held, out, flat, rows, extra):
    cs, span = held.shape[1] * held.shape[3], held.shape[4]
    c_in = out.shape[1]
    tiles = flat.shape[1] // 128
    for tile in range(tiles):
        flat[:, tile * 128 : (tile + 1) * 128] = lane_tile(held, tile, rows, span)
    for k in range(9):
        begin = k * c_in
        base = begin // 128 * 128
        reach = min(-(-(begin + c_in) // 128) * 128, flat.shape[1])
        move = one_hot(c_in, reach - base, begin - base)
        out[row_of(k, cs), :] = pick(flat[:, base:reach], move, ((1,), (1,)))
    total = None
    for v in range(2 * held.shape[2]):
        row = lax.broadcasted_iota(jnp.int32, (span, c_in), 0)
        col = lax.broadcasted_iota(jnp.int32, (span, c_in), 1)
        at = col - extra * v
        begin = rows * v % 128 + rows
        place = (at >= 0) & (at < extra) & ((row == at + begin) | (row == at + begin - span))
        part = jnp.concatenate(
            [
                pick32(held[v % 2, x, v // 2], place.astype(BF16))
                for x in range(held.shape[1])
            ],
            axis=0,
        )
        total = part if total is None else total + part
    out[row_of(9, cs), :] = total.astype(BF16)


def entry_stats(area, idx, *refs):
    images, out = refs[:PEERS], refs[PEERS]
    lanes = out.shape[1]
    first = jnp.zeros((1, lanes), F32)
    wide = jnp.zeros((1, 1), F32)
    narrow = jnp.zeros((1, 1), F32)
    c_in = lanes - 64
    for ref in images:
        x = ref[...].astype(F32)
        w = x[:, c_in : c_in + 1]
        first += jnp.sum(x * w, axis=0, keepdims=True)
        wide += jnp.sum(w, axis=0, keepdims=True)
        narrow += jnp.sum(w[:area], axis=0, keepdims=True)
    mean = first / wide
    squares = jnp.zeros((1, lanes), F32)
    for ref in images:
        x = ref[...].astype(F32)
        w = x[:, c_in : c_in + 1]
        d = x - mean
        squares += jnp.sum(d * d * w, axis=0, keepdims=True)
    out[...] = jnp.zeros_like(out)
    out[0:1, :] = mean
    out[1:2, :] = squares
    out[2:3, :] = jnp.broadcast_to(wide, (1, lanes))
    out[3:4, :] = jnp.broadcast_to(narrow, (1, lanes))


def entry_block(nz, rows, extra, area, small, idx, *refs):
    images = refs[:PEERS]
    stats, rest = refs[PEERS : PEERS + nz], refs[PEERS + nz :]
    gain, shift, messages, rest = rest[0], rest[1], rest[2:4], rest[4:]
    first, skipped, out_stats, norm, narrow, act, w_first = rest[:7]
    order, masks, flat, held = rest[7:]
    me, mine = idx[0], idx[1]
    c_in = gain.shape[1]
    lanes = norm.shape[1]
    cs = first.shape[0]
    width = first.shape[1]
    hold(idx[2], messages, held)
    assemble_first(held, w_first, flat, rows, extra)
    mean, squares, total, count = merge_rows(in_order(stats, mine, order))
    scale = lax.rsqrt(squares / total + EPS)
    norm[...] = jnp.zeros_like(norm)
    norm[0:1, :] = mean
    norm[1:2, :] = scale
    norm[2:3, :] = total
    norm[3:4, :] = count
    for k, ref in enumerate(images):
        x = ref[...]
        v = x[:, :c_in].astype(F32)
        pre = gain[...] * ((v - mean[:, :c_in]) * scale[:, :c_in]) + shift[...]
        a = gelu(pre).astype(BF16)
        for phase in range(4):
            act[phase, rows_at(me ^ k, area), :] = a[phase * area : (phase + 1) * area]
        masks[rows_at(me ^ k, area), :] = x[:area]
    ones = (lax.broadcasted_iota(jnp.int32, (8, lanes), 1) == c_in).astype(BF16)
    weight8 = lax.dot_general(
        ones, masks[...], (((1,), (1,)), ((), ())), preferred_element_type=F32
    )
    narrow[...] = weight8
    weight = weight8[0:1]
    row, col = pixel(width, area, small)
    total_first = jnp.zeros((cs, width), F32)
    for phase in range(4):
        group = lax.dot_general(
            w_first[phase_rows(phase, cs), :],
            act[phase],
            (((1,), (1,)), ((), ())),
            preferred_element_type=F32,
        )
        for at, k in enumerate(PHASES[phase]):
            y = group[at * cs : (at + 1) * cs]
            if k == 9:
                skipped[...] = y
                continue
            _, drow, dcol = STRIDED[k]
            y = moved(y, drow * small + dcol)
            total_first += jnp.where(inside(row, col, drow, dcol, small), y, 0.0)
    first[...] = total_first
    n = jnp.sum(weight, axis=1, keepdims=True)
    mean2, squares = masked_stats(total_first, weight, n)
    out_stats[...] = as_rows((mean2, squares, n))


def merge_stats(idx, *refs):
    out, order = refs[-2:]
    mean, squares, total, count = merge_rows(in_order(refs[:-2], idx[2], order))
    out[...] = jnp.zeros_like(out)
    out[0:1] = mean
    out[1:2] = squares
    out[2:3] = total
    out[3:4] = count


def add_rows(which, idx, *refs):
    out, order = refs[-2:]
    got = in_order(refs[:-2], idx[which], order)
    total = got[0]
    for g in got[1:]:
        total = total + g
    out[...] = total


def act_block(nz, idx, *refs):
    value, params = refs[:2]
    stats, rest = refs[2 : 2 + nz], refs[2 + nz :]
    if rest[-1].shape[1] == 128:
        cot, normed, scales, outs, order, stack = (*rest[:3], rest[3:-2], *rest[-2:])
    else:
        cot, normed, scales, outs, order = (None, *rest[:2], rest[2:-1], rest[-1])
    mean, squares, total, _ = merge_rows(in_order(stats, idx[1], order))
    rows = jnp.concatenate(
        [mean, lax.rsqrt(squares / total + EPS), total, jnp.zeros((5, mean.shape[1]), F32)], axis=0
    )
    cols = as_columns(rows)
    norm = (value[...] - cols[:, 0:1]) * cols[:, 1:2]
    normed[...] = norm
    act = gelu(params[:, 0:1] * norm + params[:, 1:2]).astype(BF16)
    cs, width = norm.shape
    if cot is not None:
        c = cot[...].astype(F32)
        stack[...] = jnp.concatenate([c, c], axis=0).T
    for k, out in enumerate(outs):
        out[:, :width] = act
        if cot is not None:
            out[:, width:] = stack[rows_at(idx[0] ^ k, cs), :].astype(BF16)
    scales[...] = cols


def conv_block(nx, added, last, rows, section, area, small, idx, *refs):
    pieces = refs[:PEERS]
    narrow, rest = refs[PEERS], refs[PEERS + 1 :]
    if last:
        weights, rest = rest[0], rest[1:]
    else:
        messages, rest = rest[:nx], rest[nx:]
    base, rest = (rest[0], rest[1:]) if added else (None, rest)
    me = idx[0]
    cs, width = pieces[0].shape[0], narrow.shape[1]
    if last:
        outs, act, spread = rest[:PEERS], rest[PEERS], rest[PEERS + 1]
    else:
        value, out_stats, act, whole, spread, held = rest
        hold(idx[2], messages, held, section)
        assemble(held, whole, rows)
        weights = whole
    for k, ref in enumerate(pieces):
        act[rows_at(me ^ k, cs), :] = ref[:, :width]
    spread[...] = jnp.dot(weights[...], act[...], preferred_element_type=F32)
    row, col = pixel(width, area, small)
    total = base[...] if added else jnp.zeros((cs, width), F32)
    for k, (_, drow, dcol) in enumerate(OFFSETS):
        y = moved(spread[k * cs : (k + 1) * cs, :], drow * small + dcol)
        total += jnp.where(inside(row, col, drow, dcol, small), y, 0.0)
    if last:
        result = total.astype(BF16)
        lane = lax.broadcasted_iota(jnp.int32, (width, 128), 0)
        slot = lax.broadcasted_iota(jnp.int32, (width, 128), 1)
        for k, out in enumerate(outs):
            out[...] = pick(result, (lane == (me ^ k) * area + slot).astype(BF16))
    else:
        value[...] = total
        weight = narrow[0:1, :]
        n = jnp.sum(weight, axis=1, keepdims=True)
        mean, squares = masked_stats(total, weight, n)
        out_stats[...] = as_rows((mean, squares, n))


def join_result(idx, *refs):
    pieces, (out, stack) = refs[:PEERS], refs[PEERS:]
    cs = pieces[0].shape[0]
    for k, ref in enumerate(pieces):
        stack[rows_at(idx[0] ^ k, cs), :] = ref[:, -128:].astype(F32)
    out[...] = stack[...].T[: out.shape[0]].astype(BF16)


def spread_grad(grad, shifted, area, small, offs, row_at):
    cs, width = grad.shape
    row, col = pixel(width, area, small)
    for k, (_, drow, dcol) in enumerate(offs):
        g = moved(grad, -(drow * small + dcol))
        g = jnp.where(inside(row, col, -drow, -dcol, small), g, 0.0)
        shifted[row_at(k, cs), :] = g.astype(BF16)


def plain_rows(k, cs):
    return slice(k * cs, (k + 1) * cs)


def push_back(me, weights, shifted, partial, outs):
    cs, width = outs[0].shape[0], shifted.shape[1]
    partial[...] = lax.dot_general(
        weights[...], shifted[...], (((0,), (0,)), ((), ())), preferred_element_type=F32
    )
    for k, out in enumerate(outs):
        out[:, :width] = partial[rows_at(me ^ k, cs), :].astype(BF16)


def last_back(nx, rows, area, small, idx, *refs):
    pieces, messages, rest = refs[:PEERS], refs[PEERS : PEERS + nx], refs[PEERS + nx :]
    cot, shifted, weights = rest[:3]
    outs = rest[3 : PEERS + 3]
    partial, held = rest[PEERS + 3 :]
    hold(idx[2], messages, held)
    assemble(held, weights, rows)
    me = idx[0]
    cs, width = cot.shape
    image = lax.broadcasted_iota(jnp.int32, (1, width), 1) // area
    grad = jnp.zeros((cs, width), F32)
    for k, ref in enumerate(pieces):
        tiled = jnp.concatenate([ref[:, width:].astype(F32)] * (width // 128), axis=1)
        grad = jnp.where(image == (me ^ k), tiled, grad)
    cot[...] = grad
    spread_grad(grad, shifted, area, small, OFFSETS, plain_rows)
    push_back(me, weights, shifted, partial, outs)


def gelu_back(idx, *refs):
    pieces = refs[:PEERS]
    normed, params, grad_pre, sums = refs[PEERS:]
    width = normed.shape[1]
    grad = pieces[0][:, :width].astype(F32)
    for ref in pieces[1:]:
        grad += ref[:, :width].astype(F32)
    norm = normed[...]
    g = gelu_slope(params[:, 0:1] * norm + params[:, 1:2]) * grad
    grad_pre[...] = g
    sums[...] = as_rows(
        (jnp.sum(g * norm, axis=1, keepdims=True), jnp.sum(g, axis=1, keepdims=True))
    )


def norm_back(nz, added, last, area, small, idx, *refs):
    grad_pre, normed, scales, params, narrow = refs[:5]
    sums = refs[5 : 5 + nz]
    rest = refs[5 + nz :]
    base, rest = (rest[0], rest[1:]) if added else (None, rest)
    me = idx[0]
    cs, width = grad_pre.shape
    order = rest[-1]
    got = in_order(sums, idx[1], order)
    total = got[0]
    for g in got[1:]:
        total = total + g
    cols = as_columns(total)
    gain_grad, shift_grad = cols[:, 0:1], cols[:, 1:2]
    norm = normed[...]
    back = params[:, 0:1] * scales[:, 1:2] * (
        grad_pre[...]
        - narrow[0:1, :] * (shift_grad + norm * gain_grad) / scales[:, 2:3]
    )
    if added:
        back = base[...] + back
    grad = back.astype(BF16).astype(F32)
    if not last:
        riders = ()
        if not added:
            riders, rest = rest[:PEERS], rest[PEERS:]
        weights, sums_out, shifted = rest[:3]
        outs, partial = rest[3 : 3 + PEERS], rest[3 + PEERS]
        for rider, out in zip(riders, outs):
            out[:, width:] = rider[...]
        if added:
            grad_out, outs, partial = rest[3], rest[4 : 4 + PEERS], rest[4 + PEERS]
            grad_out[...] = grad.astype(BF16)
        sums_out[...] = total
        spread_grad(grad, shifted, area, small, OFFSETS, plain_rows)
        push_back(me, weights, shifted, partial, outs)
    else:
        weights, grad_skip, sums_out, shifted = rest[:4]
        outs, partial = rest[4 : 4 + PEERS], rest[4 + PEERS]
        sums_out[...] = total
        spread_grad(grad, shifted, area, small, STRIDED[:9], row_of)
        shifted[row_of(9, cs), :] = grad_skip[...]
        for phase in range(4):
            partial[phase] = lax.dot_general(
                shifted[phase_rows(phase, cs), :],
                weights[phase_rows(phase, cs), :],
                (((0,), (0,)), ((), ())),
                preferred_element_type=F32,
            )
        for k, out in enumerate(outs):
            for phase in range(4):
                out[phase * area : (phase + 1) * area, :] = partial[
                    phase, rows_at(me ^ k, area), :
                ].astype(BF16)


def part_halves(core, units, own, other):
    own[...] = units[core]
    other[...] = units[1 - core].astype(BF16)


def weight_grad(rows, idx, shifted, act, own, other, full, units):
    full[...] = lax.dot_general(
        shifted[...], act[...], (((1,), (1,)), ((), ())), preferred_element_type=F32
    )
    ny, cs, span = own.shape
    tiles = full.shape[1] // 128
    for v in range(2 * ny):
        begin = rows * v % 128
        parts = []
        for q in range((begin + rows + 127) // 128):
            k, p = divmod(rows * v // 128 + q, tiles)
            parts.append(full[k * cs : (k + 1) * cs, p * 128 : (p + 1) * 128])
        window = jnp.concatenate(parts, axis=1)
        units[v % 2, v // 2] = moved(window, begin)[:, :span]
    part_halves(idx[2] % 2, units, own, other)


def weight_grad_first(rows, extra, idx, shifted, act, own, other, flat, units):
    ny, cs, span = own.shape
    c_in = act.shape[2]
    flat[...] = jnp.zeros_like(flat)
    skip = None
    for phase in range(4):
        group = jnp.dot(
            shifted[phase_rows(phase, cs), :], act[phase], preferred_element_type=F32
        ).astype(BF16)
        for at, k in enumerate(PHASES[phase]):
            grad = group[at * cs : (at + 1) * cs]
            if k == 9:
                skip = grad
                continue
            begin = k * c_in
            base = begin // 128 * 128
            reach = -(-(begin + c_in) // 128) * 128
            move = one_hot(c_in, reach - base, begin - base)
            flat[:, base:reach] += jnp.dot(grad, move, preferred_element_type=F32)
    lane = lax.broadcasted_iota(jnp.int32, (1, span), 1)
    for v in range(2 * ny):
        begin = rows * v % 128
        base = rows * v - begin
        window = moved(flat[:, base : base + span + 128], begin)[:, :span]
        row = lax.broadcasted_iota(jnp.int32, (c_in, span), 0)
        col = lax.broadcasted_iota(jnp.int32, (c_in, span), 1)
        place = (row >= extra * v) & (row < extra * (v + 1)) & (col == row - extra * v + rows)
        tail = pick32(skip, place.astype(BF16))
        units[v % 2, v // 2] = jnp.where(lane < rows, window, 0.0) + tail
    part_halves(idx[2] % 2, units, own, other)


def reduce_core(count, idx, *refs):
    own, other, outs, total = refs[:count], refs[count : 2 * count], refs[2 * count : -1], refs[-1]
    cb = outs[0].shape[1]
    at = 0
    for a, b in zip(own, other):
        span = a.shape[2]
        total[:, :, at : at + span] = a[...] + b[...].astype(F32)
        at += span
    for k, out in enumerate(outs):
        for j in range(total.shape[0]):
            out[j] = total[j, rows_at(idx[2] // 2 ^ k, cb), :].astype(out.dtype)


def reduce_side(sides, idx, *refs):
    out = refs[-1]
    at = 0
    for n in range(0, len(refs) - 1, sides):
        total = refs[n][...]
        for ref in refs[n + 1 : n + sides]:
            total += ref[...].astype(F32)
        out[:, :, at : at + total.shape[2]] = total.astype(BF16)
        at += total.shape[2]


def fold(nz, fy, idx, got, out):
    cs = got.shape[1]
    for f in range(fy):
        total = got[f].astype(F32)
        for z in range(1, nz):
            total += got[z * fy + f].astype(F32)
        out[f * cs : (f + 1) * cs, :] = total.astype(BF16)


def own_rows(count, spans, idx, *refs):
    pieces, outs, stack = refs[:count], refs[count:-1], refs[-1]
    for k, ref in enumerate(pieces):
        at = idx[2] ^ k
        stack[at % 2, at // 2] = ref[...]
    sides, height = stack.shape[1], stack.shape[2]
    fy_cb = [(f, x) for f in range(PEERS) for x in range(sides)]
    cb = height // PEERS
    for half in range(2):
        whole = jnp.concatenate(
            [stack[half, x, f * cb : (f + 1) * cb, :].astype(F32) for f, x in fy_cb], axis=0
        ).T
        at = 0
        for span, group in spans:
            begin = at
            for n in group:
                out = outs[n]
                rows = out.shape[0] // 2
                out[half * rows : (half + 1) * rows, :] = whole[begin : begin + rows]
                begin += rows
            at += span


def entry_back(small, idx, *refs):
    pieces = refs[:PEERS]
    image, norm, gain, shift, grad_pre, sums = refs[PEERS:]
    c_in = gain.shape[1]
    side = 2 * small
    grad = pieces[0][...].astype(F32)
    for ref in pieces[1:]:
        grad += ref[...].astype(F32)
    order = pixel_order(small, side * side, lambda y, x: y * side + x)
    high = grad.astype(BF16)
    low = (grad - high.astype(F32)).astype(BF16)
    grad = sum(
        lax.dot_general(order, part, (((0,), (0,)), ((), ())), preferred_element_type=F32)
        for part in (high, low)
    )
    normed = (image[...].astype(F32) - norm[0:1, :c_in]) * norm[1:2, :c_in]
    g = gelu_slope(gain[...] * normed + shift[...]) * grad
    grad_pre[...] = g
    sums[...] = jnp.zeros_like(sums)
    sums[0:1, :c_in] = jnp.sum(g * normed, axis=0, keepdims=True)
    sums[1:2, :c_in] = jnp.sum(g, axis=0, keepdims=True)


def bundle(idx, first, second, third, sums, out):
    out[...] = jnp.zeros_like(out)
    out[0:8, :] = sums[...]
    for k, ref in enumerate((first, second, third)):
        out[8 + 2 * k : 10 + 2 * k, : ref.shape[1]] = ref[0:2]


def unbundle(idx, *refs):
    out, six, order = refs[-3:]
    got = in_order(refs[:-3], idx[0], order)
    total = got[0][0:8]
    for g in got[1:]:
        total = total + g[0:8]
    out[...] = total
    cs = six.shape[1] // PEERS
    six[...] = jnp.concatenate([g[8:16, :cs] for g in got], axis=1)


def entry_grad(nz, idx, *refs):
    sums = refs[:nz]
    grad_pre, image, weight, norm, gain, gain_grad, shift_grad, out, order = refs[nz:]
    got = in_order(sums, idx[1], order)
    total = got[0]
    for g in got[1:]:
        total = total + g
    gain_grad[...] = total[0:1]
    shift_grad[...] = total[1:2]
    c_in = gain.shape[1]
    scale = norm[1:2, :c_in]
    normed = (image[...].astype(F32) - norm[0:1, :c_in]) * scale
    out[...] = gain[...] * scale * (
        grad_pre[...]
        - weight[:, 0:1]
        * (shift_grad[0:1, :c_in] + normed * gain_grad[0:1, :c_in])
        / norm[2:3, :c_in]
    )


def program(
    nx,
    ny,
    images,
    valid_count,
    pixel_mask,
    gain_entry,
    shift_entry,
    conv_first,
    gain_middle,
    shift_middle,
    conv_second,
    projection,
    gain_inner,
    shift_inner,
    conv_third,
    gain_last,
    shift_last,
    conv_fourth,
    cotangent,
):
    fy = PEERS
    nz = ny // fy
    sides = nx // 2
    side, c_in = images.shape[1], images.shape[3]
    small = side // 2
    area = small * small
    c_out = conv_first.shape[1]
    cs = c_out // PEERS
    cb = cs // sides
    width = PEERS * area
    lanes = c_in + 64
    padded = span_of(c_in)
    gx, gy = lax.axis_index("gx"), lax.axis_index("gy")
    me = gy % fy
    mine = gy // fy
    run = Order(jnp.stack([me, mine, gx, gy]).astype(jnp.int32))
    part = functools.partial

    def to_slice(piece, k):
        return lax.ppermute(piece, "gy", [(j, j // fy * fy + (j % fy ^ k)) for j in range(ny)])

    def share(pieces):
        return [pieces[0]] + [to_slice(pieces[k], k) for k in range(1, PEERS)]

    def to_gx(piece, k):
        return lax.ppermute(piece, "gx", [(i, i ^ k) for i in range(nx)])

    def pool_gx(piece):
        return [piece] + [to_gx(piece, k) for k in range(1, nx)]

    def pool_z(piece):
        out = [piece]
        for k in range(1, nz):
            perm = [(j, (j // fy ^ k) * fy + j % fy) for j in range(ny)]
            out.append(lax.ppermute(piece, "gy", perm))
        return out

    def over_x(block):
        return {0: block, **{k: to_gx(block, k) for k in range(2, nx, 2)}}

    def over_core(held, *then):
        held = {k: after(v, *then) for k, v in held.items()} if then else dict(held)
        for k in list(held):
            held[k + 1] = to_gx(held[k], 1)
        return [held[k] for k in sorted(held)]

    def turn(block):
        return lax.all_to_all(block, "gy", 0, 0, tiled=True)

    unit_first, unit_skip = conv_first.shape[0] // 2, projection.shape[0] // 2
    unit_mid = conv_second.shape[0] // 2
    span_first, span_mid = span_of(unit_first + unit_skip), span_of(unit_mid)
    tile, tile16 = shape((cs, width)), shape((cs, width), BF16)
    long16 = shape((cs, width + 128), BF16)
    cols, stat, entry_stat = shape((cs, 128)), shape((8, cs)), shape((8, lanes))
    shifted16 = shape((9 * cs, width), BF16)
    full16 = shape((c_out, width), BF16)
    whole16 = shape((9 * cs, c_out), BF16)

    def halves(span, channels):
        return pltpu.VMEM((2, cs // channels, ny, channels, span), BF16)

    def ready(span, channels, *weights):
        out = shape((ny, channels, span), BF16)
        return run(part(entry_weights, cs, fy, (len(weights),)), out, weights, cost=24)

    def merge(pieces, kernel):
        like = pieces[0].shape
        return run(kernel, shape(like), pieces, [pltpu.VMEM((nx, *like), F32)])

    add_gx = part(add_rows, 2)

    def activate(value, params, pooled, cot=None):
        more = [] if cot is None else [cot]
        outs = [tile16] if cot is None else [long16] * PEERS
        return run(
            part(act_block, nz),
            [tile, cols] + outs,
            [value, params, *pooled, *more],
            [pltpu.VMEM((nz, 8, cs), F32)]
            + ([] if cot is None else [pltpu.VMEM((c_out, 128), F32)]),
        )

    def convolve(pieces, weights, base, last=False):
        more = [] if base is None else [base]
        outs = [shape((cs, 128), BF16)] * PEERS + [full16]
        return run(
            part(conv_block, nx, base is not None, last, unit_mid, 0, area, small),
            outs if last else [tile, stat, full16, whole16],
            [*pieces, narrow, *weights, *more],
            [pltpu.VMEM((9 * cs, width), F32)] + ([] if last else [halves(span_mid, cb)]),
            cost=25,
        )

    def slope(parts, normed, params):
        return run(gelu_back, [tile, stat], [*parts, normed, params])

    def back(grad_pre, normed, scales, params, pooled, weights, base, riders=()):
        more = list(riders) if base is None else [base]
        return run(
            part(norm_back, nz, base is not None, False, area, small),
            [stat, shifted16]
            + ([long16] * PEERS if base is None else [tile16] * (PEERS + 1)),
            [grad_pre, normed, scales, params, narrow, *pooled, *more, weights],
            [pltpu.VMEM((c_out, width), F32), pltpu.VMEM((nz, 8, cs), F32)],
            cost=18,
        )

    def grad_of(kernel, span, shifted, act, scratch):
        own, other = run(
            kernel,
            [shape((ny, cs, span)), shape((ny, cs, span), BF16)],
            [shifted, act],
            [scratch, pltpu.VMEM((2, ny, cs, span), F32)],
            cost=28,
        )
        return own, to_gx(other, 1)

    def grad_mid(shifted, act):
        return grad_of(
            part(weight_grad, unit_mid), span_mid, shifted, act, pltpu.VMEM((9 * cs, c_out), F32)
        )

    def over_pair(own, other):
        span = own.shape[2]
        return run(
            part(reduce_core, 1),
            [shape((ny, cb, span))] + [shape((ny, cb, span), BF16)] * (sides - 1),
            [own, other],
            [pltpu.VMEM((ny, cs, span), F32)],
        )

    def to_sides(parts, *then):
        parts = [after(p, *then) for p in parts] if then else parts
        return [parts[0]] + [to_gx(parts[k], 2 * k) for k in range(1, sides)]

    def over_sides(*groups):
        span = sum(parts[0].shape[2] for parts in groups)
        return run(
            part(reduce_side, sides),
            shape((ny, cb, span), BF16),
            [p for parts in groups for p in parts],
        )

    def folded(got):
        out = shape((fy * cb, got.shape[2]), BF16)
        return over_core(over_x(run(part(fold, nz, fy), out, [got])))

    def rows_of(pieces, spans, *rows):
        return run(
            part(own_rows, nx, spans),
            [shape((r, c_out)) for r in rows],
            pieces,
            [pltpu.VMEM((2, sides, fy * cb, pieces[0].shape[1]), BF16)],
            cost=30,
        )

    def own(gain, shift):
        pair = jnp.stack([gain, shift], axis=1)
        return lax.dynamic_slice_in_dim(pair, me * cs, cs, axis=0)

    p_middle = own(gain_middle, shift_middle)
    p_inner = own(gain_inner, shift_inner)
    p_last = own(gain_last, shift_last)
    g_entry, s_entry = gain_entry[None], shift_entry[None]
    pixels = images.reshape(side * side, c_in)

    image, wide = run(
        part(entry_image, small),
        [shape((4 * area, lanes), BF16), shape((4 * area, 128))],
        [pixels, pixel_mask.reshape(side, side), valid_count],
        scalars=1,
    )
    group = share([image] * PEERS)
    out_first = ready(span_first, cs, conv_first, projection)
    stats = run(part(entry_stats, area), entry_stat, group)
    pieces = pool_gx(stats)
    got_first = over_core({0: turn(after(out_first, *group[1:]))})
    out_second = ready(span_mid, cb, conv_second)
    pooled = pool_z(merge(pieces, merge_stats))
    got_second = turn(after(out_second, pooled[-1]))
    out_third = ready(span_mid, cb, conv_third)
    out_fourth = ready(span_mid, cb, conv_fourth)
    first, skipped, stats, norm_one, narrow, act_one, w_first = run(
        part(entry_block, nz, unit_first, unit_skip, area, small),
        [
            tile,
            tile,
            stat,
            entry_stat,
            shape((8, width)),
            shape((4, width, c_in), BF16),
            shape((10 * cs, c_in), BF16),
        ],
        [*group, *pooled, g_entry, s_entry, *got_first],
        [
            pltpu.VMEM((nz, 8, lanes), F32),
            pltpu.VMEM((width, lanes), BF16),
            pltpu.VMEM((cs, span_of(9 * c_in)), BF16),
            halves(span_first, cs),
        ],
        cost=40,
    )

    merged = merge(pool_gx(stats), merge_stats)
    got_second = over_x(after(got_second, merged))
    pooled = pool_z(merged)
    got_third = turn(after(out_third, pooled[-1]))
    normed_two, scale_two, *messages = activate(
        first, p_middle, pooled, cotangent.reshape(area, c_out)
    )
    pieces = share(messages)
    got_second = over_core(got_second, *pieces[1:])
    hidden, stats, act_two, w_second = convolve(pieces, got_second, skipped)
    cot_parts = pieces
    got_fourth = turn(after(out_fourth, stats))
    merged = merge(pool_gx(stats), merge_stats)
    got_third = over_x(after(got_third, merged))
    pooled = pool_z(merged)
    normed_three, scale_three, act = activate(hidden, p_inner, pooled)
    got_fourth = over_x(after(got_fourth, pooled[-1]))
    pieces = share([act] * PEERS)
    got_third = over_core(got_third, *pieces[1:])
    third, stats, act_three, w_third = convolve(pieces, got_third, None)
    got_fourth = over_core(got_fourth, stats)
    merged = merge(pool_gx(stats), merge_stats)

    cot, shifted_four, w_fourth, *parts = run(
        part(last_back, nx, unit_mid, area, small),
        [tile, shifted16, whole16] + [tile16] * PEERS,
        [*cot_parts, *got_fourth],
        [pltpu.VMEM((c_out, width), F32), halves(span_mid, cb)],
        cost=18,
    )
    parts = share(parts)
    normed_four, scale_four, act = activate(third, p_last, pool_z(merged))
    pieces = share([act] * PEERS)
    grad_pre, sums = slope(parts, normed_four, p_last)
    sums = pool_gx(sums)
    *riders, act_four = convolve(pieces, [w_fourth], hidden, last=True)
    sums = pool_z(merge(sums, add_gx))
    fourth = grad_mid(shifted_four, act_four)
    last_sums, shifted_three, *parts = back(
        grad_pre, normed_four, scale_four, p_last, sums, w_third, None, riders
    )
    parts = share(parts)
    fourth = over_pair(*fourth)
    grad_pre, sums = slope(parts, normed_three, p_inner)
    sums = pool_gx(sums)
    third = grad_mid(shifted_three, act_three)
    merged = merge(sums, add_gx)
    fourth = to_sides(fourth, merged)
    sums = pool_z(merged)
    out = run(
        join_result, shape((area, c_out), BF16), parts, [pltpu.VMEM((c_out, 128), F32)]
    )
    inner_sums, shifted_two, grad_hidden, *parts = back(
        grad_pre, normed_three, scale_three, p_inner, sums, w_second, cot
    )
    parts = share(parts)
    third = over_pair(*third)
    grad_pre, sums = slope(parts, normed_two, p_middle)
    sums = pool_gx(sums)
    second = grad_mid(shifted_two, act_two)
    merged = merge(sums, add_gx)
    third = to_sides(third, merged)
    middle_sums, shifted_one, *parts = run(
        part(norm_back, nz, False, True, area, small),
        [stat, shape((10 * cs, width), BF16)] + [shape((4 * area, c_in), BF16)] * PEERS,
        [
            grad_pre,
            normed_two,
            scale_two,
            p_middle,
            narrow,
            *pool_z(merged),
            w_first,
            grad_hidden,
        ],
        [pltpu.VMEM((4, width, c_in), F32), pltpu.VMEM((nz, 8, cs), F32)],
        cost=18,
    )

    parts = share(parts)
    second = to_sides(over_pair(after(second[0], *parts[1:]), second[1]))
    late = turn(over_sides(fourth, third))
    first = grad_of(
        part(weight_grad_first, unit_first, unit_skip),
        span_first,
        shifted_one,
        act_one,
        pltpu.VMEM((cs, span_of(9 * c_in + span_first + 128)), F32),
    )
    grad_pre, sums = run(
        part(entry_back, small),
        [shape((4 * area, c_in)), shape((8, padded))],
        [*parts, pixels, norm_one, g_entry, s_entry],
    )
    message = run(bundle, shape((16, padded)), [middle_sums, inner_sums, last_sums, sums])
    message = share([message] * PEERS)
    first = to_sides(over_pair(*first))
    sums, six = run(
        unbundle,
        [shape((8, padded)), shape((8, c_out))],
        message,
        [pltpu.VMEM((PEERS, 16, padded), F32)],
    )
    sums = pool_z(merge(pool_gx(sums), add_gx))
    early = turn(over_sides(second, first))
    gain_entry_grad, shift_entry_grad, image_grad = run(
        part(entry_grad, nz),
        [shape((1, padded)), shape((1, padded)), shape((4 * area, c_in))],
        [*sums, grad_pre, pixels, wide, norm_one, g_entry],
        [pltpu.VMEM((nz, 8, padded), F32)],
    )
    late = folded(late)
    early = folded(early)
    fourth_grad, third_grad = rows_of(
        late, ((span_mid, (0,)), (span_mid, (1,))), 2 * unit_mid, 2 * unit_mid
    )
    second_grad, first_grad, skip_grad = rows_of(
        early,
        ((span_mid, (0,)), (span_first, (1, 2))),
        2 * unit_mid,
        2 * unit_first,
        2 * unit_skip,
    )
    return (
        out.reshape(1, small, small, c_out),
        image_grad.reshape(1, side, side, c_in),
        gain_entry_grad[0, :c_in],
        shift_entry_grad[0, :c_in],
        first_grad,
        six[0],
        six[1],
        second_grad,
        skip_grad,
        six[2],
        six[3],
        third_grad,
        six[4],
        six[5],
        fourth_grad,
    )


def solution(mesh):
    whole = P(("gx", "gy"), None, None, None)
    rows = P("gy", None)
    return jax.shard_map(
        functools.partial(program, mesh.shape["gx"], mesh.shape["gy"]),
        mesh=mesh,
        in_specs=(
            whole,
            P(("gx", "gy")),
            P(("gx", "gy"), None, None),
            P(),
            P(),
            rows,
            P(),
            P(),
            rows,
            rows,
            P(),
            P(),
            rows,
            P(),
            P(),
            rows,
            whole,
        ),
        out_specs=(
            whole, whole, P(), P(), rows, P(), P(), rows, rows, P(), P(), rows, P(), P(), rows,
        ),
        check_vma=False,
    )
```

```python
import functools

import jax
import jax.numpy as jnp
from jax import lax
from jax.experimental import pallas as pl
from jax.experimental.pallas import tpu as pltpu
from jax.sharding import PartitionSpec as P

EPS = 1e-05
COST = 6 * 10**7
F32 = jnp.float32
BF16 = jnp.bfloat16
PEERS = 4
C0 = 0.7978845608028654
C1 = 0.044715
VMEM = pl.BlockSpec(memory_space=pltpu.VMEM)
SMEM = pl.BlockSpec(memory_space=pltpu.SMEM)


def gelu(v):
    return 0.5 * v * (1.0 + jnp.tanh(C0 * (v + C1 * (v * v * v))))


def gelu_slope(v):
    t = jnp.tanh(C0 * (v + C1 * (v * v * v)))
    return 0.5 * (1.0 + t) + 0.5 * v * (1.0 - t * t) * (C0 * (1.0 + 3.0 * C1 * (v * v)))


def after(value, *others):
    return lax.optimization_barrier((value, *others))[0]


class Far:
    def __init__(self, near, far, sem):
        self.near, self.shape, self.dtype = near, near.shape, near.dtype
        self.copy = pltpu.make_async_copy(near, far, sem)
        self.sent = False

    def __getitem__(self, at):
        return self.near[at]

    def __setitem__(self, at, value):
        self.near[at] = value

    def send(self):
        if not self.sent:
            self.copy.start()
            self.sent = True


def send(ref):
    if isinstance(ref, Far):
        ref.send()


def with_far(kernel, n_in, n_out, far, *refs):
    ins, outs, rest = refs[:n_in], list(refs[n_in : n_in + n_out]), list(refs[n_in + n_out :])
    if far:
        sems = rest.pop()
        near = rest[len(rest) - len(far) :]
        del rest[len(rest) - len(far) :]
        for n, at in enumerate(far):
            outs[at] = Far(near[n], outs[at], sems.at[n])
    kernel(*ins, *outs, *rest)
    for at in far:
        outs[at].send()
    for at in far:
        outs[at].copy.wait()


class Order:
    def __init__(self, idx):
        self.idx = idx
        self.last = ()

    def __call__(self, kernel, outs, args, scratch=(), scalars=0, cost=7, far=()):
        idx = after(self.idx, *self.last)
        many = isinstance(outs, (list, tuple))
        shapes = list(outs) if many else [outs]
        more = [pltpu.VMEM(shapes[at].shape, shapes[at].dtype) for at in far]
        if far:
            more.append(pltpu.SemaphoreType.DMA((len(far),)))
        got = pl.pallas_call(
            functools.partial(with_far, kernel, 1 + len(args), len(shapes), tuple(far)),
            out_shape=shapes,
            in_specs=[SMEM] + [VMEM] * (len(args) - scalars) + [SMEM] * scalars,
            out_specs=[
                pl.BlockSpec(memory_space=pl.ANY) if at in far else VMEM
                for at in range(len(shapes))
            ],
            scratch_shapes=list(scratch) + more,
            compiler_params=pltpu.CompilerParams(vmem_limit_bytes=16 * 1024 * 1024),
            cost_estimate=pl.CostEstimate(
                flops=cost * COST, bytes_accessed=1024, transcendentals=0
            ),
        )(idx, *args)
        near = [v for at, v in enumerate(got) if at not in far]
        self.last = (near[0] if near else got[0],)
        return got if many else got[0]


def shape(dims, dtype=F32):
    return jax.ShapeDtypeStruct(dims, dtype)


def rows_at(index, count):
    return pl.ds(pl.multiple_of(index * count, count), count)


def as_rows(parts):
    height = parts[0].shape[0]
    lane = lax.broadcasted_iota(jnp.int32, (height, 128), 1)
    out = jnp.zeros((height, 128), F32)
    for k, part in enumerate(parts):
        out = jnp.where(lane == k, part, out)
    return out.T[0:8]


def as_columns(rows):
    return jnp.concatenate([rows, jnp.zeros((120, rows.shape[1]), F32)], axis=0).T


def in_order(refs, me, scratch):
    for k, ref in enumerate(refs):
        scratch[me ^ k] = ref[...]
    return [scratch[k] for k in range(len(refs))]


def merge_moments(stats):
    total = sum(n for _, _, n in stats)
    mean = sum(n * m for m, _, n in stats) / total
    squares = sum(q + n * (m - mean) * (m - mean) for m, q, n in stats)
    return mean, squares, total


def merge_rows(refs):
    mean, squares, total = merge_moments([(g[0:1], g[1:2], g[2:3]) for g in refs])
    return mean, squares, total, sum(g[3:4] for g in refs)


def pixel(width, area, small):
    lane = lax.broadcasted_iota(jnp.int32, (1, width), 1) % area
    return lane // small, lane % small


def inside(row, col, drow, dcol, small):
    return (row + drow >= 0) & (row + drow < small) & (col + dcol >= 0) & (col + dcol < small)


def moved(value, step):
    shift = (-step) % value.shape[1]
    return pltpu.roll(value, shift, 1) if shift else value


OFFSETS = [(0, krow - 1, kcol - 1) for krow in range(3) for kcol in range(3)]

STRIDED = [
    ((krow != 1) * 2 + (kcol != 1), -(krow == 0), -(kcol == 0))
    for krow in range(3)
    for kcol in range(3)
] + [(0, 0, 0)]
PLACED = sorted(range(10), key=lambda k: (STRIDED[k][0], k))
PHASES = [[k for k in PLACED if STRIDED[k][0] == phase] for phase in range(4)]


def row_of(k, cs):
    at = PLACED.index(k)
    return slice(at * cs, (at + 1) * cs)


def phase_rows(phase, cs):
    first, last = PHASES[phase][0], PHASES[phase][-1]
    return slice(PLACED.index(first) * cs, (PLACED.index(last) + 1) * cs)


def masked_stats(value, weight, n):
    mean = jnp.sum(value * weight, axis=1, keepdims=True) / n
    centred = value - mean
    return mean, jnp.sum(weight * centred * centred, axis=1, keepdims=True)


def span_of(rows):
    return -(-rows // 128) * 128


def one_hot(height, width, shift):
    row = lax.broadcasted_iota(jnp.int32, (height, width), 0)
    col = lax.broadcasted_iota(jnp.int32, (height, width), 1)
    return (col == row + shift).astype(BF16)


def pick32(left, right, dims=((1,), (0,))):
    return lax.dot_general(left, right, (dims, ((), ())), preferred_element_type=F32)


def pick(left, right, dims=((1,), (0,))):
    return pick32(left, right, dims).astype(BF16)


def lane_tile(held, tile, rows, span):
    sides, ny = held.shape[1], held.shape[2]
    lane = lax.broadcasted_iota(jnp.int32, (1, 128), 1)
    out = None
    for v in range(2 * ny):
        begin = rows * v - tile * 128
        if begin >= 128 or begin + rows <= 0:
            continue
        at = (tile - rows * v // 128) * 128 % span
        part = jnp.concatenate(
            [held[v % 2, x, v // 2, :, at : at + 128].astype(F32) for x in range(sides)], axis=0
        )
        if begin > 0 or begin + rows < 128:
            own = (lane >= begin) & (lane < begin + rows)
            part = jnp.where(own, part, 0.0)
        out = part if out is None else out + part
    return out.astype(BF16)


def pixel_order(small, width, of):
    area = small * small
    row = lax.broadcasted_iota(jnp.int32, (4 * area, width), 0)
    col = lax.broadcasted_iota(jnp.int32, (4 * area, width), 1)
    phase, pix = row // area, row % area
    y = 2 * (pix // small) + phase // 2
    x = 2 * (pix % small) + phase % 2
    return (col == of(y, x)).astype(BF16)


def entry_image(small, idx, image, mask, valid, out, weight):
    side = 2 * small
    c_in = image.shape[1]
    count = side * side
    order = pixel_order(small, count, lambda y, x: y * side + x)
    out[:, :c_in] = pick(order, image[...])
    live = (valid[0] > 0).astype(F32)
    row = lax.broadcasted_iota(jnp.int32, (count, side), 0)
    col = lax.broadcasted_iota(jnp.int32, (count, side), 1)
    by_row = jnp.dot(
        (row // side == col).astype(BF16),
        mask[...].astype(F32).astype(BF16),
        preferred_element_type=F32,
    )
    column = jnp.sum(jnp.where(row % side == col, by_row, 0.0), axis=1, keepdims=True) * live
    lane = lax.broadcasted_iota(jnp.int32, (count, 128), 1)
    spread = jnp.where(lane == 0, column, 0.0)
    weight[...] = spread
    out[:, c_in:] = pick(order, spread.astype(BF16))[:, : out.shape[1] - c_in]


def entry_weights(cs, fy, sections, idx, *refs):
    weights, out = list(refs[:-1]), refs[-1]
    ny, cb, lanes = out.shape
    span = lanes // len(sections)
    gx, gy = idx[2], idx[3]
    core, side = gx % 2, (gx // 2 if cb < cs else 0)
    c_out = weights[0].shape[1]
    row = lax.broadcasted_iota(jnp.int32, (fy * cb, c_out), 0)
    col = lax.broadcasted_iota(jnp.int32, (fy * cb, c_out), 1)
    chosen = (col == row // cb * cs + side * cb + row % cb).astype(BF16)
    for n, count in enumerate(sections):
        begin = weights[0].shape[0] // 2 * (2 * gy + core) % 128
        total = None
        for _ in range(count):
            weight = weights.pop(0)
            rows = weight.shape[0]
            half = rows // 2
            mine = pick(chosen, weight[...], ((1,), (1,)))
            row = lax.broadcasted_iota(jnp.int32, (rows, span), 0) - core * half
            col = lax.broadcasted_iota(jnp.int32, (rows, span), 1)
            place = (row >= 0) & (row < half) & (
                (col == row + begin) | (col == row + begin - span)
            )
            part = pick32(mine, place.astype(BF16))
            total = part if total is None else total + part
            begin = begin + half
        for j in range(ny):
            out[j, :, n * span : (n + 1) * span] = total[
                (j % fy) * cb : (j % fy + 1) * cb
            ].astype(BF16)


def hold(gx, messages, held, section=0):
    span = held.shape[4]
    for k, ref in enumerate(messages):
        at = gx ^ k
        side = at // 2 if held.shape[1] > 1 else 0
        held[at % 2, side] = ref[:, :, section * span : (section + 1) * span]


def assemble(held, out, rows):
    cs, span = held.shape[1] * held.shape[3], held.shape[4]
    tiles = out.shape[1] // 128
    for k in range(9):
        for q in range(tiles):
            out[k * cs : (k + 1) * cs, q * 128 : (q + 1) * 128] = lane_tile(
                held, tiles * k + q, rows, span
            )


def assemble_first(held, out, flat, rows, extra):
    cs, span = held.shape[1] * held.shape[3], held.shape[4]
    c_in = out.shape[1]
    tiles = flat.shape[1] // 128
    for tile in range(tiles):
        flat[:, tile * 128 : (tile + 1) * 128] = lane_tile(held, tile, rows, span)
    for k in range(9):
        begin = k * c_in
        base = begin // 128 * 128
        reach = min(-(-(begin + c_in) // 128) * 128, flat.shape[1])
        move = one_hot(c_in, reach - base, begin - base)
        out[row_of(k, cs), :] = pick(flat[:, base:reach], move, ((1,), (1,)))
    total = None
    for v in range(2 * held.shape[2]):
        row = lax.broadcasted_iota(jnp.int32, (span, c_in), 0)
        col = lax.broadcasted_iota(jnp.int32, (span, c_in), 1)
        at = col - extra * v
        begin = rows * v % 128 + rows
        place = (at >= 0) & (at < extra) & ((row == at + begin) | (row == at + begin - span))
        part = jnp.concatenate(
            [
                pick32(held[v % 2, x, v // 2], place.astype(BF16))
                for x in range(held.shape[1])
            ],
            axis=0,
        )
        total = part if total is None else total + part
    out[row_of(9, cs), :] = total.astype(BF16)


def entry_stats(area, idx, *refs):
    images, out = refs[:PEERS], refs[PEERS]
    lanes = out.shape[1]
    first = jnp.zeros((1, lanes), F32)
    wide = jnp.zeros((1, 1), F32)
    narrow = jnp.zeros((1, 1), F32)
    c_in = lanes - 64
    for ref in images:
        x = ref[...].astype(F32)
        w = x[:, c_in : c_in + 1]
        first += jnp.sum(x * w, axis=0, keepdims=True)
        wide += jnp.sum(w, axis=0, keepdims=True)
        narrow += jnp.sum(w[:area], axis=0, keepdims=True)
    mean = first / wide
    squares = jnp.zeros((1, lanes), F32)
    for ref in images:
        x = ref[...].astype(F32)
        w = x[:, c_in : c_in + 1]
        d = x - mean
        squares += jnp.sum(d * d * w, axis=0, keepdims=True)
    out[...] = jnp.zeros_like(out)
    out[0:1, :] = mean
    out[1:2, :] = squares
    out[2:3, :] = jnp.broadcast_to(wide, (1, lanes))
    out[3:4, :] = jnp.broadcast_to(narrow, (1, lanes))


def entry_block(nz, nx, rows, extra, area, small, idx, *refs):
    images = refs[:PEERS]
    stats, rest = refs[PEERS : PEERS + nz], refs[PEERS + nz :]
    gain, shift, messages, rest = rest[0], rest[1], rest[2 : 2 + nx], rest[2 + nx :]
    first, skipped, out_stats, norm, narrow, act, w_first = rest[:7]
    order, masks, flat, held = rest[7:]
    me, mine = idx[0], idx[1]
    c_in = gain.shape[1]
    lanes = norm.shape[1]
    cs = first.shape[0]
    width = first.shape[1]
    hold(idx[2], messages, held)
    assemble_first(held, w_first, flat, rows, extra)
    send(w_first)
    mean, squares, total, count = merge_rows(in_order(stats, mine, order))
    scale = lax.rsqrt(squares / total + EPS)
    norm[...] = jnp.zeros_like(norm)
    norm[0:1, :] = mean
    norm[1:2, :] = scale
    norm[2:3, :] = total
    norm[3:4, :] = count
    for k, ref in enumerate(images):
        x = ref[...]
        v = x[:, :c_in].astype(F32)
        pre = gain[...] * ((v - mean[:, :c_in]) * scale[:, :c_in]) + shift[...]
        a = gelu(pre).astype(BF16)
        for phase in range(4):
            act[phase, rows_at(me ^ k, area), :] = a[phase * area : (phase + 1) * area]
        masks[rows_at(me ^ k, area), :] = x[:area]
    send(act)
    send(norm)
    ones = (lax.broadcasted_iota(jnp.int32, (8, lanes), 1) == c_in).astype(BF16)
    weight8 = lax.dot_general(
        ones, masks[...], (((1,), (1,)), ((), ())), preferred_element_type=F32
    )
    narrow[...] = weight8
    weight = weight8[0:1]
    row, col = pixel(width, area, small)
    total_first = jnp.zeros((cs, width), F32)
    for phase in range(4):
        group = lax.dot_general(
            w_first[phase_rows(phase, cs), :],
            act[phase],
            (((1,), (1,)), ((), ())),
            preferred_element_type=F32,
        )
        for at, k in enumerate(PHASES[phase]):
            y = group[at * cs : (at + 1) * cs]
            if k == 9:
                skipped[...] = y
                continue
            _, drow, dcol = STRIDED[k]
            y = moved(y, drow * small + dcol)
            total_first += jnp.where(inside(row, col, drow, dcol, small), y, 0.0)
    first[...] = total_first
    n = jnp.sum(weight, axis=1, keepdims=True)
    mean2, squares = masked_stats(total_first, weight, n)
    out_stats[...] = as_rows((mean2, squares, n))


def merge_stats(idx, *refs):
    out, order = refs[-2:]
    mean, squares, total, count = merge_rows(in_order(refs[:-2], idx[2], order))
    out[...] = jnp.zeros_like(out)
    out[0:1] = mean
    out[1:2] = squares
    out[2:3] = total
    out[3:4] = count


def add_rows(which, idx, *refs):
    out, order = refs[-2:]
    got = in_order(refs[:-2], idx[which], order)
    total = got[0]
    for g in got[1:]:
        total = total + g
    out[...] = total


def act_block(nz, idx, *refs):
    value, params = refs[:2]
    stats, rest = refs[2 : 2 + nz], refs[2 + nz :]
    if rest[-1].shape[1] == 128:
        cot, normed, scales, outs, order, stack = (*rest[:3], rest[3:-2], *rest[-2:])
    else:
        cot, normed, scales, outs, order = (None, *rest[:2], rest[2:-1], rest[-1])
    mean, squares, total, _ = merge_rows(in_order(stats, idx[1], order))
    rows = jnp.concatenate(
        [mean, lax.rsqrt(squares / total + EPS), total, jnp.zeros((5, mean.shape[1]), F32)], axis=0
    )
    cols = as_columns(rows)
    norm = (value[...] - cols[:, 0:1]) * cols[:, 1:2]
    normed[...] = norm
    send(normed)
    scales[...] = cols
    send(scales)
    act = gelu(params[:, 0:1] * norm + params[:, 1:2]).astype(BF16)
    cs, width = norm.shape
    if cot is not None:
        c = cot[...].astype(F32)
        stack[...] = jnp.concatenate([c, c], axis=0).T
    for k, out in enumerate(outs):
        out[:, :width] = act
        if cot is not None:
            out[:, width:] = stack[rows_at(idx[0] ^ k, cs), :].astype(BF16)


def conv_block(nx, added, last, rows, section, area, small, idx, *refs):
    pieces = refs[:PEERS]
    narrow, rest = refs[PEERS], refs[PEERS + 1 :]
    if last:
        weights, rest = rest[0], rest[1:]
    else:
        messages, rest = rest[:nx], rest[nx:]
    base, rest = (rest[0], rest[1:]) if added else (None, rest)
    me = idx[0]
    cs, width = pieces[0].shape[0], narrow.shape[1]
    if last:
        outs, act, spread = rest[:PEERS], rest[PEERS], rest[PEERS + 1]
    else:
        value, out_stats, act, whole, spread, held = rest
        hold(idx[2], messages, held, section)
        assemble(held, whole, rows)
        send(whole)
        weights = whole
    for k, ref in enumerate(pieces):
        act[rows_at(me ^ k, cs), :] = ref[:, :width]
    send(act)
    spread[...] = jnp.dot(weights[...], act[...], preferred_element_type=F32)
    row, col = pixel(width, area, small)
    total = base[...] if added else jnp.zeros((cs, width), F32)
    for k, (_, drow, dcol) in enumerate(OFFSETS):
        y = moved(spread[k * cs : (k + 1) * cs, :], drow * small + dcol)
        total += jnp.where(inside(row, col, drow, dcol, small), y, 0.0)
    if last:
        result = total.astype(BF16)
        lane = lax.broadcasted_iota(jnp.int32, (width, 128), 0)
        slot = lax.broadcasted_iota(jnp.int32, (width, 128), 1)
        for k, out in enumerate(outs):
            out[...] = pick(result, (lane == (me ^ k) * area + slot).astype(BF16))
    else:
        value[...] = total
        weight = narrow[0:1, :]
        n = jnp.sum(weight, axis=1, keepdims=True)
        mean, squares = masked_stats(total, weight, n)
        out_stats[...] = as_rows((mean, squares, n))


def join_result(idx, *refs):
    pieces, (out, stack) = refs[:PEERS], refs[PEERS:]
    cs = pieces[0].shape[0]
    for k, ref in enumerate(pieces):
        stack[rows_at(idx[0] ^ k, cs), :] = ref[:, -128:].astype(F32)
    out[...] = stack[...].T[: out.shape[0]].astype(BF16)


def spread_grad(grad, shifted, area, small, offs, row_at):
    cs, width = grad.shape
    row, col = pixel(width, area, small)
    for k, (_, drow, dcol) in enumerate(offs):
        g = moved(grad, -(drow * small + dcol))
        g = jnp.where(inside(row, col, -drow, -dcol, small), g, 0.0)
        shifted[row_at(k, cs), :] = g.astype(BF16)


def plain_rows(k, cs):
    return slice(k * cs, (k + 1) * cs)


def push_back(me, weights, shifted, partial, outs):
    cs, width = outs[0].shape[0], shifted.shape[1]
    partial[...] = lax.dot_general(
        weights[...], shifted[...], (((0,), (0,)), ((), ())), preferred_element_type=F32
    )
    for k, out in enumerate(outs):
        out[:, :width] = partial[rows_at(me ^ k, cs), :].astype(BF16)


def last_back(nx, rows, area, small, idx, *refs):
    pieces, messages, rest = refs[:PEERS], refs[PEERS : PEERS + nx], refs[PEERS + nx :]
    cot, shifted, weights = rest[:3]
    outs = rest[3 : PEERS + 3]
    partial, held = rest[PEERS + 3 :]
    hold(idx[2], messages, held)
    assemble(held, weights, rows)
    me = idx[0]
    cs, width = cot.shape
    image = lax.broadcasted_iota(jnp.int32, (1, width), 1) // area
    grad = jnp.zeros((cs, width), F32)
    for k, ref in enumerate(pieces):
        tiled = jnp.concatenate([ref[:, width:].astype(F32)] * (width // 128), axis=1)
        grad = jnp.where(image == (me ^ k), tiled, grad)
    cot[...] = grad
    spread_grad(grad, shifted, area, small, OFFSETS, plain_rows)
    push_back(me, weights, shifted, partial, outs)


def gelu_back(idx, *refs):
    pieces = refs[:PEERS]
    normed, params, grad_pre, sums = refs[PEERS:]
    width = normed.shape[1]
    grad = pieces[0][:, :width].astype(F32)
    for ref in pieces[1:]:
        grad += ref[:, :width].astype(F32)
    norm = normed[...]
    g = gelu_slope(params[:, 0:1] * norm + params[:, 1:2]) * grad
    grad_pre[...] = g
    sums[...] = as_rows(
        (jnp.sum(g * norm, axis=1, keepdims=True), jnp.sum(g, axis=1, keepdims=True))
    )


def norm_back(nz, added, last, area, small, idx, *refs):
    grad_pre, normed, scales, params, narrow = refs[:5]
    sums = refs[5 : 5 + nz]
    rest = refs[5 + nz :]
    base, rest = (rest[0], rest[1:]) if added else (None, rest)
    me = idx[0]
    cs, width = grad_pre.shape
    order = rest[-1]
    got = in_order(sums, idx[1], order)
    total = got[0]
    for g in got[1:]:
        total = total + g
    cols = as_columns(total)
    gain_grad, shift_grad = cols[:, 0:1], cols[:, 1:2]
    norm = normed[...]
    back = params[:, 0:1] * scales[:, 1:2] * (
        grad_pre[...]
        - narrow[0:1, :] * (shift_grad + norm * gain_grad) / scales[:, 2:3]
    )
    if added:
        back = base[...] + back
    grad = back.astype(BF16).astype(F32)
    if not last:
        riders = ()
        if not added:
            riders, rest = rest[:PEERS], rest[PEERS:]
        weights, sums_out, shifted = rest[:3]
        outs, partial = rest[3 : 3 + PEERS], rest[3 + PEERS]
        for rider, out in zip(riders, outs):
            out[:, width:] = rider[...]
        if added:
            grad_out, outs, partial = rest[3], rest[4 : 4 + PEERS], rest[4 + PEERS]
            grad_out[...] = grad.astype(BF16)
        sums_out[...] = total
        spread_grad(grad, shifted, area, small, OFFSETS, plain_rows)
        push_back(me, weights, shifted, partial, outs)
    else:
        weights, grad_skip, sums_out, shifted = rest[:4]
        outs, partial = rest[4 : 4 + PEERS], rest[4 + PEERS]
        sums_out[...] = total
        spread_grad(grad, shifted, area, small, STRIDED[:9], row_of)
        shifted[row_of(9, cs), :] = grad_skip[...]
        for phase in range(4):
            partial[phase] = lax.dot_general(
                shifted[phase_rows(phase, cs), :],
                weights[phase_rows(phase, cs), :],
                (((0,), (0,)), ((), ())),
                preferred_element_type=F32,
            )
        for k, out in enumerate(outs):
            for phase in range(4):
                out[phase * area : (phase + 1) * area, :] = partial[
                    phase, rows_at(me ^ k, area), :
                ].astype(BF16)


def part_halves(core, units, own, other):
    own[...] = units[core]
    other[...] = units[1 - core].astype(BF16)


def weight_grad(rows, idx, shifted, act, own, other, full, units):
    full[...] = lax.dot_general(
        shifted[...], act[...], (((1,), (1,)), ((), ())), preferred_element_type=F32
    )
    ny, cs, span = own.shape
    tiles = full.shape[1] // 128
    for v in range(2 * ny):
        begin = rows * v % 128
        parts = []
        for q in range((begin + rows + 127) // 128):
            k, p = divmod(rows * v // 128 + q, tiles)
            parts.append(full[k * cs : (k + 1) * cs, p * 128 : (p + 1) * 128])
        window = jnp.concatenate(parts, axis=1)
        units[v % 2, v // 2] = moved(window, begin)[:, :span]
    part_halves(idx[2] % 2, units, own, other)


def weight_grad_first(rows, extra, idx, shifted, act, own, other, flat, units):
    ny, cs, span = own.shape
    c_in = act.shape[2]
    flat[...] = jnp.zeros_like(flat)
    skip = None
    for phase in range(4):
        group = jnp.dot(
            shifted[phase_rows(phase, cs), :], act[phase], preferred_element_type=F32
        ).astype(BF16)
        for at, k in enumerate(PHASES[phase]):
            grad = group[at * cs : (at + 1) * cs]
            if k == 9:
                skip = grad
                continue
            begin = k * c_in
            base = begin // 128 * 128
            reach = -(-(begin + c_in) // 128) * 128
            move = one_hot(c_in, reach - base, begin - base)
            flat[:, base:reach] += jnp.dot(grad, move, preferred_element_type=F32)
    lane = lax.broadcasted_iota(jnp.int32, (1, span), 1)
    for v in range(2 * ny):
        begin = rows * v % 128
        base = rows * v - begin
        window = moved(flat[:, base : base + span + 128], begin)[:, :span]
        row = lax.broadcasted_iota(jnp.int32, (c_in, span), 0)
        col = lax.broadcasted_iota(jnp.int32, (c_in, span), 1)
        place = (row >= extra * v) & (row < extra * (v + 1)) & (col == row - extra * v + rows)
        tail = pick32(skip, place.astype(BF16))
        units[v % 2, v // 2] = jnp.where(lane < rows, window, 0.0) + tail
    part_halves(idx[2] % 2, units, own, other)


def reduce_core(count, idx, *refs):
    own, other, outs, total = refs[:count], refs[count : 2 * count], refs[2 * count : -1], refs[-1]
    cb = outs[0].shape[1]
    at = 0
    for a, b in zip(own, other):
        span = a.shape[2]
        total[:, :, at : at + span] = a[...] + b[...].astype(F32)
        at += span
    for k, out in enumerate(outs):
        for j in range(total.shape[0]):
            out[j] = total[j, rows_at(idx[2] // 2 ^ k, cb), :].astype(out.dtype)


def reduce_side(sizes, idx, *refs):
    refs, out = refs[:-1], refs[-1]
    at = 0
    for size in sizes:
        total = refs[0][...].astype(F32)
        for ref in refs[1:size]:
            total += ref[...].astype(F32)
        out[:, :, at : at + total.shape[2]] = total.astype(BF16)
        refs = refs[size:]
        at += total.shape[2]


def fold(nz, fy, idx, got, out):
    cs = got.shape[1]
    for f in range(fy):
        total = got[f].astype(F32)
        for z in range(1, nz):
            total += got[z * fy + f].astype(F32)
        out[f * cs : (f + 1) * cs, :] = total.astype(BF16)


def own_rows(count, spans, idx, *refs):
    pieces, outs, stack = refs[:count], refs[count:-1], refs[-1]
    for k, ref in enumerate(pieces):
        at = idx[2] ^ k
        stack[at % 2, at // 2] = ref[...]
    sides, height = stack.shape[1], stack.shape[2]
    fy_cb = [(f, x) for f in range(PEERS) for x in range(sides)]
    cb = height // PEERS
    for half in range(2):
        whole = jnp.concatenate(
            [stack[half, x, f * cb : (f + 1) * cb, :].astype(F32) for f, x in fy_cb], axis=0
        ).T
        at = 0
        for span, group in spans:
            begin = at
            for n in group:
                out = outs[n]
                rows = out.shape[0] // 2
                out[half * rows : (half + 1) * rows, :] = whole[begin : begin + rows]
                begin += rows
            at += span


def entry_back(small, idx, *refs):
    pieces = refs[:PEERS]
    image, norm, gain, shift, grad_pre, sums = refs[PEERS:]
    c_in = gain.shape[1]
    side = 2 * small
    grad = pieces[0][...].astype(F32)
    for ref in pieces[1:]:
        grad += ref[...].astype(F32)
    order = pixel_order(small, side * side, lambda y, x: y * side + x)
    high = grad.astype(BF16)
    low = (grad - high.astype(F32)).astype(BF16)
    grad = sum(
        lax.dot_general(order, part, (((0,), (0,)), ((), ())), preferred_element_type=F32)
        for part in (high, low)
    )
    normed = (image[...].astype(F32) - norm[0:1, :c_in]) * norm[1:2, :c_in]
    g = gelu_slope(gain[...] * normed + shift[...]) * grad
    grad_pre[...] = g
    sums[...] = jnp.zeros_like(sums)
    sums[0:1, :c_in] = jnp.sum(g * normed, axis=0, keepdims=True)
    sums[1:2, :c_in] = jnp.sum(g, axis=0, keepdims=True)


def bundle(idx, first, second, third, sums, out):
    out[...] = jnp.zeros_like(out)
    out[0:8, :] = sums[...]
    for k, ref in enumerate((first, second, third)):
        out[8 + 2 * k : 10 + 2 * k, : ref.shape[1]] = ref[0:2]


def unbundle(idx, *refs):
    out, six, order = refs[-3:]
    got = in_order(refs[:-3], idx[0], order)
    total = got[0][0:8]
    for g in got[1:]:
        total = total + g[0:8]
    out[...] = total
    cs = six.shape[1] // PEERS
    six[...] = jnp.concatenate([g[8:16, :cs] for g in got], axis=1)


def entry_grad(nz, idx, *refs):
    sums = refs[:nz]
    grad_pre, image, weight, norm, gain, gain_grad, shift_grad, out, order = refs[nz:]
    got = in_order(sums, idx[1], order)
    total = got[0]
    for g in got[1:]:
        total = total + g
    gain_grad[...] = total[0:1]
    shift_grad[...] = total[1:2]
    c_in = gain.shape[1]
    scale = norm[1:2, :c_in]
    normed = (image[...].astype(F32) - norm[0:1, :c_in]) * scale
    out[...] = gain[...] * scale * (
        grad_pre[...]
        - weight[:, 0:1]
        * (shift_grad[0:1, :c_in] + normed * gain_grad[0:1, :c_in])
        / norm[2:3, :c_in]
    )


def program(
    nx,
    ny,
    images,
    valid_count,
    pixel_mask,
    gain_entry,
    shift_entry,
    conv_first,
    gain_middle,
    shift_middle,
    conv_second,
    projection,
    gain_inner,
    shift_inner,
    conv_third,
    gain_last,
    shift_last,
    conv_fourth,
    cotangent,
):
    fy = PEERS
    nz = ny // fy
    sides = nx // 2
    side, c_in = images.shape[1], images.shape[3]
    small = side // 2
    area = small * small
    c_out = conv_first.shape[1]
    cs = c_out // PEERS
    cb = cs // sides
    width = PEERS * area
    lanes = c_in + 64
    padded = span_of(c_in)
    gx, gy = lax.axis_index("gx"), lax.axis_index("gy")
    me = gy % fy
    mine = gy // fy
    run = Order(jnp.stack([me, mine, gx, gy]).astype(jnp.int32))
    part = functools.partial

    def to_slice(piece, k):
        return lax.ppermute(piece, "gy", [(j, j // fy * fy + (j % fy ^ k)) for j in range(ny)])

    def share(pieces):
        return [pieces[0]] + [to_slice(pieces[k], k) for k in range(1, PEERS)]

    def to_gx(piece, k):
        return lax.ppermute(piece, "gx", [(i, i ^ k) for i in range(nx)])

    def pool_gx(piece):
        return [piece] + [to_gx(piece, k) for k in range(1, nx)]

    def pool_z(piece):
        out = [piece]
        for k in range(1, nz):
            perm = [(j, (j // fy ^ k) * fy + j % fy) for j in range(ny)]
            out.append(lax.ppermute(piece, "gy", perm))
        return out

    def over_x(block):
        return {0: block, **{k: to_gx(block, k) for k in range(2, nx, 2)}}

    def over_core(held, *then):
        held = {k: after(v, *then) for k, v in held.items()} if then else dict(held)
        for k in list(held):
            held[k + 1] = to_gx(held[k], 1)
        return [held[k] for k in sorted(held)]

    def turn(block):
        return lax.all_to_all(block, "gy", 0, 0, tiled=True)

    unit_first, unit_skip = conv_first.shape[0] // 2, projection.shape[0] // 2
    unit_mid = conv_second.shape[0] // 2
    span_first, span_mid = span_of(unit_first + unit_skip), span_of(unit_mid)
    tile, tile16 = shape((cs, width)), shape((cs, width), BF16)
    long16 = shape((cs, width + 128), BF16)
    cols, stat, entry_stat = shape((cs, 128)), shape((8, cs)), shape((8, lanes))
    shifted16 = shape((9 * cs, width), BF16)
    full16 = shape((c_out, width), BF16)
    whole16 = shape((9 * cs, c_out), BF16)

    def halves(span, channels):
        return pltpu.VMEM((2, cs // channels, ny, channels, span), BF16)

    def ready(span, channels, *weights):
        out = shape((ny, channels, span), BF16)
        return run(part(entry_weights, cs, fy, (len(weights),)), out, weights, cost=24)

    def merge(pieces, kernel):
        like = pieces[0].shape
        return run(kernel, shape(like), pieces, [pltpu.VMEM((nx, *like), F32)])

    add_gx = part(add_rows, 2)

    def activate(value, params, pooled, cot=None):
        more = [] if cot is None else [cot]
        outs = [tile16] if cot is None else [long16] * PEERS
        return run(
            part(act_block, nz),
            [tile, cols] + outs,
            [value, params, *pooled, *more],
            [pltpu.VMEM((nz, 8, cs), F32)]
            + ([] if cot is None else [pltpu.VMEM((c_out, 128), F32)]),
            far=(0, 1),
        )

    def convolve(pieces, weights, base, last=False):
        more = [] if base is None else [base]
        outs = [shape((cs, 128), BF16)] * PEERS + [full16]
        return run(
            part(conv_block, nx, base is not None, last, unit_mid, 0, area, small),
            outs if last else [tile, stat, full16, whole16],
            [*pieces, narrow, *weights, *more],
            [pltpu.VMEM((9 * cs, width), F32)] + ([] if last else [halves(span_mid, cb)]),
            cost=25,
            far=() if last else (2, 3),
        )

    def slope(parts, normed, params):
        return run(gelu_back, [tile, stat], [*parts, normed, params])

    def back(grad_pre, normed, scales, params, pooled, weights, base, riders=()):
        more = list(riders) if base is None else [base]
        return run(
            part(norm_back, nz, base is not None, False, area, small),
            [stat, shifted16]
            + ([long16] * PEERS if base is None else [tile16] * (PEERS + 1)),
            [grad_pre, normed, scales, params, narrow, *pooled, *more, weights],
            [pltpu.VMEM((c_out, width), F32), pltpu.VMEM((nz, 8, cs), F32)],
            cost=18,
        )

    def grad_of(kernel, span, shifted, act, scratch):
        own, other = run(
            kernel,
            [shape((ny, cs, span)), shape((ny, cs, span), BF16)],
            [shifted, act],
            [scratch, pltpu.VMEM((2, ny, cs, span), F32)],
            cost=28,
        )
        return own, to_gx(other, 1)

    def grad_mid(shifted, act):
        return grad_of(
            part(weight_grad, unit_mid), span_mid, shifted, act, pltpu.VMEM((9 * cs, c_out), F32)
        )

    def over_pair(own, other):
        span = own.shape[2]
        return run(
            part(reduce_core, 1),
            [shape((ny, cb, span))] + [shape((ny, cb, span), BF16)] * (sides - 1),
            [own, other],
            [pltpu.VMEM((ny, cs, span), F32)],
        )

    def to_sides(parts, *then):
        parts = [after(p, *then) for p in parts] if then else parts
        return [parts[0]] + [to_gx(parts[k], 2 * k) for k in range(1, sides)]

    def over_sides(*groups):
        span = sum(parts[0].shape[2] for parts in groups)
        return run(
            part(reduce_side, tuple(len(parts) for parts in groups)),
            shape((ny, cb, span), BF16),
            [p for parts in groups for p in parts],
        )

    def folded(got):
        out = shape((fy * cb, got.shape[2]), BF16)
        return over_core(over_x(run(part(fold, nz, fy), out, [got])))

    def rows_of(pieces, spans, *rows):
        return run(
            part(own_rows, nx, spans),
            [shape((r, c_out)) for r in rows],
            pieces,
            [pltpu.VMEM((2, sides, fy * cb, pieces[0].shape[1]), BF16)],
            cost=30,
        )

    def own(gain, shift):
        pair = jnp.stack([gain, shift], axis=1)
        return lax.dynamic_slice_in_dim(pair, me * cs, cs, axis=0)

    p_middle = own(gain_middle, shift_middle)
    p_inner = own(gain_inner, shift_inner)
    p_last = own(gain_last, shift_last)
    g_entry, s_entry = gain_entry[None], shift_entry[None]
    pixels = images.reshape(side * side, c_in)

    image, wide = run(
        part(entry_image, small),
        [shape((4 * area, lanes), BF16), shape((4 * area, 128))],
        [pixels, pixel_mask.reshape(side, side), valid_count],
        scalars=1,
    )
    group = share([image] * PEERS)
    out_first = ready(span_first, cb, conv_first, projection)
    stats = run(part(entry_stats, area), entry_stat, group)
    pieces = pool_gx(stats)
    got_first = turn(after(out_first, *group[1:]))
    merged = merge([after(pieces[0], got_first)] + pieces[1:], merge_stats)
    got_first = over_core(over_x(got_first))
    pooled = pool_z(merged)
    out_second = ready(span_mid, cb, conv_second)
    got_second = turn(after(out_second, pooled[-1]))
    first, skipped, stats, norm_one, narrow, act_one, w_first = run(
        part(entry_block, nz, nx, unit_first, unit_skip, area, small),
        [
            tile,
            tile,
            stat,
            entry_stat,
            shape((8, width)),
            shape((4, width, c_in), BF16),
            shape((10 * cs, c_in), BF16),
        ],
        [*group, *pooled, g_entry, s_entry, *got_first],
        [
            pltpu.VMEM((nz, 8, lanes), F32),
            pltpu.VMEM((width, lanes), BF16),
            pltpu.VMEM((cs, span_of(9 * c_in)), BF16),
            halves(span_first, cb),
        ],
        cost=40,
        far=(3, 5, 6),
    )

    pieces = pool_gx(stats)
    out_third = ready(span_mid, cb, conv_third)
    merged = merge(pieces, merge_stats)
    got_second = over_x(after(got_second, merged))
    pooled = pool_z(merged)
    out_fourth = ready(span_mid, cb, conv_fourth)
    got_third = turn(after(out_third, pooled[-1]))
    normed_two, scale_two, *messages = activate(
        first, p_middle, pooled, cotangent.reshape(area, c_out)
    )
    pieces = share(messages)
    got_second = over_core(got_second, *pieces[1:])
    hidden, stats, act_two, w_second = convolve(pieces, got_second, skipped)
    cot_parts = pieces
    got_fourth = turn(after(out_fourth, stats))
    merged = merge(pool_gx(stats), merge_stats)
    got_third = over_x(after(got_third, merged))
    pooled = pool_z(merged)
    normed_three, scale_three, act = activate(hidden, p_inner, pooled)
    got_fourth = over_x(after(got_fourth, pooled[-1]))
    pieces = share([act] * PEERS)
    got_third = over_core(got_third, *pieces[1:])
    third, stats, act_three, w_third = convolve(pieces, got_third, None)
    merged = merge(pool_gx(stats), merge_stats)
    got_fourth = over_core(got_fourth, merged)

    cot, shifted_four, w_fourth, *parts = run(
        part(last_back, nx, unit_mid, area, small),
        [tile, shifted16, whole16] + [tile16] * PEERS,
        [*cot_parts, *got_fourth],
        [pltpu.VMEM((c_out, width), F32), halves(span_mid, cb)],
        cost=18,
    )
    parts = share(parts)
    normed_four, scale_four, act = activate(third, p_last, pool_z(merged))
    pieces = share([act] * PEERS)
    grad_pre, sums = slope(parts, normed_four, p_last)
    sums = pool_gx(sums)
    *riders, act_four = convolve(pieces, [w_fourth], hidden, last=True)
    sums = pool_z(merge(sums, add_gx))
    fourth = grad_mid(shifted_four, act_four)
    last_sums, shifted_three, *parts = back(
        grad_pre, normed_four, scale_four, p_last, sums, w_third, None, riders
    )
    parts = share(parts)
    fourth = over_pair(*fourth)
    grad_pre, sums = slope(parts, normed_three, p_inner)
    sums = pool_gx(sums)
    third = grad_mid(shifted_three, act_three)
    merged = merge(sums, add_gx)
    fourth = to_sides(fourth, merged)
    sums = pool_z(merged)
    out = run(
        join_result, shape((area, c_out), BF16), parts, [pltpu.VMEM((c_out, 128), F32)]
    )
    inner_sums, shifted_two, grad_hidden, *parts = back(
        grad_pre, normed_three, scale_three, p_inner, sums, w_second, cot
    )
    parts = share(parts)
    third = over_pair(*third)
    grad_pre, sums = slope(parts, normed_two, p_middle)
    sums = pool_gx(sums)
    second = grad_mid(shifted_two, act_two)
    merged = merge(sums, add_gx)
    third = to_sides(third, merged)
    sums = pool_z(merged)
    fourth = over_sides(fourth)
    middle_sums, shifted_one, *parts = run(
        part(norm_back, nz, False, True, area, small),
        [stat, shape((10 * cs, width), BF16)] + [shape((4 * area, c_in), BF16)] * PEERS,
        [
            grad_pre,
            normed_two,
            scale_two,
            p_middle,
            narrow,
            *sums,
            w_first,
            grad_hidden,
        ],
        [pltpu.VMEM((4, width, c_in), F32), pltpu.VMEM((nz, 8, cs), F32)],
        cost=18,
    )

    first = grad_of(
        part(weight_grad_first, unit_first, unit_skip),
        span_first,
        shifted_one,
        act_one,
        pltpu.VMEM((cs, span_of(9 * c_in + span_first + 128)), F32),
    )
    parts = share(parts)
    late = turn(over_sides([after(fourth, *parts[1:])], third))
    second = to_sides(over_pair(*second))
    first = to_sides(over_pair(*first))
    grad_pre, sums = run(
        part(entry_back, small),
        [shape((4 * area, c_in)), shape((8, padded))],
        [*parts, pixels, norm_one, g_entry, s_entry],
        cost=13,
    )
    message = run(bundle, shape((16, padded)), [middle_sums, inner_sums, last_sums, sums])
    message = share([message] * PEERS)
    second = over_sides(second)
    sums, six = run(
        unbundle,
        [shape((8, padded)), shape((8, c_out))],
        message,
        [pltpu.VMEM((PEERS, 16, padded), F32)],
    )
    sums = pool_z(merge(pool_gx(sums), add_gx))
    early = turn(after(over_sides([second], first), sums[-1]))
    gain_entry_grad, shift_entry_grad, image_grad = run(
        part(entry_grad, nz),
        [shape((1, padded)), shape((1, padded)), shape((4 * area, c_in))],
        [*sums, grad_pre, pixels, wide, norm_one, g_entry],
        [pltpu.VMEM((nz, 8, padded), F32)],
    )
    late = folded(late)
    early = folded(early)
    fourth_grad, third_grad = rows_of(
        late, ((span_mid, (0,)), (span_mid, (1,))), 2 * unit_mid, 2 * unit_mid
    )
    second_grad, first_grad, skip_grad = rows_of(
        early,
        ((span_mid, (0,)), (span_first, (1, 2))),
        2 * unit_mid,
        2 * unit_first,
        2 * unit_skip,
    )
    return (
        out.reshape(1, small, small, c_out),
        image_grad.reshape(1, side, side, c_in),
        gain_entry_grad[0, :c_in],
        shift_entry_grad[0, :c_in],
        first_grad,
        six[0],
        six[1],
        second_grad,
        skip_grad,
        six[2],
        six[3],
        third_grad,
        six[4],
        six[5],
        fourth_grad,
    )


def solution(mesh):
    whole = P(("gx", "gy"), None, None, None)
    rows = P("gy", None)
    return jax.shard_map(
        functools.partial(program, mesh.shape["gx"], mesh.shape["gy"]),
        mesh=mesh,
        in_specs=(
            whole,
            P(("gx", "gy")),
            P(("gx", "gy"), None, None),
            P(),
            P(),
            rows,
            P(),
            P(),
            rows,
            rows,
            P(),
            P(),
            rows,
            P(),
            P(),
            rows,
            whole,
        ),
        out_specs=(
            whole, whole, P(), P(), rows, P(), P(), rows, rows, P(), P(), rows, P(), P(), rows,
        ),
        check_vma=False,
    )
```

```python
import functools

import jax
import jax.numpy as jnp
from jax import lax
from jax.experimental import pallas as pl
from jax.experimental.pallas import tpu as pltpu
from jax.sharding import PartitionSpec as P

EPS = 1e-05
COST = 6 * 10**7
F32 = jnp.float32
BF16 = jnp.bfloat16
PEERS = 4
C0 = 0.7978845608028654
C1 = 0.044715
VMEM = pl.BlockSpec(memory_space=pltpu.VMEM)
SMEM = pl.BlockSpec(memory_space=pltpu.SMEM)


def gelu(v):
    return 0.5 * v * (1.0 + jnp.tanh(C0 * (v + C1 * (v * v * v))))


def gelu_slope(v):
    t = jnp.tanh(C0 * (v + C1 * (v * v * v)))
    return 0.5 * (1.0 + t) + 0.5 * v * (1.0 - t * t) * (C0 * (1.0 + 3.0 * C1 * (v * v)))


def after(value, *others):
    return lax.optimization_barrier((value, *others))[0]


class Far:
    def __init__(self, near, far, sem):
        self.near, self.shape, self.dtype = near, near.shape, near.dtype
        self.copy = pltpu.make_async_copy(near, far, sem)
        self.sent = False

    def __getitem__(self, at):
        return self.near[at]

    def __setitem__(self, at, value):
        self.near[at] = value

    def send(self):
        if not self.sent:
            self.copy.start()
            self.sent = True


def send(ref):
    if isinstance(ref, Far):
        ref.send()


def with_far(kernel, n_in, n_out, far, *refs):
    ins, outs, rest = refs[:n_in], list(refs[n_in : n_in + n_out]), list(refs[n_in + n_out :])
    if far:
        sems = rest.pop()
        near = rest[len(rest) - len(far) :]
        del rest[len(rest) - len(far) :]
        for n, at in enumerate(far):
            outs[at] = Far(near[n], outs[at], sems.at[n])
    kernel(*ins, *outs, *rest)
    for at in far:
        outs[at].send()
    for at in far:
        outs[at].copy.wait()


class Order:
    def __init__(self, idx):
        self.idx = idx
        self.last = ()

    def __call__(self, kernel, outs, args, scratch=(), scalars=0, cost=7, far=()):
        idx = after(self.idx, *self.last)
        many = isinstance(outs, (list, tuple))
        shapes = list(outs) if many else [outs]
        more = [pltpu.VMEM(shapes[at].shape, shapes[at].dtype) for at in far]
        if far:
            more.append(pltpu.SemaphoreType.DMA((len(far),)))
        got = pl.pallas_call(
            functools.partial(with_far, kernel, 1 + len(args), len(shapes), tuple(far)),
            out_shape=shapes,
            in_specs=[SMEM] + [VMEM] * (len(args) - scalars) + [SMEM] * scalars,
            out_specs=[
                pl.BlockSpec(memory_space=pl.ANY) if at in far else VMEM
                for at in range(len(shapes))
            ],
            scratch_shapes=list(scratch) + more,
            compiler_params=pltpu.CompilerParams(vmem_limit_bytes=16 * 1024 * 1024),
            cost_estimate=pl.CostEstimate(
                flops=cost * COST, bytes_accessed=1024, transcendentals=0
            ),
        )(idx, *args)
        near = [v for at, v in enumerate(got) if at not in far]
        self.last = (near[0] if near else got[0],)
        return got if many else got[0]


def shape(dims, dtype=F32):
    return jax.ShapeDtypeStruct(dims, dtype)


def rows_at(index, count):
    return pl.ds(pl.multiple_of(index * count, count), count)


def as_rows(parts):
    height = parts[0].shape[0]
    lane = lax.broadcasted_iota(jnp.int32, (height, 128), 1)
    out = jnp.zeros((height, 128), F32)
    for k, part in enumerate(parts):
        out = jnp.where(lane == k, part, out)
    return out.T[0:8]


def as_columns(rows):
    return jnp.concatenate([rows, jnp.zeros((120, rows.shape[1]), F32)], axis=0).T


def in_order(refs, me, scratch):
    for k, ref in enumerate(refs):
        scratch[me ^ k] = ref[...]
    return [scratch[k] for k in range(len(refs))]


def merge_moments(stats):
    total = sum(n for _, _, n in stats)
    mean = sum(n * m for m, _, n in stats) / total
    squares = sum(q + n * (m - mean) * (m - mean) for m, q, n in stats)
    return mean, squares, total


def merge_rows(refs):
    mean, squares, total = merge_moments([(g[0:1], g[1:2], g[2:3]) for g in refs])
    return mean, squares, total, sum(g[3:4] for g in refs)


def pixel(width, area, small):
    lane = lax.broadcasted_iota(jnp.int32, (1, width), 1) % area
    return lane // small, lane % small


def inside(row, col, drow, dcol, small):
    return (row + drow >= 0) & (row + drow < small) & (col + dcol >= 0) & (col + dcol < small)


def moved(value, step):
    shift = (-step) % value.shape[1]
    return pltpu.roll(value, shift, 1) if shift else value


OFFSETS = [(0, krow - 1, kcol - 1) for krow in range(3) for kcol in range(3)]

STRIDED = [
    ((krow != 1) * 2 + (kcol != 1), -(krow == 0), -(kcol == 0))
    for krow in range(3)
    for kcol in range(3)
] + [(0, 0, 0)]
PLACED = sorted(range(10), key=lambda k: (STRIDED[k][0], k))
PHASES = [[k for k in PLACED if STRIDED[k][0] == phase] for phase in range(4)]


def row_of(k, cs):
    at = PLACED.index(k)
    return slice(at * cs, (at + 1) * cs)


def phase_rows(phase, cs):
    first, last = PHASES[phase][0], PHASES[phase][-1]
    return slice(PLACED.index(first) * cs, (PLACED.index(last) + 1) * cs)


def masked_stats(value, weight, n):
    mean = jnp.sum(value * weight, axis=1, keepdims=True) / n
    centred = value - mean
    return mean, jnp.sum(weight * centred * centred, axis=1, keepdims=True)


def span_of(rows):
    return -(-rows // 128) * 128


def one_hot(height, width, shift):
    row = lax.broadcasted_iota(jnp.int32, (height, width), 0)
    col = lax.broadcasted_iota(jnp.int32, (height, width), 1)
    return (col == row + shift).astype(BF16)


def pick32(left, right, dims=((1,), (0,))):
    return lax.dot_general(left, right, (dims, ((), ())), preferred_element_type=F32)


def pick(left, right, dims=((1,), (0,))):
    return pick32(left, right, dims).astype(BF16)


def lane_tile(held, tile, rows, span):
    sides, ny = held.shape[1], held.shape[2]
    lane = lax.broadcasted_iota(jnp.int32, (1, 128), 1)
    out = None
    for v in range(2 * ny):
        begin = rows * v - tile * 128
        if begin >= 128 or begin + rows <= 0:
            continue
        at = (tile - rows * v // 128) * 128 % span
        part = jnp.concatenate(
            [held[v % 2, x, v // 2, :, at : at + 128].astype(F32) for x in range(sides)], axis=0
        )
        if begin > 0 or begin + rows < 128:
            own = (lane >= begin) & (lane < begin + rows)
            part = jnp.where(own, part, 0.0)
        out = part if out is None else out + part
    return out.astype(BF16)


def pixel_order(small, width, of):
    area = small * small
    row = lax.broadcasted_iota(jnp.int32, (4 * area, width), 0)
    col = lax.broadcasted_iota(jnp.int32, (4 * area, width), 1)
    phase, pix = row // area, row % area
    y = 2 * (pix // small) + phase // 2
    x = 2 * (pix % small) + phase % 2
    return (col == of(y, x)).astype(BF16)


def entry_image(small, idx, image, mask, valid, out, weight):
    side = 2 * small
    c_in = image.shape[1]
    count = side * side
    order = pixel_order(small, count, lambda y, x: y * side + x)
    out[:, :c_in] = pick(order, image[...])
    live = (valid[0] > 0).astype(F32)
    row = lax.broadcasted_iota(jnp.int32, (count, side), 0)
    col = lax.broadcasted_iota(jnp.int32, (count, side), 1)
    by_row = jnp.dot(
        (row // side == col).astype(BF16),
        mask[...].astype(F32).astype(BF16),
        preferred_element_type=F32,
    )
    column = jnp.sum(jnp.where(row % side == col, by_row, 0.0), axis=1, keepdims=True) * live
    lane = lax.broadcasted_iota(jnp.int32, (count, 128), 1)
    spread = jnp.where(lane == 0, column, 0.0)
    weight[...] = spread
    out[:, c_in:] = pick(order, spread.astype(BF16))[:, : out.shape[1] - c_in]


def entry_weights(cs, fy, sections, idx, *refs):
    weights, out = list(refs[:-1]), refs[-1]
    ny, cb, lanes = out.shape
    span = lanes // len(sections)
    gx, gy = idx[2], idx[3]
    core, side = gx % 2, (gx // 2 if cb < cs else 0)
    c_out = weights[0].shape[1]
    row = lax.broadcasted_iota(jnp.int32, (fy * cb, c_out), 0)
    col = lax.broadcasted_iota(jnp.int32, (fy * cb, c_out), 1)
    chosen = (col == row // cb * cs + side * cb + row % cb).astype(BF16)
    for n, count in enumerate(sections):
        begin = weights[0].shape[0] // 2 * (2 * gy + core) % 128
        total = None
        for _ in range(count):
            weight = weights.pop(0)
            rows = weight.shape[0]
            half = rows // 2
            mine = pick(chosen, weight[...], ((1,), (1,)))
            row = lax.broadcasted_iota(jnp.int32, (rows, span), 0) - core * half
            col = lax.broadcasted_iota(jnp.int32, (rows, span), 1)
            place = (row >= 0) & (row < half) & (
                (col == row + begin) | (col == row + begin - span)
            )
            part = pick32(mine, place.astype(BF16))
            total = part if total is None else total + part
            begin = begin + half
        for j in range(ny):
            out[j, :, n * span : (n + 1) * span] = total[
                (j % fy) * cb : (j % fy + 1) * cb
            ].astype(BF16)


def hold(gx, messages, held, section=0):
    span = held.shape[4]
    for k, ref in enumerate(messages):
        at = gx ^ k
        side = at // 2 if held.shape[1] > 1 else 0
        held[at % 2, side] = ref[:, :, section * span : (section + 1) * span]


def assemble(held, out, rows):
    cs, span = held.shape[1] * held.shape[3], held.shape[4]
    tiles = out.shape[1] // 128
    for k in range(9):
        for q in range(tiles):
            out[k * cs : (k + 1) * cs, q * 128 : (q + 1) * 128] = lane_tile(
                held, tiles * k + q, rows, span
            )


def assemble_first(held, out, flat, rows, extra):
    cs, span = held.shape[1] * held.shape[3], held.shape[4]
    c_in = out.shape[1]
    tiles = flat.shape[1] // 128
    for tile in range(tiles):
        flat[:, tile * 128 : (tile + 1) * 128] = lane_tile(held, tile, rows, span)
    for k in range(9):
        begin = k * c_in
        base = begin // 128 * 128
        reach = min(-(-(begin + c_in) // 128) * 128, flat.shape[1])
        move = one_hot(c_in, reach - base, begin - base)
        out[row_of(k, cs), :] = pick(flat[:, base:reach], move, ((1,), (1,)))
    total = None
    for v in range(2 * held.shape[2]):
        row = lax.broadcasted_iota(jnp.int32, (span, c_in), 0)
        col = lax.broadcasted_iota(jnp.int32, (span, c_in), 1)
        at = col - extra * v
        begin = rows * v % 128 + rows
        place = (at >= 0) & (at < extra) & ((row == at + begin) | (row == at + begin - span))
        part = jnp.concatenate(
            [
                pick32(held[v % 2, x, v // 2], place.astype(BF16))
                for x in range(held.shape[1])
            ],
            axis=0,
        )
        total = part if total is None else total + part
    out[row_of(9, cs), :] = total.astype(BF16)


def entry_stats(area, idx, *refs):
    images, out = refs[:PEERS], refs[PEERS]
    lanes = out.shape[1]
    first = jnp.zeros((1, lanes), F32)
    wide = jnp.zeros((1, 1), F32)
    narrow = jnp.zeros((1, 1), F32)
    c_in = lanes - 64
    for ref in images:
        x = ref[...].astype(F32)
        w = x[:, c_in : c_in + 1]
        first += jnp.sum(x * w, axis=0, keepdims=True)
        wide += jnp.sum(w, axis=0, keepdims=True)
        narrow += jnp.sum(w[:area], axis=0, keepdims=True)
    mean = first / wide
    squares = jnp.zeros((1, lanes), F32)
    for ref in images:
        x = ref[...].astype(F32)
        w = x[:, c_in : c_in + 1]
        d = x - mean
        squares += jnp.sum(d * d * w, axis=0, keepdims=True)
    out[...] = jnp.zeros_like(out)
    out[0:1, :] = mean
    out[1:2, :] = squares
    out[2:3, :] = jnp.broadcast_to(wide, (1, lanes))
    out[3:4, :] = jnp.broadcast_to(narrow, (1, lanes))


def entry_block(nz, nx, rows, extra, area, small, idx, *refs):
    images = refs[:PEERS]
    stats, rest = refs[PEERS : PEERS + nz], refs[PEERS + nz :]
    gain, shift, messages, rest = rest[0], rest[1], rest[2 : 2 + nx], rest[2 + nx :]
    first, skipped, out_stats, norm, narrow, act, w_first = rest[:7]
    order, masks, flat, held = rest[7:]
    me, mine = idx[0], idx[1]
    c_in = gain.shape[1]
    lanes = norm.shape[1]
    cs = first.shape[0]
    width = first.shape[1]
    hold(idx[2], messages, held)
    assemble_first(held, w_first, flat, rows, extra)
    send(w_first)
    mean, squares, total, count = merge_rows(in_order(stats, mine, order))
    scale = lax.rsqrt(squares / total + EPS)
    norm[...] = jnp.zeros_like(norm)
    norm[0:1, :] = mean
    norm[1:2, :] = scale
    norm[2:3, :] = total
    norm[3:4, :] = count
    for k, ref in enumerate(images):
        x = ref[...]
        v = x[:, :c_in].astype(F32)
        pre = gain[...] * ((v - mean[:, :c_in]) * scale[:, :c_in]) + shift[...]
        a = gelu(pre).astype(BF16)
        for phase in range(4):
            act[phase, rows_at(me ^ k, area), :] = a[phase * area : (phase + 1) * area]
        masks[rows_at(me ^ k, area), :] = x[:area]
    send(act)
    send(norm)
    ones = (lax.broadcasted_iota(jnp.int32, (8, lanes), 1) == c_in).astype(BF16)
    weight8 = lax.dot_general(
        ones, masks[...], (((1,), (1,)), ((), ())), preferred_element_type=F32
    )
    narrow[...] = weight8
    weight = weight8[0:1]
    row, col = pixel(width, area, small)
    total_first = jnp.zeros((cs, width), F32)
    for phase in range(4):
        group = lax.dot_general(
            w_first[phase_rows(phase, cs), :],
            act[phase],
            (((1,), (1,)), ((), ())),
            preferred_element_type=F32,
        )
        for at, k in enumerate(PHASES[phase]):
            y = group[at * cs : (at + 1) * cs]
            if k == 9:
                skipped[...] = y
                continue
            _, drow, dcol = STRIDED[k]
            y = moved(y, drow * small + dcol)
            total_first += jnp.where(inside(row, col, drow, dcol, small), y, 0.0)
    first[...] = total_first
    n = jnp.sum(weight, axis=1, keepdims=True)
    mean2, squares = masked_stats(total_first, weight, n)
    out_stats[...] = as_rows((mean2, squares, n))


def merge_stats(idx, *refs):
    out, order = refs[-2:]
    mean, squares, total, count = merge_rows(in_order(refs[:-2], idx[2], order))
    out[...] = jnp.zeros_like(out)
    out[0:1] = mean
    out[1:2] = squares
    out[2:3] = total
    out[3:4] = count


def add_rows(which, idx, *refs):
    out, order = refs[-2:]
    got = in_order(refs[:-2], idx[which], order)
    total = got[0]
    for g in got[1:]:
        total = total + g
    out[...] = total


def act_block(nz, idx, *refs):
    value, params = refs[:2]
    stats, rest = refs[2 : 2 + nz], refs[2 + nz :]
    if rest[-1].shape[1] == 128:
        cot, normed, scales, outs, order, stack = (*rest[:3], rest[3:-2], *rest[-2:])
    else:
        cot, normed, scales, outs, order = (None, *rest[:2], rest[2:-1], rest[-1])
    mean, squares, total, _ = merge_rows(in_order(stats, idx[1], order))
    rows = jnp.concatenate(
        [mean, lax.rsqrt(squares / total + EPS), total, jnp.zeros((5, mean.shape[1]), F32)], axis=0
    )
    cols = as_columns(rows)
    norm = (value[...] - cols[:, 0:1]) * cols[:, 1:2]
    normed[...] = norm
    send(normed)
    scales[...] = cols
    send(scales)
    act = gelu(params[:, 0:1] * norm + params[:, 1:2]).astype(BF16)
    cs, width = norm.shape
    if cot is not None:
        c = cot[...].astype(F32)
        stack[...] = jnp.concatenate([c, c], axis=0).T
    for k, out in enumerate(outs):
        out[:, :width] = act
        if cot is not None:
            out[:, width:] = stack[rows_at(idx[0] ^ k, cs), :].astype(BF16)


def conv_block(nx, added, last, rows, section, area, small, idx, *refs):
    pieces = refs[:PEERS]
    narrow, rest = refs[PEERS], refs[PEERS + 1 :]
    if last:
        weights, rest = rest[0], rest[1:]
    else:
        messages, rest = rest[:nx], rest[nx:]
    base, rest = (rest[0], rest[1:]) if added else (None, rest)
    me = idx[0]
    cs, width = pieces[0].shape[0], narrow.shape[1]
    if last:
        outs, act, spread = rest[:PEERS], rest[PEERS], rest[PEERS + 1]
    else:
        value, out_stats, act, whole, spread, held = rest
        hold(idx[2], messages, held, section)
        assemble(held, whole, rows)
        send(whole)
        weights = whole
    for k, ref in enumerate(pieces):
        act[rows_at(me ^ k, cs), :] = ref[:, :width]
    send(act)
    spread[...] = jnp.dot(weights[...], act[...], preferred_element_type=F32)
    row, col = pixel(width, area, small)
    total = base[...] if added else jnp.zeros((cs, width), F32)
    for k, (_, drow, dcol) in enumerate(OFFSETS):
        y = moved(spread[k * cs : (k + 1) * cs, :], drow * small + dcol)
        total += jnp.where(inside(row, col, drow, dcol, small), y, 0.0)
    if last:
        result = total.astype(BF16)
        lane = lax.broadcasted_iota(jnp.int32, (width, 128), 0)
        slot = lax.broadcasted_iota(jnp.int32, (width, 128), 1)
        for k, out in enumerate(outs):
            out[...] = pick(result, (lane == (me ^ k) * area + slot).astype(BF16))
    else:
        value[...] = total
        weight = narrow[0:1, :]
        n = jnp.sum(weight, axis=1, keepdims=True)
        mean, squares = masked_stats(total, weight, n)
        out_stats[...] = as_rows((mean, squares, n))


def join_result(idx, *refs):
    pieces, (out, stack) = refs[:PEERS], refs[PEERS:]
    cs = pieces[0].shape[0]
    for k, ref in enumerate(pieces):
        stack[rows_at(idx[0] ^ k, cs), :] = ref[:, -128:].astype(F32)
    out[...] = stack[...].T[: out.shape[0]].astype(BF16)


def spread_grad(grad, shifted, area, small, offs, row_at):
    cs, width = grad.shape
    row, col = pixel(width, area, small)
    for k, (_, drow, dcol) in enumerate(offs):
        g = moved(grad, -(drow * small + dcol))
        g = jnp.where(inside(row, col, -drow, -dcol, small), g, 0.0)
        shifted[row_at(k, cs), :] = g.astype(BF16)


def plain_rows(k, cs):
    return slice(k * cs, (k + 1) * cs)


def push_back(me, weights, shifted, partial, outs):
    cs, width = outs[0].shape[0], shifted.shape[1]
    partial[...] = lax.dot_general(
        weights[...], shifted[...], (((0,), (0,)), ((), ())), preferred_element_type=F32
    )
    for k, out in enumerate(outs):
        out[:, :width] = partial[rows_at(me ^ k, cs), :].astype(BF16)


def last_back(nx, rows, section, area, small, idx, *refs):
    pieces, messages, rest = refs[:PEERS], refs[PEERS : PEERS + nx], refs[PEERS + nx :]
    cot, shifted, weights = rest[:3]
    outs = rest[3 : PEERS + 3]
    partial, held = rest[PEERS + 3 :]
    hold(idx[2], messages, held, section)
    assemble(held, weights, rows)
    send(weights)
    me = idx[0]
    cs, width = cot.shape
    image = lax.broadcasted_iota(jnp.int32, (1, width), 1) // area
    grad = jnp.zeros((cs, width), F32)
    for k, ref in enumerate(pieces):
        tiled = jnp.concatenate([ref[:, width:].astype(F32)] * (width // 128), axis=1)
        grad = jnp.where(image == (me ^ k), tiled, grad)
    cot[...] = grad
    send(cot)
    spread_grad(grad, shifted, area, small, OFFSETS, plain_rows)
    send(shifted)
    push_back(me, weights, shifted, partial, outs)


def gelu_back(idx, *refs):
    pieces = refs[:PEERS]
    normed, params, grad_pre, sums = refs[PEERS:]
    width = normed.shape[1]
    grad = pieces[0][:, :width].astype(F32)
    for ref in pieces[1:]:
        grad += ref[:, :width].astype(F32)
    norm = normed[...]
    g = gelu_slope(params[:, 0:1] * norm + params[:, 1:2]) * grad
    grad_pre[...] = g
    sums[...] = as_rows(
        (jnp.sum(g * norm, axis=1, keepdims=True), jnp.sum(g, axis=1, keepdims=True))
    )


def norm_back(nz, added, last, area, small, idx, *refs):
    grad_pre, normed, scales, params, narrow = refs[:5]
    sums = refs[5 : 5 + nz]
    rest = refs[5 + nz :]
    base, rest = (rest[0], rest[1:]) if added else (None, rest)
    me = idx[0]
    cs, width = grad_pre.shape
    order = rest[-1]
    got = in_order(sums, idx[1], order)
    total = got[0]
    for g in got[1:]:
        total = total + g
    cols = as_columns(total)
    gain_grad, shift_grad = cols[:, 0:1], cols[:, 1:2]
    norm = normed[...]
    back = params[:, 0:1] * scales[:, 1:2] * (
        grad_pre[...]
        - narrow[0:1, :] * (shift_grad + norm * gain_grad) / scales[:, 2:3]
    )
    if added:
        back = base[...] + back
    grad = back.astype(BF16).astype(F32)
    if not last:
        riders = ()
        if not added:
            riders, rest = rest[:PEERS], rest[PEERS:]
        weights, sums_out, shifted = rest[:3]
        outs, partial = rest[3 : 3 + PEERS], rest[3 + PEERS]
        for rider, out in zip(riders, outs):
            out[:, width:] = rider[...]
        if added:
            grad_out, outs, partial = rest[3], rest[4 : 4 + PEERS], rest[4 + PEERS]
            grad_out[...] = grad.astype(BF16)
        sums_out[...] = total
        spread_grad(grad, shifted, area, small, OFFSETS, plain_rows)
        push_back(me, weights, shifted, partial, outs)
    else:
        weights, grad_skip, sums_out, shifted = rest[:4]
        outs, partial = rest[4 : 4 + PEERS], rest[4 + PEERS]
        sums_out[...] = total
        spread_grad(grad, shifted, area, small, STRIDED[:9], row_of)
        shifted[row_of(9, cs), :] = grad_skip[...]
        for phase in range(4):
            partial[phase] = lax.dot_general(
                shifted[phase_rows(phase, cs), :],
                weights[phase_rows(phase, cs), :],
                (((0,), (0,)), ((), ())),
                preferred_element_type=F32,
            )
        for k, out in enumerate(outs):
            for phase in range(4):
                out[phase * area : (phase + 1) * area, :] = partial[
                    phase, rows_at(me ^ k, area), :
                ].astype(BF16)


def part_halves(core, units, own, other):
    own[...] = units[core]
    other[...] = units[1 - core].astype(BF16)


def weight_grad(rows, idx, shifted, act, own, other, full, units):
    full[...] = lax.dot_general(
        shifted[...], act[...], (((1,), (1,)), ((), ())), preferred_element_type=F32
    )
    ny, cs, span = own.shape
    tiles = full.shape[1] // 128
    for v in range(2 * ny):
        begin = rows * v % 128
        parts = []
        for q in range((begin + rows + 127) // 128):
            k, p = divmod(rows * v // 128 + q, tiles)
            parts.append(full[k * cs : (k + 1) * cs, p * 128 : (p + 1) * 128])
        window = jnp.concatenate(parts, axis=1)
        units[v % 2, v // 2] = moved(window, begin)[:, :span]
    part_halves(idx[2] % 2, units, own, other)


def weight_grad_first(rows, extra, idx, shifted, act, own, other, flat, units):
    ny, cs, span = own.shape
    c_in = act.shape[2]
    flat[...] = jnp.zeros_like(flat)
    skip = None
    for phase in range(4):
        group = jnp.dot(
            shifted[phase_rows(phase, cs), :], act[phase], preferred_element_type=F32
        ).astype(BF16)
        for at, k in enumerate(PHASES[phase]):
            grad = group[at * cs : (at + 1) * cs]
            if k == 9:
                skip = grad
                continue
            begin = k * c_in
            base = begin // 128 * 128
            reach = -(-(begin + c_in) // 128) * 128
            move = one_hot(c_in, reach - base, begin - base)
            flat[:, base:reach] += jnp.dot(grad, move, preferred_element_type=F32)
    lane = lax.broadcasted_iota(jnp.int32, (1, span), 1)
    for v in range(2 * ny):
        begin = rows * v % 128
        base = rows * v - begin
        window = moved(flat[:, base : base + span + 128], begin)[:, :span]
        row = lax.broadcasted_iota(jnp.int32, (c_in, span), 0)
        col = lax.broadcasted_iota(jnp.int32, (c_in, span), 1)
        place = (row >= extra * v) & (row < extra * (v + 1)) & (col == row - extra * v + rows)
        tail = pick32(skip, place.astype(BF16))
        units[v % 2, v // 2] = jnp.where(lane < rows, window, 0.0) + tail
    part_halves(idx[2] % 2, units, own, other)


def reduce_core(count, idx, *refs):
    own, other, outs, total = refs[:count], refs[count : 2 * count], refs[2 * count : -1], refs[-1]
    cb = outs[0].shape[1]
    at = 0
    for a, b in zip(own, other):
        span = a.shape[2]
        total[:, :, at : at + span] = a[...] + b[...].astype(F32)
        at += span
    for k, out in enumerate(outs):
        for j in range(total.shape[0]):
            out[j] = total[j, rows_at(idx[2] // 2 ^ k, cb), :].astype(out.dtype)


def reduce_side(sizes, idx, *refs):
    refs, out = refs[:-1], refs[-1]
    at = 0
    for size in sizes:
        total = refs[0][...].astype(F32)
        for ref in refs[1:size]:
            total += ref[...].astype(F32)
        out[:, :, at : at + total.shape[2]] = total.astype(BF16)
        refs = refs[size:]
        at += total.shape[2]


def fold(nz, fy, idx, got, out):
    cs = got.shape[1]
    for f in range(fy):
        total = got[f].astype(F32)
        for z in range(1, nz):
            total += got[z * fy + f].astype(F32)
        out[f * cs : (f + 1) * cs, :] = total.astype(BF16)


def own_rows(count, spans, idx, *refs):
    pieces, outs, stack = refs[:count], refs[count:-1], refs[-1]
    for k, ref in enumerate(pieces):
        at = idx[2] ^ k
        stack[at % 2, at // 2] = ref[...]
    sides, height = stack.shape[1], stack.shape[2]
    fy_cb = [(f, x) for f in range(PEERS) for x in range(sides)]
    cb = height // PEERS
    for half in range(2):
        whole = jnp.concatenate(
            [stack[half, x, f * cb : (f + 1) * cb, :].astype(F32) for f, x in fy_cb], axis=0
        ).T
        at = 0
        for span, group in spans:
            begin = at
            for n in group:
                out = outs[n]
                rows = out.shape[0] // 2
                out[half * rows : (half + 1) * rows, :] = whole[begin : begin + rows]
                begin += rows
            at += span


def entry_back(small, idx, *refs):
    pieces = refs[:PEERS]
    image, norm, gain, shift, grad_pre, sums = refs[PEERS:]
    c_in = gain.shape[1]
    side = 2 * small
    grad = pieces[0][...].astype(F32)
    for ref in pieces[1:]:
        grad += ref[...].astype(F32)
    order = pixel_order(small, side * side, lambda y, x: y * side + x)
    high = grad.astype(BF16)
    low = (grad - high.astype(F32)).astype(BF16)
    grad = sum(
        lax.dot_general(order, part, (((0,), (0,)), ((), ())), preferred_element_type=F32)
        for part in (high, low)
    )
    normed = (image[...].astype(F32) - norm[0:1, :c_in]) * norm[1:2, :c_in]
    g = gelu_slope(gain[...] * normed + shift[...]) * grad
    grad_pre[...] = g
    sums[...] = jnp.zeros_like(sums)
    sums[0:1, :c_in] = jnp.sum(g * normed, axis=0, keepdims=True)
    sums[1:2, :c_in] = jnp.sum(g, axis=0, keepdims=True)


def bundle(idx, first, second, third, sums, out):
    out[...] = jnp.zeros_like(out)
    out[0:8, :] = sums[...]
    for k, ref in enumerate((first, second, third)):
        out[8 + 2 * k : 10 + 2 * k, : ref.shape[1]] = ref[0:2]


def unbundle(idx, *refs):
    out, six, order = refs[-3:]
    got = in_order(refs[:-3], idx[0], order)
    total = got[0][0:8]
    for g in got[1:]:
        total = total + g[0:8]
    out[...] = total
    cs = six.shape[1] // PEERS
    six[...] = jnp.concatenate([g[8:16, :cs] for g in got], axis=1)


def entry_grad(nz, idx, *refs):
    sums = refs[:nz]
    grad_pre, image, weight, norm, gain, gain_grad, shift_grad, out, order = refs[nz:]
    got = in_order(sums, idx[1], order)
    total = got[0]
    for g in got[1:]:
        total = total + g
    gain_grad[...] = total[0:1]
    shift_grad[...] = total[1:2]
    c_in = gain.shape[1]
    scale = norm[1:2, :c_in]
    normed = (image[...].astype(F32) - norm[0:1, :c_in]) * scale
    out[...] = gain[...] * scale * (
        grad_pre[...]
        - weight[:, 0:1]
        * (shift_grad[0:1, :c_in] + normed * gain_grad[0:1, :c_in])
        / norm[2:3, :c_in]
    )


def program(
    nx,
    ny,
    images,
    valid_count,
    pixel_mask,
    gain_entry,
    shift_entry,
    conv_first,
    gain_middle,
    shift_middle,
    conv_second,
    projection,
    gain_inner,
    shift_inner,
    conv_third,
    gain_last,
    shift_last,
    conv_fourth,
    cotangent,
):
    fy = PEERS
    nz = ny // fy
    sides = nx // 2
    side, c_in = images.shape[1], images.shape[3]
    small = side // 2
    area = small * small
    c_out = conv_first.shape[1]
    cs = c_out // PEERS
    cb = cs // sides
    width = PEERS * area
    lanes = c_in + 64
    padded = span_of(c_in)
    gx, gy = lax.axis_index("gx"), lax.axis_index("gy")
    me = gy % fy
    mine = gy // fy
    run = Order(jnp.stack([me, mine, gx, gy]).astype(jnp.int32))
    part = functools.partial

    def to_slice(piece, k):
        return lax.ppermute(piece, "gy", [(j, j // fy * fy + (j % fy ^ k)) for j in range(ny)])

    def share(pieces):
        return [pieces[0]] + [to_slice(pieces[k], k) for k in range(1, PEERS)]

    def to_gx(piece, k):
        return lax.ppermute(piece, "gx", [(i, i ^ k) for i in range(nx)])

    def pool_gx(piece):
        return [piece] + [to_gx(piece, k) for k in range(1, nx)]

    def pool_z(piece):
        out = [piece]
        for k in range(1, nz):
            perm = [(j, (j // fy ^ k) * fy + j % fy) for j in range(ny)]
            out.append(lax.ppermute(piece, "gy", perm))
        return out

    def over_x(block):
        return {0: block, **{k: to_gx(block, k) for k in range(2, nx, 2)}}

    def over_core(held, *then):
        held = {k: after(v, *then) for k, v in held.items()} if then else dict(held)
        for k in list(held):
            held[k + 1] = to_gx(held[k], 1)
        return [held[k] for k in sorted(held)]

    def turn(block):
        return lax.all_to_all(block, "gy", 0, 0, tiled=True)

    unit_first, unit_skip = conv_first.shape[0] // 2, projection.shape[0] // 2
    unit_mid = conv_second.shape[0] // 2
    span_first, span_mid = span_of(unit_first + unit_skip), span_of(unit_mid)
    tile, tile16 = shape((cs, width)), shape((cs, width), BF16)
    long16 = shape((cs, width + 128), BF16)
    cols, stat, entry_stat = shape((cs, 128)), shape((8, cs)), shape((8, lanes))
    shifted16 = shape((9 * cs, width), BF16)
    full16 = shape((c_out, width), BF16)
    whole16 = shape((9 * cs, c_out), BF16)

    def halves(span, channels):
        return pltpu.VMEM((2, cs // channels, ny, channels, span), BF16)

    def ready(span, sections, *weights):
        out = shape((ny, cb, span * len(sections)), BF16)
        return run(
            part(entry_weights, cs, fy, sections), out, weights, cost=24 * len(sections)
        )

    def merge(pieces, kernel):
        like = pieces[0].shape
        return run(kernel, shape(like), pieces, [pltpu.VMEM((nx, *like), F32)])

    add_gx = part(add_rows, 2)

    def activate(value, params, pooled, cot=None):
        more = [] if cot is None else [cot]
        outs = [tile16] if cot is None else [long16] * PEERS
        return run(
            part(act_block, nz),
            [tile, cols] + outs,
            [value, params, *pooled, *more],
            [pltpu.VMEM((nz, 8, cs), F32)]
            + ([] if cot is None else [pltpu.VMEM((c_out, 128), F32)]),
            far=(0, 1),
        )

    def convolve(pieces, weights, base, last=False):
        more = [] if base is None else [base]
        outs = [shape((cs, 128), BF16)] * PEERS + [full16]
        return run(
            part(conv_block, nx, base is not None, last, unit_mid, 0, area, small),
            outs if last else [tile, stat, full16, whole16],
            [*pieces, narrow, *weights, *more],
            [pltpu.VMEM((9 * cs, width), F32)] + ([] if last else [halves(span_mid, cb)]),
            cost=25,
            far=() if last else (2, 3),
        )

    def slope(parts, normed, params):
        return run(gelu_back, [tile, stat], [*parts, normed, params])

    def back(grad_pre, normed, scales, params, pooled, weights, base, riders=()):
        more = list(riders) if base is None else [base]
        return run(
            part(norm_back, nz, base is not None, False, area, small),
            [stat, shifted16]
            + ([long16] * PEERS if base is None else [tile16] * (PEERS + 1)),
            [grad_pre, normed, scales, params, narrow, *pooled, *more, weights],
            [pltpu.VMEM((c_out, width), F32), pltpu.VMEM((nz, 8, cs), F32)],
            cost=18,
        )

    def grad_of(kernel, span, shifted, act, scratch):
        own, other = run(
            kernel,
            [shape((ny, cs, span)), shape((ny, cs, span), BF16)],
            [shifted, act],
            [scratch, pltpu.VMEM((2, ny, cs, span), F32)],
            cost=28,
        )
        return own, to_gx(other, 1)

    def grad_mid(shifted, act):
        return grad_of(
            part(weight_grad, unit_mid), span_mid, shifted, act, pltpu.VMEM((9 * cs, c_out), F32)
        )

    def over_pair(own, other):
        span = own.shape[2]
        return run(
            part(reduce_core, 1),
            [shape((ny, cb, span))] + [shape((ny, cb, span), BF16)] * (sides - 1),
            [own, other],
            [pltpu.VMEM((ny, cs, span), F32)],
        )

    def to_sides(parts, *then):
        parts = [after(p, *then) for p in parts] if then else parts
        return [parts[0]] + [to_gx(parts[k], 2 * k) for k in range(1, sides)]

    def over_sides(*groups):
        span = sum(parts[0].shape[2] for parts in groups)
        return run(
            part(reduce_side, tuple(len(parts) for parts in groups)),
            shape((ny, cb, span), BF16),
            [p for parts in groups for p in parts],
        )

    def folded(got):
        out = shape((fy * cb, got.shape[2]), BF16)
        return over_core(over_x(run(part(fold, nz, fy), out, [got])))

    def rows_of(pieces, spans, *rows):
        return run(
            part(own_rows, nx, spans),
            [shape((r, c_out)) for r in rows],
            pieces,
            [pltpu.VMEM((2, sides, fy * cb, pieces[0].shape[1]), BF16)],
            cost=30,
        )

    def own(gain, shift):
        pair = jnp.stack([gain, shift], axis=1)
        return lax.dynamic_slice_in_dim(pair, me * cs, cs, axis=0)

    p_middle = own(gain_middle, shift_middle)
    p_inner = own(gain_inner, shift_inner)
    p_last = own(gain_last, shift_last)
    g_entry, s_entry = gain_entry[None], shift_entry[None]
    pixels = images.reshape(side * side, c_in)

    image, wide = run(
        part(entry_image, small),
        [shape((4 * area, lanes), BF16), shape((4 * area, 128))],
        [pixels, pixel_mask.reshape(side, side), valid_count],
        scalars=1,
    )
    group = share([image] * PEERS)
    out_first = ready(span_first, (2,), conv_first, projection)
    stats = run(part(entry_stats, area), entry_stat, group)
    pieces = pool_gx(stats)
    got_first = turn(after(out_first, *group[1:]))
    got_first = over_core(over_x(after(got_first, *pieces[1:])))
    pooled = pool_z(merge(pieces, merge_stats))
    out_second = ready(span_mid, (1,), conv_second)
    got_second = turn(after(out_second, pooled[-1]))
    out_late = ready(span_mid, (1, 1), conv_third, conv_fourth)
    first, skipped, stats, norm_one, narrow, act_one, w_first = run(
        part(entry_block, nz, nx, unit_first, unit_skip, area, small),
        [
            tile,
            tile,
            stat,
            entry_stat,
            shape((8, width)),
            shape((4, width, c_in), BF16),
            shape((10 * cs, c_in), BF16),
        ],
        [*group, *pooled, g_entry, s_entry, *got_first],
        [
            pltpu.VMEM((nz, 8, lanes), F32),
            pltpu.VMEM((width, lanes), BF16),
            pltpu.VMEM((cs, span_of(9 * c_in)), BF16),
            halves(span_first, cb),
        ],
        cost=40,
        far=(3, 5, 6),
    )

    merged = merge(pool_gx(stats), merge_stats)
    got_second = over_x(after(got_second, merged))
    pooled = pool_z(merged)
    got_late = turn(after(out_late, pooled[-1]))
    normed_two, scale_two, *messages = activate(
        first, p_middle, pooled, cotangent.reshape(area, c_out)
    )
    pieces = share(messages)
    got_second = over_core(got_second, *pieces[1:])
    hidden, stats, act_two, w_second = convolve(pieces, got_second, skipped)
    cot_parts = pieces
    merged = merge(pool_gx(stats), merge_stats)
    got_late = over_x(after(got_late, merged))
    pooled = pool_z(merged)
    normed_three, scale_three, act = activate(hidden, p_inner, pooled)
    pieces = share([act] * PEERS)
    got_late = over_core(got_late, *pieces[1:])
    third, stats, act_three, w_third = convolve(pieces, got_late, None)
    merged = merge(pool_gx(stats), merge_stats)

    cot, shifted_four, w_fourth, *parts = run(
        part(last_back, nx, unit_mid, 1, area, small),
        [tile, shifted16, whole16] + [tile16] * PEERS,
        [*cot_parts, *got_late],
        [pltpu.VMEM((c_out, width), F32), halves(span_mid, cb)],
        cost=18,
        far=(0, 1, 2),
    )
    parts = share(parts)
    normed_four, scale_four, act = activate(third, p_last, pool_z(merged))
    pieces = share([act] * PEERS)
    grad_pre, sums = slope(parts, normed_four, p_last)
    sums = pool_gx(sums)
    *riders, act_four = convolve(pieces, [w_fourth], hidden, last=True)
    sums = pool_z(merge(sums, add_gx))
    fourth = grad_mid(shifted_four, act_four)
    last_sums, shifted_three, *parts = back(
        grad_pre, normed_four, scale_four, p_last, sums, w_third, None, riders
    )
    parts = share(parts)
    fourth = over_pair(*fourth)
    grad_pre, sums = slope(parts, normed_three, p_inner)
    sums = pool_gx(sums)
    third = grad_mid(shifted_three, act_three)
    merged = merge(sums, add_gx)
    fourth = to_sides(fourth, merged)
    sums = pool_z(merged)
    out = run(
        join_result, shape((area, c_out), BF16), parts, [pltpu.VMEM((c_out, 128), F32)]
    )
    inner_sums, shifted_two, grad_hidden, *parts = back(
        grad_pre, normed_three, scale_three, p_inner, sums, w_second, cot
    )
    parts = share(parts)
    third = over_pair(*third)
    grad_pre, sums = slope(parts, normed_two, p_middle)
    sums = pool_gx(sums)
    second = grad_mid(shifted_two, act_two)
    merged = merge(sums, add_gx)
    third = to_sides(third, merged)
    sums = pool_z(merged)
    fourth = over_sides(fourth)
    second = to_sides(over_pair(*second), merged)
    middle_sums, shifted_one, *parts = run(
        part(norm_back, nz, False, True, area, small),
        [stat, shape((10 * cs, width), BF16)] + [shape((4 * area, c_in), BF16)] * PEERS,
        [
            grad_pre,
            normed_two,
            scale_two,
            p_middle,
            narrow,
            *sums,
            w_first,
            grad_hidden,
        ],
        [pltpu.VMEM((4, width, c_in), F32), pltpu.VMEM((nz, 8, cs), F32)],
        cost=18,
    )

    first = grad_of(
        part(weight_grad_first, unit_first, unit_skip),
        span_first,
        shifted_one,
        act_one,
        pltpu.VMEM((cs, span_of(9 * c_in + span_first + 128)), F32),
    )
    parts = share(parts)
    late = turn(over_sides([after(fourth, *parts[1:])], third))
    first = to_sides(over_pair(*first))
    grad_pre, sums = run(
        part(entry_back, small),
        [shape((4 * area, c_in)), shape((8, padded))],
        [*parts, pixels, norm_one, g_entry, s_entry],
        cost=13,
    )
    message = run(bundle, shape((16, padded)), [middle_sums, inner_sums, last_sums, sums])
    message = share([message] * PEERS)
    second = over_sides(second)
    early = over_sides([second], first)
    sums, six = run(
        unbundle,
        [shape((8, padded)), shape((8, c_out))],
        message,
        [pltpu.VMEM((PEERS, 16, padded), F32)],
    )
    early = turn(after(early, sums))
    sums = pool_z(merge(pool_gx(sums), add_gx))
    late = folded(late)
    fourth_grad, third_grad = rows_of(
        late, ((span_mid, (0,)), (span_mid, (1,))), 2 * unit_mid, 2 * unit_mid
    )
    early = folded(early)
    gain_entry_grad, shift_entry_grad, image_grad = run(
        part(entry_grad, nz),
        [shape((1, padded)), shape((1, padded)), shape((4 * area, c_in))],
        [*sums, grad_pre, pixels, wide, norm_one, g_entry],
        [pltpu.VMEM((nz, 8, padded), F32)],
    )
    second_grad, first_grad, skip_grad = rows_of(
        early,
        ((span_mid, (0,)), (span_first, (1, 2))),
        2 * unit_mid,
        2 * unit_first,
        2 * unit_skip,
    )
    return (
        out.reshape(1, small, small, c_out),
        image_grad.reshape(1, side, side, c_in),
        gain_entry_grad[0, :c_in],
        shift_entry_grad[0, :c_in],
        first_grad,
        six[0],
        six[1],
        second_grad,
        skip_grad,
        six[2],
        six[3],
        third_grad,
        six[4],
        six[5],
        fourth_grad,
    )


def solution(mesh):
    whole = P(("gx", "gy"), None, None, None)
    rows = P("gy", None)
    return jax.shard_map(
        functools.partial(program, mesh.shape["gx"], mesh.shape["gy"]),
        mesh=mesh,
        in_specs=(
            whole,
            P(("gx", "gy")),
            P(("gx", "gy"), None, None),
            P(),
            P(),
            rows,
            P(),
            P(),
            rows,
            rows,
            P(),
            P(),
            rows,
            P(),
            P(),
            rows,
            whole,
        ),
        out_specs=(
            whole, whole, P(), P(), rows, P(), P(), rows, rows, P(), P(), rows, P(), P(), rows,
        ),
        check_vma=False,
    )
```

```python
import functools

import jax
import jax.numpy as jnp
from jax import lax
from jax.experimental import pallas as pl
from jax.experimental.pallas import tpu as pltpu
from jax.sharding import PartitionSpec as P

EPS = 1e-05
COST = 6 * 10**7
F32 = jnp.float32
BF16 = jnp.bfloat16
PEERS = 4
C0 = 0.7978845608028654
C1 = 0.044715
VMEM = pl.BlockSpec(memory_space=pltpu.VMEM)
SMEM = pl.BlockSpec(memory_space=pltpu.SMEM)


def gelu(v):
    return 0.5 * v * (1.0 + jnp.tanh(C0 * (v + C1 * (v * v * v))))


def gelu_slope(v):
    t = jnp.tanh(C0 * (v + C1 * (v * v * v)))
    return 0.5 * (1.0 + t) + 0.5 * v * (1.0 - t * t) * (C0 * (1.0 + 3.0 * C1 * (v * v)))


def after(value, *others):
    return lax.optimization_barrier((value, *others))[0]


class Far:
    def __init__(self, near, far, sem):
        self.near, self.shape, self.dtype = near, near.shape, near.dtype
        self.copy = pltpu.make_async_copy(near, far, sem)
        self.sent = False

    def __getitem__(self, at):
        return self.near[at]

    def __setitem__(self, at, value):
        self.near[at] = value

    def send(self):
        if not self.sent:
            self.copy.start()
            self.sent = True


def send(ref):
    if isinstance(ref, Far):
        ref.send()


def with_far(kernel, n_in, n_out, far, *refs):
    ins, outs, rest = refs[:n_in], list(refs[n_in : n_in + n_out]), list(refs[n_in + n_out :])
    if far:
        sems = rest.pop()
        near = rest[len(rest) - len(far) :]
        del rest[len(rest) - len(far) :]
        for n, at in enumerate(far):
            outs[at] = Far(near[n], outs[at], sems.at[n])
    kernel(*ins, *outs, *rest)
    for at in far:
        outs[at].send()
    for at in far:
        outs[at].copy.wait()


class Order:
    def __init__(self, idx):
        self.idx = idx
        self.last = ()

    def __call__(self, kernel, outs, args, scratch=(), scalars=0, cost=7, far=()):
        idx = after(self.idx, *self.last)
        many = isinstance(outs, (list, tuple))
        shapes = list(outs) if many else [outs]
        more = [pltpu.VMEM(shapes[at].shape, shapes[at].dtype) for at in far]
        if far:
            more.append(pltpu.SemaphoreType.DMA((len(far),)))
        got = pl.pallas_call(
            functools.partial(with_far, kernel, 1 + len(args), len(shapes), tuple(far)),
            out_shape=shapes,
            in_specs=[SMEM] + [VMEM] * (len(args) - scalars) + [SMEM] * scalars,
            out_specs=[
                pl.BlockSpec(memory_space=pl.ANY) if at in far else VMEM
                for at in range(len(shapes))
            ],
            scratch_shapes=list(scratch) + more,
            compiler_params=pltpu.CompilerParams(vmem_limit_bytes=16 * 1024 * 1024),
            cost_estimate=pl.CostEstimate(
                flops=cost * COST, bytes_accessed=1024, transcendentals=0
            ),
        )(idx, *args)
        near = [v for at, v in enumerate(got) if at not in far]
        self.last = (near[0] if near else got[0],)
        return got if many else got[0]


def shape(dims, dtype=F32):
    return jax.ShapeDtypeStruct(dims, dtype)


def rows_at(index, count):
    return pl.ds(pl.multiple_of(index * count, count), count)


def as_rows(parts):
    height = parts[0].shape[0]
    lane = lax.broadcasted_iota(jnp.int32, (height, 128), 1)
    out = jnp.zeros((height, 128), F32)
    for k, part in enumerate(parts):
        out = jnp.where(lane == k, part, out)
    return out.T[0:8]


def as_columns(rows):
    return jnp.concatenate([rows, jnp.zeros((120, rows.shape[1]), F32)], axis=0).T


def in_order(refs, me, scratch):
    for k, ref in enumerate(refs):
        scratch[me ^ k] = ref[...]
    return [scratch[k] for k in range(len(refs))]


def merge_moments(stats):
    total = sum(n for _, _, n in stats)
    mean = sum(n * m for m, _, n in stats) / total
    squares = sum(q + n * (m - mean) * (m - mean) for m, q, n in stats)
    return mean, squares, total


def merge_rows(refs):
    mean, squares, total = merge_moments([(g[0:1], g[1:2], g[2:3]) for g in refs])
    return mean, squares, total, sum(g[3:4] for g in refs)


def pixel(width, area, small):
    lane = lax.broadcasted_iota(jnp.int32, (1, width), 1) % area
    return lane // small, lane % small


def inside(row, col, drow, dcol, small):
    return (row + drow >= 0) & (row + drow < small) & (col + dcol >= 0) & (col + dcol < small)


def moved(value, step):
    shift = (-step) % value.shape[1]
    return pltpu.roll(value, shift, 1) if shift else value


OFFSETS = [(0, krow - 1, kcol - 1) for krow in range(3) for kcol in range(3)]

STRIDED = [
    ((krow != 1) * 2 + (kcol != 1), -(krow == 0), -(kcol == 0))
    for krow in range(3)
    for kcol in range(3)
] + [(0, 0, 0)]
PLACED = sorted(range(10), key=lambda k: (STRIDED[k][0], k))
PHASES = [[k for k in PLACED if STRIDED[k][0] == phase] for phase in range(4)]


def row_of(k, cs):
    at = PLACED.index(k)
    return slice(at * cs, (at + 1) * cs)


def phase_rows(phase, cs):
    first, last = PHASES[phase][0], PHASES[phase][-1]
    return slice(PLACED.index(first) * cs, (PLACED.index(last) + 1) * cs)


def masked_stats(value, weight, n):
    mean = jnp.sum(value * weight, axis=1, keepdims=True) / n
    centred = value - mean
    return mean, jnp.sum(weight * centred * centred, axis=1, keepdims=True)


def span_of(rows):
    return -(-rows // 128) * 128


def one_hot(height, width, shift):
    row = lax.broadcasted_iota(jnp.int32, (height, width), 0)
    col = lax.broadcasted_iota(jnp.int32, (height, width), 1)
    return (col == row + shift).astype(BF16)


def pick32(left, right, dims=((1,), (0,))):
    return lax.dot_general(left, right, (dims, ((), ())), preferred_element_type=F32)


def pick(left, right, dims=((1,), (0,))):
    return pick32(left, right, dims).astype(BF16)


def lane_tile(held, tile, rows, span):
    sides, ny = held.shape[1], held.shape[2]
    lane = lax.broadcasted_iota(jnp.int32, (1, 128), 1)
    out = None
    for v in range(2 * ny):
        begin = rows * v - tile * 128
        if begin >= 128 or begin + rows <= 0:
            continue
        at = (tile - rows * v // 128) * 128 % span
        part = jnp.concatenate(
            [held[v % 2, x, v // 2, :, at : at + 128].astype(F32) for x in range(sides)], axis=0
        )
        if begin > 0 or begin + rows < 128:
            own = (lane >= begin) & (lane < begin + rows)
            part = jnp.where(own, part, 0.0)
        out = part if out is None else out + part
    return out.astype(BF16)


def pixel_order(small, width, of):
    area = small * small
    row = lax.broadcasted_iota(jnp.int32, (4 * area, width), 0)
    col = lax.broadcasted_iota(jnp.int32, (4 * area, width), 1)
    phase, pix = row // area, row % area
    y = 2 * (pix // small) + phase // 2
    x = 2 * (pix % small) + phase % 2
    return (col == of(y, x)).astype(BF16)


def entry_image(small, idx, image, mask, valid, out, weight):
    side = 2 * small
    c_in = image.shape[1]
    count = side * side
    order = pixel_order(small, count, lambda y, x: y * side + x)
    out[:, :c_in] = pick(order, image[...])
    live = (valid[0] > 0).astype(F32)
    row = lax.broadcasted_iota(jnp.int32, (count, side), 0)
    col = lax.broadcasted_iota(jnp.int32, (count, side), 1)
    by_row = jnp.dot(
        (row // side == col).astype(BF16),
        mask[...].astype(F32).astype(BF16),
        preferred_element_type=F32,
    )
    column = jnp.sum(jnp.where(row % side == col, by_row, 0.0), axis=1, keepdims=True) * live
    lane = lax.broadcasted_iota(jnp.int32, (count, 128), 1)
    spread = jnp.where(lane == 0, column, 0.0)
    weight[...] = spread
    out[:, c_in:] = pick(order, spread.astype(BF16))[:, : out.shape[1] - c_in]


def entry_weights(cs, fy, sections, idx, *refs):
    weights, out = list(refs[:-1]), refs[-1]
    ny, cb, lanes = out.shape
    span = lanes // len(sections)
    gx, gy = idx[2], idx[3]
    core, side = gx % 2, (gx // 2 if cb < cs else 0)
    c_out = weights[0].shape[1]
    row = lax.broadcasted_iota(jnp.int32, (fy * cb, c_out), 0)
    col = lax.broadcasted_iota(jnp.int32, (fy * cb, c_out), 1)
    chosen = (col == row // cb * cs + side * cb + row % cb).astype(BF16)
    for n, count in enumerate(sections):
        begin = weights[0].shape[0] // 2 * (2 * gy + core) % 128
        total = None
        for _ in range(count):
            weight = weights.pop(0)
            rows = weight.shape[0]
            half = rows // 2
            mine = pick(chosen, weight[...], ((1,), (1,)))
            row = lax.broadcasted_iota(jnp.int32, (rows, span), 0) - core * half
            col = lax.broadcasted_iota(jnp.int32, (rows, span), 1)
            place = (row >= 0) & (row < half) & (
                (col == row + begin) | (col == row + begin - span)
            )
            part = pick32(mine, place.astype(BF16))
            total = part if total is None else total + part
            begin = begin + half
        for j in range(ny):
            out[j, :, n * span : (n + 1) * span] = total[
                (j % fy) * cb : (j % fy + 1) * cb
            ].astype(BF16)


def hold(gx, messages, held, section=0):
    span = held.shape[4]
    for k, ref in enumerate(messages):
        at = gx ^ k
        side = at // 2 if held.shape[1] > 1 else 0
        held[at % 2, side] = ref[:, :, section * span : (section + 1) * span]


def assemble(held, out, rows):
    cs, span = held.shape[1] * held.shape[3], held.shape[4]
    tiles = out.shape[1] // 128
    for k in range(9):
        for q in range(tiles):
            out[k * cs : (k + 1) * cs, q * 128 : (q + 1) * 128] = lane_tile(
                held, tiles * k + q, rows, span
            )


def assemble_first(held, out, flat, rows, extra):
    cs, span = held.shape[1] * held.shape[3], held.shape[4]
    c_in = out.shape[1]
    tiles = flat.shape[1] // 128
    for tile in range(tiles):
        flat[:, tile * 128 : (tile + 1) * 128] = lane_tile(held, tile, rows, span)
    for k in range(9):
        begin = k * c_in
        base = begin // 128 * 128
        reach = min(-(-(begin + c_in) // 128) * 128, flat.shape[1])
        move = one_hot(c_in, reach - base, begin - base)
        out[row_of(k, cs), :] = pick(flat[:, base:reach], move, ((1,), (1,)))
    total = None
    for v in range(2 * held.shape[2]):
        row = lax.broadcasted_iota(jnp.int32, (span, c_in), 0)
        col = lax.broadcasted_iota(jnp.int32, (span, c_in), 1)
        at = col - extra * v
        begin = rows * v % 128 + rows
        place = (at >= 0) & (at < extra) & ((row == at + begin) | (row == at + begin - span))
        part = jnp.concatenate(
            [
                pick32(held[v % 2, x, v // 2], place.astype(BF16))
                for x in range(held.shape[1])
            ],
            axis=0,
        )
        total = part if total is None else total + part
    out[row_of(9, cs), :] = total.astype(BF16)


def entry_stats(area, idx, *refs):
    images, out = refs[:PEERS], refs[PEERS]
    lanes = out.shape[1]
    first = jnp.zeros((1, lanes), F32)
    wide = jnp.zeros((1, 1), F32)
    narrow = jnp.zeros((1, 1), F32)
    c_in = lanes - 64
    for ref in images:
        x = ref[...].astype(F32)
        w = x[:, c_in : c_in + 1]
        first += jnp.sum(x * w, axis=0, keepdims=True)
        wide += jnp.sum(w, axis=0, keepdims=True)
        narrow += jnp.sum(w[:area], axis=0, keepdims=True)
    mean = first / wide
    squares = jnp.zeros((1, lanes), F32)
    for ref in images:
        x = ref[...].astype(F32)
        w = x[:, c_in : c_in + 1]
        d = x - mean
        squares += jnp.sum(d * d * w, axis=0, keepdims=True)
    out[...] = jnp.zeros_like(out)
    out[0:1, :] = mean
    out[1:2, :] = squares
    out[2:3, :] = jnp.broadcast_to(wide, (1, lanes))
    out[3:4, :] = jnp.broadcast_to(narrow, (1, lanes))


def entry_block(nz, nx, rows, extra, area, small, idx, *refs):
    images = refs[:PEERS]
    stats, rest = refs[PEERS : PEERS + nz], refs[PEERS + nz :]
    gain, shift, messages, rest = rest[0], rest[1], rest[2 : 2 + nx], rest[2 + nx :]
    first, skipped, out_stats, norm, narrow, act, w_first = rest[:7]
    order, masks, flat, held = rest[7:]
    me, mine = idx[0], idx[1]
    c_in = gain.shape[1]
    lanes = norm.shape[1]
    cs = first.shape[0]
    width = first.shape[1]
    hold(idx[2], messages, held)
    assemble_first(held, w_first, flat, rows, extra)
    send(w_first)
    mean, squares, total, count = merge_rows(in_order(stats, mine, order))
    scale = lax.rsqrt(squares / total + EPS)
    norm[...] = jnp.zeros_like(norm)
    norm[0:1, :] = mean
    norm[1:2, :] = scale
    norm[2:3, :] = total
    norm[3:4, :] = count
    for k, ref in enumerate(images):
        x = ref[...]
        v = x[:, :c_in].astype(F32)
        pre = gain[...] * ((v - mean[:, :c_in]) * scale[:, :c_in]) + shift[...]
        a = gelu(pre).astype(BF16)
        for phase in range(4):
            act[phase, rows_at(me ^ k, area), :] = a[phase * area : (phase + 1) * area]
        masks[rows_at(me ^ k, area), :] = x[:area]
    send(act)
    send(norm)
    ones = (lax.broadcasted_iota(jnp.int32, (8, lanes), 1) == c_in).astype(BF16)
    weight8 = lax.dot_general(
        ones, masks[...], (((1,), (1,)), ((), ())), preferred_element_type=F32
    )
    narrow[...] = weight8
    weight = weight8[0:1]
    row, col = pixel(width, area, small)
    total_first = jnp.zeros((cs, width), F32)
    for phase in range(4):
        group = lax.dot_general(
            w_first[phase_rows(phase, cs), :],
            act[phase],
            (((1,), (1,)), ((), ())),
            preferred_element_type=F32,
        )
        for at, k in enumerate(PHASES[phase]):
            y = group[at * cs : (at + 1) * cs]
            if k == 9:
                skipped[...] = y
                continue
            _, drow, dcol = STRIDED[k]
            y = moved(y, drow * small + dcol)
            total_first += jnp.where(inside(row, col, drow, dcol, small), y, 0.0)
    first[...] = total_first
    n = jnp.sum(weight, axis=1, keepdims=True)
    mean2, squares = masked_stats(total_first, weight, n)
    out_stats[...] = as_rows((mean2, squares, n))


def merge_stats(idx, *refs):
    out, order = refs[-2:]
    mean, squares, total, count = merge_rows(in_order(refs[:-2], idx[2], order))
    out[...] = jnp.zeros_like(out)
    out[0:1] = mean
    out[1:2] = squares
    out[2:3] = total
    out[3:4] = count


def add_rows(which, idx, *refs):
    out, order = refs[-2:]
    got = in_order(refs[:-2], idx[which], order)
    total = got[0]
    for g in got[1:]:
        total = total + g
    out[...] = total


def act_block(nz, idx, *refs):
    value, params = refs[:2]
    stats, rest = refs[2 : 2 + nz], refs[2 + nz :]
    if rest[-1].shape[1] == 128:
        cot, normed, scales, outs, order, stack = (*rest[:3], rest[3:-2], *rest[-2:])
    else:
        cot, normed, scales, outs, order = (None, *rest[:2], rest[2:-1], rest[-1])
    mean, squares, total, _ = merge_rows(in_order(stats, idx[1], order))
    rows = jnp.concatenate(
        [mean, lax.rsqrt(squares / total + EPS), total, jnp.zeros((5, mean.shape[1]), F32)], axis=0
    )
    cols = as_columns(rows)
    norm = (value[...] - cols[:, 0:1]) * cols[:, 1:2]
    normed[...] = norm
    send(normed)
    scales[...] = cols
    send(scales)
    act = gelu(params[:, 0:1] * norm + params[:, 1:2]).astype(BF16)
    cs, width = norm.shape
    if cot is not None:
        c = cot[...].astype(F32)
        stack[...] = jnp.concatenate([c, c], axis=0).T
    for k, out in enumerate(outs):
        out[:, :width] = act
        if cot is not None:
            out[:, width:] = stack[rows_at(idx[0] ^ k, cs), :].astype(BF16)


def conv_block(nx, added, last, rows, section, area, small, idx, *refs):
    pieces = refs[:PEERS]
    narrow, rest = refs[PEERS], refs[PEERS + 1 :]
    if last:
        weights, rest = rest[0], rest[1:]
    else:
        messages, rest = rest[:nx], rest[nx:]
    base, rest = (rest[0], rest[1:]) if added else (None, rest)
    me = idx[0]
    cs, width = pieces[0].shape[0], narrow.shape[1]
    if last:
        outs, act, spread = rest[:PEERS], rest[PEERS], rest[PEERS + 1]
    else:
        value, out_stats, act, whole, spread, held = rest
        hold(idx[2], messages, held, section)
        assemble(held, whole, rows)
        send(whole)
        weights = whole
    for k, ref in enumerate(pieces):
        act[rows_at(me ^ k, cs), :] = ref[:, :width]
    send(act)
    spread[...] = jnp.dot(weights[...], act[...], preferred_element_type=F32)
    row, col = pixel(width, area, small)
    total = base[...] if added else jnp.zeros((cs, width), F32)
    for k, (_, drow, dcol) in enumerate(OFFSETS):
        y = moved(spread[k * cs : (k + 1) * cs, :], drow * small + dcol)
        total += jnp.where(inside(row, col, drow, dcol, small), y, 0.0)
    if last:
        result = total.astype(BF16)
        lane = lax.broadcasted_iota(jnp.int32, (width, 128), 0)
        slot = lax.broadcasted_iota(jnp.int32, (width, 128), 1)
        for k, out in enumerate(outs):
            out[...] = pick(result, (lane == (me ^ k) * area + slot).astype(BF16))
    else:
        value[...] = total
        weight = narrow[0:1, :]
        n = jnp.sum(weight, axis=1, keepdims=True)
        mean, squares = masked_stats(total, weight, n)
        out_stats[...] = as_rows((mean, squares, n))


def join_result(idx, *refs):
    pieces, (out, stack) = refs[:PEERS], refs[PEERS:]
    cs = pieces[0].shape[0]
    for k, ref in enumerate(pieces):
        stack[rows_at(idx[0] ^ k, cs), :] = ref[:, -128:].astype(F32)
    out[...] = stack[...].T[: out.shape[0]].astype(BF16)


def spread_grad(grad, shifted, area, small, offs, row_at):
    cs, width = grad.shape
    row, col = pixel(width, area, small)
    for k, (_, drow, dcol) in enumerate(offs):
        g = moved(grad, -(drow * small + dcol))
        g = jnp.where(inside(row, col, -drow, -dcol, small), g, 0.0)
        shifted[row_at(k, cs), :] = g.astype(BF16)


def plain_rows(k, cs):
    return slice(k * cs, (k + 1) * cs)


def push_back(me, weights, shifted, partial, outs):
    cs, width = outs[0].shape[0], shifted.shape[1]
    partial[...] = lax.dot_general(
        weights[...], shifted[...], (((0,), (0,)), ((), ())), preferred_element_type=F32
    )
    for k, out in enumerate(outs):
        out[:, :width] = partial[rows_at(me ^ k, cs), :].astype(BF16)


def last_back(nx, rows, section, area, small, idx, *refs):
    pieces, messages, rest = refs[:PEERS], refs[PEERS : PEERS + nx], refs[PEERS + nx :]
    cot, shifted, weights = rest[:3]
    outs = rest[3 : PEERS + 3]
    partial, held = rest[PEERS + 3 :]
    hold(idx[2], messages, held, section)
    assemble(held, weights, rows)
    send(weights)
    me = idx[0]
    cs, width = cot.shape
    image = lax.broadcasted_iota(jnp.int32, (1, width), 1) // area
    grad = jnp.zeros((cs, width), F32)
    for k, ref in enumerate(pieces):
        tiled = jnp.concatenate([ref[:, width:].astype(F32)] * (width // 128), axis=1)
        grad = jnp.where(image == (me ^ k), tiled, grad)
    cot[...] = grad
    send(cot)
    spread_grad(grad, shifted, area, small, OFFSETS, plain_rows)
    send(shifted)
    push_back(me, weights, shifted, partial, outs)


def gelu_back(idx, *refs):
    pieces = refs[:PEERS]
    normed, params, grad_pre, sums = refs[PEERS:]
    width = normed.shape[1]
    grad = pieces[0][:, :width].astype(F32)
    for ref in pieces[1:]:
        grad += ref[:, :width].astype(F32)
    norm = normed[...]
    g = gelu_slope(params[:, 0:1] * norm + params[:, 1:2]) * grad
    grad_pre[...] = g
    sums[...] = as_rows(
        (jnp.sum(g * norm, axis=1, keepdims=True), jnp.sum(g, axis=1, keepdims=True))
    )


def norm_back(nz, added, last, area, small, idx, *refs):
    grad_pre, normed, scales, params, narrow = refs[:5]
    sums = refs[5 : 5 + nz]
    rest = refs[5 + nz :]
    base, rest = (rest[0], rest[1:]) if added else (None, rest)
    me = idx[0]
    cs, width = grad_pre.shape
    order = rest[-1]
    got = in_order(sums, idx[1], order)
    total = got[0]
    for g in got[1:]:
        total = total + g
    cols = as_columns(total)
    gain_grad, shift_grad = cols[:, 0:1], cols[:, 1:2]
    norm = normed[...]
    back = params[:, 0:1] * scales[:, 1:2] * (
        grad_pre[...]
        - narrow[0:1, :] * (shift_grad + norm * gain_grad) / scales[:, 2:3]
    )
    if added:
        back = base[...] + back
    grad = back.astype(BF16).astype(F32)
    if not last:
        riders = ()
        if not added:
            riders, rest = rest[:PEERS], rest[PEERS:]
        weights, sums_out, shifted = rest[:3]
        outs, partial = rest[3 : 3 + PEERS], rest[3 + PEERS]
        for rider, out in zip(riders, outs):
            out[:, width:] = rider[...]
        if added:
            grad_out, outs, partial = rest[3], rest[4 : 4 + PEERS], rest[4 + PEERS]
            grad_out[...] = grad.astype(BF16)
        sums_out[...] = total
        spread_grad(grad, shifted, area, small, OFFSETS, plain_rows)
        push_back(me, weights, shifted, partial, outs)
    else:
        weights, grad_skip, sums_out, shifted = rest[:4]
        outs, partial = rest[4 : 4 + PEERS], rest[4 + PEERS]
        sums_out[...] = total
        spread_grad(grad, shifted, area, small, STRIDED[:9], row_of)
        shifted[row_of(9, cs), :] = grad_skip[...]
        for phase in range(4):
            partial[phase] = lax.dot_general(
                shifted[phase_rows(phase, cs), :],
                weights[phase_rows(phase, cs), :],
                (((0,), (0,)), ((), ())),
                preferred_element_type=F32,
            )
        for k, out in enumerate(outs):
            for phase in range(4):
                out[phase * area : (phase + 1) * area, :] = partial[
                    phase, rows_at(me ^ k, area), :
                ].astype(BF16)


def part_halves(core, units, own, other):
    own[...] = units[core]
    other[...] = units[1 - core].astype(BF16)


def weight_grad(rows, idx, shifted, act, own, other, full, units):
    full[...] = lax.dot_general(
        shifted[...], act[...], (((1,), (1,)), ((), ())), preferred_element_type=F32
    )
    ny, cs, span = own.shape
    tiles = full.shape[1] // 128
    for v in range(2 * ny):
        begin = rows * v % 128
        parts = []
        for q in range((begin + rows + 127) // 128):
            k, p = divmod(rows * v // 128 + q, tiles)
            parts.append(full[k * cs : (k + 1) * cs, p * 128 : (p + 1) * 128])
        window = jnp.concatenate(parts, axis=1)
        units[v % 2, v // 2] = moved(window, begin)[:, :span]
    part_halves(idx[2] % 2, units, own, other)


def weight_grad_first(rows, extra, idx, shifted, act, own, other, flat, units):
    ny, cs, span = own.shape
    c_in = act.shape[2]
    flat[...] = jnp.zeros_like(flat)
    skip = None
    for phase in range(4):
        group = jnp.dot(
            shifted[phase_rows(phase, cs), :], act[phase], preferred_element_type=F32
        ).astype(BF16)
        for at, k in enumerate(PHASES[phase]):
            grad = group[at * cs : (at + 1) * cs]
            if k == 9:
                skip = grad
                continue
            begin = k * c_in
            base = begin // 128 * 128
            reach = -(-(begin + c_in) // 128) * 128
            move = one_hot(c_in, reach - base, begin - base)
            flat[:, base:reach] += jnp.dot(grad, move, preferred_element_type=F32)
    lane = lax.broadcasted_iota(jnp.int32, (1, span), 1)
    for v in range(2 * ny):
        begin = rows * v % 128
        base = rows * v - begin
        window = moved(flat[:, base : base + span + 128], begin)[:, :span]
        row = lax.broadcasted_iota(jnp.int32, (c_in, span), 0)
        col = lax.broadcasted_iota(jnp.int32, (c_in, span), 1)
        place = (row >= extra * v) & (row < extra * (v + 1)) & (col == row - extra * v + rows)
        tail = pick32(skip, place.astype(BF16))
        units[v % 2, v // 2] = jnp.where(lane < rows, window, 0.0) + tail
    part_halves(idx[2] % 2, units, own, other)


def reduce_core(count, idx, *refs):
    own, other, outs, total = refs[:count], refs[count : 2 * count], refs[2 * count : -1], refs[-1]
    cb = outs[0].shape[1]
    at = 0
    for a, b in zip(own, other):
        span = a.shape[2]
        total[:, :, at : at + span] = a[...] + b[...].astype(F32)
        at += span
    for k, out in enumerate(outs):
        for j in range(total.shape[0]):
            out[j] = total[j, rows_at(idx[2] // 2 ^ k, cb), :].astype(out.dtype)


def reduce_side(sizes, idx, *refs):
    refs, out = refs[:-1], refs[-1]
    at = 0
    for size in sizes:
        total = refs[0][...].astype(F32)
        for ref in refs[1:size]:
            total += ref[...].astype(F32)
        out[:, :, at : at + total.shape[2]] = total.astype(BF16)
        refs = refs[size:]
        at += total.shape[2]


def fold(nz, fy, idx, got, out):
    cs = got.shape[1]
    for f in range(fy):
        total = got[f].astype(F32)
        for z in range(1, nz):
            total += got[z * fy + f].astype(F32)
        out[f * cs : (f + 1) * cs, :] = total.astype(BF16)


def own_rows(count, spans, idx, *refs):
    pieces, outs, stack = refs[:count], refs[count:-1], refs[-1]
    for k, ref in enumerate(pieces):
        at = idx[2] ^ k
        stack[at % 2, at // 2] = ref[...]
    sides, height = stack.shape[1], stack.shape[2]
    fy_cb = [(f, x) for f in range(PEERS) for x in range(sides)]
    cb = height // PEERS
    for half in range(2):
        whole = jnp.concatenate(
            [stack[half, x, f * cb : (f + 1) * cb, :].astype(F32) for f, x in fy_cb], axis=0
        ).T
        at = 0
        for span, group in spans:
            begin = at
            for n in group:
                out = outs[n]
                rows = out.shape[0] // 2
                out[half * rows : (half + 1) * rows, :] = whole[begin : begin + rows]
                begin += rows
            at += span


def entry_back(small, idx, *refs):
    pieces = refs[:PEERS]
    image, norm, gain, shift, grad_pre, sums = refs[PEERS:]
    c_in = gain.shape[1]
    side = 2 * small
    grad = pieces[0][...].astype(F32)
    for ref in pieces[1:]:
        grad += ref[...].astype(F32)
    order = pixel_order(small, side * side, lambda y, x: y * side + x)
    high = grad.astype(BF16)
    low = (grad - high.astype(F32)).astype(BF16)
    grad = sum(
        lax.dot_general(order, part, (((0,), (0,)), ((), ())), preferred_element_type=F32)
        for part in (high, low)
    )
    normed = (image[...].astype(F32) - norm[0:1, :c_in]) * norm[1:2, :c_in]
    g = gelu_slope(gain[...] * normed + shift[...]) * grad
    grad_pre[...] = g
    sums[...] = jnp.zeros_like(sums)
    sums[0:1, :c_in] = jnp.sum(g * normed, axis=0, keepdims=True)
    sums[1:2, :c_in] = jnp.sum(g, axis=0, keepdims=True)


def bundle(idx, first, second, third, sums, out):
    out[...] = jnp.zeros_like(out)
    out[0:8, :] = sums[...]
    for k, ref in enumerate((first, second, third)):
        out[8 + 2 * k : 10 + 2 * k, : ref.shape[1]] = ref[0:2]


def unbundle(idx, *refs):
    out, six, order = refs[-3:]
    got = in_order(refs[:-3], idx[0], order)
    total = got[0][0:8]
    for g in got[1:]:
        total = total + g[0:8]
    out[...] = total
    cs = six.shape[1] // PEERS
    six[...] = jnp.concatenate([g[8:16, :cs] for g in got], axis=1)


def entry_grad(nz, idx, *refs):
    sums = refs[:nz]
    grad_pre, image, weight, norm, gain, gain_grad, shift_grad, out, order = refs[nz:]
    got = in_order(sums, idx[1], order)
    total = got[0]
    for g in got[1:]:
        total = total + g
    gain_grad[...] = total[0:1]
    shift_grad[...] = total[1:2]
    c_in = gain.shape[1]
    scale = norm[1:2, :c_in]
    normed = (image[...].astype(F32) - norm[0:1, :c_in]) * scale
    out[...] = gain[...] * scale * (
        grad_pre[...]
        - weight[:, 0:1]
        * (shift_grad[0:1, :c_in] + normed * gain_grad[0:1, :c_in])
        / norm[2:3, :c_in]
    )


def program(
    nx,
    ny,
    images,
    valid_count,
    pixel_mask,
    gain_entry,
    shift_entry,
    conv_first,
    gain_middle,
    shift_middle,
    conv_second,
    projection,
    gain_inner,
    shift_inner,
    conv_third,
    gain_last,
    shift_last,
    conv_fourth,
    cotangent,
):
    fy = PEERS
    nz = ny // fy
    sides = nx // 2
    side, c_in = images.shape[1], images.shape[3]
    small = side // 2
    area = small * small
    c_out = conv_first.shape[1]
    cs = c_out // PEERS
    cb = cs // sides
    width = PEERS * area
    lanes = c_in + 64
    padded = span_of(c_in)
    gx, gy = lax.axis_index("gx"), lax.axis_index("gy")
    me = gy % fy
    mine = gy // fy
    run = Order(jnp.stack([me, mine, gx, gy]).astype(jnp.int32))
    part = functools.partial

    def to_slice(piece, k):
        return lax.ppermute(piece, "gy", [(j, j // fy * fy + (j % fy ^ k)) for j in range(ny)])

    def share(pieces):
        return [pieces[0]] + [to_slice(pieces[k], k) for k in range(1, PEERS)]

    def to_gx(piece, k):
        return lax.ppermute(piece, "gx", [(i, i ^ k) for i in range(nx)])

    def pool_gx(piece):
        return [piece] + [to_gx(piece, k) for k in range(1, nx)]

    def pool_z(piece):
        out = [piece]
        for k in range(1, nz):
            perm = [(j, (j // fy ^ k) * fy + j % fy) for j in range(ny)]
            out.append(lax.ppermute(piece, "gy", perm))
        return out

    def over_x(block):
        return {0: block, **{k: to_gx(block, k) for k in range(2, nx, 2)}}

    def over_core(held, *then):
        held = {k: after(v, *then) for k, v in held.items()} if then else dict(held)
        for k in list(held):
            held[k + 1] = to_gx(held[k], 1)
        return [held[k] for k in sorted(held)]

    def turn(block):
        return lax.all_to_all(block, "gy", 0, 0, tiled=True)

    unit_first, unit_skip = conv_first.shape[0] // 2, projection.shape[0] // 2
    unit_mid = conv_second.shape[0] // 2
    span_first, span_mid = span_of(unit_first + unit_skip), span_of(unit_mid)
    tile, tile16 = shape((cs, width)), shape((cs, width), BF16)
    long16 = shape((cs, width + 128), BF16)
    cols, stat, entry_stat = shape((cs, 128)), shape((8, cs)), shape((8, lanes))
    shifted16 = shape((9 * cs, width), BF16)
    full16 = shape((c_out, width), BF16)
    whole16 = shape((9 * cs, c_out), BF16)

    def halves(span, channels):
        return pltpu.VMEM((2, cs // channels, ny, channels, span), BF16)

    def ready(span, sections, *weights):
        out = shape((ny, cb, span * len(sections)), BF16)
        return run(
            part(entry_weights, cs, fy, sections), out, weights, cost=24 * len(sections)
        )

    def merge(pieces, kernel):
        like = pieces[0].shape
        return run(kernel, shape(like), pieces, [pltpu.VMEM((nx, *like), F32)])

    add_gx = part(add_rows, 2)

    def activate(value, params, pooled, cot=None):
        more = [] if cot is None else [cot]
        outs = [tile16] if cot is None else [long16] * PEERS
        return run(
            part(act_block, nz),
            [tile, cols] + outs,
            [value, params, *pooled, *more],
            [pltpu.VMEM((nz, 8, cs), F32)]
            + ([] if cot is None else [pltpu.VMEM((c_out, 128), F32)]),
            far=(0, 1),
        )

    def convolve(pieces, weights, base, section=0, last=False):
        more = [] if base is None else [base]
        outs = [shape((cs, 128), BF16)] * PEERS + [full16]
        return run(
            part(conv_block, nx, base is not None, last, unit_mid, section, area, small),
            outs if last else [tile, stat, full16, whole16],
            [*pieces, narrow, *weights, *more],
            [pltpu.VMEM((9 * cs, width), F32)] + ([] if last else [halves(span_mid, cb)]),
            cost=25,
            far=() if last else (2, 3),
        )

    def slope(parts, normed, params):
        return run(gelu_back, [tile, stat], [*parts, normed, params])

    def back(grad_pre, normed, scales, params, pooled, weights, base, riders=()):
        more = list(riders) if base is None else [base]
        return run(
            part(norm_back, nz, base is not None, False, area, small),
            [stat, shifted16]
            + ([long16] * PEERS if base is None else [tile16] * (PEERS + 1)),
            [grad_pre, normed, scales, params, narrow, *pooled, *more, weights],
            [pltpu.VMEM((c_out, width), F32), pltpu.VMEM((nz, 8, cs), F32)],
            cost=18,
        )

    def grad_of(kernel, span, shifted, act, scratch):
        own, other = run(
            kernel,
            [shape((ny, cs, span)), shape((ny, cs, span), BF16)],
            [shifted, act],
            [scratch, pltpu.VMEM((2, ny, cs, span), F32)],
            cost=28,
        )
        return own, to_gx(other, 1)

    def grad_mid(shifted, act):
        return grad_of(
            part(weight_grad, unit_mid), span_mid, shifted, act, pltpu.VMEM((9 * cs, c_out), F32)
        )

    def over_pair(own, other):
        span = own.shape[2]
        return run(
            part(reduce_core, 1),
            [shape((ny, cb, span))] + [shape((ny, cb, span), BF16)] * (sides - 1),
            [own, other],
            [pltpu.VMEM((ny, cs, span), F32)],
        )

    def to_sides(parts, *then):
        parts = [after(p, *then) for p in parts] if then else parts
        return [parts[0]] + [to_gx(parts[k], 2 * k) for k in range(1, sides)]

    def over_sides(*groups):
        span = sum(parts[0].shape[2] for parts in groups)
        return run(
            part(reduce_side, tuple(len(parts) for parts in groups)),
            shape((ny, cb, span), BF16),
            [p for parts in groups for p in parts],
        )

    def folded(got):
        out = shape((fy * cb, got.shape[2]), BF16)
        return over_core(over_x(run(part(fold, nz, fy), out, [got])))

    def rows_of(pieces, spans, *rows):
        return run(
            part(own_rows, nx, spans),
            [shape((r, c_out)) for r in rows],
            pieces,
            [pltpu.VMEM((2, sides, fy * cb, pieces[0].shape[1]), BF16)],
            cost=30,
        )

    def own(gain, shift):
        pair = jnp.stack([gain, shift], axis=1)
        return lax.dynamic_slice_in_dim(pair, me * cs, cs, axis=0)

    p_middle = own(gain_middle, shift_middle)
    p_inner = own(gain_inner, shift_inner)
    p_last = own(gain_last, shift_last)
    g_entry, s_entry = gain_entry[None], shift_entry[None]
    pixels = images.reshape(side * side, c_in)

    image, wide = run(
        part(entry_image, small),
        [shape((4 * area, lanes), BF16), shape((4 * area, 128))],
        [pixels, pixel_mask.reshape(side, side), valid_count],
        scalars=1,
    )
    group = share([image] * PEERS)
    out_first = ready(span_first, (2,), conv_first, projection)
    stats = run(part(entry_stats, area), entry_stat, group)
    pieces = pool_gx(stats)
    got_first = turn(after(out_first, *group[1:]))
    got_first = over_core(over_x(after(got_first, *pieces[1:])))
    pooled = pool_z(merge(pieces, merge_stats))
    out_middle = ready(span_mid, (1, 1), conv_second, conv_third)
    got_middle = turn(after(out_middle, pooled[-1]))
    out_fourth = ready(span_mid, (1,), conv_fourth)
    first, skipped, stats, norm_one, narrow, act_one, w_first = run(
        part(entry_block, nz, nx, unit_first, unit_skip, area, small),
        [
            tile,
            tile,
            stat,
            entry_stat,
            shape((8, width)),
            shape((4, width, c_in), BF16),
            shape((10 * cs, c_in), BF16),
        ],
        [*group, *pooled, g_entry, s_entry, *got_first],
        [
            pltpu.VMEM((nz, 8, lanes), F32),
            pltpu.VMEM((width, lanes), BF16),
            pltpu.VMEM((cs, span_of(9 * c_in)), BF16),
            halves(span_first, cb),
        ],
        cost=40,
        far=(3, 5, 6),
    )

    merged = merge(pool_gx(stats), merge_stats)
    got_middle = over_x(after(got_middle, merged))
    pooled = pool_z(merged)
    got_fourth = turn(after(out_fourth, pooled[-1]))
    normed_two, scale_two, *messages = activate(
        first, p_middle, pooled, cotangent.reshape(area, c_out)
    )
    pieces = share(messages)
    got_middle = over_core(got_middle, *pieces[1:])
    hidden, stats, act_two, w_second = convolve(pieces, got_middle, skipped)
    cot_parts = pieces
    merged = merge(pool_gx(stats), merge_stats)
    got_fourth = over_x(after(got_fourth, merged))
    pooled = pool_z(merged)
    normed_three, scale_three, act = activate(hidden, p_inner, pooled)
    pieces = share([act] * PEERS)
    third, stats, act_three, w_third = convolve(pieces, got_middle, None, section=1)
    got_fourth = over_core(got_fourth, stats)
    merged = merge(pool_gx(stats), merge_stats)

    cot, shifted_four, w_fourth, *parts = run(
        part(last_back, nx, unit_mid, 0, area, small),
        [tile, shifted16, whole16] + [tile16] * PEERS,
        [*cot_parts, *got_fourth],
        [pltpu.VMEM((c_out, width), F32), halves(span_mid, cb)],
        cost=18,
        far=(0, 1, 2),
    )
    parts = share(parts)
    normed_four, scale_four, act = activate(third, p_last, pool_z(merged))
    pieces = share([act] * PEERS)
    grad_pre, sums = slope(parts, normed_four, p_last)
    sums = pool_gx(sums)
    *riders, act_four = convolve(pieces, [w_fourth], hidden, last=True)
    sums = pool_z(merge(sums, add_gx))
    fourth = grad_mid(shifted_four, act_four)
    last_sums, shifted_three, *parts = back(
        grad_pre, normed_four, scale_four, p_last, sums, w_third, None, riders
    )
    parts = share(parts)
    fourth = over_pair(*fourth)
    grad_pre, sums = slope(parts, normed_three, p_inner)
    sums = pool_gx(sums)
    third = grad_mid(shifted_three, act_three)
    merged = merge(sums, add_gx)
    fourth = to_sides(fourth, merged)
    sums = pool_z(merged)
    out = run(
        join_result, shape((area, c_out), BF16), parts, [pltpu.VMEM((c_out, 128), F32)]
    )
    inner_sums, shifted_two, grad_hidden, *parts = back(
        grad_pre, normed_three, scale_three, p_inner, sums, w_second, cot
    )
    parts = share(parts)
    third = to_sides(over_pair(*third))
    fourth = over_sides(fourth)
    grad_pre, sums = slope(parts, normed_two, p_middle)
    sums = pool_gx(sums)
    late = over_sides([fourth], third)
    second = grad_mid(shifted_two, act_two)
    merged = merge(sums, add_gx)
    sums = pool_z(merged)
    late = turn(after(late, sums[-1]))
    second = to_sides(over_pair(*second), merged)
    middle_sums, shifted_one, *parts = run(
        part(norm_back, nz, False, True, area, small),
        [stat, shape((10 * cs, width), BF16)] + [shape((4 * area, c_in), BF16)] * PEERS,
        [
            grad_pre,
            normed_two,
            scale_two,
            p_middle,
            narrow,
            *sums,
            w_first,
            grad_hidden,
        ],
        [pltpu.VMEM((4, width, c_in), F32), pltpu.VMEM((nz, 8, cs), F32)],
        cost=18,
    )

    first = grad_of(
        part(weight_grad_first, unit_first, unit_skip),
        span_first,
        shifted_one,
        act_one,
        pltpu.VMEM((cs, span_of(9 * c_in + span_first + 128)), F32),
    )
    parts = share(parts)
    first = to_sides(over_pair(after(first[0], parts[1]), first[1]))
    second = over_sides(second)
    grad_pre, sums = run(
        part(entry_back, small),
        [shape((4 * area, c_in)), shape((8, padded))],
        [*parts, pixels, norm_one, g_entry, s_entry],
        cost=13,
    )
    message = run(bundle, shape((16, padded)), [middle_sums, inner_sums, last_sums, sums])
    message = share([message] * PEERS)
    early = turn(over_sides([second], first))
    sums, six = run(
        unbundle,
        [shape((8, padded)), shape((8, c_out))],
        message,
        [pltpu.VMEM((PEERS, 16, padded), F32)],
    )
    sums = pool_z(merge(pool_gx(sums), add_gx))
    late = folded(late)
    early = folded(early)
    gain_entry_grad, shift_entry_grad, image_grad = run(
        part(entry_grad, nz),
        [shape((1, padded)), shape((1, padded)), shape((4 * area, c_in))],
        [*sums, grad_pre, pixels, wide, norm_one, g_entry],
        [pltpu.VMEM((nz, 8, padded), F32)],
    )
    fourth_grad, third_grad = rows_of(
        late, ((span_mid, (0,)), (span_mid, (1,))), 2 * unit_mid, 2 * unit_mid
    )
    second_grad, first_grad, skip_grad = rows_of(
        early,
        ((span_mid, (0,)), (span_first, (1, 2))),
        2 * unit_mid,
        2 * unit_first,
        2 * unit_skip,
    )
    return (
        out.reshape(1, small, small, c_out),
        image_grad.reshape(1, side, side, c_in),
        gain_entry_grad[0, :c_in],
        shift_entry_grad[0, :c_in],
        first_grad,
        six[0],
        six[1],
        second_grad,
        skip_grad,
        six[2],
        six[3],
        third_grad,
        six[4],
        six[5],
        fourth_grad,
    )


def solution(mesh):
    whole = P(("gx", "gy"), None, None, None)
    rows = P("gy", None)
    return jax.shard_map(
        functools.partial(program, mesh.shape["gx"], mesh.shape["gy"]),
        mesh=mesh,
        in_specs=(
            whole,
            P(("gx", "gy")),
            P(("gx", "gy"), None, None),
            P(),
            P(),
            rows,
            P(),
            P(),
            rows,
            rows,
            P(),
            P(),
            rows,
            P(),
            P(),
            rows,
            whole,
        ),
        out_specs=(
            whole, whole, P(), P(), rows, P(), P(), rows, rows, P(), P(), rows, P(), P(), rows,
        ),
        check_vma=False,
    )
```

```python
import functools

import jax
import jax.numpy as jnp
from jax import lax
from jax.experimental import pallas as pl
from jax.experimental.pallas import tpu as pltpu
from jax.sharding import PartitionSpec as P

EPS = 1e-05
COST = 6 * 10**7
F32 = jnp.float32
BF16 = jnp.bfloat16
PEERS = 4
C0 = 0.7978845608028654
C1 = 0.044715
VMEM = pl.BlockSpec(memory_space=pltpu.VMEM)
SMEM = pl.BlockSpec(memory_space=pltpu.SMEM)


def gelu(v):
    return 0.5 * v * (1.0 + jnp.tanh(C0 * (v + C1 * (v * v * v))))


def gelu_slope(v):
    t = jnp.tanh(C0 * (v + C1 * (v * v * v)))
    return 0.5 * (1.0 + t) + 0.5 * v * (1.0 - t * t) * (C0 * (1.0 + 3.0 * C1 * (v * v)))


def after(value, *others):
    return lax.optimization_barrier((value, *others))[0]


class Far:
    def __init__(self, near, far, sem):
        self.near, self.shape, self.dtype = near, near.shape, near.dtype
        self.copy = pltpu.make_async_copy(near, far, sem)
        self.sent = False

    def __getitem__(self, at):
        return self.near[at]

    def __setitem__(self, at, value):
        self.near[at] = value

    def send(self):
        if not self.sent:
            self.copy.start()
            self.sent = True


def send(ref):
    if isinstance(ref, Far):
        ref.send()


def with_far(kernel, n_in, n_out, far, *refs):
    ins, outs, rest = refs[:n_in], list(refs[n_in : n_in + n_out]), list(refs[n_in + n_out :])
    if far:
        sems = rest.pop()
        near = rest[len(rest) - len(far) :]
        del rest[len(rest) - len(far) :]
        for n, at in enumerate(far):
            outs[at] = Far(near[n], outs[at], sems.at[n])
    kernel(*ins, *outs, *rest)
    for at in far:
        outs[at].send()
    for at in far:
        outs[at].copy.wait()


class Order:
    def __init__(self, idx):
        self.idx = idx
        self.last = ()

    def __call__(self, kernel, outs, args, scratch=(), scalars=0, cost=7, far=()):
        idx = after(self.idx, *self.last)
        many = isinstance(outs, (list, tuple))
        shapes = list(outs) if many else [outs]
        more = [pltpu.VMEM(shapes[at].shape, shapes[at].dtype) for at in far]
        if far:
            more.append(pltpu.SemaphoreType.DMA((len(far),)))
        got = pl.pallas_call(
            functools.partial(with_far, kernel, 1 + len(args), len(shapes), tuple(far)),
            out_shape=shapes,
            in_specs=[SMEM] + [VMEM] * (len(args) - scalars) + [SMEM] * scalars,
            out_specs=[
                pl.BlockSpec(memory_space=pl.ANY) if at in far else VMEM
                for at in range(len(shapes))
            ],
            scratch_shapes=list(scratch) + more,
            compiler_params=pltpu.CompilerParams(vmem_limit_bytes=16 * 1024 * 1024),
            cost_estimate=pl.CostEstimate(
                flops=cost * COST, bytes_accessed=1024, transcendentals=0
            ),
        )(idx, *args)
        near = [v for at, v in enumerate(got) if at not in far]
        self.last = (near[0] if near else got[0],)
        return got if many else got[0]


def shape(dims, dtype=F32):
    return jax.ShapeDtypeStruct(dims, dtype)


def rows_at(index, count):
    return pl.ds(pl.multiple_of(index * count, count), count)


def as_rows(parts):
    height = parts[0].shape[0]
    lane = lax.broadcasted_iota(jnp.int32, (height, 128), 1)
    out = jnp.zeros((height, 128), F32)
    for k, part in enumerate(parts):
        out = jnp.where(lane == k, part, out)
    return out.T[0:8]


def as_columns(rows):
    return jnp.concatenate([rows, jnp.zeros((120, rows.shape[1]), F32)], axis=0).T


def in_order(refs, me, scratch):
    for k, ref in enumerate(refs):
        scratch[me ^ k] = ref[...]
    return [scratch[k] for k in range(len(refs))]


def merge_moments(stats):
    total = sum(n for _, _, n in stats)
    mean = sum(n * m for m, _, n in stats) / total
    squares = sum(q + n * (m - mean) * (m - mean) for m, q, n in stats)
    return mean, squares, total


def merge_rows(refs):
    mean, squares, total = merge_moments([(g[0:1], g[1:2], g[2:3]) for g in refs])
    return mean, squares, total, sum(g[3:4] for g in refs)


def pixel(width, area, small):
    lane = lax.broadcasted_iota(jnp.int32, (1, width), 1) % area
    return lane // small, lane % small


def inside(row, col, drow, dcol, small):
    return (row + drow >= 0) & (row + drow < small) & (col + dcol >= 0) & (col + dcol < small)


def moved(value, step):
    shift = (-step) % value.shape[1]
    return pltpu.roll(value, shift, 1) if shift else value


OFFSETS = [(0, krow - 1, kcol - 1) for krow in range(3) for kcol in range(3)]

STRIDED = [
    ((krow != 1) * 2 + (kcol != 1), -(krow == 0), -(kcol == 0))
    for krow in range(3)
    for kcol in range(3)
] + [(0, 0, 0)]
PLACED = sorted(range(10), key=lambda k: (STRIDED[k][0], k))
PHASES = [[k for k in PLACED if STRIDED[k][0] == phase] for phase in range(4)]


def row_of(k, cs):
    at = PLACED.index(k)
    return slice(at * cs, (at + 1) * cs)


def phase_rows(phase, cs):
    first, last = PHASES[phase][0], PHASES[phase][-1]
    return slice(PLACED.index(first) * cs, (PLACED.index(last) + 1) * cs)


def masked_stats(value, weight, n):
    mean = jnp.sum(value * weight, axis=1, keepdims=True) / n
    centred = value - mean
    return mean, jnp.sum(weight * centred * centred, axis=1, keepdims=True)


def span_of(rows):
    return -(-rows // 128) * 128


def one_hot(height, width, shift):
    row = lax.broadcasted_iota(jnp.int32, (height, width), 0)
    col = lax.broadcasted_iota(jnp.int32, (height, width), 1)
    return (col == row + shift).astype(BF16)


def pick32(left, right, dims=((1,), (0,))):
    return lax.dot_general(left, right, (dims, ((), ())), preferred_element_type=F32)


def pick(left, right, dims=((1,), (0,))):
    return pick32(left, right, dims).astype(BF16)


def lane_tile(held, tile, rows, span):
    sides, ny = held.shape[1], held.shape[2]
    lane = lax.broadcasted_iota(jnp.int32, (1, 128), 1)
    out = None
    for v in range(2 * ny):
        begin = rows * v - tile * 128
        if begin >= 128 or begin + rows <= 0:
            continue
        at = (tile - rows * v // 128) * 128 % span
        part = jnp.concatenate(
            [held[v % 2, x, v // 2, :, at : at + 128].astype(F32) for x in range(sides)], axis=0
        )
        if begin > 0 or begin + rows < 128:
            own = (lane >= begin) & (lane < begin + rows)
            part = jnp.where(own, part, 0.0)
        out = part if out is None else out + part
    return out.astype(BF16)


def pixel_order(small, width, of):
    area = small * small
    row = lax.broadcasted_iota(jnp.int32, (4 * area, width), 0)
    col = lax.broadcasted_iota(jnp.int32, (4 * area, width), 1)
    phase, pix = row // area, row % area
    y = 2 * (pix // small) + phase // 2
    x = 2 * (pix % small) + phase % 2
    return (col == of(y, x)).astype(BF16)


def entry_image(small, idx, image, mask, valid, out, weight):
    side = 2 * small
    c_in = image.shape[1]
    count = side * side
    order = pixel_order(small, count, lambda y, x: y * side + x)
    out[:, :c_in] = pick(order, image[...])
    live = (valid[0] > 0).astype(F32)
    row = lax.broadcasted_iota(jnp.int32, (count, side), 0)
    col = lax.broadcasted_iota(jnp.int32, (count, side), 1)
    by_row = jnp.dot(
        (row // side == col).astype(BF16),
        mask[...].astype(F32).astype(BF16),
        preferred_element_type=F32,
    )
    column = jnp.sum(jnp.where(row % side == col, by_row, 0.0), axis=1, keepdims=True) * live
    lane = lax.broadcasted_iota(jnp.int32, (count, 128), 1)
    spread = jnp.where(lane == 0, column, 0.0)
    weight[...] = spread
    out[:, c_in:] = pick(order, spread.astype(BF16))[:, : out.shape[1] - c_in]


def entry_weights(cs, fy, sections, idx, *refs):
    weights, out = list(refs[:-1]), refs[-1]
    ny, cb, lanes = out.shape
    span = lanes // len(sections)
    gx, gy = idx[2], idx[3]
    core, side = gx % 2, (gx // 2 if cb < cs else 0)
    c_out = weights[0].shape[1]
    row = lax.broadcasted_iota(jnp.int32, (fy * cb, c_out), 0)
    col = lax.broadcasted_iota(jnp.int32, (fy * cb, c_out), 1)
    chosen = (col == row // cb * cs + side * cb + row % cb).astype(BF16)
    for n, count in enumerate(sections):
        begin = weights[0].shape[0] // 2 * (2 * gy + core) % 128
        total = None
        for _ in range(count):
            weight = weights.pop(0)
            rows = weight.shape[0]
            half = rows // 2
            mine = pick(chosen, weight[...], ((1,), (1,)))
            row = lax.broadcasted_iota(jnp.int32, (rows, span), 0) - core * half
            col = lax.broadcasted_iota(jnp.int32, (rows, span), 1)
            place = (row >= 0) & (row < half) & (
                (col == row + begin) | (col == row + begin - span)
            )
            part = pick32(mine, place.astype(BF16))
            total = part if total is None else total + part
            begin = begin + half
        for j in range(ny):
            out[j, :, n * span : (n + 1) * span] = total[
                (j % fy) * cb : (j % fy + 1) * cb
            ].astype(BF16)


def hold(gx, messages, held, section=0):
    span = held.shape[4]
    for k, ref in enumerate(messages):
        at = gx ^ k
        side = at // 2 if held.shape[1] > 1 else 0
        held[at % 2, side] = ref[:, :, section * span : (section + 1) * span]


def assemble(held, out, rows):
    cs, span = held.shape[1] * held.shape[3], held.shape[4]
    tiles = out.shape[1] // 128
    for k in range(9):
        for q in range(tiles):
            out[k * cs : (k + 1) * cs, q * 128 : (q + 1) * 128] = lane_tile(
                held, tiles * k + q, rows, span
            )


def assemble_first(held, out, flat, rows, extra):
    cs, span = held.shape[1] * held.shape[3], held.shape[4]
    c_in = out.shape[1]
    tiles = flat.shape[1] // 128
    for tile in range(tiles):
        flat[:, tile * 128 : (tile + 1) * 128] = lane_tile(held, tile, rows, span)
    for k in range(9):
        begin = k * c_in
        base = begin // 128 * 128
        reach = min(-(-(begin + c_in) // 128) * 128, flat.shape[1])
        move = one_hot(c_in, reach - base, begin - base)
        out[row_of(k, cs), :] = pick(flat[:, base:reach], move, ((1,), (1,)))
    total = None
    for v in range(2 * held.shape[2]):
        row = lax.broadcasted_iota(jnp.int32, (span, c_in), 0)
        col = lax.broadcasted_iota(jnp.int32, (span, c_in), 1)
        at = col - extra * v
        begin = rows * v % 128 + rows
        place = (at >= 0) & (at < extra) & ((row == at + begin) | (row == at + begin - span))
        part = jnp.concatenate(
            [
                pick32(held[v % 2, x, v // 2], place.astype(BF16))
                for x in range(held.shape[1])
            ],
            axis=0,
        )
        total = part if total is None else total + part
    out[row_of(9, cs), :] = total.astype(BF16)


def entry_stats(area, idx, *refs):
    images, out = refs[:PEERS], refs[PEERS]
    lanes = out.shape[1]
    first = jnp.zeros((1, lanes), F32)
    wide = jnp.zeros((1, 1), F32)
    narrow = jnp.zeros((1, 1), F32)
    c_in = lanes - 64
    for ref in images:
        x = ref[...].astype(F32)
        w = x[:, c_in : c_in + 1]
        first += jnp.sum(x * w, axis=0, keepdims=True)
        wide += jnp.sum(w, axis=0, keepdims=True)
        narrow += jnp.sum(w[:area], axis=0, keepdims=True)
    mean = first / wide
    squares = jnp.zeros((1, lanes), F32)
    for ref in images:
        x = ref[...].astype(F32)
        w = x[:, c_in : c_in + 1]
        d = x - mean
        squares += jnp.sum(d * d * w, axis=0, keepdims=True)
    out[...] = jnp.zeros_like(out)
    out[0:1, :] = mean
    out[1:2, :] = squares
    out[2:3, :] = jnp.broadcast_to(wide, (1, lanes))
    out[3:4, :] = jnp.broadcast_to(narrow, (1, lanes))


def entry_block(nz, nx, rows, extra, area, small, idx, *refs):
    images = refs[:PEERS]
    stats, rest = refs[PEERS : PEERS + nz], refs[PEERS + nz :]
    gain, shift, messages, rest = rest[0], rest[1], rest[2 : 2 + nx], rest[2 + nx :]
    first, skipped, out_stats, norm, narrow, act, w_first = rest[:7]
    order, masks, flat, held = rest[7:]
    me, mine = idx[0], idx[1]
    c_in = gain.shape[1]
    lanes = norm.shape[1]
    cs = first.shape[0]
    width = first.shape[1]
    hold(idx[2], messages, held)
    assemble_first(held, w_first, flat, rows, extra)
    send(w_first)
    mean, squares, total, count = merge_rows(in_order(stats, mine, order))
    scale = lax.rsqrt(squares / total + EPS)
    norm[...] = jnp.zeros_like(norm)
    norm[0:1, :] = mean
    norm[1:2, :] = scale
    norm[2:3, :] = total
    norm[3:4, :] = count
    for k, ref in enumerate(images):
        x = ref[...]
        v = x[:, :c_in].astype(F32)
        pre = gain[...] * ((v - mean[:, :c_in]) * scale[:, :c_in]) + shift[...]
        a = gelu(pre).astype(BF16)
        for phase in range(4):
            act[phase, rows_at(me ^ k, area), :] = a[phase * area : (phase + 1) * area]
        masks[rows_at(me ^ k, area), :] = x[:area]
    send(act)
    send(norm)
    ones = (lax.broadcasted_iota(jnp.int32, (8, lanes), 1) == c_in).astype(BF16)
    weight8 = lax.dot_general(
        ones, masks[...], (((1,), (1,)), ((), ())), preferred_element_type=F32
    )
    narrow[...] = weight8
    weight = weight8[0:1]
    row, col = pixel(width, area, small)
    total_first = jnp.zeros((cs, width), F32)
    for phase in range(4):
        group = lax.dot_general(
            w_first[phase_rows(phase, cs), :],
            act[phase],
            (((1,), (1,)), ((), ())),
            preferred_element_type=F32,
        )
        for at, k in enumerate(PHASES[phase]):
            y = group[at * cs : (at + 1) * cs]
            if k == 9:
                skipped[...] = y
                continue
            _, drow, dcol = STRIDED[k]
            y = moved(y, drow * small + dcol)
            total_first += jnp.where(inside(row, col, drow, dcol, small), y, 0.0)
    first[...] = total_first
    n = jnp.sum(weight, axis=1, keepdims=True)
    mean2, squares = masked_stats(total_first, weight, n)
    out_stats[...] = as_rows((mean2, squares, n))


def merge_stats(idx, *refs):
    out, order = refs[-2:]
    mean, squares, total, count = merge_rows(in_order(refs[:-2], idx[2], order))
    out[...] = jnp.zeros_like(out)
    out[0:1] = mean
    out[1:2] = squares
    out[2:3] = total
    out[3:4] = count


def add_rows(which, idx, *refs):
    out, order = refs[-2:]
    got = in_order(refs[:-2], idx[which], order)
    total = got[0]
    for g in got[1:]:
        total = total + g
    out[...] = total


def act_block(nz, idx, *refs):
    value, params = refs[:2]
    stats, rest = refs[2 : 2 + nz], refs[2 + nz :]
    if rest[-1].shape[1] == 128:
        cot, normed, scales, outs, order, stack = (*rest[:3], rest[3:-2], *rest[-2:])
    else:
        cot, normed, scales, outs, order = (None, *rest[:2], rest[2:-1], rest[-1])
    mean, squares, total, _ = merge_rows(in_order(stats, idx[1], order))
    rows = jnp.concatenate(
        [mean, lax.rsqrt(squares / total + EPS), total, jnp.zeros((5, mean.shape[1]), F32)], axis=0
    )
    cols = as_columns(rows)
    norm = (value[...] - cols[:, 0:1]) * cols[:, 1:2]
    normed[...] = norm
    send(normed)
    scales[...] = cols
    send(scales)
    act = gelu(params[:, 0:1] * norm + params[:, 1:2]).astype(BF16)
    cs, width = norm.shape
    if cot is not None:
        c = cot[...].astype(F32)
        stack[...] = jnp.concatenate([c, c], axis=0).T
    for k, out in enumerate(outs):
        out[:, :width] = act
        if cot is not None:
            out[:, width:] = stack[rows_at(idx[0] ^ k, cs), :].astype(BF16)


def conv_block(nx, added, last, rows, section, area, small, idx, *refs):
    pieces = refs[:PEERS]
    narrow, rest = refs[PEERS], refs[PEERS + 1 :]
    if last:
        weights, rest = rest[0], rest[1:]
    else:
        messages, rest = rest[:nx], rest[nx:]
    base, rest = (rest[0], rest[1:]) if added else (None, rest)
    me = idx[0]
    cs, width = pieces[0].shape[0], narrow.shape[1]
    if last:
        outs, act, spread = rest[:PEERS], rest[PEERS], rest[PEERS + 1]
    else:
        value, out_stats, act, whole, spread, held = rest
        hold(idx[2], messages, held, section)
        assemble(held, whole, rows)
        send(whole)
        weights = whole
    for k, ref in enumerate(pieces):
        act[rows_at(me ^ k, cs), :] = ref[:, :width]
    send(act)
    spread[...] = jnp.dot(weights[...], act[...], preferred_element_type=F32)
    row, col = pixel(width, area, small)
    total = base[...] if added else jnp.zeros((cs, width), F32)
    for k, (_, drow, dcol) in enumerate(OFFSETS):
        y = moved(spread[k * cs : (k + 1) * cs, :], drow * small + dcol)
        total += jnp.where(inside(row, col, drow, dcol, small), y, 0.0)
    if last:
        result = total.astype(BF16)
        lane = lax.broadcasted_iota(jnp.int32, (width, 128), 0)
        slot = lax.broadcasted_iota(jnp.int32, (width, 128), 1)
        for k, out in enumerate(outs):
            out[...] = pick(result, (lane == (me ^ k) * area + slot).astype(BF16))
    else:
        value[...] = total
        weight = narrow[0:1, :]
        n = jnp.sum(weight, axis=1, keepdims=True)
        mean, squares = masked_stats(total, weight, n)
        out_stats[...] = as_rows((mean, squares, n))


def join_result(idx, *refs):
    pieces, (out, stack) = refs[:PEERS], refs[PEERS:]
    cs = pieces[0].shape[0]
    for k, ref in enumerate(pieces):
        stack[rows_at(idx[0] ^ k, cs), :] = ref[:, -128:].astype(F32)
    out[...] = stack[...].T[: out.shape[0]].astype(BF16)


def spread_grad(grad, shifted, area, small, offs, row_at):
    cs, width = grad.shape
    row, col = pixel(width, area, small)
    for k, (_, drow, dcol) in enumerate(offs):
        g = moved(grad, -(drow * small + dcol))
        g = jnp.where(inside(row, col, -drow, -dcol, small), g, 0.0)
        shifted[row_at(k, cs), :] = g.astype(BF16)


def plain_rows(k, cs):
    return slice(k * cs, (k + 1) * cs)


def push_back(me, weights, shifted, partial, outs):
    cs, width = outs[0].shape[0], shifted.shape[1]
    partial[...] = lax.dot_general(
        weights[...], shifted[...], (((0,), (0,)), ((), ())), preferred_element_type=F32
    )
    for k, out in enumerate(outs):
        out[:, :width] = partial[rows_at(me ^ k, cs), :].astype(BF16)


def last_back(nx, rows, section, area, small, idx, *refs):
    pieces, messages, rest = refs[:PEERS], refs[PEERS : PEERS + nx], refs[PEERS + nx :]
    cot, shifted, weights = rest[:3]
    outs = rest[3 : PEERS + 3]
    partial, held = rest[PEERS + 3 :]
    hold(idx[2], messages, held, section)
    assemble(held, weights, rows)
    send(weights)
    me = idx[0]
    cs, width = cot.shape
    image = lax.broadcasted_iota(jnp.int32, (1, width), 1) // area
    grad = jnp.zeros((cs, width), F32)
    for k, ref in enumerate(pieces):
        tiled = jnp.concatenate([ref[:, width:].astype(F32)] * (width // 128), axis=1)
        grad = jnp.where(image == (me ^ k), tiled, grad)
    cot[...] = grad
    send(cot)
    spread_grad(grad, shifted, area, small, OFFSETS, plain_rows)
    send(shifted)
    push_back(me, weights, shifted, partial, outs)


def gelu_back(idx, *refs):
    pieces = refs[:PEERS]
    normed, params, grad_pre, sums = refs[PEERS:]
    width = normed.shape[1]
    grad = pieces[0][:, :width].astype(F32)
    for ref in pieces[1:]:
        grad += ref[:, :width].astype(F32)
    norm = normed[...]
    g = gelu_slope(params[:, 0:1] * norm + params[:, 1:2]) * grad
    grad_pre[...] = g
    sums[...] = as_rows(
        (jnp.sum(g * norm, axis=1, keepdims=True), jnp.sum(g, axis=1, keepdims=True))
    )


def norm_back(nz, added, last, area, small, idx, *refs):
    grad_pre, normed, scales, params, narrow = refs[:5]
    sums = refs[5 : 5 + nz]
    rest = refs[5 + nz :]
    base, rest = (rest[0], rest[1:]) if added else (None, rest)
    me = idx[0]
    cs, width = grad_pre.shape
    order = rest[-1]
    got = in_order(sums, idx[1], order)
    total = got[0]
    for g in got[1:]:
        total = total + g
    cols = as_columns(total)
    gain_grad, shift_grad = cols[:, 0:1], cols[:, 1:2]
    norm = normed[...]
    back = params[:, 0:1] * scales[:, 1:2] * (
        grad_pre[...]
        - narrow[0:1, :] * (shift_grad + norm * gain_grad) / scales[:, 2:3]
    )
    if added:
        back = base[...] + back
    grad = back.astype(BF16).astype(F32)
    if not last:
        riders = ()
        if not added:
            riders, rest = rest[:PEERS], rest[PEERS:]
        weights, sums_out, shifted = rest[:3]
        outs, partial = rest[3 : 3 + PEERS], rest[3 + PEERS]
        for rider, out in zip(riders, outs):
            out[:, width:] = rider[...]
        if added:
            grad_out, outs, partial = rest[3], rest[4 : 4 + PEERS], rest[4 + PEERS]
            grad_out[...] = grad.astype(BF16)
        sums_out[...] = total
        spread_grad(grad, shifted, area, small, OFFSETS, plain_rows)
        push_back(me, weights, shifted, partial, outs)
    else:
        weights, grad_skip, sums_out, shifted = rest[:4]
        outs, partial = rest[4 : 4 + PEERS], rest[4 + PEERS]
        sums_out[...] = total
        spread_grad(grad, shifted, area, small, STRIDED[:9], row_of)
        shifted[row_of(9, cs), :] = grad_skip[...]
        for phase in range(4):
            partial[phase] = lax.dot_general(
                shifted[phase_rows(phase, cs), :],
                weights[phase_rows(phase, cs), :],
                (((0,), (0,)), ((), ())),
                preferred_element_type=F32,
            )
        for k, out in enumerate(outs):
            for phase in range(4):
                out[phase * area : (phase + 1) * area, :] = partial[
                    phase, rows_at(me ^ k, area), :
                ].astype(BF16)


def part_halves(core, units, own, other):
    own[...] = units[core]
    other[...] = units[1 - core].astype(BF16)


def weight_grad(rows, idx, shifted, act, own, other, full, units):
    full[...] = lax.dot_general(
        shifted[...], act[...], (((1,), (1,)), ((), ())), preferred_element_type=F32
    )
    ny, cs, span = own.shape
    tiles = full.shape[1] // 128
    for v in range(2 * ny):
        begin = rows * v % 128
        parts = []
        for q in range((begin + rows + 127) // 128):
            k, p = divmod(rows * v // 128 + q, tiles)
            parts.append(full[k * cs : (k + 1) * cs, p * 128 : (p + 1) * 128])
        window = jnp.concatenate(parts, axis=1)
        units[v % 2, v // 2] = moved(window, begin)[:, :span]
    part_halves(idx[2] % 2, units, own, other)


def weight_grad_first(rows, extra, idx, shifted, act, own, other, flat, units):
    ny, cs, span = own.shape
    c_in = act.shape[2]
    flat[...] = jnp.zeros_like(flat)
    skip = None
    for phase in range(4):
        group = jnp.dot(
            shifted[phase_rows(phase, cs), :], act[phase], preferred_element_type=F32
        ).astype(BF16)
        for at, k in enumerate(PHASES[phase]):
            grad = group[at * cs : (at + 1) * cs]
            if k == 9:
                skip = grad
                continue
            begin = k * c_in
            base = begin // 128 * 128
            reach = -(-(begin + c_in) // 128) * 128
            move = one_hot(c_in, reach - base, begin - base)
            flat[:, base:reach] += jnp.dot(grad, move, preferred_element_type=F32)
    lane = lax.broadcasted_iota(jnp.int32, (1, span), 1)
    for v in range(2 * ny):
        begin = rows * v % 128
        base = rows * v - begin
        window = moved(flat[:, base : base + span + 128], begin)[:, :span]
        row = lax.broadcasted_iota(jnp.int32, (c_in, span), 0)
        col = lax.broadcasted_iota(jnp.int32, (c_in, span), 1)
        place = (row >= extra * v) & (row < extra * (v + 1)) & (col == row - extra * v + rows)
        tail = pick32(skip, place.astype(BF16))
        units[v % 2, v // 2] = jnp.where(lane < rows, window, 0.0) + tail
    part_halves(idx[2] % 2, units, own, other)


def reduce_core(count, idx, *refs):
    own, other, outs, total = refs[:count], refs[count : 2 * count], refs[2 * count : -1], refs[-1]
    cb = outs[0].shape[1]
    at = 0
    for a, b in zip(own, other):
        span = a.shape[2]
        total[:, :, at : at + span] = a[...] + b[...].astype(F32)
        at += span
    for k, out in enumerate(outs):
        for j in range(total.shape[0]):
            out[j] = total[j, rows_at(idx[2] // 2 ^ k, cb), :].astype(out.dtype)


def reduce_side(sizes, idx, *refs):
    refs, out = refs[:-1], refs[-1]
    at = 0
    for size in sizes:
        total = refs[0][...].astype(F32)
        for ref in refs[1:size]:
            total += ref[...].astype(F32)
        out[:, :, at : at + total.shape[2]] = total.astype(BF16)
        refs = refs[size:]
        at += total.shape[2]


def fold(nz, fy, idx, got, out):
    cs = got.shape[1]
    for f in range(fy):
        total = got[f].astype(F32)
        for z in range(1, nz):
            total += got[z * fy + f].astype(F32)
        out[f * cs : (f + 1) * cs, :] = total.astype(BF16)


def own_rows(count, spans, idx, *refs):
    pieces, outs, stack = refs[:count], refs[count:-1], refs[-1]
    for k, ref in enumerate(pieces):
        at = idx[2] ^ k
        stack[at % 2, at // 2] = ref[...]
    sides, height = stack.shape[1], stack.shape[2]
    fy_cb = [(f, x) for f in range(PEERS) for x in range(sides)]
    cb = height // PEERS
    for half in range(2):
        whole = jnp.concatenate(
            [stack[half, x, f * cb : (f + 1) * cb, :].astype(F32) for f, x in fy_cb], axis=0
        ).T
        at = 0
        for span, group in spans:
            begin = at
            for n in group:
                out = outs[n]
                rows = out.shape[0] // 2
                out[half * rows : (half + 1) * rows, :] = whole[begin : begin + rows]
                begin += rows
            at += span


def entry_back(small, idx, *refs):
    pieces = refs[:PEERS]
    image, norm, gain, shift, grad_pre, sums = refs[PEERS:]
    c_in = gain.shape[1]
    side = 2 * small
    grad = pieces[0][...].astype(F32)
    for ref in pieces[1:]:
        grad += ref[...].astype(F32)
    order = pixel_order(small, side * side, lambda y, x: y * side + x)
    high = grad.astype(BF16)
    low = (grad - high.astype(F32)).astype(BF16)
    grad = sum(
        lax.dot_general(order, part, (((0,), (0,)), ((), ())), preferred_element_type=F32)
        for part in (high, low)
    )
    normed = (image[...].astype(F32) - norm[0:1, :c_in]) * norm[1:2, :c_in]
    g = gelu_slope(gain[...] * normed + shift[...]) * grad
    grad_pre[...] = g
    sums[...] = jnp.zeros_like(sums)
    sums[0:1, :c_in] = jnp.sum(g * normed, axis=0, keepdims=True)
    sums[1:2, :c_in] = jnp.sum(g, axis=0, keepdims=True)


def bundle(idx, first, second, third, sums, out):
    out[...] = jnp.zeros_like(out)
    out[0:8, :] = sums[...]
    for k, ref in enumerate((first, second, third)):
        out[8 + 2 * k : 10 + 2 * k, : ref.shape[1]] = ref[0:2]


def unbundle(idx, *refs):
    out, six, order = refs[-3:]
    got = in_order(refs[:-3], idx[0], order)
    total = got[0][0:8]
    for g in got[1:]:
        total = total + g[0:8]
    out[...] = total
    cs = six.shape[1] // PEERS
    six[...] = jnp.concatenate([g[8:16, :cs] for g in got], axis=1)


def entry_grad(nz, idx, *refs):
    sums = refs[:nz]
    grad_pre, image, weight, norm, gain, gain_grad, shift_grad, out, order = refs[nz:]
    got = in_order(sums, idx[1], order)
    total = got[0]
    for g in got[1:]:
        total = total + g
    gain_grad[...] = total[0:1]
    shift_grad[...] = total[1:2]
    c_in = gain.shape[1]
    scale = norm[1:2, :c_in]
    normed = (image[...].astype(F32) - norm[0:1, :c_in]) * scale
    out[...] = gain[...] * scale * (
        grad_pre[...]
        - weight[:, 0:1]
        * (shift_grad[0:1, :c_in] + normed * gain_grad[0:1, :c_in])
        / norm[2:3, :c_in]
    )


def program(
    nx,
    ny,
    images,
    valid_count,
    pixel_mask,
    gain_entry,
    shift_entry,
    conv_first,
    gain_middle,
    shift_middle,
    conv_second,
    projection,
    gain_inner,
    shift_inner,
    conv_third,
    gain_last,
    shift_last,
    conv_fourth,
    cotangent,
):
    fy = PEERS
    nz = ny // fy
    sides = nx // 2
    side, c_in = images.shape[1], images.shape[3]
    small = side // 2
    area = small * small
    c_out = conv_first.shape[1]
    cs = c_out // PEERS
    cb = cs // sides
    width = PEERS * area
    lanes = c_in + 64
    padded = span_of(c_in)
    gx, gy = lax.axis_index("gx"), lax.axis_index("gy")
    me = gy % fy
    mine = gy // fy
    run = Order(jnp.stack([me, mine, gx, gy]).astype(jnp.int32))
    part = functools.partial

    def to_slice(piece, k):
        return lax.ppermute(piece, "gy", [(j, j // fy * fy + (j % fy ^ k)) for j in range(ny)])

    def share(pieces):
        return [pieces[0]] + [to_slice(pieces[k], k) for k in range(1, PEERS)]

    def to_gx(piece, k):
        return lax.ppermute(piece, "gx", [(i, i ^ k) for i in range(nx)])

    def pool_gx(piece):
        return [piece] + [to_gx(piece, k) for k in range(1, nx)]

    def pool_z(piece):
        out = [piece]
        for k in range(1, nz):
            perm = [(j, (j // fy ^ k) * fy + j % fy) for j in range(ny)]
            out.append(lax.ppermute(piece, "gy", perm))
        return out

    def over_x(block):
        return {0: block, **{k: to_gx(block, k) for k in range(2, nx, 2)}}

    def over_core(held, *then):
        held = {k: after(v, *then) for k, v in held.items()} if then else dict(held)
        for k in list(held):
            held[k + 1] = to_gx(held[k], 1)
        return [held[k] for k in sorted(held)]

    def turn(block):
        return lax.all_to_all(block, "gy", 0, 0, tiled=True)

    unit_first, unit_skip = conv_first.shape[0] // 2, projection.shape[0] // 2
    unit_mid = conv_second.shape[0] // 2
    span_first, span_mid = span_of(unit_first + unit_skip), span_of(unit_mid)
    tile, tile16 = shape((cs, width)), shape((cs, width), BF16)
    long16 = shape((cs, width + 128), BF16)
    cols, stat, entry_stat = shape((cs, 128)), shape((8, cs)), shape((8, lanes))
    shifted16 = shape((9 * cs, width), BF16)
    full16 = shape((c_out, width), BF16)
    whole16 = shape((9 * cs, c_out), BF16)

    def halves(span, channels):
        return pltpu.VMEM((2, cs // channels, ny, channels, span), BF16)

    def ready(span, sections, *weights):
        out = shape((ny, cb, span * len(sections)), BF16)
        return run(
            part(entry_weights, cs, fy, sections), out, weights, cost=24 * len(sections)
        )

    def merge(pieces, kernel):
        like = pieces[0].shape
        return run(kernel, shape(like), pieces, [pltpu.VMEM((nx, *like), F32)])

    add_gx = part(add_rows, 2)

    def activate(value, params, pooled, cot=None):
        more = [] if cot is None else [cot]
        outs = [tile16] if cot is None else [long16] * PEERS
        return run(
            part(act_block, nz),
            [tile, cols] + outs,
            [value, params, *pooled, *more],
            [pltpu.VMEM((nz, 8, cs), F32)]
            + ([] if cot is None else [pltpu.VMEM((c_out, 128), F32)]),
            far=(0, 1),
        )

    def convolve(pieces, weights, base, section=0, last=False):
        more = [] if base is None else [base]
        outs = [shape((cs, 128), BF16)] * PEERS + [full16]
        return run(
            part(conv_block, nx, base is not None, last, unit_mid, section, area, small),
            outs if last else [tile, stat, full16, whole16],
            [*pieces, narrow, *weights, *more],
            [pltpu.VMEM((9 * cs, width), F32)] + ([] if last else [halves(span_mid, cb)]),
            cost=25,
            far=() if last else (2, 3),
        )

    def slope(parts, normed, params):
        return run(gelu_back, [tile, stat], [*parts, normed, params])

    def back(grad_pre, normed, scales, params, pooled, weights, base, riders=()):
        more = list(riders) if base is None else [base]
        return run(
            part(norm_back, nz, base is not None, False, area, small),
            [stat, shifted16]
            + ([long16] * PEERS if base is None else [tile16] * (PEERS + 1)),
            [grad_pre, normed, scales, params, narrow, *pooled, *more, weights],
            [pltpu.VMEM((c_out, width), F32), pltpu.VMEM((nz, 8, cs), F32)],
            cost=18,
        )

    def grad_of(kernel, span, shifted, act, scratch):
        own, other = run(
            kernel,
            [shape((ny, cs, span)), shape((ny, cs, span), BF16)],
            [shifted, act],
            [scratch, pltpu.VMEM((2, ny, cs, span), F32)],
            cost=28,
        )
        return own, to_gx(other, 1)

    def grad_mid(shifted, act):
        return grad_of(
            part(weight_grad, unit_mid), span_mid, shifted, act, pltpu.VMEM((9 * cs, c_out), F32)
        )

    def over_pair(own, other):
        span = own.shape[2]
        return run(
            part(reduce_core, 1),
            [shape((ny, cb, span))] + [shape((ny, cb, span), BF16)] * (sides - 1),
            [own, other],
            [pltpu.VMEM((ny, cs, span), F32)],
        )

    def to_sides(parts, *then):
        parts = [after(p, *then) for p in parts] if then else parts
        return [parts[0]] + [to_gx(parts[k], 2 * k) for k in range(1, sides)]

    def over_sides(*groups):
        span = sum(parts[0].shape[2] for parts in groups)
        return run(
            part(reduce_side, tuple(len(parts) for parts in groups)),
            shape((ny, cb, span), BF16),
            [p for parts in groups for p in parts],
        )

    def folded(got):
        out = shape((fy * cb, got.shape[2]), BF16)
        return over_core(over_x(run(part(fold, nz, fy), out, [got])))

    def rows_of(pieces, spans, *rows):
        return run(
            part(own_rows, nx, spans),
            [shape((r, c_out)) for r in rows],
            pieces,
            [pltpu.VMEM((2, sides, fy * cb, pieces[0].shape[1]), BF16)],
            cost=30,
        )

    def own(gain, shift):
        pair = jnp.stack([gain, shift], axis=1)
        return lax.dynamic_slice_in_dim(pair, me * cs, cs, axis=0)

    p_middle = own(gain_middle, shift_middle)
    p_inner = own(gain_inner, shift_inner)
    p_last = own(gain_last, shift_last)
    g_entry, s_entry = gain_entry[None], shift_entry[None]
    pixels = images.reshape(side * side, c_in)

    image, wide = run(
        part(entry_image, small),
        [shape((4 * area, lanes), BF16), shape((4 * area, 128))],
        [pixels, pixel_mask.reshape(side, side), valid_count],
        scalars=1,
    )
    group = share([image] * PEERS)
    out_first = ready(span_first, (2,), conv_first, projection)
    stats = run(part(entry_stats, area), entry_stat, group)
    pieces = pool_gx(stats)
    got_first = turn(after(out_first, *group[1:]))
    got_first = over_core(over_x(after(got_first, *pieces[1:])))
    pooled = pool_z(merge(pieces, merge_stats))
    out_middle = ready(span_mid, (1, 1), conv_second, conv_third)
    got_middle = turn(after(out_middle, pooled[-1]))
    out_fourth = ready(span_mid, (1,), conv_fourth)
    first, skipped, stats, norm_one, narrow, act_one, w_first = run(
        part(entry_block, nz, nx, unit_first, unit_skip, area, small),
        [
            tile,
            tile,
            stat,
            entry_stat,
            shape((8, width)),
            shape((4, width, c_in), BF16),
            shape((10 * cs, c_in), BF16),
        ],
        [*group, *pooled, g_entry, s_entry, *got_first],
        [
            pltpu.VMEM((nz, 8, lanes), F32),
            pltpu.VMEM((width, lanes), BF16),
            pltpu.VMEM((cs, span_of(9 * c_in)), BF16),
            halves(span_first, cb),
        ],
        cost=40,
        far=(3, 5, 6),
    )

    merged = merge(pool_gx(stats), merge_stats)
    got_middle = over_x(after(got_middle, merged))
    pooled = pool_z(merged)
    got_fourth = turn(after(out_fourth, pooled[-1]))
    normed_two, scale_two, *messages = activate(
        first, p_middle, pooled, cotangent.reshape(area, c_out)
    )
    pieces = share(messages)
    got_middle = over_core(got_middle, *pieces[1:])
    hidden, stats, act_two, w_second = convolve(pieces, got_middle, skipped)
    cot_parts = pieces
    merged = merge(pool_gx(stats), merge_stats)
    got_fourth = over_x(after(got_fourth, merged))
    pooled = pool_z(merged)
    normed_three, scale_three, act = activate(hidden, p_inner, pooled)
    pieces = share([act] * PEERS)
    third, stats, act_three, w_third = convolve(pieces, got_middle, None, section=1)
    got_fourth = over_core(got_fourth, stats)
    merged = merge(pool_gx(stats), merge_stats)

    cot, shifted_four, w_fourth, *parts = run(
        part(last_back, nx, unit_mid, 0, area, small),
        [tile, shifted16, whole16] + [tile16] * PEERS,
        [*cot_parts, *got_fourth],
        [pltpu.VMEM((c_out, width), F32), halves(span_mid, cb)],
        cost=18,
        far=(0, 1, 2),
    )
    parts = share(parts)
    normed_four, scale_four, act = activate(third, p_last, pool_z(merged))
    pieces = share([act] * PEERS)
    grad_pre, sums = slope(parts, normed_four, p_last)
    sums = pool_gx(sums)
    *riders, act_four = convolve(pieces, [w_fourth], hidden, last=True)
    sums = pool_z(merge(sums, add_gx))
    fourth = grad_mid(shifted_four, act_four)
    last_sums, shifted_three, *parts = back(
        grad_pre, normed_four, scale_four, p_last, sums, w_third, None, riders
    )
    parts = share(parts)
    fourth = over_pair(*fourth)
    grad_pre, sums = slope(parts, normed_three, p_inner)
    sums = pool_gx(sums)
    third = grad_mid(shifted_three, act_three)
    merged = merge(sums, add_gx)
    fourth = to_sides(fourth, merged)
    sums = pool_z(merged)
    out = run(
        join_result, shape((area, c_out), BF16), parts, [pltpu.VMEM((c_out, 128), F32)]
    )
    inner_sums, shifted_two, grad_hidden, *parts = back(
        grad_pre, normed_three, scale_three, p_inner, sums, w_second, cot
    )
    parts = share(parts)
    third = over_pair(*third)
    grad_pre, sums = slope(parts, normed_two, p_middle)
    sums = pool_gx(sums)
    fourth = over_sides(fourth)
    second = grad_mid(shifted_two, act_two)
    merged = merge(sums, add_gx)
    third = to_sides(third, merged)
    sums = pool_z(merged)
    second = to_sides(over_pair(*second), merged)
    middle_sums, shifted_one, *parts = run(
        part(norm_back, nz, False, True, area, small),
        [stat, shape((10 * cs, width), BF16)] + [shape((4 * area, c_in), BF16)] * PEERS,
        [
            grad_pre,
            normed_two,
            scale_two,
            p_middle,
            narrow,
            *sums,
            w_first,
            grad_hidden,
        ],
        [pltpu.VMEM((4, width, c_in), F32), pltpu.VMEM((nz, 8, cs), F32)],
        cost=18,
    )

    late = turn(over_sides([fourth], third))
    parts = share(parts)
    first = grad_of(
        part(weight_grad_first, unit_first, unit_skip),
        span_first,
        shifted_one,
        act_one,
        pltpu.VMEM((cs, span_of(9 * c_in + span_first + 128)), F32),
    )
    first = to_sides(over_pair(*first))
    second = over_sides(second)
    early = turn(over_sides([second], first))
    grad_pre, sums = run(
        part(entry_back, small),
        [shape((4 * area, c_in)), shape((8, padded))],
        [*parts, pixels, norm_one, g_entry, s_entry],
        cost=13,
    )
    message = run(bundle, shape((16, padded)), [middle_sums, inner_sums, last_sums, sums])
    message = share([message] * PEERS)
    late = folded(late)
    sums, six = run(
        unbundle,
        [shape((8, padded)), shape((8, c_out))],
        message,
        [pltpu.VMEM((PEERS, 16, padded), F32)],
    )
    sums = pool_z(merge(pool_gx(sums), add_gx))
    fourth_grad, third_grad = rows_of(
        late, ((span_mid, (0,)), (span_mid, (1,))), 2 * unit_mid, 2 * unit_mid
    )
    early = folded(early)
    gain_entry_grad, shift_entry_grad, image_grad = run(
        part(entry_grad, nz),
        [shape((1, padded)), shape((1, padded)), shape((4 * area, c_in))],
        [*sums, grad_pre, pixels, wide, norm_one, g_entry],
        [pltpu.VMEM((nz, 8, padded), F32)],
    )
    second_grad, first_grad, skip_grad = rows_of(
        early,
        ((span_mid, (0,)), (span_first, (1, 2))),
        2 * unit_mid,
        2 * unit_first,
        2 * unit_skip,
    )
    return (
        out.reshape(1, small, small, c_out),
        image_grad.reshape(1, side, side, c_in),
        gain_entry_grad[0, :c_in],
        shift_entry_grad[0, :c_in],
        first_grad,
        six[0],
        six[1],
        second_grad,
        skip_grad,
        six[2],
        six[3],
        third_grad,
        six[4],
        six[5],
        fourth_grad,
    )


def solution(mesh):
    whole = P(("gx", "gy"), None, None, None)
    rows = P("gy", None)
    return jax.shard_map(
        functools.partial(program, mesh.shape["gx"], mesh.shape["gy"]),
        mesh=mesh,
        in_specs=(
            whole,
            P(("gx", "gy")),
            P(("gx", "gy"), None, None),
            P(),
            P(),
            rows,
            P(),
            P(),
            rows,
            rows,
            P(),
            P(),
            rows,
            P(),
            P(),
            rows,
            whole,
        ),
        out_specs=(
            whole, whole, P(), P(), rows, P(), P(), rows, rows, P(), P(), rows, P(), P(), rows,
        ),
        check_vma=False,
    )
```

```python
import functools

import jax
import jax.numpy as jnp
from jax import lax
from jax.experimental import pallas as pl
from jax.experimental.pallas import tpu as pltpu
from jax.sharding import PartitionSpec as P

EPS = 1e-05
COST = 6 * 10**7
F32 = jnp.float32
BF16 = jnp.bfloat16
PEERS = 4
C0 = 0.7978845608028654
C1 = 0.044715
VMEM = pl.BlockSpec(memory_space=pltpu.VMEM)
SMEM = pl.BlockSpec(memory_space=pltpu.SMEM)


def gelu(v):
    return 0.5 * v * (1.0 + jnp.tanh(C0 * (v + C1 * (v * v * v))))


def gelu_slope(v):
    t = jnp.tanh(C0 * (v + C1 * (v * v * v)))
    return 0.5 * (1.0 + t) + 0.5 * v * (1.0 - t * t) * (C0 * (1.0 + 3.0 * C1 * (v * v)))


def after(value, *others):
    return lax.optimization_barrier((value, *others))[0]


class Far:
    def __init__(self, near, far, sem):
        self.near, self.shape, self.dtype = near, near.shape, near.dtype
        self.copy = pltpu.make_async_copy(near, far, sem)
        self.sent = False

    def __getitem__(self, at):
        return self.near[at]

    def __setitem__(self, at, value):
        self.near[at] = value

    def send(self):
        if not self.sent:
            self.copy.start()
            self.sent = True


def send(ref):
    if isinstance(ref, Far):
        ref.send()


def with_far(kernel, n_in, n_out, far, *refs):
    ins, outs, rest = refs[:n_in], list(refs[n_in : n_in + n_out]), list(refs[n_in + n_out :])
    if far:
        sems = rest.pop()
        near = rest[len(rest) - len(far) :]
        del rest[len(rest) - len(far) :]
        for n, at in enumerate(far):
            outs[at] = Far(near[n], outs[at], sems.at[n])
    kernel(*ins, *outs, *rest)
    for at in far:
        outs[at].send()
    for at in far:
        outs[at].copy.wait()


class Order:
    def __init__(self, idx):
        self.idx = idx
        self.last = ()

    def __call__(self, kernel, outs, args, scratch=(), scalars=0, cost=7, far=()):
        idx = after(self.idx, *self.last)
        many = isinstance(outs, (list, tuple))
        shapes = list(outs) if many else [outs]
        more = [pltpu.VMEM(shapes[at].shape, shapes[at].dtype) for at in far]
        if far:
            more.append(pltpu.SemaphoreType.DMA((len(far),)))
        got = pl.pallas_call(
            functools.partial(with_far, kernel, 1 + len(args), len(shapes), tuple(far)),
            out_shape=shapes,
            in_specs=[SMEM] + [VMEM] * (len(args) - scalars) + [SMEM] * scalars,
            out_specs=[
                pl.BlockSpec(memory_space=pl.ANY) if at in far else VMEM
                for at in range(len(shapes))
            ],
            scratch_shapes=list(scratch) + more,
            compiler_params=pltpu.CompilerParams(vmem_limit_bytes=16 * 1024 * 1024),
            cost_estimate=pl.CostEstimate(
                flops=cost * COST, bytes_accessed=1024, transcendentals=0
            ),
        )(idx, *args)
        near = [v for at, v in enumerate(got) if at not in far]
        self.last = (near[0] if near else got[0],)
        return got if many else got[0]


def shape(dims, dtype=F32):
    return jax.ShapeDtypeStruct(dims, dtype)


def rows_at(index, count):
    return pl.ds(pl.multiple_of(index * count, count), count)


def as_rows(parts):
    height = parts[0].shape[0]
    lane = lax.broadcasted_iota(jnp.int32, (height, 128), 1)
    out = jnp.zeros((height, 128), F32)
    for k, part in enumerate(parts):
        out = jnp.where(lane == k, part, out)
    return out.T[0:8]


def as_columns(rows):
    return jnp.concatenate([rows, jnp.zeros((120, rows.shape[1]), F32)], axis=0).T


def in_order(refs, me, scratch):
    for k, ref in enumerate(refs):
        scratch[me ^ k] = ref[...]
    return [scratch[k] for k in range(len(refs))]


def merge_moments(stats):
    total = sum(n for _, _, n in stats)
    mean = sum(n * m for m, _, n in stats) / total
    squares = sum(q + n * (m - mean) * (m - mean) for m, q, n in stats)
    return mean, squares, total


def merge_rows(refs):
    mean, squares, total = merge_moments([(g[0:1], g[1:2], g[2:3]) for g in refs])
    return mean, squares, total, sum(g[3:4] for g in refs)


def pixel(width, area, small):
    lane = lax.broadcasted_iota(jnp.int32, (1, width), 1) % area
    return lane // small, lane % small


def inside(row, col, drow, dcol, small):
    return (row + drow >= 0) & (row + drow < small) & (col + dcol >= 0) & (col + dcol < small)


def moved(value, step):
    shift = (-step) % value.shape[1]
    return pltpu.roll(value, shift, 1) if shift else value


OFFSETS = [(0, krow - 1, kcol - 1) for krow in range(3) for kcol in range(3)]

STRIDED = [
    ((krow != 1) * 2 + (kcol != 1), -(krow == 0), -(kcol == 0))
    for krow in range(3)
    for kcol in range(3)
] + [(0, 0, 0)]
PLACED = sorted(range(10), key=lambda k: (STRIDED[k][0], k))
PHASES = [[k for k in PLACED if STRIDED[k][0] == phase] for phase in range(4)]


def row_of(k, cs):
    at = PLACED.index(k)
    return slice(at * cs, (at + 1) * cs)


def phase_rows(phase, cs):
    first, last = PHASES[phase][0], PHASES[phase][-1]
    return slice(PLACED.index(first) * cs, (PLACED.index(last) + 1) * cs)


def masked_stats(value, weight, n):
    mean = jnp.sum(value * weight, axis=1, keepdims=True) / n
    centred = value - mean
    return mean, jnp.sum(weight * centred * centred, axis=1, keepdims=True)


def span_of(rows):
    return -(-rows // 128) * 128


def one_hot(height, width, shift):
    row = lax.broadcasted_iota(jnp.int32, (height, width), 0)
    col = lax.broadcasted_iota(jnp.int32, (height, width), 1)
    return (col == row + shift).astype(BF16)


def pick32(left, right, dims=((1,), (0,))):
    return lax.dot_general(left, right, (dims, ((), ())), preferred_element_type=F32)


def pick(left, right, dims=((1,), (0,))):
    return pick32(left, right, dims).astype(BF16)


def lane_tile(held, tile, rows, span):
    sides, ny = held.shape[1], held.shape[2]
    lane = lax.broadcasted_iota(jnp.int32, (1, 128), 1)
    out = None
    for v in range(2 * ny):
        begin = rows * v - tile * 128
        if begin >= 128 or begin + rows <= 0:
            continue
        at = (tile - rows * v // 128) * 128 % span
        part = jnp.concatenate(
            [held[v % 2, x, v // 2, :, at : at + 128].astype(F32) for x in range(sides)], axis=0
        )
        if begin > 0 or begin + rows < 128:
            own = (lane >= begin) & (lane < begin + rows)
            part = jnp.where(own, part, 0.0)
        out = part if out is None else out + part
    return out.astype(BF16)


def pixel_order(small, width, of):
    area = small * small
    row = lax.broadcasted_iota(jnp.int32, (4 * area, width), 0)
    col = lax.broadcasted_iota(jnp.int32, (4 * area, width), 1)
    phase, pix = row // area, row % area
    y = 2 * (pix // small) + phase // 2
    x = 2 * (pix % small) + phase % 2
    return (col == of(y, x)).astype(BF16)


def entry_image(small, idx, image, mask, valid, out, weight):
    side = 2 * small
    c_in = image.shape[1]
    count = side * side
    order = pixel_order(small, count, lambda y, x: y * side + x)
    out[:, :c_in] = pick(order, image[...])
    live = (valid[0] > 0).astype(F32)
    row = lax.broadcasted_iota(jnp.int32, (count, side), 0)
    col = lax.broadcasted_iota(jnp.int32, (count, side), 1)
    by_row = jnp.dot(
        (row // side == col).astype(BF16),
        mask[...].astype(F32).astype(BF16),
        preferred_element_type=F32,
    )
    column = jnp.sum(jnp.where(row % side == col, by_row, 0.0), axis=1, keepdims=True) * live
    lane = lax.broadcasted_iota(jnp.int32, (count, 128), 1)
    spread = jnp.where(lane == 0, column, 0.0)
    weight[...] = spread
    out[:, c_in:] = pick(order, spread.astype(BF16))[:, : out.shape[1] - c_in]


def entry_weights(cs, fy, sections, idx, *refs):
    weights, out = list(refs[:-1]), refs[-1]
    ny, cb, lanes = out.shape
    span = lanes // len(sections)
    gx, gy = idx[2], idx[3]
    core, side = gx % 2, (gx // 2 if cb < cs else 0)
    c_out = weights[0].shape[1]
    row = lax.broadcasted_iota(jnp.int32, (fy * cb, c_out), 0)
    col = lax.broadcasted_iota(jnp.int32, (fy * cb, c_out), 1)
    chosen = (col == row // cb * cs + side * cb + row % cb).astype(BF16)
    for n, count in enumerate(sections):
        begin = weights[0].shape[0] // 2 * (2 * gy + core) % 128
        total = None
        for _ in range(count):
            weight = weights.pop(0)
            rows = weight.shape[0]
            half = rows // 2
            mine = pick(chosen, weight[...], ((1,), (1,)))
            row = lax.broadcasted_iota(jnp.int32, (rows, span), 0) - core * half
            col = lax.broadcasted_iota(jnp.int32, (rows, span), 1)
            place = (row >= 0) & (row < half) & (
                (col == row + begin) | (col == row + begin - span)
            )
            part = pick32(mine, place.astype(BF16))
            total = part if total is None else total + part
            begin = begin + half
        for j in range(ny):
            out[j, :, n * span : (n + 1) * span] = total[
                (j % fy) * cb : (j % fy + 1) * cb
            ].astype(BF16)


def hold(gx, messages, held, section=0):
    span = held.shape[4]
    for k, ref in enumerate(messages):
        at = gx ^ k
        side = at // 2 if held.shape[1] > 1 else 0
        held[at % 2, side] = ref[:, :, section * span : (section + 1) * span]


def assemble(held, out, rows):
    cs, span = held.shape[1] * held.shape[3], held.shape[4]
    tiles = out.shape[1] // 128
    for k in range(9):
        for q in range(tiles):
            out[k * cs : (k + 1) * cs, q * 128 : (q + 1) * 128] = lane_tile(
                held, tiles * k + q, rows, span
            )


def assemble_first(held, out, flat, rows, extra):
    cs, span = held.shape[1] * held.shape[3], held.shape[4]
    c_in = out.shape[1]
    tiles = flat.shape[1] // 128
    for tile in range(tiles):
        flat[:, tile * 128 : (tile + 1) * 128] = lane_tile(held, tile, rows, span)
    for k in range(9):
        begin = k * c_in
        base = begin // 128 * 128
        reach = min(-(-(begin + c_in) // 128) * 128, flat.shape[1])
        move = one_hot(c_in, reach - base, begin - base)
        out[row_of(k, cs), :] = pick(flat[:, base:reach], move, ((1,), (1,)))
    total = None
    for v in range(2 * held.shape[2]):
        row = lax.broadcasted_iota(jnp.int32, (span, c_in), 0)
        col = lax.broadcasted_iota(jnp.int32, (span, c_in), 1)
        at = col - extra * v
        begin = rows * v % 128 + rows
        place = (at >= 0) & (at < extra) & ((row == at + begin) | (row == at + begin - span))
        part = jnp.concatenate(
            [
                pick32(held[v % 2, x, v // 2], place.astype(BF16))
                for x in range(held.shape[1])
            ],
            axis=0,
        )
        total = part if total is None else total + part
    out[row_of(9, cs), :] = total.astype(BF16)


def entry_stats(area, idx, *refs):
    images, out = refs[:PEERS], refs[PEERS]
    lanes = out.shape[1]
    first = jnp.zeros((1, lanes), F32)
    wide = jnp.zeros((1, 1), F32)
    narrow = jnp.zeros((1, 1), F32)
    c_in = lanes - 64
    for ref in images:
        x = ref[...].astype(F32)
        w = x[:, c_in : c_in + 1]
        first += jnp.sum(x * w, axis=0, keepdims=True)
        wide += jnp.sum(w, axis=0, keepdims=True)
        narrow += jnp.sum(w[:area], axis=0, keepdims=True)
    mean = first / wide
    squares = jnp.zeros((1, lanes), F32)
    for ref in images:
        x = ref[...].astype(F32)
        w = x[:, c_in : c_in + 1]
        d = x - mean
        squares += jnp.sum(d * d * w, axis=0, keepdims=True)
    out[...] = jnp.zeros_like(out)
    out[0:1, :] = mean
    out[1:2, :] = squares
    out[2:3, :] = jnp.broadcast_to(wide, (1, lanes))
    out[3:4, :] = jnp.broadcast_to(narrow, (1, lanes))


def entry_block(nz, nx, rows, extra, area, small, idx, *refs):
    images = refs[:PEERS]
    stats, rest = refs[PEERS : PEERS + nz], refs[PEERS + nz :]
    gain, shift, messages, rest = rest[0], rest[1], rest[2 : 2 + nx], rest[2 + nx :]
    first, skipped, out_stats, norm, narrow, act, w_first = rest[:7]
    order, masks, flat, held = rest[7:]
    me, mine = idx[0], idx[1]
    c_in = gain.shape[1]
    lanes = norm.shape[1]
    cs = first.shape[0]
    width = first.shape[1]
    hold(idx[2], messages, held)
    assemble_first(held, w_first, flat, rows, extra)
    send(w_first)
    mean, squares, total, count = merge_rows(in_order(stats, mine, order))
    scale = lax.rsqrt(squares / total + EPS)
    norm[...] = jnp.zeros_like(norm)
    norm[0:1, :] = mean
    norm[1:2, :] = scale
    norm[2:3, :] = total
    norm[3:4, :] = count
    for k, ref in enumerate(images):
        x = ref[...]
        v = x[:, :c_in].astype(F32)
        pre = gain[...] * ((v - mean[:, :c_in]) * scale[:, :c_in]) + shift[...]
        a = gelu(pre).astype(BF16)
        for phase in range(4):
            act[phase, rows_at(me ^ k, area), :] = a[phase * area : (phase + 1) * area]
        masks[rows_at(me ^ k, area), :] = x[:area]
    send(act)
    send(norm)
    ones = (lax.broadcasted_iota(jnp.int32, (8, lanes), 1) == c_in).astype(BF16)
    weight8 = lax.dot_general(
        ones, masks[...], (((1,), (1,)), ((), ())), preferred_element_type=F32
    )
    narrow[...] = weight8
    weight = weight8[0:1]
    row, col = pixel(width, area, small)
    total_first = jnp.zeros((cs, width), F32)
    for phase in range(4):
        group = lax.dot_general(
            w_first[phase_rows(phase, cs), :],
            act[phase],
            (((1,), (1,)), ((), ())),
            preferred_element_type=F32,
        )
        for at, k in enumerate(PHASES[phase]):
            y = group[at * cs : (at + 1) * cs]
            if k == 9:
                skipped[...] = y
                continue
            _, drow, dcol = STRIDED[k]
            y = moved(y, drow * small + dcol)
            total_first += jnp.where(inside(row, col, drow, dcol, small), y, 0.0)
    first[...] = total_first
    n = jnp.sum(weight, axis=1, keepdims=True)
    mean2, squares = masked_stats(total_first, weight, n)
    out_stats[...] = as_rows((mean2, squares, n))


def merge_stats(idx, *refs):
    out, order = refs[-2:]
    mean, squares, total, count = merge_rows(in_order(refs[:-2], idx[2], order))
    out[...] = jnp.zeros_like(out)
    out[0:1] = mean
    out[1:2] = squares
    out[2:3] = total
    out[3:4] = count


def add_rows(which, idx, *refs):
    out, order = refs[-2:]
    got = in_order(refs[:-2], idx[which], order)
    total = got[0]
    for g in got[1:]:
        total = total + g
    out[...] = total


def act_block(nz, idx, *refs):
    value, params = refs[:2]
    stats, rest = refs[2 : 2 + nz], refs[2 + nz :]
    if rest[-1].shape[1] == 128:
        cot, normed, scales, outs, order, stack = (*rest[:3], rest[3:-2], *rest[-2:])
    else:
        cot, normed, scales, outs, order = (None, *rest[:2], rest[2:-1], rest[-1])
    mean, squares, total, _ = merge_rows(in_order(stats, idx[1], order))
    rows = jnp.concatenate(
        [mean, lax.rsqrt(squares / total + EPS), total, jnp.zeros((5, mean.shape[1]), F32)], axis=0
    )
    cols = as_columns(rows)
    norm = (value[...] - cols[:, 0:1]) * cols[:, 1:2]
    normed[...] = norm
    send(normed)
    scales[...] = cols
    send(scales)
    act = gelu(params[:, 0:1] * norm + params[:, 1:2]).astype(BF16)
    cs, width = norm.shape
    if cot is not None:
        c = cot[...].astype(F32)
        stack[...] = jnp.concatenate([c, c], axis=0).T
    for k, out in enumerate(outs):
        out[:, :width] = act
        if cot is not None:
            out[:, width:] = stack[rows_at(idx[0] ^ k, cs), :].astype(BF16)


def conv_block(nx, added, last, rows, section, area, small, idx, *refs):
    pieces = refs[:PEERS]
    narrow, rest = refs[PEERS], refs[PEERS + 1 :]
    if last:
        weights, rest = rest[0], rest[1:]
    else:
        messages, rest = rest[:nx], rest[nx:]
    base, rest = (rest[0], rest[1:]) if added else (None, rest)
    me = idx[0]
    cs, width = pieces[0].shape[0], narrow.shape[1]
    if last:
        outs, act, spread = rest[:PEERS], rest[PEERS], rest[PEERS + 1]
    else:
        value, out_stats, act, whole, spread, held = rest
        hold(idx[2], messages, held, section)
        assemble(held, whole, rows)
        send(whole)
        weights = whole
    for k, ref in enumerate(pieces):
        act[rows_at(me ^ k, cs), :] = ref[:, :width]
    send(act)
    spread[...] = jnp.dot(weights[...], act[...], preferred_element_type=F32)
    row, col = pixel(width, area, small)
    total = base[...] if added else jnp.zeros((cs, width), F32)
    for k, (_, drow, dcol) in enumerate(OFFSETS):
        y = moved(spread[k * cs : (k + 1) * cs, :], drow * small + dcol)
        total += jnp.where(inside(row, col, drow, dcol, small), y, 0.0)
    if last:
        result = total.astype(BF16)
        lane = lax.broadcasted_iota(jnp.int32, (width, 128), 0)
        slot = lax.broadcasted_iota(jnp.int32, (width, 128), 1)
        for k, out in enumerate(outs):
            out[...] = pick(result, (lane == (me ^ k) * area + slot).astype(BF16))
    else:
        value[...] = total
        weight = narrow[0:1, :]
        n = jnp.sum(weight, axis=1, keepdims=True)
        mean, squares = masked_stats(total, weight, n)
        out_stats[...] = as_rows((mean, squares, n))


def join_result(idx, *refs):
    pieces, (out, stack) = refs[:PEERS], refs[PEERS:]
    cs = pieces[0].shape[0]
    for k, ref in enumerate(pieces):
        stack[rows_at(idx[0] ^ k, cs), :] = ref[:, -128:].astype(F32)
    out[...] = stack[...].T[: out.shape[0]].astype(BF16)


def spread_grad(grad, shifted, area, small, offs, row_at):
    cs, width = grad.shape
    row, col = pixel(width, area, small)
    for k, (_, drow, dcol) in enumerate(offs):
        g = moved(grad, -(drow * small + dcol))
        g = jnp.where(inside(row, col, -drow, -dcol, small), g, 0.0)
        shifted[row_at(k, cs), :] = g.astype(BF16)


def plain_rows(k, cs):
    return slice(k * cs, (k + 1) * cs)


def push_back(me, weights, shifted, partial, outs):
    cs, width = outs[0].shape[0], shifted.shape[1]
    partial[...] = lax.dot_general(
        weights[...], shifted[...], (((0,), (0,)), ((), ())), preferred_element_type=F32
    )
    for k, out in enumerate(outs):
        out[:, :width] = partial[rows_at(me ^ k, cs), :].astype(BF16)


def last_back(nx, rows, section, area, small, idx, *refs):
    pieces, messages, rest = refs[:PEERS], refs[PEERS : PEERS + nx], refs[PEERS + nx :]
    cot, shifted, weights = rest[:3]
    outs = rest[3 : PEERS + 3]
    partial, held = rest[PEERS + 3 :]
    hold(idx[2], messages, held, section)
    assemble(held, weights, rows)
    send(weights)
    me = idx[0]
    cs, width = cot.shape
    image = lax.broadcasted_iota(jnp.int32, (1, width), 1) // area
    grad = jnp.zeros((cs, width), F32)
    for k, ref in enumerate(pieces):
        tiled = jnp.concatenate([ref[:, width:].astype(F32)] * (width // 128), axis=1)
        grad = jnp.where(image == (me ^ k), tiled, grad)
    cot[...] = grad
    send(cot)
    spread_grad(grad, shifted, area, small, OFFSETS, plain_rows)
    send(shifted)
    push_back(me, weights, shifted, partial, outs)


def gelu_back(idx, *refs):
    pieces = refs[:PEERS]
    normed, params, grad_pre, sums = refs[PEERS:]
    width = normed.shape[1]
    grad = pieces[0][:, :width].astype(F32)
    for ref in pieces[1:]:
        grad += ref[:, :width].astype(F32)
    norm = normed[...]
    g = gelu_slope(params[:, 0:1] * norm + params[:, 1:2]) * grad
    grad_pre[...] = g
    sums[...] = as_rows(
        (jnp.sum(g * norm, axis=1, keepdims=True), jnp.sum(g, axis=1, keepdims=True))
    )


def norm_back(nz, added, last, area, small, idx, *refs):
    grad_pre, normed, scales, params, narrow = refs[:5]
    sums = refs[5 : 5 + nz]
    rest = refs[5 + nz :]
    base, rest = (rest[0], rest[1:]) if added else (None, rest)
    me = idx[0]
    cs, width = grad_pre.shape
    order = rest[-1]
    got = in_order(sums, idx[1], order)
    total = got[0]
    for g in got[1:]:
        total = total + g
    cols = as_columns(total)
    gain_grad, shift_grad = cols[:, 0:1], cols[:, 1:2]
    norm = normed[...]
    back = params[:, 0:1] * scales[:, 1:2] * (
        grad_pre[...]
        - narrow[0:1, :] * (shift_grad + norm * gain_grad) / scales[:, 2:3]
    )
    if added:
        back = base[...] + back
    grad = back.astype(BF16).astype(F32)
    if not last:
        riders = ()
        if not added:
            riders, rest = rest[:PEERS], rest[PEERS:]
        weights, sums_out, shifted = rest[:3]
        outs, partial = rest[3 : 3 + PEERS], rest[3 + PEERS]
        for rider, out in zip(riders, outs):
            out[:, width:] = rider[...]
        if added:
            grad_out, outs, partial = rest[3], rest[4 : 4 + PEERS], rest[4 + PEERS]
            grad_out[...] = grad.astype(BF16)
        sums_out[...] = total
        spread_grad(grad, shifted, area, small, OFFSETS, plain_rows)
        push_back(me, weights, shifted, partial, outs)
    else:
        weights, grad_skip, sums_out, shifted = rest[:4]
        outs, partial = rest[4 : 4 + PEERS], rest[4 + PEERS]
        sums_out[...] = total
        spread_grad(grad, shifted, area, small, STRIDED[:9], row_of)
        shifted[row_of(9, cs), :] = grad_skip[...]
        for phase in range(4):
            partial[phase] = lax.dot_general(
                shifted[phase_rows(phase, cs), :],
                weights[phase_rows(phase, cs), :],
                (((0,), (0,)), ((), ())),
                preferred_element_type=F32,
            )
        for k, out in enumerate(outs):
            for phase in range(4):
                out[phase * area : (phase + 1) * area, :] = partial[
                    phase, rows_at(me ^ k, area), :
                ].astype(BF16)


def part_halves(core, units, own, other):
    own[...] = units[core]
    other[...] = units[1 - core].astype(BF16)


def weight_grad(rows, idx, shifted, act, own, other, full, units):
    full[...] = lax.dot_general(
        shifted[...], act[...], (((1,), (1,)), ((), ())), preferred_element_type=F32
    )
    ny, cs, span = own.shape
    tiles = full.shape[1] // 128
    for v in range(2 * ny):
        begin = rows * v % 128
        parts = []
        for q in range((begin + rows + 127) // 128):
            k, p = divmod(rows * v // 128 + q, tiles)
            parts.append(full[k * cs : (k + 1) * cs, p * 128 : (p + 1) * 128])
        window = jnp.concatenate(parts, axis=1)
        units[v % 2, v // 2] = moved(window, begin)[:, :span]
    part_halves(idx[2] % 2, units, own, other)


def weight_grad_first(rows, extra, idx, shifted, act, own, other, flat, units):
    ny, cs, span = own.shape
    c_in = act.shape[2]
    flat[...] = jnp.zeros_like(flat)
    skip = None
    for phase in range(4):
        group = jnp.dot(
            shifted[phase_rows(phase, cs), :], act[phase], preferred_element_type=F32
        ).astype(BF16)
        for at, k in enumerate(PHASES[phase]):
            grad = group[at * cs : (at + 1) * cs]
            if k == 9:
                skip = grad
                continue
            begin = k * c_in
            base = begin // 128 * 128
            reach = -(-(begin + c_in) // 128) * 128
            move = one_hot(c_in, reach - base, begin - base)
            flat[:, base:reach] += jnp.dot(grad, move, preferred_element_type=F32)
    lane = lax.broadcasted_iota(jnp.int32, (1, span), 1)
    for v in range(2 * ny):
        begin = rows * v % 128
        base = rows * v - begin
        window = moved(flat[:, base : base + span + 128], begin)[:, :span]
        row = lax.broadcasted_iota(jnp.int32, (c_in, span), 0)
        col = lax.broadcasted_iota(jnp.int32, (c_in, span), 1)
        place = (row >= extra * v) & (row < extra * (v + 1)) & (col == row - extra * v + rows)
        tail = pick32(skip, place.astype(BF16))
        units[v % 2, v // 2] = jnp.where(lane < rows, window, 0.0) + tail
    part_halves(idx[2] % 2, units, own, other)


def reduce_core(count, idx, *refs):
    own, other, outs, total = refs[:count], refs[count : 2 * count], refs[2 * count : -1], refs[-1]
    cb = outs[0].shape[1]
    at = 0
    for a, b in zip(own, other):
        span = a.shape[2]
        total[:, :, at : at + span] = a[...] + b[...].astype(F32)
        at += span
    for k, out in enumerate(outs):
        for j in range(total.shape[0]):
            out[j] = total[j, rows_at(idx[2] // 2 ^ k, cb), :].astype(out.dtype)


def reduce_side(sizes, idx, *refs):
    refs, out = refs[:-1], refs[-1]
    at = 0
    for size in sizes:
        total = refs[0][...].astype(F32)
        for ref in refs[1:size]:
            total += ref[...].astype(F32)
        out[:, :, at : at + total.shape[2]] = total.astype(BF16)
        refs = refs[size:]
        at += total.shape[2]


def fold(nz, fy, idx, got, out):
    cs = got.shape[1]
    for f in range(fy):
        total = got[f].astype(F32)
        for z in range(1, nz):
            total += got[z * fy + f].astype(F32)
        out[f * cs : (f + 1) * cs, :] = total.astype(BF16)


def own_rows(count, spans, idx, *refs):
    pieces, outs, stack = refs[:count], refs[count:-1], refs[-1]
    for k, ref in enumerate(pieces):
        at = idx[2] ^ k
        stack[at % 2, at // 2] = ref[...]
    sides, height = stack.shape[1], stack.shape[2]
    fy_cb = [(f, x) for f in range(PEERS) for x in range(sides)]
    cb = height // PEERS
    for half in range(2):
        whole = jnp.concatenate(
            [stack[half, x, f * cb : (f + 1) * cb, :].astype(F32) for f, x in fy_cb], axis=0
        ).T
        at = 0
        for span, group in spans:
            begin = at
            for n in group:
                out = outs[n]
                rows = out.shape[0] // 2
                out[half * rows : (half + 1) * rows, :] = whole[begin : begin + rows]
                begin += rows
            at += span


def entry_back(small, idx, *refs):
    pieces = refs[:PEERS]
    image, norm, gain, shift, grad_pre, sums = refs[PEERS:]
    c_in = gain.shape[1]
    side = 2 * small
    grad = pieces[0][...].astype(F32)
    for ref in pieces[1:]:
        grad += ref[...].astype(F32)
    order = pixel_order(small, side * side, lambda y, x: y * side + x)
    high = grad.astype(BF16)
    low = (grad - high.astype(F32)).astype(BF16)
    grad = sum(
        lax.dot_general(order, part, (((0,), (0,)), ((), ())), preferred_element_type=F32)
        for part in (high, low)
    )
    normed = (image[...].astype(F32) - norm[0:1, :c_in]) * norm[1:2, :c_in]
    g = gelu_slope(gain[...] * normed + shift[...]) * grad
    grad_pre[...] = g
    sums[...] = jnp.zeros_like(sums)
    sums[0:1, :c_in] = jnp.sum(g * normed, axis=0, keepdims=True)
    sums[1:2, :c_in] = jnp.sum(g, axis=0, keepdims=True)


def bundle(idx, first, second, third, sums, out):
    out[...] = jnp.zeros_like(out)
    out[0:8, :] = sums[...]
    for k, ref in enumerate((first, second, third)):
        out[8 + 2 * k : 10 + 2 * k, : ref.shape[1]] = ref[0:2]


def unbundle(idx, *refs):
    out, six, order = refs[-3:]
    got = in_order(refs[:-3], idx[0], order)
    total = got[0][0:8]
    for g in got[1:]:
        total = total + g[0:8]
    out[...] = total
    cs = six.shape[1] // PEERS
    six[...] = jnp.concatenate([g[8:16, :cs] for g in got], axis=1)


def entry_grad(nz, idx, *refs):
    sums = refs[:nz]
    grad_pre, image, weight, norm, gain, gain_grad, shift_grad, out, order = refs[nz:]
    got = in_order(sums, idx[1], order)
    total = got[0]
    for g in got[1:]:
        total = total + g
    gain_grad[...] = total[0:1]
    shift_grad[...] = total[1:2]
    c_in = gain.shape[1]
    scale = norm[1:2, :c_in]
    normed = (image[...].astype(F32) - norm[0:1, :c_in]) * scale
    out[...] = gain[...] * scale * (
        grad_pre[...]
        - weight[:, 0:1]
        * (shift_grad[0:1, :c_in] + normed * gain_grad[0:1, :c_in])
        / norm[2:3, :c_in]
    )


def program(
    nx,
    ny,
    images,
    valid_count,
    pixel_mask,
    gain_entry,
    shift_entry,
    conv_first,
    gain_middle,
    shift_middle,
    conv_second,
    projection,
    gain_inner,
    shift_inner,
    conv_third,
    gain_last,
    shift_last,
    conv_fourth,
    cotangent,
):
    fy = PEERS
    nz = ny // fy
    sides = nx // 2
    side, c_in = images.shape[1], images.shape[3]
    small = side // 2
    area = small * small
    c_out = conv_first.shape[1]
    cs = c_out // PEERS
    cb = cs // sides
    width = PEERS * area
    lanes = c_in + 64
    padded = span_of(c_in)
    gx, gy = lax.axis_index("gx"), lax.axis_index("gy")
    me = gy % fy
    mine = gy // fy
    run = Order(jnp.stack([me, mine, gx, gy]).astype(jnp.int32))
    part = functools.partial

    def to_slice(piece, k):
        return lax.ppermute(piece, "gy", [(j, j // fy * fy + (j % fy ^ k)) for j in range(ny)])

    def share(pieces):
        return [pieces[0]] + [to_slice(pieces[k], k) for k in range(1, PEERS)]

    def to_gx(piece, k):
        return lax.ppermute(piece, "gx", [(i, i ^ k) for i in range(nx)])

    def pool_gx(piece):
        return [piece] + [to_gx(piece, k) for k in range(1, nx)]

    def pool_z(piece):
        out = [piece]
        for k in range(1, nz):
            perm = [(j, (j // fy ^ k) * fy + j % fy) for j in range(ny)]
            out.append(lax.ppermute(piece, "gy", perm))
        return out

    def over_x(block):
        return {0: block, **{k: to_gx(block, k) for k in range(2, nx, 2)}}

    def over_core(held, *then):
        held = {k: after(v, *then) for k, v in held.items()} if then else dict(held)
        for k in list(held):
            held[k + 1] = to_gx(held[k], 1)
        return [held[k] for k in sorted(held)]

    def turn(block):
        return lax.all_to_all(block, "gy", 0, 0, tiled=True)

    unit_first, unit_skip = conv_first.shape[0] // 2, projection.shape[0] // 2
    unit_mid = conv_second.shape[0] // 2
    span_first, span_mid = span_of(unit_first + unit_skip), span_of(unit_mid)
    tile, tile16 = shape((cs, width)), shape((cs, width), BF16)
    long16 = shape((cs, width + 128), BF16)
    cols, stat, entry_stat = shape((cs, 128)), shape((8, cs)), shape((8, lanes))
    shifted16 = shape((9 * cs, width), BF16)
    full16 = shape((c_out, width), BF16)
    whole16 = shape((9 * cs, c_out), BF16)

    def halves(span, channels):
        return pltpu.VMEM((2, cs // channels, ny, channels, span), BF16)

    def ready(span, sections, *weights):
        out = shape((ny, cb, span * len(sections)), BF16)
        return run(
            part(entry_weights, cs, fy, sections), out, weights, cost=24 * len(sections)
        )

    def merge(pieces, kernel):
        like = pieces[0].shape
        return run(kernel, shape(like), pieces, [pltpu.VMEM((nx, *like), F32)])

    add_gx = part(add_rows, 2)

    def activate(value, params, pooled, cot=None):
        more = [] if cot is None else [cot]
        outs = [tile16] if cot is None else [long16] * PEERS
        return run(
            part(act_block, nz),
            [tile, cols] + outs,
            [value, params, *pooled, *more],
            [pltpu.VMEM((nz, 8, cs), F32)]
            + ([] if cot is None else [pltpu.VMEM((c_out, 128), F32)]),
            far=(0, 1),
        )

    def convolve(pieces, weights, base, section=0, last=False):
        more = [] if base is None else [base]
        outs = [shape((cs, 128), BF16)] * PEERS + [full16]
        return run(
            part(conv_block, nx, base is not None, last, unit_mid, section, area, small),
            outs if last else [tile, stat, full16, whole16],
            [*pieces, narrow, *weights, *more],
            [pltpu.VMEM((9 * cs, width), F32)] + ([] if last else [halves(span_mid, cb)]),
            cost=25,
            far=() if last else (2, 3),
        )

    def slope(parts, normed, params):
        return run(gelu_back, [tile, stat], [*parts, normed, params])

    def back(grad_pre, normed, scales, params, pooled, weights, base, riders=()):
        more = list(riders) if base is None else [base]
        return run(
            part(norm_back, nz, base is not None, False, area, small),
            [stat, shifted16]
            + ([long16] * PEERS if base is None else [tile16] * (PEERS + 1)),
            [grad_pre, normed, scales, params, narrow, *pooled, *more, weights],
            [pltpu.VMEM((c_out, width), F32), pltpu.VMEM((nz, 8, cs), F32)],
            cost=18,
        )

    def grad_of(kernel, span, shifted, act, scratch):
        own, other = run(
            kernel,
            [shape((ny, cs, span)), shape((ny, cs, span), BF16)],
            [shifted, act],
            [scratch, pltpu.VMEM((2, ny, cs, span), F32)],
            cost=28,
        )
        return own, to_gx(other, 1)

    def grad_mid(shifted, act):
        return grad_of(
            part(weight_grad, unit_mid), span_mid, shifted, act, pltpu.VMEM((9 * cs, c_out), F32)
        )

    def over_pair(own, other):
        span = own.shape[2]
        return run(
            part(reduce_core, 1),
            [shape((ny, cb, span))] + [shape((ny, cb, span), BF16)] * (sides - 1),
            [own, other],
            [pltpu.VMEM((ny, cs, span), F32)],
        )

    def to_sides(parts, *then):
        parts = [after(p, *then) for p in parts] if then else parts
        return [parts[0]] + [to_gx(parts[k], 2 * k) for k in range(1, sides)]

    def over_sides(*groups):
        span = sum(parts[0].shape[2] for parts in groups)
        return run(
            part(reduce_side, tuple(len(parts) for parts in groups)),
            shape((ny, cb, span), BF16),
            [p for parts in groups for p in parts],
        )

    def folded(got):
        out = shape((fy * cb, got.shape[2]), BF16)
        return over_x(run(part(fold, nz, fy), out, [got]))

    def rows_of(pieces, spans, *rows):
        return run(
            part(own_rows, nx, spans),
            [shape((r, c_out)) for r in rows],
            pieces,
            [pltpu.VMEM((2, sides, fy * cb, pieces[0].shape[1]), BF16)],
            cost=30,
        )

    def own(gain, shift):
        pair = jnp.stack([gain, shift], axis=1)
        return lax.dynamic_slice_in_dim(pair, me * cs, cs, axis=0)

    p_middle = own(gain_middle, shift_middle)
    p_inner = own(gain_inner, shift_inner)
    p_last = own(gain_last, shift_last)
    g_entry, s_entry = gain_entry[None], shift_entry[None]
    pixels = images.reshape(side * side, c_in)

    image, wide = run(
        part(entry_image, small),
        [shape((4 * area, lanes), BF16), shape((4 * area, 128))],
        [pixels, pixel_mask.reshape(side, side), valid_count],
        scalars=1,
    )
    group = share([image] * PEERS)
    out_first = ready(span_first, (2,), conv_first, projection)
    stats = run(part(entry_stats, area), entry_stat, group)
    pieces = pool_gx(stats)
    got_first = turn(after(out_first, *group[1:]))
    got_first = over_core(over_x(after(got_first, *pieces[1:])))
    pooled = pool_z(merge(pieces, merge_stats))
    out_middle = ready(span_mid, (1, 1), conv_second, conv_third)
    got_middle = turn(after(out_middle, pooled[-1]))
    out_fourth = ready(span_mid, (1,), conv_fourth)
    first, skipped, stats, norm_one, narrow, act_one, w_first = run(
        part(entry_block, nz, nx, unit_first, unit_skip, area, small),
        [
            tile,
            tile,
            stat,
            entry_stat,
            shape((8, width)),
            shape((4, width, c_in), BF16),
            shape((10 * cs, c_in), BF16),
        ],
        [*group, *pooled, g_entry, s_entry, *got_first],
        [
            pltpu.VMEM((nz, 8, lanes), F32),
            pltpu.VMEM((width, lanes), BF16),
            pltpu.VMEM((cs, span_of(9 * c_in)), BF16),
            halves(span_first, cb),
        ],
        cost=40,
        far=(3, 5, 6),
    )

    merged = merge(pool_gx(stats), merge_stats)
    got_middle = over_x(after(got_middle, merged))
    pooled = pool_z(merged)
    got_fourth = turn(after(out_fourth, pooled[-1]))
    normed_two, scale_two, *messages = activate(
        first, p_middle, pooled, cotangent.reshape(area, c_out)
    )
    pieces = share(messages)
    got_middle = over_core(got_middle, *pieces[1:])
    hidden, stats, act_two, w_second = convolve(pieces, got_middle, skipped)
    cot_parts = pieces
    merged = merge(pool_gx(stats), merge_stats)
    pooled = pool_z(merged)
    got_fourth = over_x(after(got_fourth, pooled[-1]))
    normed_three, scale_three, act = activate(hidden, p_inner, pooled)
    pieces = share([act] * PEERS)
    third, stats, act_three, w_third = convolve(pieces, got_middle, None, section=1)
    got_fourth = over_core(got_fourth, stats)
    merged = merge(pool_gx(stats), merge_stats)

    cot, shifted_four, w_fourth, *parts = run(
        part(last_back, nx, unit_mid, 0, area, small),
        [tile, shifted16, whole16] + [tile16] * PEERS,
        [*cot_parts, *got_fourth],
        [pltpu.VMEM((c_out, width), F32), halves(span_mid, cb)],
        cost=18,
        far=(0, 1, 2),
    )
    parts = share(parts)
    normed_four, scale_four, act = activate(third, p_last, pool_z(merged))
    pieces = share([act] * PEERS)
    grad_pre, sums = slope(parts, normed_four, p_last)
    sums = pool_gx(sums)
    *riders, act_four = convolve(pieces, [w_fourth], hidden, last=True)
    sums = pool_z(merge(sums, add_gx))
    fourth = grad_mid(shifted_four, act_four)
    last_sums, shifted_three, *parts = back(
        grad_pre, normed_four, scale_four, p_last, sums, w_third, None, riders
    )
    parts = share(parts)
    fourth = over_pair(*fourth)
    grad_pre, sums = slope(parts, normed_three, p_inner)
    sums = pool_gx(sums)
    third = grad_mid(shifted_three, act_three)
    merged = merge(sums, add_gx)
    fourth = to_sides(fourth, merged)
    sums = pool_z(merged)
    out = run(
        join_result, shape((area, c_out), BF16), parts, [pltpu.VMEM((c_out, 128), F32)]
    )
    inner_sums, shifted_two, grad_hidden, *parts = back(
        grad_pre, normed_three, scale_three, p_inner, sums, w_second, cot
    )
    parts = share(parts)
    third = over_pair(*third)
    grad_pre, sums = slope(parts, normed_two, p_middle)
    sums = pool_gx(sums)
    fourth = over_sides(fourth)
    second = grad_mid(shifted_two, act_two)
    merged = merge(sums, add_gx)
    third = to_sides(third, merged)
    sums = pool_z(merged)
    second = to_sides(over_pair(*second), merged)
    middle_sums, shifted_one, *parts = run(
        part(norm_back, nz, False, True, area, small),
        [stat, shape((10 * cs, width), BF16)] + [shape((4 * area, c_in), BF16)] * PEERS,
        [
            grad_pre,
            normed_two,
            scale_two,
            p_middle,
            narrow,
            *sums,
            w_first,
            grad_hidden,
        ],
        [pltpu.VMEM((4, width, c_in), F32), pltpu.VMEM((nz, 8, cs), F32)],
        cost=18,
    )

    late = turn(over_sides([fourth], third))
    parts = share(parts)
    second = over_sides(second)
    first = grad_of(
        part(weight_grad_first, unit_first, unit_skip),
        span_first,
        shifted_one,
        act_one,
        pltpu.VMEM((cs, span_of(9 * c_in + span_first + 128)), F32),
    )
    first = to_sides(over_pair(*first))
    early = turn(over_sides([second], first))
    grad_pre, sums = run(
        part(entry_back, small),
        [shape((4 * area, c_in)), shape((8, padded))],
        [*parts, pixels, norm_one, g_entry, s_entry],
        cost=13,
    )
    message = run(bundle, shape((16, padded)), [middle_sums, inner_sums, last_sums, sums])
    message = share([message] * PEERS)
    late = folded(late)
    sums, six = run(
        unbundle,
        [shape((8, padded)), shape((8, c_out))],
        message,
        [pltpu.VMEM((PEERS, 16, padded), F32)],
    )
    merged = merge(pool_gx(sums), add_gx)
    sums = pool_z(merged)
    early = folded(early)
    fourth_grad, third_grad = rows_of(
        over_core(late, merged),
        ((span_mid, (0,)), (span_mid, (1,))),
        2 * unit_mid,
        2 * unit_mid,
    )
    gain_entry_grad, shift_entry_grad, image_grad = run(
        part(entry_grad, nz),
        [shape((1, padded)), shape((1, padded)), shape((4 * area, c_in))],
        [*sums, grad_pre, pixels, wide, norm_one, g_entry],
        [pltpu.VMEM((nz, 8, padded), F32)],
    )
    second_grad, first_grad, skip_grad = rows_of(
        over_core(early),
        ((span_mid, (0,)), (span_first, (1, 2))),
        2 * unit_mid,
        2 * unit_first,
        2 * unit_skip,
    )
    return (
        out.reshape(1, small, small, c_out),
        image_grad.reshape(1, side, side, c_in),
        gain_entry_grad[0, :c_in],
        shift_entry_grad[0, :c_in],
        first_grad,
        six[0],
        six[1],
        second_grad,
        skip_grad,
        six[2],
        six[3],
        third_grad,
        six[4],
        six[5],
        fourth_grad,
    )


def solution(mesh):
    whole = P(("gx", "gy"), None, None, None)
    rows = P("gy", None)
    return jax.shard_map(
        functools.partial(program, mesh.shape["gx"], mesh.shape["gy"]),
        mesh=mesh,
        in_specs=(
            whole,
            P(("gx", "gy")),
            P(("gx", "gy"), None, None),
            P(),
            P(),
            rows,
            P(),
            P(),
            rows,
            rows,
            P(),
            P(),
            rows,
            P(),
            P(),
            rows,
            whole,
        ),
        out_specs=(
            whole, whole, P(), P(), rows, P(), P(), rows, rows, P(), P(), rows, P(), P(), rows,
        ),
        check_vma=False,
    )
```

```python
import functools

import jax
import jax.numpy as jnp
from jax import lax
from jax.experimental import pallas as pl
from jax.experimental.pallas import tpu as pltpu
from jax.sharding import PartitionSpec as P

EPS = 1e-05
COST = 6 * 10**7
F32 = jnp.float32
BF16 = jnp.bfloat16
PEERS = 4
C0 = 0.7978845608028654
C1 = 0.044715
VMEM = pl.BlockSpec(memory_space=pltpu.VMEM)
SMEM = pl.BlockSpec(memory_space=pltpu.SMEM)


def gelu(v):
    return 0.5 * v * (1.0 + jnp.tanh(C0 * (v + C1 * (v * v * v))))


def gelu_slope(v):
    t = jnp.tanh(C0 * (v + C1 * (v * v * v)))
    return 0.5 * (1.0 + t) + 0.5 * v * (1.0 - t * t) * (C0 * (1.0 + 3.0 * C1 * (v * v)))


def after(value, *others):
    return lax.optimization_barrier((value, *others))[0]


class Far:
    def __init__(self, near, far, sem):
        self.near, self.shape, self.dtype = near, near.shape, near.dtype
        self.copy = pltpu.make_async_copy(near, far, sem)
        self.sent = False

    def __getitem__(self, at):
        return self.near[at]

    def __setitem__(self, at, value):
        self.near[at] = value

    def send(self):
        if not self.sent:
            self.copy.start()
            self.sent = True


def send(ref):
    if isinstance(ref, Far):
        ref.send()


def with_far(kernel, n_in, n_out, far, *refs):
    ins, outs, rest = refs[:n_in], list(refs[n_in : n_in + n_out]), list(refs[n_in + n_out :])
    if far:
        sems = rest.pop()
        near = rest[len(rest) - len(far) :]
        del rest[len(rest) - len(far) :]
        for n, at in enumerate(far):
            outs[at] = Far(near[n], outs[at], sems.at[n])
    kernel(*ins, *outs, *rest)
    for at in far:
        outs[at].send()
    for at in far:
        outs[at].copy.wait()


class Order:
    def __init__(self, idx):
        self.idx = idx
        self.last = ()

    def __call__(self, kernel, outs, args, scratch=(), scalars=0, cost=7, far=()):
        idx = after(self.idx, *self.last)
        many = isinstance(outs, (list, tuple))
        shapes = list(outs) if many else [outs]
        more = [pltpu.VMEM(shapes[at].shape, shapes[at].dtype) for at in far]
        if far:
            more.append(pltpu.SemaphoreType.DMA((len(far),)))
        got = pl.pallas_call(
            functools.partial(with_far, kernel, 1 + len(args), len(shapes), tuple(far)),
            out_shape=shapes,
            in_specs=[SMEM] + [VMEM] * (len(args) - scalars) + [SMEM] * scalars,
            out_specs=[
                pl.BlockSpec(memory_space=pl.ANY) if at in far else VMEM
                for at in range(len(shapes))
            ],
            scratch_shapes=list(scratch) + more,
            compiler_params=pltpu.CompilerParams(vmem_limit_bytes=16 * 1024 * 1024),
            cost_estimate=pl.CostEstimate(
                flops=cost * COST, bytes_accessed=1024, transcendentals=0
            ),
        )(idx, *args)
        near = [v for at, v in enumerate(got) if at not in far]
        self.last = (near[0] if near else got[0],)
        return got if many else got[0]


def shape(dims, dtype=F32):
    return jax.ShapeDtypeStruct(dims, dtype)


def rows_at(index, count):
    return pl.ds(pl.multiple_of(index * count, count), count)


def as_rows(parts):
    height = parts[0].shape[0]
    lane = lax.broadcasted_iota(jnp.int32, (height, 128), 1)
    out = jnp.zeros((height, 128), F32)
    for k, part in enumerate(parts):
        out = jnp.where(lane == k, part, out)
    return out.T[0:8]


def as_columns(rows):
    return jnp.concatenate([rows, jnp.zeros((120, rows.shape[1]), F32)], axis=0).T


def in_order(refs, me, scratch):
    for k, ref in enumerate(refs):
        scratch[me ^ k] = ref[...]
    return [scratch[k] for k in range(len(refs))]


def merge_moments(stats):
    total = sum(n for _, _, n in stats)
    mean = sum(n * m for m, _, n in stats) / total
    squares = sum(q + n * (m - mean) * (m - mean) for m, q, n in stats)
    return mean, squares, total


def merge_rows(refs):
    mean, squares, total = merge_moments([(g[0:1], g[1:2], g[2:3]) for g in refs])
    return mean, squares, total, sum(g[3:4] for g in refs)


def pixel(width, area, small):
    lane = lax.broadcasted_iota(jnp.int32, (1, width), 1) % area
    return lane // small, lane % small


def inside(row, col, drow, dcol, small):
    return (row + drow >= 0) & (row + drow < small) & (col + dcol >= 0) & (col + dcol < small)


def moved(value, step):
    shift = (-step) % value.shape[1]
    return pltpu.roll(value, shift, 1) if shift else value


OFFSETS = [(0, krow - 1, kcol - 1) for krow in range(3) for kcol in range(3)]

STRIDED = [
    ((krow != 1) * 2 + (kcol != 1), -(krow == 0), -(kcol == 0))
    for krow in range(3)
    for kcol in range(3)
] + [(0, 0, 0)]
PLACED = sorted(range(10), key=lambda k: (STRIDED[k][0], k))
PHASES = [[k for k in PLACED if STRIDED[k][0] == phase] for phase in range(4)]


def row_of(k, cs):
    at = PLACED.index(k)
    return slice(at * cs, (at + 1) * cs)


def phase_rows(phase, cs):
    first, last = PHASES[phase][0], PHASES[phase][-1]
    return slice(PLACED.index(first) * cs, (PLACED.index(last) + 1) * cs)


def masked_stats(value, weight, n):
    mean = jnp.sum(value * weight, axis=1, keepdims=True) / n
    centred = value - mean
    return mean, jnp.sum(weight * centred * centred, axis=1, keepdims=True)


def span_of(rows):
    return -(-rows // 128) * 128


def one_hot(height, width, shift):
    row = lax.broadcasted_iota(jnp.int32, (height, width), 0)
    col = lax.broadcasted_iota(jnp.int32, (height, width), 1)
    return (col == row + shift).astype(BF16)


def pick32(left, right, dims=((1,), (0,))):
    return lax.dot_general(left, right, (dims, ((), ())), preferred_element_type=F32)


def pick(left, right, dims=((1,), (0,))):
    return pick32(left, right, dims).astype(BF16)


def lane_tile(held, tile, rows, span):
    sides, ny = held.shape[1], held.shape[2]
    lane = lax.broadcasted_iota(jnp.int32, (1, 128), 1)
    out = None
    for v in range(2 * ny):
        begin = rows * v - tile * 128
        if begin >= 128 or begin + rows <= 0:
            continue
        at = (tile - rows * v // 128) * 128 % span
        part = jnp.concatenate(
            [held[v % 2, x, v // 2, :, at : at + 128].astype(F32) for x in range(sides)], axis=0
        )
        if begin > 0 or begin + rows < 128:
            own = (lane >= begin) & (lane < begin + rows)
            part = jnp.where(own, part, 0.0)
        out = part if out is None else out + part
    return out.astype(BF16)


def pixel_order(small, width, of):
    area = small * small
    row = lax.broadcasted_iota(jnp.int32, (4 * area, width), 0)
    col = lax.broadcasted_iota(jnp.int32, (4 * area, width), 1)
    phase, pix = row // area, row % area
    y = 2 * (pix // small) + phase // 2
    x = 2 * (pix % small) + phase % 2
    return (col == of(y, x)).astype(BF16)


def entry_image(small, idx, image, mask, valid, out, weight):
    side = 2 * small
    c_in = image.shape[1]
    count = side * side
    order = pixel_order(small, count, lambda y, x: y * side + x)
    out[:, :c_in] = pick(order, image[...])
    live = (valid[0] > 0).astype(F32)
    row = lax.broadcasted_iota(jnp.int32, (count, side), 0)
    col = lax.broadcasted_iota(jnp.int32, (count, side), 1)
    by_row = jnp.dot(
        (row // side == col).astype(BF16),
        mask[...].astype(F32).astype(BF16),
        preferred_element_type=F32,
    )
    column = jnp.sum(jnp.where(row % side == col, by_row, 0.0), axis=1, keepdims=True) * live
    lane = lax.broadcasted_iota(jnp.int32, (count, 128), 1)
    spread = jnp.where(lane == 0, column, 0.0)
    weight[...] = spread
    out[:, c_in:] = pick(order, spread.astype(BF16))[:, : out.shape[1] - c_in]


def entry_weights(cs, fy, sections, idx, *refs):
    weights, out = list(refs[:-1]), refs[-1]
    ny, cb, lanes = out.shape
    span = lanes // len(sections)
    gx, gy = idx[2], idx[3]
    core, side = gx % 2, (gx // 2 if cb < cs else 0)
    c_out = weights[0].shape[1]
    row = lax.broadcasted_iota(jnp.int32, (fy * cb, c_out), 0)
    col = lax.broadcasted_iota(jnp.int32, (fy * cb, c_out), 1)
    chosen = (col == row // cb * cs + side * cb + row % cb).astype(BF16)
    for n, count in enumerate(sections):
        begin = weights[0].shape[0] // 2 * (2 * gy + core) % 128
        total = None
        for _ in range(count):
            weight = weights.pop(0)
            rows = weight.shape[0]
            half = rows // 2
            mine = pick(chosen, weight[...], ((1,), (1,)))
            row = lax.broadcasted_iota(jnp.int32, (rows, span), 0) - core * half
            col = lax.broadcasted_iota(jnp.int32, (rows, span), 1)
            place = (row >= 0) & (row < half) & (
                (col == row + begin) | (col == row + begin - span)
            )
            part = pick32(mine, place.astype(BF16))
            total = part if total is None else total + part
            begin = begin + half
        for j in range(ny):
            out[j, :, n * span : (n + 1) * span] = total[
                (j % fy) * cb : (j % fy + 1) * cb
            ].astype(BF16)


def hold(gx, messages, held, section=0):
    span = held.shape[4]
    for k, ref in enumerate(messages):
        at = gx ^ k
        side = at // 2 if held.shape[1] > 1 else 0
        held[at % 2, side] = ref[:, :, section * span : (section + 1) * span]


def assemble(held, out, rows):
    cs, span = held.shape[1] * held.shape[3], held.shape[4]
    tiles = out.shape[1] // 128
    for k in range(9):
        for q in range(tiles):
            out[k * cs : (k + 1) * cs, q * 128 : (q + 1) * 128] = lane_tile(
                held, tiles * k + q, rows, span
            )


def assemble_first(held, out, flat, rows, extra):
    cs, span = held.shape[1] * held.shape[3], held.shape[4]
    c_in = out.shape[1]
    tiles = flat.shape[1] // 128
    for tile in range(tiles):
        flat[:, tile * 128 : (tile + 1) * 128] = lane_tile(held, tile, rows, span)
    for k in range(9):
        begin = k * c_in
        base = begin // 128 * 128
        reach = min(-(-(begin + c_in) // 128) * 128, flat.shape[1])
        move = one_hot(c_in, reach - base, begin - base)
        out[row_of(k, cs), :] = pick(flat[:, base:reach], move, ((1,), (1,)))
    total = None
    for v in range(2 * held.shape[2]):
        row = lax.broadcasted_iota(jnp.int32, (span, c_in), 0)
        col = lax.broadcasted_iota(jnp.int32, (span, c_in), 1)
        at = col - extra * v
        begin = rows * v % 128 + rows
        place = (at >= 0) & (at < extra) & ((row == at + begin) | (row == at + begin - span))
        part = jnp.concatenate(
            [
                pick32(held[v % 2, x, v // 2], place.astype(BF16))
                for x in range(held.shape[1])
            ],
            axis=0,
        )
        total = part if total is None else total + part
    out[row_of(9, cs), :] = total.astype(BF16)


def entry_stats(area, idx, *refs):
    images, out = refs[:PEERS], refs[PEERS]
    lanes = out.shape[1]
    first = jnp.zeros((1, lanes), F32)
    wide = jnp.zeros((1, 1), F32)
    narrow = jnp.zeros((1, 1), F32)
    c_in = lanes - 64
    for ref in images:
        x = ref[...].astype(F32)
        w = x[:, c_in : c_in + 1]
        first += jnp.sum(x * w, axis=0, keepdims=True)
        wide += jnp.sum(w, axis=0, keepdims=True)
        narrow += jnp.sum(w[:area], axis=0, keepdims=True)
    mean = first / wide
    squares = jnp.zeros((1, lanes), F32)
    for ref in images:
        x = ref[...].astype(F32)
        w = x[:, c_in : c_in + 1]
        d = x - mean
        squares += jnp.sum(d * d * w, axis=0, keepdims=True)
    out[...] = jnp.zeros_like(out)
    out[0:1, :] = mean
    out[1:2, :] = squares
    out[2:3, :] = jnp.broadcast_to(wide, (1, lanes))
    out[3:4, :] = jnp.broadcast_to(narrow, (1, lanes))


def entry_block(nz, nx, rows, extra, area, small, idx, *refs):
    images = refs[:PEERS]
    stats, rest = refs[PEERS : PEERS + nz], refs[PEERS + nz :]
    gain, shift, messages, rest = rest[0], rest[1], rest[2 : 2 + nx], rest[2 + nx :]
    first, skipped, out_stats, norm, narrow, act, w_first = rest[:7]
    order, masks, flat, held = rest[7:]
    me, mine = idx[0], idx[1]
    c_in = gain.shape[1]
    lanes = norm.shape[1]
    cs = first.shape[0]
    width = first.shape[1]
    hold(idx[2], messages, held)
    assemble_first(held, w_first, flat, rows, extra)
    send(w_first)
    mean, squares, total, count = merge_rows(in_order(stats, mine, order))
    scale = lax.rsqrt(squares / total + EPS)
    norm[...] = jnp.zeros_like(norm)
    norm[0:1, :] = mean
    norm[1:2, :] = scale
    norm[2:3, :] = total
    norm[3:4, :] = count
    for k, ref in enumerate(images):
        x = ref[...]
        v = x[:, :c_in].astype(F32)
        pre = gain[...] * ((v - mean[:, :c_in]) * scale[:, :c_in]) + shift[...]
        a = gelu(pre).astype(BF16)
        for phase in range(4):
            act[phase, rows_at(me ^ k, area), :] = a[phase * area : (phase + 1) * area]
        masks[rows_at(me ^ k, area), :] = x[:area]
    send(act)
    send(norm)
    ones = (lax.broadcasted_iota(jnp.int32, (8, lanes), 1) == c_in).astype(BF16)
    weight8 = lax.dot_general(
        ones, masks[...], (((1,), (1,)), ((), ())), preferred_element_type=F32
    )
    narrow[...] = weight8
    weight = weight8[0:1]
    row, col = pixel(width, area, small)
    total_first = jnp.zeros((cs, width), F32)
    for phase in range(4):
        group = lax.dot_general(
            w_first[phase_rows(phase, cs), :],
            act[phase],
            (((1,), (1,)), ((), ())),
            preferred_element_type=F32,
        )
        for at, k in enumerate(PHASES[phase]):
            y = group[at * cs : (at + 1) * cs]
            if k == 9:
                skipped[...] = y
                continue
            _, drow, dcol = STRIDED[k]
            y = moved(y, drow * small + dcol)
            total_first += jnp.where(inside(row, col, drow, dcol, small), y, 0.0)
    first[...] = total_first
    n = jnp.sum(weight, axis=1, keepdims=True)
    mean2, squares = masked_stats(total_first, weight, n)
    out_stats[...] = as_rows((mean2, squares, n))


def merge_stats(idx, *refs):
    out, order = refs[-2:]
    mean, squares, total, count = merge_rows(in_order(refs[:-2], idx[2], order))
    out[...] = jnp.zeros_like(out)
    out[0:1] = mean
    out[1:2] = squares
    out[2:3] = total
    out[3:4] = count


def add_rows(which, idx, *refs):
    out, order = refs[-2:]
    got = in_order(refs[:-2], idx[which], order)
    total = got[0]
    for g in got[1:]:
        total = total + g
    out[...] = total


def act_block(nz, idx, *refs):
    value, params = refs[:2]
    stats, rest = refs[2 : 2 + nz], refs[2 + nz :]
    if rest[-1].shape[1] == 128:
        cot, normed, scales, outs, order, stack = (*rest[:3], rest[3:-2], *rest[-2:])
    else:
        cot, normed, scales, outs, order = (None, *rest[:2], rest[2:-1], rest[-1])
    mean, squares, total, _ = merge_rows(in_order(stats, idx[1], order))
    rows = jnp.concatenate(
        [mean, lax.rsqrt(squares / total + EPS), total, jnp.zeros((5, mean.shape[1]), F32)], axis=0
    )
    cols = as_columns(rows)
    norm = (value[...] - cols[:, 0:1]) * cols[:, 1:2]
    normed[...] = norm
    send(normed)
    scales[...] = cols
    send(scales)
    act = gelu(params[:, 0:1] * norm + params[:, 1:2]).astype(BF16)
    cs, width = norm.shape
    if cot is not None:
        c = cot[...].astype(F32)
        stack[...] = jnp.concatenate([c, c], axis=0).T
    for k, out in enumerate(outs):
        out[:, :width] = act
        if cot is not None:
            out[:, width:] = stack[rows_at(idx[0] ^ k, cs), :].astype(BF16)


def conv_block(nx, added, last, rows, section, area, small, idx, *refs):
    pieces = refs[:PEERS]
    narrow, rest = refs[PEERS], refs[PEERS + 1 :]
    if last:
        weights, rest = rest[0], rest[1:]
    else:
        messages, rest = rest[:nx], rest[nx:]
    base, rest = (rest[0], rest[1:]) if added else (None, rest)
    me = idx[0]
    cs, width = pieces[0].shape[0], narrow.shape[1]
    if last:
        outs, act, spread = rest[:PEERS], rest[PEERS], rest[PEERS + 1]
    else:
        value, out_stats, act, whole, spread, held = rest
        hold(idx[2], messages, held, section)
        assemble(held, whole, rows)
        send(whole)
        weights = whole
    for k, ref in enumerate(pieces):
        act[rows_at(me ^ k, cs), :] = ref[:, :width]
    send(act)
    spread[...] = jnp.dot(weights[...], act[...], preferred_element_type=F32)
    row, col = pixel(width, area, small)
    total = base[...] if added else jnp.zeros((cs, width), F32)
    for k, (_, drow, dcol) in enumerate(OFFSETS):
        y = moved(spread[k * cs : (k + 1) * cs, :], drow * small + dcol)
        total += jnp.where(inside(row, col, drow, dcol, small), y, 0.0)
    if last:
        result = total.astype(BF16)
        lane = lax.broadcasted_iota(jnp.int32, (width, 128), 0)
        slot = lax.broadcasted_iota(jnp.int32, (width, 128), 1)
        for k, out in enumerate(outs):
            out[...] = pick(result, (lane == (me ^ k) * area + slot).astype(BF16))
    else:
        value[...] = total
        weight = narrow[0:1, :]
        n = jnp.sum(weight, axis=1, keepdims=True)
        mean, squares = masked_stats(total, weight, n)
        out_stats[...] = as_rows((mean, squares, n))


def join_result(idx, *refs):
    pieces, (out, stack) = refs[:PEERS], refs[PEERS:]
    cs = pieces[0].shape[0]
    for k, ref in enumerate(pieces):
        stack[rows_at(idx[0] ^ k, cs), :] = ref[:, -128:].astype(F32)
    out[...] = stack[...].T[: out.shape[0]].astype(BF16)


def spread_grad(grad, shifted, area, small, offs, row_at):
    cs, width = grad.shape
    row, col = pixel(width, area, small)
    for k, (_, drow, dcol) in enumerate(offs):
        g = moved(grad, -(drow * small + dcol))
        g = jnp.where(inside(row, col, -drow, -dcol, small), g, 0.0)
        shifted[row_at(k, cs), :] = g.astype(BF16)


def plain_rows(k, cs):
    return slice(k * cs, (k + 1) * cs)


def push_back(me, weights, shifted, partial, outs):
    cs, width = outs[0].shape[0], shifted.shape[1]
    partial[...] = lax.dot_general(
        weights[...], shifted[...], (((0,), (0,)), ((), ())), preferred_element_type=F32
    )
    for k, out in enumerate(outs):
        out[:, :width] = partial[rows_at(me ^ k, cs), :].astype(BF16)


def last_back(nx, rows, section, area, small, idx, *refs):
    pieces, messages, rest = refs[:PEERS], refs[PEERS : PEERS + nx], refs[PEERS + nx :]
    cot, shifted, weights = rest[:3]
    outs = rest[3 : PEERS + 3]
    partial, held = rest[PEERS + 3 :]
    hold(idx[2], messages, held, section)
    assemble(held, weights, rows)
    send(weights)
    me = idx[0]
    cs, width = cot.shape
    image = lax.broadcasted_iota(jnp.int32, (1, width), 1) // area
    grad = jnp.zeros((cs, width), F32)
    for k, ref in enumerate(pieces):
        tiled = jnp.concatenate([ref[:, width:].astype(F32)] * (width // 128), axis=1)
        grad = jnp.where(image == (me ^ k), tiled, grad)
    cot[...] = grad
    send(cot)
    spread_grad(grad, shifted, area, small, OFFSETS, plain_rows)
    send(shifted)
    push_back(me, weights, shifted, partial, outs)


def gelu_back(idx, *refs):
    pieces = refs[:PEERS]
    normed, params, grad_pre, sums = refs[PEERS:]
    width = normed.shape[1]
    grad = pieces[0][:, :width].astype(F32)
    for ref in pieces[1:]:
        grad += ref[:, :width].astype(F32)
    norm = normed[...]
    g = gelu_slope(params[:, 0:1] * norm + params[:, 1:2]) * grad
    grad_pre[...] = g
    sums[...] = as_rows(
        (jnp.sum(g * norm, axis=1, keepdims=True), jnp.sum(g, axis=1, keepdims=True))
    )


def norm_back(nz, added, last, area, small, idx, *refs):
    grad_pre, normed, scales, params, narrow = refs[:5]
    sums = refs[5 : 5 + nz]
    rest = refs[5 + nz :]
    base, rest = (rest[0], rest[1:]) if added else (None, rest)
    me = idx[0]
    cs, width = grad_pre.shape
    order = rest[-1]
    got = in_order(sums, idx[1], order)
    total = got[0]
    for g in got[1:]:
        total = total + g
    cols = as_columns(total)
    gain_grad, shift_grad = cols[:, 0:1], cols[:, 1:2]
    norm = normed[...]
    back = params[:, 0:1] * scales[:, 1:2] * (
        grad_pre[...]
        - narrow[0:1, :] * (shift_grad + norm * gain_grad) / scales[:, 2:3]
    )
    if added:
        back = base[...] + back
    grad = back.astype(BF16).astype(F32)
    if not last:
        riders = ()
        if not added:
            riders, rest = rest[:PEERS], rest[PEERS:]
        weights, sums_out, shifted = rest[:3]
        outs, partial = rest[3 : 3 + PEERS], rest[3 + PEERS]
        for rider, out in zip(riders, outs):
            out[:, width:] = rider[...]
        if added:
            grad_out, outs, partial = rest[3], rest[4 : 4 + PEERS], rest[4 + PEERS]
            grad_out[...] = grad.astype(BF16)
        sums_out[...] = total
        spread_grad(grad, shifted, area, small, OFFSETS, plain_rows)
        push_back(me, weights, shifted, partial, outs)
    else:
        weights, grad_skip, sums_out, shifted = rest[:4]
        outs, partial = rest[4 : 4 + PEERS], rest[4 + PEERS]
        sums_out[...] = total
        spread_grad(grad, shifted, area, small, STRIDED[:9], row_of)
        shifted[row_of(9, cs), :] = grad_skip[...]
        for phase in range(4):
            partial[phase] = lax.dot_general(
                shifted[phase_rows(phase, cs), :],
                weights[phase_rows(phase, cs), :],
                (((0,), (0,)), ((), ())),
                preferred_element_type=F32,
            )
        for k, out in enumerate(outs):
            for phase in range(4):
                out[phase * area : (phase + 1) * area, :] = partial[
                    phase, rows_at(me ^ k, area), :
                ].astype(BF16)


def part_halves(core, units, own, other):
    own[...] = units[core]
    other[...] = units[1 - core].astype(BF16)


def weight_grad(rows, idx, shifted, act, own, other, full, units):
    full[...] = lax.dot_general(
        shifted[...], act[...], (((1,), (1,)), ((), ())), preferred_element_type=F32
    )
    ny, cs, span = own.shape
    tiles = full.shape[1] // 128
    for v in range(2 * ny):
        begin = rows * v % 128
        parts = []
        for q in range((begin + rows + 127) // 128):
            k, p = divmod(rows * v // 128 + q, tiles)
            parts.append(full[k * cs : (k + 1) * cs, p * 128 : (p + 1) * 128])
        window = jnp.concatenate(parts, axis=1)
        units[v % 2, v // 2] = moved(window, begin)[:, :span]
    part_halves(idx[2] % 2, units, own, other)


def weight_grad_first(rows, extra, idx, shifted, act, own, other, flat, units):
    ny, cs, span = own.shape
    c_in = act.shape[2]
    flat[...] = jnp.zeros_like(flat)
    skip = None
    for phase in range(4):
        group = jnp.dot(
            shifted[phase_rows(phase, cs), :], act[phase], preferred_element_type=F32
        ).astype(BF16)
        for at, k in enumerate(PHASES[phase]):
            grad = group[at * cs : (at + 1) * cs]
            if k == 9:
                skip = grad
                continue
            begin = k * c_in
            base = begin // 128 * 128
            reach = -(-(begin + c_in) // 128) * 128
            move = one_hot(c_in, reach - base, begin - base)
            flat[:, base:reach] += jnp.dot(grad, move, preferred_element_type=F32)
    lane = lax.broadcasted_iota(jnp.int32, (1, span), 1)
    for v in range(2 * ny):
        begin = rows * v % 128
        base = rows * v - begin
        window = moved(flat[:, base : base + span + 128], begin)[:, :span]
        row = lax.broadcasted_iota(jnp.int32, (c_in, span), 0)
        col = lax.broadcasted_iota(jnp.int32, (c_in, span), 1)
        place = (row >= extra * v) & (row < extra * (v + 1)) & (col == row - extra * v + rows)
        tail = pick32(skip, place.astype(BF16))
        units[v % 2, v // 2] = jnp.where(lane < rows, window, 0.0) + tail
    part_halves(idx[2] % 2, units, own, other)


def reduce_core(count, idx, *refs):
    own, other, outs, total = refs[:count], refs[count : 2 * count], refs[2 * count : -1], refs[-1]
    cb = outs[0].shape[1]
    at = 0
    for a, b in zip(own, other):
        span = a.shape[2]
        total[:, :, at : at + span] = a[...] + b[...].astype(F32)
        at += span
    for k, out in enumerate(outs):
        for j in range(total.shape[0]):
            out[j] = total[j, rows_at(idx[2] // 2 ^ k, cb), :].astype(out.dtype)


def reduce_side(sizes, idx, *refs):
    refs, out = refs[:-1], refs[-1]
    at = 0
    for size in sizes:
        total = refs[0][...].astype(F32)
        for ref in refs[1:size]:
            total += ref[...].astype(F32)
        out[:, :, at : at + total.shape[2]] = total.astype(BF16)
        refs = refs[size:]
        at += total.shape[2]


def fold(nz, fy, idx, got, out):
    cs = got.shape[1]
    for f in range(fy):
        total = got[f].astype(F32)
        for z in range(1, nz):
            total += got[z * fy + f].astype(F32)
        out[f * cs : (f + 1) * cs, :] = total.astype(BF16)


def own_rows(count, spans, idx, *refs):
    pieces, outs, stack = refs[:count], refs[count:-1], refs[-1]
    for k, ref in enumerate(pieces):
        at = idx[2] ^ k
        stack[at % 2, at // 2] = ref[...]
    sides, height = stack.shape[1], stack.shape[2]
    fy_cb = [(f, x) for f in range(PEERS) for x in range(sides)]
    cb = height // PEERS
    for half in range(2):
        whole = jnp.concatenate(
            [stack[half, x, f * cb : (f + 1) * cb, :].astype(F32) for f, x in fy_cb], axis=0
        ).T
        at = 0
        for span, group in spans:
            begin = at
            for n in group:
                out = outs[n]
                rows = out.shape[0] // 2
                out[half * rows : (half + 1) * rows, :] = whole[begin : begin + rows]
                begin += rows
            at += span


def entry_back(small, idx, *refs):
    pieces = refs[:PEERS]
    image, norm, gain, shift, grad_pre, sums = refs[PEERS:]
    c_in = gain.shape[1]
    side = 2 * small
    grad = pieces[0][...].astype(F32)
    for ref in pieces[1:]:
        grad += ref[...].astype(F32)
    order = pixel_order(small, side * side, lambda y, x: y * side + x)
    high = grad.astype(BF16)
    low = (grad - high.astype(F32)).astype(BF16)
    grad = sum(
        lax.dot_general(order, part, (((0,), (0,)), ((), ())), preferred_element_type=F32)
        for part in (high, low)
    )
    normed = (image[...].astype(F32) - norm[0:1, :c_in]) * norm[1:2, :c_in]
    g = gelu_slope(gain[...] * normed + shift[...]) * grad
    grad_pre[...] = g
    sums[...] = jnp.zeros_like(sums)
    sums[0:1, :c_in] = jnp.sum(g * normed, axis=0, keepdims=True)
    sums[1:2, :c_in] = jnp.sum(g, axis=0, keepdims=True)


def bundle(idx, first, second, third, sums, out):
    out[...] = jnp.zeros_like(out)
    out[0:8, :] = sums[...]
    for k, ref in enumerate((first, second, third)):
        out[8 + 2 * k : 10 + 2 * k, : ref.shape[1]] = ref[0:2]


def unbundle(idx, *refs):
    out, six, order = refs[-3:]
    got = in_order(refs[:-3], idx[0], order)
    total = got[0][0:8]
    for g in got[1:]:
        total = total + g[0:8]
    out[...] = total
    cs = six.shape[1] // PEERS
    six[...] = jnp.concatenate([g[8:16, :cs] for g in got], axis=1)


def entry_grad(nz, idx, *refs):
    sums = refs[:nz]
    grad_pre, image, weight, norm, gain, gain_grad, shift_grad, out, order = refs[nz:]
    got = in_order(sums, idx[1], order)
    total = got[0]
    for g in got[1:]:
        total = total + g
    gain_grad[...] = total[0:1]
    shift_grad[...] = total[1:2]
    c_in = gain.shape[1]
    scale = norm[1:2, :c_in]
    normed = (image[...].astype(F32) - norm[0:1, :c_in]) * scale
    out[...] = gain[...] * scale * (
        grad_pre[...]
        - weight[:, 0:1]
        * (shift_grad[0:1, :c_in] + normed * gain_grad[0:1, :c_in])
        / norm[2:3, :c_in]
    )


def program(
    nx,
    ny,
    images,
    valid_count,
    pixel_mask,
    gain_entry,
    shift_entry,
    conv_first,
    gain_middle,
    shift_middle,
    conv_second,
    projection,
    gain_inner,
    shift_inner,
    conv_third,
    gain_last,
    shift_last,
    conv_fourth,
    cotangent,
):
    fy = PEERS
    nz = ny // fy
    sides = nx // 2
    side, c_in = images.shape[1], images.shape[3]
    small = side // 2
    area = small * small
    c_out = conv_first.shape[1]
    cs = c_out // PEERS
    cb = cs // sides
    width = PEERS * area
    lanes = c_in + 64
    padded = span_of(c_in)
    gx, gy = lax.axis_index("gx"), lax.axis_index("gy")
    me = gy % fy
    mine = gy // fy
    run = Order(jnp.stack([me, mine, gx, gy]).astype(jnp.int32))
    part = functools.partial

    def to_slice(piece, k):
        return lax.ppermute(piece, "gy", [(j, j // fy * fy + (j % fy ^ k)) for j in range(ny)])

    def share(pieces):
        return [pieces[0]] + [to_slice(pieces[k], k) for k in range(1, PEERS)]

    def to_gx(piece, k):
        return lax.ppermute(piece, "gx", [(i, i ^ k) for i in range(nx)])

    def pool_gx(piece):
        return [piece] + [to_gx(piece, k) for k in range(1, nx)]

    def pool_z(piece):
        out = [piece]
        for k in range(1, nz):
            perm = [(j, (j // fy ^ k) * fy + j % fy) for j in range(ny)]
            out.append(lax.ppermute(piece, "gy", perm))
        return out

    def over_x(block):
        return {0: block, **{k: to_gx(block, k) for k in range(2, nx, 2)}}

    def over_core(held, *then):
        held = {k: after(v, *then) for k, v in held.items()} if then else dict(held)
        for k in list(held):
            held[k + 1] = to_gx(held[k], 1)
        return [held[k] for k in sorted(held)]

    def turn(block):
        return lax.all_to_all(block, "gy", 0, 0, tiled=True)

    unit_first, unit_skip = conv_first.shape[0] // 2, projection.shape[0] // 2
    unit_mid = conv_second.shape[0] // 2
    span_first, span_mid = span_of(unit_first + unit_skip), span_of(unit_mid)
    tile, tile16 = shape((cs, width)), shape((cs, width), BF16)
    long16 = shape((cs, width + 128), BF16)
    cols, stat, entry_stat = shape((cs, 128)), shape((8, cs)), shape((8, lanes))
    shifted16 = shape((9 * cs, width), BF16)
    full16 = shape((c_out, width), BF16)
    whole16 = shape((9 * cs, c_out), BF16)

    def halves(span, channels):
        return pltpu.VMEM((2, cs // channels, ny, channels, span), BF16)

    def ready(span, sections, *weights):
        out = shape((ny, cb, span * len(sections)), BF16)
        return run(
            part(entry_weights, cs, fy, sections), out, weights, cost=24 * len(sections)
        )

    def merge(pieces, kernel):
        like = pieces[0].shape
        return run(kernel, shape(like), pieces, [pltpu.VMEM((nx, *like), F32)])

    add_gx = part(add_rows, 2)

    def activate(value, params, pooled, cot=None):
        more = [] if cot is None else [cot]
        outs = [tile16] if cot is None else [long16] * PEERS
        return run(
            part(act_block, nz),
            [tile, cols] + outs,
            [value, params, *pooled, *more],
            [pltpu.VMEM((nz, 8, cs), F32)]
            + ([] if cot is None else [pltpu.VMEM((c_out, 128), F32)]),
            far=(0, 1),
        )

    def convolve(pieces, weights, base, section=0, last=False):
        more = [] if base is None else [base]
        outs = [shape((cs, 128), BF16)] * PEERS + [full16]
        return run(
            part(conv_block, nx, base is not None, last, unit_mid, section, area, small),
            outs if last else [tile, stat, full16, whole16],
            [*pieces, narrow, *weights, *more],
            [pltpu.VMEM((9 * cs, width), F32)] + ([] if last else [halves(span_mid, cb)]),
            cost=25,
            far=() if last else (2, 3),
        )

    def slope(parts, normed, params):
        return run(gelu_back, [tile, stat], [*parts, normed, params])

    def back(grad_pre, normed, scales, params, pooled, weights, base, riders=()):
        more = list(riders) if base is None else [base]
        return run(
            part(norm_back, nz, base is not None, False, area, small),
            [stat, shifted16]
            + ([long16] * PEERS if base is None else [tile16] * (PEERS + 1)),
            [grad_pre, normed, scales, params, narrow, *pooled, *more, weights],
            [pltpu.VMEM((c_out, width), F32), pltpu.VMEM((nz, 8, cs), F32)],
            cost=18,
        )

    def grad_of(kernel, span, shifted, act, scratch):
        own, other = run(
            kernel,
            [shape((ny, cs, span)), shape((ny, cs, span), BF16)],
            [shifted, act],
            [scratch, pltpu.VMEM((2, ny, cs, span), F32)],
            cost=28,
        )
        return own, to_gx(other, 1)

    def grad_mid(shifted, act):
        return grad_of(
            part(weight_grad, unit_mid), span_mid, shifted, act, pltpu.VMEM((9 * cs, c_out), F32)
        )

    def over_pair(own, other):
        span = own.shape[2]
        return run(
            part(reduce_core, 1),
            [shape((ny, cb, span))] + [shape((ny, cb, span), BF16)] * (sides - 1),
            [own, other],
            [pltpu.VMEM((ny, cs, span), F32)],
        )

    def to_sides(parts, *then):
        parts = [after(p, *then) for p in parts] if then else parts
        return [parts[0]] + [to_gx(parts[k], 2 * k) for k in range(1, sides)]

    def over_sides(*groups):
        span = sum(parts[0].shape[2] for parts in groups)
        return run(
            part(reduce_side, tuple(len(parts) for parts in groups)),
            shape((ny, cb, span), BF16),
            [p for parts in groups for p in parts],
        )

    def folded(got):
        out = shape((fy * cb, got.shape[2]), BF16)
        return over_x(run(part(fold, nz, fy), out, [got]))

    def rows_of(pieces, spans, *rows):
        return run(
            part(own_rows, nx, spans),
            [shape((r, c_out)) for r in rows],
            pieces,
            [pltpu.VMEM((2, sides, fy * cb, pieces[0].shape[1]), BF16)],
            cost=30,
        )

    def own(gain, shift):
        pair = jnp.stack([gain, shift], axis=1)
        return lax.dynamic_slice_in_dim(pair, me * cs, cs, axis=0)

    p_middle = own(gain_middle, shift_middle)
    p_inner = own(gain_inner, shift_inner)
    p_last = own(gain_last, shift_last)
    g_entry, s_entry = gain_entry[None], shift_entry[None]
    pixels = images.reshape(side * side, c_in)

    image, wide = run(
        part(entry_image, small),
        [shape((4 * area, lanes), BF16), shape((4 * area, 128))],
        [pixels, pixel_mask.reshape(side, side), valid_count],
        scalars=1,
    )
    group = share([image] * PEERS)
    out_first = ready(span_first, (2,), conv_first, projection)
    stats = run(part(entry_stats, area), entry_stat, group)
    pieces = pool_gx(stats)
    got_first = turn(after(out_first, *group[1:]))
    got_first = over_core(over_x(after(got_first, *pieces[1:])))
    pooled = pool_z(merge(pieces, merge_stats))
    out_middle = ready(span_mid, (1, 1), conv_second, conv_third)
    got_middle = turn(after(out_middle, pooled[-1], got_first[2]))
    out_fourth = ready(span_mid, (1,), conv_fourth)
    first, skipped, stats, norm_one, narrow, act_one, w_first = run(
        part(entry_block, nz, nx, unit_first, unit_skip, area, small),
        [
            tile,
            tile,
            stat,
            entry_stat,
            shape((8, width)),
            shape((4, width, c_in), BF16),
            shape((10 * cs, c_in), BF16),
        ],
        [*group, *pooled, g_entry, s_entry, *got_first],
        [
            pltpu.VMEM((nz, 8, lanes), F32),
            pltpu.VMEM((width, lanes), BF16),
            pltpu.VMEM((cs, span_of(9 * c_in)), BF16),
            halves(span_first, cb),
        ],
        cost=40,
        far=(3, 5, 6),
    )

    merged = merge(pool_gx(stats), merge_stats)
    got_middle = over_x(after(got_middle, merged))
    pooled = pool_z(merged)
    got_fourth = turn(after(out_fourth, pooled[-1]))
    normed_two, scale_two, *messages = activate(
        first, p_middle, pooled, cotangent.reshape(area, c_out)
    )
    pieces = share(messages)
    got_middle = over_core(got_middle, *pieces[1:])
    hidden, stats, act_two, w_second = convolve(pieces, got_middle, skipped)
    cot_parts = pieces
    merged = merge(pool_gx(stats), merge_stats)
    pooled = pool_z(merged)
    got_fourth = over_x(after(got_fourth, pooled[-1]))
    normed_three, scale_three, act = activate(hidden, p_inner, pooled)
    pieces = share([act] * PEERS)
    third, stats, act_three, w_third = convolve(pieces, got_middle, None, section=1)
    got_fourth = over_core(got_fourth, stats)
    merged = merge(pool_gx(stats), merge_stats)

    cot, shifted_four, w_fourth, *parts = run(
        part(last_back, nx, unit_mid, 0, area, small),
        [tile, shifted16, whole16] + [tile16] * PEERS,
        [*cot_parts, *got_fourth],
        [pltpu.VMEM((c_out, width), F32), halves(span_mid, cb)],
        cost=18,
        far=(0, 1, 2),
    )
    parts = share(parts)
    normed_four, scale_four, act = activate(third, p_last, pool_z(merged))
    pieces = share([act] * PEERS)
    grad_pre, sums = slope(parts, normed_four, p_last)
    sums = pool_gx(sums)
    *riders, act_four = convolve(pieces, [w_fourth], hidden, last=True)
    sums = pool_z(merge(sums, add_gx))
    fourth = grad_mid(shifted_four, act_four)
    last_sums, shifted_three, *parts = back(
        grad_pre, normed_four, scale_four, p_last, sums, w_third, None, riders
    )
    parts = share(parts)
    fourth = over_pair(*fourth)
    grad_pre, sums = slope(parts, normed_three, p_inner)
    sums = pool_gx(sums)
    third = grad_mid(shifted_three, act_three)
    merged = merge(sums, add_gx)
    fourth = to_sides(fourth, merged)
    sums = pool_z(merged)
    out = run(
        join_result, shape((area, c_out), BF16), parts, [pltpu.VMEM((c_out, 128), F32)]
    )
    inner_sums, shifted_two, grad_hidden, *parts = back(
        grad_pre, normed_three, scale_three, p_inner, sums, w_second, cot
    )
    parts = share(parts)
    third = over_pair(*third)
    grad_pre, sums = slope(parts, normed_two, p_middle)
    sums = pool_gx(sums)
    fourth = over_sides(fourth)
    second = grad_mid(shifted_two, act_two)
    merged = merge(sums, add_gx)
    third = to_sides(third, merged)
    sums = pool_z(merged)
    second = to_sides(over_pair(*second), merged)
    middle_sums, shifted_one, *parts = run(
        part(norm_back, nz, False, True, area, small),
        [stat, shape((10 * cs, width), BF16)] + [shape((4 * area, c_in), BF16)] * PEERS,
        [
            grad_pre,
            normed_two,
            scale_two,
            p_middle,
            narrow,
            *sums,
            w_first,
            grad_hidden,
        ],
        [pltpu.VMEM((4, width, c_in), F32), pltpu.VMEM((nz, 8, cs), F32)],
        cost=18,
    )

    late = turn(over_sides([fourth], third))
    parts = share(parts)
    second = over_sides(second)
    first = grad_of(
        part(weight_grad_first, unit_first, unit_skip),
        span_first,
        shifted_one,
        act_one,
        pltpu.VMEM((cs, span_of(9 * c_in + span_first + 128)), F32),
    )
    first = to_sides(over_pair(*first))
    early = turn(over_sides([after(second, *parts[1:])], first))
    grad_pre, sums = run(
        part(entry_back, small),
        [shape((4 * area, c_in)), shape((8, padded))],
        [*parts, pixels, norm_one, g_entry, s_entry],
        cost=13,
    )
    message = run(bundle, shape((16, padded)), [middle_sums, inner_sums, last_sums, sums])
    message = share([message] * PEERS)
    late = folded(late)
    sums, six = run(
        unbundle,
        [shape((8, padded)), shape((8, c_out))],
        message,
        [pltpu.VMEM((PEERS, 16, padded), F32)],
    )
    sums = pool_gx(sums)
    early = folded(early)
    merged = merge(sums, add_gx)
    sums = pool_z(merged)
    fourth_grad, third_grad = rows_of(
        over_core(late, merged),
        ((span_mid, (0,)), (span_mid, (1,))),
        2 * unit_mid,
        2 * unit_mid,
    )
    gain_entry_grad, shift_entry_grad, image_grad = run(
        part(entry_grad, nz),
        [shape((1, padded)), shape((1, padded)), shape((4 * area, c_in))],
        [*sums, grad_pre, pixels, wide, norm_one, g_entry],
        [pltpu.VMEM((nz, 8, padded), F32)],
    )
    second_grad, first_grad, skip_grad = rows_of(
        over_core(early),
        ((span_mid, (0,)), (span_first, (1, 2))),
        2 * unit_mid,
        2 * unit_first,
        2 * unit_skip,
    )
    return (
        out.reshape(1, small, small, c_out),
        image_grad.reshape(1, side, side, c_in),
        gain_entry_grad[0, :c_in],
        shift_entry_grad[0, :c_in],
        first_grad,
        six[0],
        six[1],
        second_grad,
        skip_grad,
        six[2],
        six[3],
        third_grad,
        six[4],
        six[5],
        fourth_grad,
    )


def solution(mesh):
    whole = P(("gx", "gy"), None, None, None)
    rows = P("gy", None)
    return jax.shard_map(
        functools.partial(program, mesh.shape["gx"], mesh.shape["gy"]),
        mesh=mesh,
        in_specs=(
            whole,
            P(("gx", "gy")),
            P(("gx", "gy"), None, None),
            P(),
            P(),
            rows,
            P(),
            P(),
            rows,
            rows,
            P(),
            P(),
            rows,
            P(),
            P(),
            rows,
            whole,
        ),
        out_specs=(
            whole, whole, P(), P(), rows, P(), P(), rows, rows, P(), P(), rows, P(), P(), rows,
        ),
        check_vma=False,
    )
```

```python
import functools

import jax
import jax.numpy as jnp
from jax import lax
from jax.experimental import pallas as pl
from jax.experimental.pallas import tpu as pltpu
from jax.sharding import PartitionSpec as P

EPS = 1e-05
COST = 6 * 10**7
F32 = jnp.float32
BF16 = jnp.bfloat16
PEERS = 4
C0 = 0.7978845608028654
C1 = 0.044715
VMEM = pl.BlockSpec(memory_space=pltpu.VMEM)
SMEM = pl.BlockSpec(memory_space=pltpu.SMEM)


def gelu(v):
    return 0.5 * v * (1.0 + jnp.tanh(C0 * (v + C1 * (v * v * v))))


def gelu_slope(v):
    t = jnp.tanh(C0 * (v + C1 * (v * v * v)))
    return 0.5 * (1.0 + t) + 0.5 * v * (1.0 - t * t) * (C0 * (1.0 + 3.0 * C1 * (v * v)))


def after(value, *others):
    return lax.optimization_barrier((value, *others))[0]


class Far:
    def __init__(self, near, far, sem):
        self.near, self.shape, self.dtype = near, near.shape, near.dtype
        self.copy = pltpu.make_async_copy(near, far, sem)
        self.sent = False

    def __getitem__(self, at):
        return self.near[at]

    def __setitem__(self, at, value):
        self.near[at] = value

    def send(self):
        if not self.sent:
            self.copy.start()
            self.sent = True


def send(ref):
    if isinstance(ref, Far):
        ref.send()


def with_far(kernel, n_in, n_out, far, *refs):
    ins, outs, rest = refs[:n_in], list(refs[n_in : n_in + n_out]), list(refs[n_in + n_out :])
    if far:
        sems = rest.pop()
        near = rest[len(rest) - len(far) :]
        del rest[len(rest) - len(far) :]
        for n, at in enumerate(far):
            outs[at] = Far(near[n], outs[at], sems.at[n])
    kernel(*ins, *outs, *rest)
    for at in far:
        outs[at].send()
    for at in far:
        outs[at].copy.wait()


class Order:
    def __init__(self, idx):
        self.idx = idx
        self.last = ()

    def __call__(self, kernel, outs, args, scratch=(), scalars=0, cost=7, far=()):
        idx = after(self.idx, *self.last)
        many = isinstance(outs, (list, tuple))
        shapes = list(outs) if many else [outs]
        more = [pltpu.VMEM(shapes[at].shape, shapes[at].dtype) for at in far]
        if far:
            more.append(pltpu.SemaphoreType.DMA((len(far),)))
        got = pl.pallas_call(
            functools.partial(with_far, kernel, 1 + len(args), len(shapes), tuple(far)),
            out_shape=shapes,
            in_specs=[SMEM] + [VMEM] * (len(args) - scalars) + [SMEM] * scalars,
            out_specs=[
                pl.BlockSpec(memory_space=pl.ANY) if at in far else VMEM
                for at in range(len(shapes))
            ],
            scratch_shapes=list(scratch) + more,
            compiler_params=pltpu.CompilerParams(vmem_limit_bytes=16 * 1024 * 1024),
            cost_estimate=pl.CostEstimate(
                flops=cost * COST, bytes_accessed=1024, transcendentals=0
            ),
        )(idx, *args)
        near = [v for at, v in enumerate(got) if at not in far]
        self.last = (near[0] if near else got[0],)
        return got if many else got[0]


def shape(dims, dtype=F32):
    return jax.ShapeDtypeStruct(dims, dtype)


def rows_at(index, count):
    return pl.ds(pl.multiple_of(index * count, count), count)


def as_rows(parts):
    height = parts[0].shape[0]
    lane = lax.broadcasted_iota(jnp.int32, (height, 128), 1)
    out = jnp.zeros((height, 128), F32)
    for k, part in enumerate(parts):
        out = jnp.where(lane == k, part, out)
    return out.T[0:8]


def as_columns(rows):
    return jnp.concatenate([rows, jnp.zeros((120, rows.shape[1]), F32)], axis=0).T


def in_order(refs, me, scratch):
    for k, ref in enumerate(refs):
        scratch[me ^ k] = ref[...]
    return [scratch[k] for k in range(len(refs))]


def merge_moments(stats):
    total = sum(n for _, _, n in stats)
    mean = sum(n * m for m, _, n in stats) / total
    squares = sum(q + n * (m - mean) * (m - mean) for m, q, n in stats)
    return mean, squares, total


def merge_rows(refs):
    mean, squares, total = merge_moments([(g[0:1], g[1:2], g[2:3]) for g in refs])
    return mean, squares, total, sum(g[3:4] for g in refs)


def pixel(width, area, small):
    lane = lax.broadcasted_iota(jnp.int32, (1, width), 1) % area
    return lane // small, lane % small


def inside(row, col, drow, dcol, small):
    return (row + drow >= 0) & (row + drow < small) & (col + dcol >= 0) & (col + dcol < small)


def moved(value, step):
    shift = (-step) % value.shape[1]
    return pltpu.roll(value, shift, 1) if shift else value


OFFSETS = [(0, krow - 1, kcol - 1) for krow in range(3) for kcol in range(3)]

STRIDED = [
    ((krow != 1) * 2 + (kcol != 1), -(krow == 0), -(kcol == 0))
    for krow in range(3)
    for kcol in range(3)
] + [(0, 0, 0)]
PLACED = sorted(range(10), key=lambda k: (STRIDED[k][0], k))
PHASES = [[k for k in PLACED if STRIDED[k][0] == phase] for phase in range(4)]


def row_of(k, cs):
    at = PLACED.index(k)
    return slice(at * cs, (at + 1) * cs)


def phase_rows(phase, cs):
    first, last = PHASES[phase][0], PHASES[phase][-1]
    return slice(PLACED.index(first) * cs, (PLACED.index(last) + 1) * cs)


def masked_stats(value, weight, n):
    mean = jnp.sum(value * weight, axis=1, keepdims=True) / n
    centred = value - mean
    return mean, jnp.sum(weight * centred * centred, axis=1, keepdims=True)


def span_of(rows):
    return -(-rows // 128) * 128


def one_hot(height, width, shift):
    row = lax.broadcasted_iota(jnp.int32, (height, width), 0)
    col = lax.broadcasted_iota(jnp.int32, (height, width), 1)
    return (col == row + shift).astype(BF16)


def pick32(left, right, dims=((1,), (0,))):
    return lax.dot_general(left, right, (dims, ((), ())), preferred_element_type=F32)


def pick(left, right, dims=((1,), (0,))):
    return pick32(left, right, dims).astype(BF16)


def lane_tile(held, tile, rows, span):
    sides, ny = held.shape[1], held.shape[2]
    lane = lax.broadcasted_iota(jnp.int32, (1, 128), 1)
    out = None
    for v in range(2 * ny):
        begin = rows * v - tile * 128
        if begin >= 128 or begin + rows <= 0:
            continue
        at = (tile - rows * v // 128) * 128 % span
        part = jnp.concatenate(
            [held[v % 2, x, v // 2, :, at : at + 128].astype(F32) for x in range(sides)], axis=0
        )
        if begin > 0 or begin + rows < 128:
            own = (lane >= begin) & (lane < begin + rows)
            part = jnp.where(own, part, 0.0)
        out = part if out is None else out + part
    return out.astype(BF16)


def pixel_order(small, width, of):
    area = small * small
    row = lax.broadcasted_iota(jnp.int32, (4 * area, width), 0)
    col = lax.broadcasted_iota(jnp.int32, (4 * area, width), 1)
    phase, pix = row // area, row % area
    y = 2 * (pix // small) + phase // 2
    x = 2 * (pix % small) + phase % 2
    return (col == of(y, x)).astype(BF16)


def entry_image(small, idx, image, mask, valid, out, weight):
    side = 2 * small
    c_in = image.shape[1]
    count = side * side
    order = pixel_order(small, count, lambda y, x: y * side + x)
    out[:, :c_in] = pick(order, image[...])
    live = (valid[0] > 0).astype(F32)
    row = lax.broadcasted_iota(jnp.int32, (count, side), 0)
    col = lax.broadcasted_iota(jnp.int32, (count, side), 1)
    by_row = jnp.dot(
        (row // side == col).astype(BF16),
        mask[...].astype(F32).astype(BF16),
        preferred_element_type=F32,
    )
    column = jnp.sum(jnp.where(row % side == col, by_row, 0.0), axis=1, keepdims=True) * live
    lane = lax.broadcasted_iota(jnp.int32, (count, 128), 1)
    spread = jnp.where(lane == 0, column, 0.0)
    weight[...] = spread
    out[:, c_in:] = pick(order, spread.astype(BF16))[:, : out.shape[1] - c_in]


def entry_weights(cs, fy, sections, idx, *refs):
    weights, out = list(refs[:-1]), refs[-1]
    ny, cb, lanes = out.shape
    span = lanes // len(sections)
    gx, gy = idx[2], idx[3]
    core, side = gx % 2, (gx // 2 if cb < cs else 0)
    c_out = weights[0].shape[1]
    row = lax.broadcasted_iota(jnp.int32, (fy * cb, c_out), 0)
    col = lax.broadcasted_iota(jnp.int32, (fy * cb, c_out), 1)
    chosen = (col == row // cb * cs + side * cb + row % cb).astype(BF16)
    for n, count in enumerate(sections):
        begin = weights[0].shape[0] // 2 * (2 * gy + core) % 128
        total = None
        for _ in range(count):
            weight = weights.pop(0)
            rows = weight.shape[0]
            half = rows // 2
            mine = pick(chosen, weight[...], ((1,), (1,)))
            row = lax.broadcasted_iota(jnp.int32, (rows, span), 0) - core * half
            col = lax.broadcasted_iota(jnp.int32, (rows, span), 1)
            place = (row >= 0) & (row < half) & (
                (col == row + begin) | (col == row + begin - span)
            )
            part = pick32(mine, place.astype(BF16))
            total = part if total is None else total + part
            begin = begin + half
        for j in range(ny):
            out[j, :, n * span : (n + 1) * span] = total[
                (j % fy) * cb : (j % fy + 1) * cb
            ].astype(BF16)


def hold(gx, messages, held, section=0):
    span = held.shape[4]
    for k, ref in enumerate(messages):
        at = gx ^ k
        side = at // 2 if held.shape[1] > 1 else 0
        held[at % 2, side] = ref[:, :, section * span : (section + 1) * span]


def assemble(held, out, rows):
    cs, span = held.shape[1] * held.shape[3], held.shape[4]
    tiles = out.shape[1] // 128
    for k in range(9):
        for q in range(tiles):
            out[k * cs : (k + 1) * cs, q * 128 : (q + 1) * 128] = lane_tile(
                held, tiles * k + q, rows, span
            )


def assemble_first(held, out, flat, rows, extra):
    cs, span = held.shape[1] * held.shape[3], held.shape[4]
    c_in = out.shape[1]
    tiles = flat.shape[1] // 128
    for tile in range(tiles):
        flat[:, tile * 128 : (tile + 1) * 128] = lane_tile(held, tile, rows, span)
    for k in range(9):
        begin = k * c_in
        base = begin // 128 * 128
        reach = min(-(-(begin + c_in) // 128) * 128, flat.shape[1])
        move = one_hot(c_in, reach - base, begin - base)
        out[row_of(k, cs), :] = pick(flat[:, base:reach], move, ((1,), (1,)))
    total = None
    for v in range(2 * held.shape[2]):
        row = lax.broadcasted_iota(jnp.int32, (span, c_in), 0)
        col = lax.broadcasted_iota(jnp.int32, (span, c_in), 1)
        at = col - extra * v
        begin = rows * v % 128 + rows
        place = (at >= 0) & (at < extra) & ((row == at + begin) | (row == at + begin - span))
        part = jnp.concatenate(
            [
                pick32(held[v % 2, x, v // 2], place.astype(BF16))
                for x in range(held.shape[1])
            ],
            axis=0,
        )
        total = part if total is None else total + part
    out[row_of(9, cs), :] = total.astype(BF16)


def entry_stats(area, idx, *refs):
    images, out = refs[:PEERS], refs[PEERS]
    lanes = out.shape[1]
    first = jnp.zeros((1, lanes), F32)
    wide = jnp.zeros((1, 1), F32)
    narrow = jnp.zeros((1, 1), F32)
    c_in = lanes - 64
    for ref in images:
        x = ref[...].astype(F32)
        w = x[:, c_in : c_in + 1]
        first += jnp.sum(x * w, axis=0, keepdims=True)
        wide += jnp.sum(w, axis=0, keepdims=True)
        narrow += jnp.sum(w[:area], axis=0, keepdims=True)
    mean = first / wide
    squares = jnp.zeros((1, lanes), F32)
    for ref in images:
        x = ref[...].astype(F32)
        w = x[:, c_in : c_in + 1]
        d = x - mean
        squares += jnp.sum(d * d * w, axis=0, keepdims=True)
    out[...] = jnp.zeros_like(out)
    out[0:1, :] = mean
    out[1:2, :] = squares
    out[2:3, :] = jnp.broadcast_to(wide, (1, lanes))
    out[3:4, :] = jnp.broadcast_to(narrow, (1, lanes))


def entry_block(nz, nx, rows, extra, area, small, idx, *refs):
    images = refs[:PEERS]
    stats, rest = refs[PEERS : PEERS + nz], refs[PEERS + nz :]
    gain, shift, messages, rest = rest[0], rest[1], rest[2 : 2 + nx], rest[2 + nx :]
    first, skipped, out_stats, norm, narrow, act, w_first = rest[:7]
    order, masks, flat, held = rest[7:]
    me, mine = idx[0], idx[1]
    c_in = gain.shape[1]
    lanes = norm.shape[1]
    cs = first.shape[0]
    width = first.shape[1]
    hold(idx[2], messages, held)
    assemble_first(held, w_first, flat, rows, extra)
    send(w_first)
    mean, squares, total, count = merge_rows(in_order(stats, mine, order))
    scale = lax.rsqrt(squares / total + EPS)
    norm[...] = jnp.zeros_like(norm)
    norm[0:1, :] = mean
    norm[1:2, :] = scale
    norm[2:3, :] = total
    norm[3:4, :] = count
    for k, ref in enumerate(images):
        x = ref[...]
        v = x[:, :c_in].astype(F32)
        pre = gain[...] * ((v - mean[:, :c_in]) * scale[:, :c_in]) + shift[...]
        a = gelu(pre).astype(BF16)
        for phase in range(4):
            act[phase, rows_at(me ^ k, area), :] = a[phase * area : (phase + 1) * area]
        masks[rows_at(me ^ k, area), :] = x[:area]
    send(act)
    send(norm)
    ones = (lax.broadcasted_iota(jnp.int32, (8, lanes), 1) == c_in).astype(BF16)
    weight8 = lax.dot_general(
        ones, masks[...], (((1,), (1,)), ((), ())), preferred_element_type=F32
    )
    narrow[...] = weight8
    weight = weight8[0:1]
    row, col = pixel(width, area, small)
    total_first = jnp.zeros((cs, width), F32)
    for phase in range(4):
        group = lax.dot_general(
            w_first[phase_rows(phase, cs), :],
            act[phase],
            (((1,), (1,)), ((), ())),
            preferred_element_type=F32,
        )
        for at, k in enumerate(PHASES[phase]):
            y = group[at * cs : (at + 1) * cs]
            if k == 9:
                skipped[...] = y
                continue
            _, drow, dcol = STRIDED[k]
            y = moved(y, drow * small + dcol)
            total_first += jnp.where(inside(row, col, drow, dcol, small), y, 0.0)
    first[...] = total_first
    n = jnp.sum(weight, axis=1, keepdims=True)
    mean2, squares = masked_stats(total_first, weight, n)
    out_stats[...] = as_rows((mean2, squares, n))


def merge_stats(idx, *refs):
    out, order = refs[-2:]
    mean, squares, total, count = merge_rows(in_order(refs[:-2], idx[2], order))
    out[...] = jnp.zeros_like(out)
    out[0:1] = mean
    out[1:2] = squares
    out[2:3] = total
    out[3:4] = count


def add_rows(which, idx, *refs):
    out, order = refs[-2:]
    got = in_order(refs[:-2], idx[which], order)
    total = got[0]
    for g in got[1:]:
        total = total + g
    out[...] = total


def act_block(nz, idx, *refs):
    value, params = refs[:2]
    stats, rest = refs[2 : 2 + nz], refs[2 + nz :]
    if rest[-1].shape[1] == 128:
        cot, normed, scales, outs, order, stack = (*rest[:3], rest[3:-2], *rest[-2:])
    else:
        cot, normed, scales, outs, order = (None, *rest[:2], rest[2:-1], rest[-1])
    mean, squares, total, _ = merge_rows(in_order(stats, idx[1], order))
    rows = jnp.concatenate(
        [mean, lax.rsqrt(squares / total + EPS), total, jnp.zeros((5, mean.shape[1]), F32)], axis=0
    )
    cols = as_columns(rows)
    norm = (value[...] - cols[:, 0:1]) * cols[:, 1:2]
    normed[...] = norm
    send(normed)
    scales[...] = cols
    send(scales)
    act = gelu(params[:, 0:1] * norm + params[:, 1:2]).astype(BF16)
    cs, width = norm.shape
    if cot is not None:
        c = cot[...].astype(F32)
        stack[...] = jnp.concatenate([c, c], axis=0).T
    for k, out in enumerate(outs):
        out[:, :width] = act
        if cot is not None:
            out[:, width:] = stack[rows_at(idx[0] ^ k, cs), :].astype(BF16)


def conv_block(nx, added, last, rows, section, area, small, idx, *refs):
    pieces = refs[:PEERS]
    narrow, rest = refs[PEERS], refs[PEERS + 1 :]
    if last:
        weights, rest = rest[0], rest[1:]
    else:
        messages, rest = rest[:nx], rest[nx:]
    base, rest = (rest[0], rest[1:]) if added else (None, rest)
    me = idx[0]
    cs, width = pieces[0].shape[0], narrow.shape[1]
    if last:
        outs, act, spread = rest[:PEERS], rest[PEERS], rest[PEERS + 1]
    else:
        value, out_stats, act, whole, spread, held = rest
        hold(idx[2], messages, held, section)
        assemble(held, whole, rows)
        send(whole)
        weights = whole
    for k, ref in enumerate(pieces):
        act[rows_at(me ^ k, cs), :] = ref[:, :width]
    send(act)
    spread[...] = jnp.dot(weights[...], act[...], preferred_element_type=F32)
    row, col = pixel(width, area, small)
    total = base[...] if added else jnp.zeros((cs, width), F32)
    for k, (_, drow, dcol) in enumerate(OFFSETS):
        y = moved(spread[k * cs : (k + 1) * cs, :], drow * small + dcol)
        total += jnp.where(inside(row, col, drow, dcol, small), y, 0.0)
    if last:
        result = total.astype(BF16)
        lane = lax.broadcasted_iota(jnp.int32, (width, 128), 0)
        slot = lax.broadcasted_iota(jnp.int32, (width, 128), 1)
        for k, out in enumerate(outs):
            out[...] = pick(result, (lane == (me ^ k) * area + slot).astype(BF16))
    else:
        value[...] = total
        weight = narrow[0:1, :]
        n = jnp.sum(weight, axis=1, keepdims=True)
        mean, squares = masked_stats(total, weight, n)
        out_stats[...] = as_rows((mean, squares, n))


def join_result(idx, *refs):
    pieces, (out, stack) = refs[:PEERS], refs[PEERS:]
    cs = pieces[0].shape[0]
    for k, ref in enumerate(pieces):
        stack[rows_at(idx[0] ^ k, cs), :] = ref[:, -128:].astype(F32)
    out[...] = stack[...].T[: out.shape[0]].astype(BF16)


def spread_grad(grad, shifted, area, small, offs, row_at):
    cs, width = grad.shape
    row, col = pixel(width, area, small)
    for k, (_, drow, dcol) in enumerate(offs):
        g = moved(grad, -(drow * small + dcol))
        g = jnp.where(inside(row, col, -drow, -dcol, small), g, 0.0)
        shifted[row_at(k, cs), :] = g.astype(BF16)


def plain_rows(k, cs):
    return slice(k * cs, (k + 1) * cs)


def push_back(me, weights, shifted, partial, outs):
    cs, width = outs[0].shape[0], shifted.shape[1]
    partial[...] = lax.dot_general(
        weights[...], shifted[...], (((0,), (0,)), ((), ())), preferred_element_type=F32
    )
    for k, out in enumerate(outs):
        out[:, :width] = partial[rows_at(me ^ k, cs), :].astype(BF16)


def last_back(nx, rows, section, area, small, idx, *refs):
    pieces, messages, rest = refs[:PEERS], refs[PEERS : PEERS + nx], refs[PEERS + nx :]
    cot, shifted, weights = rest[:3]
    outs = rest[3 : PEERS + 3]
    partial, held = rest[PEERS + 3 :]
    hold(idx[2], messages, held, section)
    assemble(held, weights, rows)
    send(weights)
    me = idx[0]
    cs, width = cot.shape
    image = lax.broadcasted_iota(jnp.int32, (1, width), 1) // area
    grad = jnp.zeros((cs, width), F32)
    for k, ref in enumerate(pieces):
        tiled = jnp.concatenate([ref[:, width:].astype(F32)] * (width // 128), axis=1)
        grad = jnp.where(image == (me ^ k), tiled, grad)
    cot[...] = grad
    send(cot)
    spread_grad(grad, shifted, area, small, OFFSETS, plain_rows)
    send(shifted)
    push_back(me, weights, shifted, partial, outs)


def gelu_back(idx, *refs):
    pieces = refs[:PEERS]
    normed, params, grad_pre, sums = refs[PEERS:]
    width = normed.shape[1]
    grad = pieces[0][:, :width].astype(F32)
    for ref in pieces[1:]:
        grad += ref[:, :width].astype(F32)
    norm = normed[...]
    g = gelu_slope(params[:, 0:1] * norm + params[:, 1:2]) * grad
    grad_pre[...] = g
    sums[...] = as_rows(
        (jnp.sum(g * norm, axis=1, keepdims=True), jnp.sum(g, axis=1, keepdims=True))
    )


def norm_back(nz, added, last, area, small, idx, *refs):
    grad_pre, normed, scales, params, narrow = refs[:5]
    sums = refs[5 : 5 + nz]
    rest = refs[5 + nz :]
    base, rest = (rest[0], rest[1:]) if added else (None, rest)
    me = idx[0]
    cs, width = grad_pre.shape
    order = rest[-1]
    got = in_order(sums, idx[1], order)
    total = got[0]
    for g in got[1:]:
        total = total + g
    cols = as_columns(total)
    gain_grad, shift_grad = cols[:, 0:1], cols[:, 1:2]
    norm = normed[...]
    back = params[:, 0:1] * scales[:, 1:2] * (
        grad_pre[...]
        - narrow[0:1, :] * (shift_grad + norm * gain_grad) / scales[:, 2:3]
    )
    if added:
        back = base[...] + back
    grad = back.astype(BF16).astype(F32)
    if not last:
        riders = ()
        if not added:
            riders, rest = rest[:PEERS], rest[PEERS:]
        weights, sums_out, shifted = rest[:3]
        outs, partial = rest[3 : 3 + PEERS], rest[3 + PEERS]
        for rider, out in zip(riders, outs):
            out[:, width:] = rider[...]
        if added:
            grad_out, outs, partial = rest[3], rest[4 : 4 + PEERS], rest[4 + PEERS]
            grad_out[...] = grad.astype(BF16)
        sums_out[...] = total
        spread_grad(grad, shifted, area, small, OFFSETS, plain_rows)
        push_back(me, weights, shifted, partial, outs)
    else:
        weights, grad_skip, sums_out, shifted = rest[:4]
        outs, partial = rest[4 : 4 + PEERS], rest[4 + PEERS]
        sums_out[...] = total
        spread_grad(grad, shifted, area, small, STRIDED[:9], row_of)
        shifted[row_of(9, cs), :] = grad_skip[...]
        for phase in range(4):
            partial[phase] = lax.dot_general(
                shifted[phase_rows(phase, cs), :],
                weights[phase_rows(phase, cs), :],
                (((0,), (0,)), ((), ())),
                preferred_element_type=F32,
            )
        for k, out in enumerate(outs):
            for phase in range(4):
                out[phase * area : (phase + 1) * area, :] = partial[
                    phase, rows_at(me ^ k, area), :
                ].astype(BF16)


def part_halves(core, units, own, other):
    own[...] = units[core]
    other[...] = units[1 - core].astype(BF16)


def weight_grad(rows, idx, shifted, act, own, other, full, units):
    full[...] = lax.dot_general(
        shifted[...], act[...], (((1,), (1,)), ((), ())), preferred_element_type=F32
    )
    ny, cs, span = own.shape
    tiles = full.shape[1] // 128
    for v in range(2 * ny):
        begin = rows * v % 128
        parts = []
        for q in range((begin + rows + 127) // 128):
            k, p = divmod(rows * v // 128 + q, tiles)
            parts.append(full[k * cs : (k + 1) * cs, p * 128 : (p + 1) * 128])
        window = jnp.concatenate(parts, axis=1)
        units[v % 2, v // 2] = moved(window, begin)[:, :span]
    part_halves(idx[2] % 2, units, own, other)


def weight_grad_first(rows, extra, idx, shifted, act, own, other, flat, units):
    ny, cs, span = own.shape
    c_in = act.shape[2]
    flat[...] = jnp.zeros_like(flat)
    skip = None
    for phase in range(4):
        group = jnp.dot(
            shifted[phase_rows(phase, cs), :], act[phase], preferred_element_type=F32
        ).astype(BF16)
        for at, k in enumerate(PHASES[phase]):
            grad = group[at * cs : (at + 1) * cs]
            if k == 9:
                skip = grad
                continue
            begin = k * c_in
            base = begin // 128 * 128
            reach = -(-(begin + c_in) // 128) * 128
            move = one_hot(c_in, reach - base, begin - base)
            flat[:, base:reach] += jnp.dot(grad, move, preferred_element_type=F32)
    lane = lax.broadcasted_iota(jnp.int32, (1, span), 1)
    for v in range(2 * ny):
        begin = rows * v % 128
        base = rows * v - begin
        window = moved(flat[:, base : base + span + 128], begin)[:, :span]
        row = lax.broadcasted_iota(jnp.int32, (c_in, span), 0)
        col = lax.broadcasted_iota(jnp.int32, (c_in, span), 1)
        place = (row >= extra * v) & (row < extra * (v + 1)) & (col == row - extra * v + rows)
        tail = pick32(skip, place.astype(BF16))
        units[v % 2, v // 2] = jnp.where(lane < rows, window, 0.0) + tail
    part_halves(idx[2] % 2, units, own, other)


def reduce_core(count, idx, *refs):
    own, other, outs, total = refs[:count], refs[count : 2 * count], refs[2 * count : -1], refs[-1]
    cb = outs[0].shape[1]
    at = 0
    for a, b in zip(own, other):
        span = a.shape[2]
        total[:, :, at : at + span] = a[...] + b[...].astype(F32)
        at += span
    for k, out in enumerate(outs):
        for j in range(total.shape[0]):
            out[j] = total[j, rows_at(idx[2] // 2 ^ k, cb), :].astype(out.dtype)


def reduce_side(sizes, idx, *refs):
    refs, out = refs[:-1], refs[-1]
    at = 0
    for size in sizes:
        total = refs[0][...].astype(F32)
        for ref in refs[1:size]:
            total += ref[...].astype(F32)
        out[:, :, at : at + total.shape[2]] = total.astype(BF16)
        refs = refs[size:]
        at += total.shape[2]


def fold(nz, fy, idx, got, out):
    cs = got.shape[1]
    for f in range(fy):
        total = got[f].astype(F32)
        for z in range(1, nz):
            total += got[z * fy + f].astype(F32)
        out[f * cs : (f + 1) * cs, :] = total.astype(BF16)


def own_rows(count, spans, idx, *refs):
    pieces, outs, stack = refs[:count], refs[count:-1], refs[-1]
    for k, ref in enumerate(pieces):
        at = idx[2] ^ k
        stack[at % 2, at // 2] = ref[...]
    sides, height = stack.shape[1], stack.shape[2]
    fy_cb = [(f, x) for f in range(PEERS) for x in range(sides)]
    cb = height // PEERS
    for half in range(2):
        whole = jnp.concatenate(
            [stack[half, x, f * cb : (f + 1) * cb, :].astype(F32) for f, x in fy_cb], axis=0
        ).T
        at = 0
        for span, group in spans:
            begin = at
            for n in group:
                out = outs[n]
                rows = out.shape[0] // 2
                out[half * rows : (half + 1) * rows, :] = whole[begin : begin + rows]
                begin += rows
            at += span


def entry_back(small, idx, *refs):
    pieces = refs[:PEERS]
    image, norm, gain, shift, grad_pre, sums = refs[PEERS:]
    c_in = gain.shape[1]
    side = 2 * small
    grad = pieces[0][...].astype(F32)
    for ref in pieces[1:]:
        grad += ref[...].astype(F32)
    order = pixel_order(small, side * side, lambda y, x: y * side + x)
    high = grad.astype(BF16)
    low = (grad - high.astype(F32)).astype(BF16)
    grad = sum(
        lax.dot_general(order, part, (((0,), (0,)), ((), ())), preferred_element_type=F32)
        for part in (high, low)
    )
    normed = (image[...].astype(F32) - norm[0:1, :c_in]) * norm[1:2, :c_in]
    g = gelu_slope(gain[...] * normed + shift[...]) * grad
    grad_pre[...] = g
    sums[...] = jnp.zeros_like(sums)
    sums[0:1, :c_in] = jnp.sum(g * normed, axis=0, keepdims=True)
    sums[1:2, :c_in] = jnp.sum(g, axis=0, keepdims=True)


def bundle(idx, first, second, third, sums, out):
    out[...] = jnp.zeros_like(out)
    out[0:8, :] = sums[...]
    for k, ref in enumerate((first, second, third)):
        out[8 + 2 * k : 10 + 2 * k, : ref.shape[1]] = ref[0:2]


def unbundle(idx, *refs):
    out, six, order = refs[-3:]
    got = in_order(refs[:-3], idx[0], order)
    total = got[0][0:8]
    for g in got[1:]:
        total = total + g[0:8]
    out[...] = total
    cs = six.shape[1] // PEERS
    six[...] = jnp.concatenate([g[8:16, :cs] for g in got], axis=1)


def entry_grad(nz, idx, *refs):
    sums = refs[:nz]
    grad_pre, image, weight, norm, gain, gain_grad, shift_grad, out, order = refs[nz:]
    got = in_order(sums, idx[1], order)
    total = got[0]
    for g in got[1:]:
        total = total + g
    gain_grad[...] = total[0:1]
    shift_grad[...] = total[1:2]
    c_in = gain.shape[1]
    scale = norm[1:2, :c_in]
    normed = (image[...].astype(F32) - norm[0:1, :c_in]) * scale
    out[...] = gain[...] * scale * (
        grad_pre[...]
        - weight[:, 0:1]
        * (shift_grad[0:1, :c_in] + normed * gain_grad[0:1, :c_in])
        / norm[2:3, :c_in]
    )


def program(
    nx,
    ny,
    images,
    valid_count,
    pixel_mask,
    gain_entry,
    shift_entry,
    conv_first,
    gain_middle,
    shift_middle,
    conv_second,
    projection,
    gain_inner,
    shift_inner,
    conv_third,
    gain_last,
    shift_last,
    conv_fourth,
    cotangent,
):
    fy = PEERS
    nz = ny // fy
    sides = nx // 2
    side, c_in = images.shape[1], images.shape[3]
    small = side // 2
    area = small * small
    c_out = conv_first.shape[1]
    cs = c_out // PEERS
    cb = cs // sides
    width = PEERS * area
    lanes = c_in + 64
    padded = span_of(c_in)
    gx, gy = lax.axis_index("gx"), lax.axis_index("gy")
    me = gy % fy
    mine = gy // fy
    run = Order(jnp.stack([me, mine, gx, gy]).astype(jnp.int32))
    part = functools.partial

    def to_slice(piece, k):
        return lax.ppermute(piece, "gy", [(j, j // fy * fy + (j % fy ^ k)) for j in range(ny)])

    def share(pieces):
        return [pieces[0]] + [to_slice(pieces[k], k) for k in range(1, PEERS)]

    def to_gx(piece, k):
        return lax.ppermute(piece, "gx", [(i, i ^ k) for i in range(nx)])

    def pool_gx(piece):
        return [piece] + [to_gx(piece, k) for k in range(1, nx)]

    def pool_z(piece):
        out = [piece]
        for k in range(1, nz):
            perm = [(j, (j // fy ^ k) * fy + j % fy) for j in range(ny)]
            out.append(lax.ppermute(piece, "gy", perm))
        return out

    def over_x(block):
        return {0: block, **{k: to_gx(block, k) for k in range(2, nx, 2)}}

    def over_core(held, *then):
        held = {k: after(v, *then) for k, v in held.items()} if then else dict(held)
        for k in list(held):
            held[k + 1] = to_gx(held[k], 1)
        return [held[k] for k in sorted(held)]

    def turn(block):
        return lax.all_to_all(block, "gy", 0, 0, tiled=True)

    unit_first, unit_skip = conv_first.shape[0] // 2, projection.shape[0] // 2
    unit_mid = conv_second.shape[0] // 2
    span_first, span_mid = span_of(unit_first + unit_skip), span_of(unit_mid)
    tile, tile16 = shape((cs, width)), shape((cs, width), BF16)
    long16 = shape((cs, width + 128), BF16)
    cols, stat, entry_stat = shape((cs, 128)), shape((8, cs)), shape((8, lanes))
    shifted16 = shape((9 * cs, width), BF16)
    full16 = shape((c_out, width), BF16)
    whole16 = shape((9 * cs, c_out), BF16)

    def halves(span, channels):
        return pltpu.VMEM((2, cs // channels, ny, channels, span), BF16)

    def ready(span, sections, *weights):
        out = shape((ny, cb, span * len(sections)), BF16)
        return run(
            part(entry_weights, cs, fy, sections), out, weights, cost=24 * len(sections)
        )

    def merge(pieces, kernel):
        like = pieces[0].shape
        return run(kernel, shape(like), pieces, [pltpu.VMEM((nx, *like), F32)])

    add_gx = part(add_rows, 2)

    def activate(value, params, pooled, cot=None):
        more = [] if cot is None else [cot]
        outs = [tile16] if cot is None else [long16] * PEERS
        return run(
            part(act_block, nz),
            [tile, cols] + outs,
            [value, params, *pooled, *more],
            [pltpu.VMEM((nz, 8, cs), F32)]
            + ([] if cot is None else [pltpu.VMEM((c_out, 128), F32)]),
            far=(0, 1),
        )

    def convolve(pieces, weights, base, section=0, last=False):
        more = [] if base is None else [base]
        outs = [shape((cs, 128), BF16)] * PEERS + [full16]
        return run(
            part(conv_block, nx, base is not None, last, unit_mid, section, area, small),
            outs if last else [tile, stat, full16, whole16],
            [*pieces, narrow, *weights, *more],
            [pltpu.VMEM((9 * cs, width), F32)] + ([] if last else [halves(span_mid, cb)]),
            cost=25,
            far=() if last else (2, 3),
        )

    def slope(parts, normed, params):
        return run(gelu_back, [tile, stat], [*parts, normed, params])

    def back(grad_pre, normed, scales, params, pooled, weights, base, riders=()):
        more = list(riders) if base is None else [base]
        return run(
            part(norm_back, nz, base is not None, False, area, small),
            [stat, shifted16]
            + ([long16] * PEERS if base is None else [tile16] * (PEERS + 1)),
            [grad_pre, normed, scales, params, narrow, *pooled, *more, weights],
            [pltpu.VMEM((c_out, width), F32), pltpu.VMEM((nz, 8, cs), F32)],
            cost=18,
        )

    def grad_of(kernel, span, shifted, act, scratch):
        own, other = run(
            kernel,
            [shape((ny, cs, span)), shape((ny, cs, span), BF16)],
            [shifted, act],
            [scratch, pltpu.VMEM((2, ny, cs, span), F32)],
            cost=28,
        )
        return own, to_gx(other, 1)

    def grad_mid(shifted, act):
        return grad_of(
            part(weight_grad, unit_mid), span_mid, shifted, act, pltpu.VMEM((9 * cs, c_out), F32)
        )

    def over_pair(own, other):
        span = own.shape[2]
        return run(
            part(reduce_core, 1),
            [shape((ny, cb, span))] + [shape((ny, cb, span), BF16)] * (sides - 1),
            [own, other],
            [pltpu.VMEM((ny, cs, span), F32)],
        )

    def to_sides(parts, *then):
        parts = [after(p, *then) for p in parts] if then else parts
        return [parts[0]] + [to_gx(parts[k], 2 * k) for k in range(1, sides)]

    def over_sides(*groups):
        span = sum(parts[0].shape[2] for parts in groups)
        return run(
            part(reduce_side, tuple(len(parts) for parts in groups)),
            shape((ny, cb, span), BF16),
            [p for parts in groups for p in parts],
        )

    def folded(got):
        out = shape((fy * cb, got.shape[2]), BF16)
        return over_x(run(part(fold, nz, fy), out, [got]))

    def rows_of(pieces, spans, *rows):
        return run(
            part(own_rows, nx, spans),
            [shape((r, c_out)) for r in rows],
            pieces,
            [pltpu.VMEM((2, sides, fy * cb, pieces[0].shape[1]), BF16)],
            cost=30,
        )

    def own(gain, shift):
        pair = jnp.stack([gain, shift], axis=1)
        return lax.dynamic_slice_in_dim(pair, me * cs, cs, axis=0)

    p_middle = own(gain_middle, shift_middle)
    p_inner = own(gain_inner, shift_inner)
    p_last = own(gain_last, shift_last)
    g_entry, s_entry = gain_entry[None], shift_entry[None]
    pixels = images.reshape(side * side, c_in)

    image, wide = run(
        part(entry_image, small),
        [shape((4 * area, lanes), BF16), shape((4 * area, 128))],
        [pixels, pixel_mask.reshape(side, side), valid_count],
        scalars=1,
    )
    group = share([image] * PEERS)
    out_first = ready(span_first, (2,), conv_first, projection)
    stats = run(part(entry_stats, area), entry_stat, group)
    pieces = pool_gx(stats)
    got_first = turn(after(out_first, *group[1:]))
    got_first = over_core(over_x(after(got_first, *pieces[1:])))
    pooled = pool_z(merge(pieces, merge_stats))
    out_middle = ready(span_mid, (1, 1), conv_second, conv_third)
    got_middle = turn(after(out_middle, pooled[-1]))
    out_fourth = ready(span_mid, (1,), conv_fourth)
    first, skipped, stats, norm_one, narrow, act_one, w_first = run(
        part(entry_block, nz, nx, unit_first, unit_skip, area, small),
        [
            tile,
            tile,
            stat,
            entry_stat,
            shape((8, width)),
            shape((4, width, c_in), BF16),
            shape((10 * cs, c_in), BF16),
        ],
        [*group, *pooled, g_entry, s_entry, *got_first],
        [
            pltpu.VMEM((nz, 8, lanes), F32),
            pltpu.VMEM((width, lanes), BF16),
            pltpu.VMEM((cs, span_of(9 * c_in)), BF16),
            halves(span_first, cb),
        ],
        cost=40,
        far=(3, 5, 6),
    )

    merged = merge(pool_gx(stats), merge_stats)
    got_middle = over_x(after(got_middle, merged))
    pooled = pool_z(merged)
    got_fourth = turn(after(out_fourth, pooled[-1]))
    normed_two, scale_two, *messages = activate(
        first, p_middle, pooled, cotangent.reshape(area, c_out)
    )
    pieces = share(messages)
    got_middle = over_core(got_middle, *pieces[1:])
    hidden, stats, act_two, w_second = convolve(pieces, got_middle, skipped)
    cot_parts = pieces
    merged = merge(pool_gx(stats), merge_stats)
    pooled = pool_z(merged)
    got_fourth = over_x(after(got_fourth, pooled[-1]))
    normed_three, scale_three, act = activate(hidden, p_inner, pooled)
    pieces = share([act] * PEERS)
    third, stats, act_three, w_third = convolve(pieces, got_middle, None, section=1)
    got_fourth = over_core(got_fourth, stats)
    merged = merge(pool_gx(stats), merge_stats)

    cot, shifted_four, w_fourth, *parts = run(
        part(last_back, nx, unit_mid, 0, area, small),
        [tile, shifted16, whole16] + [tile16] * PEERS,
        [*cot_parts, *got_fourth],
        [pltpu.VMEM((c_out, width), F32), halves(span_mid, cb)],
        cost=18,
        far=(0, 1, 2),
    )
    parts = share(parts)
    normed_four, scale_four, act = activate(third, p_last, pool_z(merged))
    pieces = share([act] * PEERS)
    grad_pre, sums = slope(parts, normed_four, p_last)
    sums = pool_gx(sums)
    *riders, act_four = convolve(pieces, [w_fourth], hidden, last=True)
    sums = pool_z(merge(sums, add_gx))
    fourth = grad_mid(shifted_four, act_four)
    last_sums, shifted_three, *parts = back(
        grad_pre, normed_four, scale_four, p_last, sums, w_third, None, riders
    )
    parts = share(parts)
    fourth = over_pair(*fourth)
    grad_pre, sums = slope(parts, normed_three, p_inner)
    sums = pool_gx(sums)
    third = grad_mid(shifted_three, act_three)
    merged = merge(sums, add_gx)
    fourth = to_sides(fourth, merged)
    sums = pool_z(merged)
    out = run(
        join_result, shape((area, c_out), BF16), parts, [pltpu.VMEM((c_out, 128), F32)]
    )
    inner_sums, shifted_two, grad_hidden, *parts = back(
        grad_pre, normed_three, scale_three, p_inner, sums, w_second, cot
    )
    parts = share(parts)
    third = over_pair(*third)
    grad_pre, sums = slope(parts, normed_two, p_middle)
    sums = pool_gx(sums)
    fourth = over_sides(fourth)
    second = grad_mid(shifted_two, act_two)
    merged = merge(sums, add_gx)
    third = to_sides(third, merged)
    sums = pool_z(merged)
    second = to_sides(over_pair(*second), merged)
    middle_sums, shifted_one, *parts = run(
        part(norm_back, nz, False, True, area, small),
        [stat, shape((10 * cs, width), BF16)] + [shape((4 * area, c_in), BF16)] * PEERS,
        [
            grad_pre,
            normed_two,
            scale_two,
            p_middle,
            narrow,
            *sums,
            w_first,
            grad_hidden,
        ],
        [pltpu.VMEM((4, width, c_in), F32), pltpu.VMEM((nz, 8, cs), F32)],
        cost=18,
    )

    parts = share(parts)
    first = grad_of(
        part(weight_grad_first, unit_first, unit_skip),
        span_first,
        shifted_one,
        act_one,
        pltpu.VMEM((cs, span_of(9 * c_in + span_first + 128)), F32),
    )
    late = turn(over_sides([after(fourth, *parts[1:])], third))
    second = over_sides(second)
    first = to_sides(over_pair(*first))
    early = turn(over_sides([second], first))
    grad_pre, sums = run(
        part(entry_back, small),
        [shape((4 * area, c_in)), shape((8, padded))],
        [*parts, pixels, norm_one, g_entry, s_entry],
        cost=13,
    )
    message = run(bundle, shape((16, padded)), [middle_sums, inner_sums, last_sums, sums])
    message = share([message] * PEERS)
    late = folded(late)
    sums, six = run(
        unbundle,
        [shape((8, padded)), shape((8, c_out))],
        message,
        [pltpu.VMEM((PEERS, 16, padded), F32)],
    )
    sums = pool_gx(sums)
    early = folded(early)
    merged = merge(sums, add_gx)
    sums = pool_z(merged)
    gain_entry_grad, shift_entry_grad, image_grad = run(
        part(entry_grad, nz),
        [shape((1, padded)), shape((1, padded)), shape((4 * area, c_in))],
        [*sums, grad_pre, pixels, wide, norm_one, g_entry],
        [pltpu.VMEM((nz, 8, padded), F32)],
    )
    fourth_grad, third_grad = rows_of(
        over_core(late, merged),
        ((span_mid, (0,)), (span_mid, (1,))),
        2 * unit_mid,
        2 * unit_mid,
    )
    second_grad, first_grad, skip_grad = rows_of(
        over_core(early, fourth_grad),
        ((span_mid, (0,)), (span_first, (1, 2))),
        2 * unit_mid,
        2 * unit_first,
        2 * unit_skip,
    )
    return (
        out.reshape(1, small, small, c_out),
        image_grad.reshape(1, side, side, c_in),
        gain_entry_grad[0, :c_in],
        shift_entry_grad[0, :c_in],
        first_grad,
        six[0],
        six[1],
        second_grad,
        skip_grad,
        six[2],
        six[3],
        third_grad,
        six[4],
        six[5],
        fourth_grad,
    )


def solution(mesh):
    whole = P(("gx", "gy"), None, None, None)
    rows = P("gy", None)
    return jax.shard_map(
        functools.partial(program, mesh.shape["gx"], mesh.shape["gy"]),
        mesh=mesh,
        in_specs=(
            whole,
            P(("gx", "gy")),
            P(("gx", "gy"), None, None),
            P(),
            P(),
            rows,
            P(),
            P(),
            rows,
            rows,
            P(),
            P(),
            rows,
            P(),
            P(),
            rows,
            whole,
        ),
        out_specs=(
            whole, whole, P(), P(), rows, P(), P(), rows, rows, P(), P(), rows, P(), P(), rows,
        ),
        check_vma=False,
    )
```

```python
import functools

import jax
import jax.numpy as jnp
from jax import lax
from jax.experimental import pallas as pl
from jax.experimental.pallas import tpu as pltpu
from jax.sharding import PartitionSpec as P

EPS = 1e-05
COST = 6 * 10**7
F32 = jnp.float32
BF16 = jnp.bfloat16
PEERS = 4
C0 = 0.7978845608028654
C1 = 0.044715
VMEM = pl.BlockSpec(memory_space=pltpu.VMEM)
SMEM = pl.BlockSpec(memory_space=pltpu.SMEM)


def gelu(v):
    return 0.5 * v * (1.0 + jnp.tanh(C0 * (v + C1 * (v * v * v))))


def gelu_slope(v):
    t = jnp.tanh(C0 * (v + C1 * (v * v * v)))
    return 0.5 * (1.0 + t) + 0.5 * v * (1.0 - t * t) * (C0 * (1.0 + 3.0 * C1 * (v * v)))


def after(value, *others):
    return lax.optimization_barrier((value, *others))[0]


class Far:
    def __init__(self, near, far, sem):
        self.near, self.shape, self.dtype = near, near.shape, near.dtype
        self.copy = pltpu.make_async_copy(near, far, sem)
        self.sent = False

    def __getitem__(self, at):
        return self.near[at]

    def __setitem__(self, at, value):
        self.near[at] = value

    def send(self):
        if not self.sent:
            self.copy.start()
            self.sent = True


def send(ref):
    if isinstance(ref, Far):
        ref.send()


def with_far(kernel, n_in, n_out, far, *refs):
    ins, outs, rest = refs[:n_in], list(refs[n_in : n_in + n_out]), list(refs[n_in + n_out :])
    if far:
        sems = rest.pop()
        near = rest[len(rest) - len(far) :]
        del rest[len(rest) - len(far) :]
        for n, at in enumerate(far):
            outs[at] = Far(near[n], outs[at], sems.at[n])
    kernel(*ins, *outs, *rest)
    for at in far:
        outs[at].send()
    for at in far:
        outs[at].copy.wait()


class Order:
    def __init__(self, idx):
        self.idx = idx
        self.last = ()

    def __call__(self, kernel, outs, args, scratch=(), scalars=0, cost=7, far=()):
        idx = after(self.idx, *self.last)
        many = isinstance(outs, (list, tuple))
        shapes = list(outs) if many else [outs]
        more = [pltpu.VMEM(shapes[at].shape, shapes[at].dtype) for at in far]
        if far:
            more.append(pltpu.SemaphoreType.DMA((len(far),)))
        got = pl.pallas_call(
            functools.partial(with_far, kernel, 1 + len(args), len(shapes), tuple(far)),
            out_shape=shapes,
            in_specs=[SMEM] + [VMEM] * (len(args) - scalars) + [SMEM] * scalars,
            out_specs=[
                pl.BlockSpec(memory_space=pl.ANY) if at in far else VMEM
                for at in range(len(shapes))
            ],
            scratch_shapes=list(scratch) + more,
            compiler_params=pltpu.CompilerParams(vmem_limit_bytes=16 * 1024 * 1024),
            cost_estimate=pl.CostEstimate(
                flops=cost * COST, bytes_accessed=1024, transcendentals=0
            ),
        )(idx, *args)
        near = [v for at, v in enumerate(got) if at not in far]
        self.last = (near[0] if near else got[0],)
        return got if many else got[0]


def shape(dims, dtype=F32):
    return jax.ShapeDtypeStruct(dims, dtype)


def rows_at(index, count):
    return pl.ds(pl.multiple_of(index * count, count), count)


def as_rows(parts):
    height = parts[0].shape[0]
    lane = lax.broadcasted_iota(jnp.int32, (height, 128), 1)
    out = jnp.zeros((height, 128), F32)
    for k, part in enumerate(parts):
        out = jnp.where(lane == k, part, out)
    return out.T[0:8]


def as_columns(rows):
    return jnp.concatenate([rows, jnp.zeros((120, rows.shape[1]), F32)], axis=0).T


def in_order(refs, me, scratch):
    for k, ref in enumerate(refs):
        scratch[me ^ k] = ref[...]
    return [scratch[k] for k in range(len(refs))]


def merge_moments(stats):
    total = sum(n for _, _, n in stats)
    mean = sum(n * m for m, _, n in stats) / total
    squares = sum(q + n * (m - mean) * (m - mean) for m, q, n in stats)
    return mean, squares, total


def merge_rows(refs):
    mean, squares, total = merge_moments([(g[0:1], g[1:2], g[2:3]) for g in refs])
    return mean, squares, total, sum(g[3:4] for g in refs)


def pixel(width, area, small):
    lane = lax.broadcasted_iota(jnp.int32, (1, width), 1) % area
    return lane // small, lane % small


def inside(row, col, drow, dcol, small):
    return (row + drow >= 0) & (row + drow < small) & (col + dcol >= 0) & (col + dcol < small)


def moved(value, step):
    shift = (-step) % value.shape[1]
    return pltpu.roll(value, shift, 1) if shift else value


OFFSETS = [(0, krow - 1, kcol - 1) for krow in range(3) for kcol in range(3)]

STRIDED = [
    ((krow != 1) * 2 + (kcol != 1), -(krow == 0), -(kcol == 0))
    for krow in range(3)
    for kcol in range(3)
] + [(0, 0, 0)]
PLACED = sorted(range(10), key=lambda k: (STRIDED[k][0], k))
PHASES = [[k for k in PLACED if STRIDED[k][0] == phase] for phase in range(4)]


def row_of(k, cs):
    at = PLACED.index(k)
    return slice(at * cs, (at + 1) * cs)


def phase_rows(phase, cs):
    first, last = PHASES[phase][0], PHASES[phase][-1]
    return slice(PLACED.index(first) * cs, (PLACED.index(last) + 1) * cs)


def masked_stats(value, weight, n):
    mean = jnp.sum(value * weight, axis=1, keepdims=True) / n
    centred = value - mean
    return mean, jnp.sum(weight * centred * centred, axis=1, keepdims=True)


def span_of(rows):
    return -(-rows // 128) * 128


def one_hot(height, width, shift):
    row = lax.broadcasted_iota(jnp.int32, (height, width), 0)
    col = lax.broadcasted_iota(jnp.int32, (height, width), 1)
    return (col == row + shift).astype(BF16)


def pick32(left, right, dims=((1,), (0,))):
    return lax.dot_general(left, right, (dims, ((), ())), preferred_element_type=F32)


def pick(left, right, dims=((1,), (0,))):
    return pick32(left, right, dims).astype(BF16)


def lane_tile(held, tile, rows, span):
    sides, ny = held.shape[1], held.shape[2]
    lane = lax.broadcasted_iota(jnp.int32, (1, 128), 1)
    out = None
    for v in range(2 * ny):
        begin = rows * v - tile * 128
        if begin >= 128 or begin + rows <= 0:
            continue
        at = (tile - rows * v // 128) * 128 % span
        part = jnp.concatenate(
            [held[v % 2, x, v // 2, :, at : at + 128].astype(F32) for x in range(sides)], axis=0
        )
        if begin > 0 or begin + rows < 128:
            own = (lane >= begin) & (lane < begin + rows)
            part = jnp.where(own, part, 0.0)
        out = part if out is None else out + part
    return out.astype(BF16)


def pixel_order(small, width, of):
    area = small * small
    row = lax.broadcasted_iota(jnp.int32, (4 * area, width), 0)
    col = lax.broadcasted_iota(jnp.int32, (4 * area, width), 1)
    phase, pix = row // area, row % area
    y = 2 * (pix // small) + phase // 2
    x = 2 * (pix % small) + phase % 2
    return (col == of(y, x)).astype(BF16)


def entry_image(small, idx, image, mask, valid, out, weight):
    side = 2 * small
    c_in = image.shape[1]
    count = side * side
    order = pixel_order(small, count, lambda y, x: y * side + x)
    out[:, :c_in] = pick(order, image[...])
    live = (valid[0] > 0).astype(F32)
    row = lax.broadcasted_iota(jnp.int32, (count, side), 0)
    col = lax.broadcasted_iota(jnp.int32, (count, side), 1)
    by_row = jnp.dot(
        (row // side == col).astype(BF16),
        mask[...].astype(F32).astype(BF16),
        preferred_element_type=F32,
    )
    column = jnp.sum(jnp.where(row % side == col, by_row, 0.0), axis=1, keepdims=True) * live
    lane = lax.broadcasted_iota(jnp.int32, (count, 128), 1)
    spread = jnp.where(lane == 0, column, 0.0)
    weight[...] = spread
    out[:, c_in:] = pick(order, spread.astype(BF16))[:, : out.shape[1] - c_in]


def entry_weights(cs, fy, sections, idx, *refs):
    weights, out = list(refs[:-1]), refs[-1]
    ny, cb, lanes = out.shape
    span = lanes // len(sections)
    gx, gy = idx[2], idx[3]
    core, side = gx % 2, (gx // 2 if cb < cs else 0)
    c_out = weights[0].shape[1]
    row = lax.broadcasted_iota(jnp.int32, (fy * cb, c_out), 0)
    col = lax.broadcasted_iota(jnp.int32, (fy * cb, c_out), 1)
    chosen = (col == row // cb * cs + side * cb + row % cb).astype(BF16)
    for n, count in enumerate(sections):
        begin = weights[0].shape[0] // 2 * (2 * gy + core) % 128
        total = None
        for _ in range(count):
            weight = weights.pop(0)
            rows = weight.shape[0]
            half = rows // 2
            mine = pick(chosen, weight[...], ((1,), (1,)))
            row = lax.broadcasted_iota(jnp.int32, (rows, span), 0) - core * half
            col = lax.broadcasted_iota(jnp.int32, (rows, span), 1)
            place = (row >= 0) & (row < half) & (
                (col == row + begin) | (col == row + begin - span)
            )
            part = pick32(mine, place.astype(BF16))
            total = part if total is None else total + part
            begin = begin + half
        for j in range(ny):
            out[j, :, n * span : (n + 1) * span] = total[
                (j % fy) * cb : (j % fy + 1) * cb
            ].astype(BF16)


def hold(gx, messages, held, section=0):
    span = held.shape[4]
    for k, ref in enumerate(messages):
        at = gx ^ k
        side = at // 2 if held.shape[1] > 1 else 0
        held[at % 2, side] = ref[:, :, section * span : (section + 1) * span]


def assemble(held, out, rows):
    cs, span = held.shape[1] * held.shape[3], held.shape[4]
    tiles = out.shape[1] // 128
    for k in range(9):
        for q in range(tiles):
            out[k * cs : (k + 1) * cs, q * 128 : (q + 1) * 128] = lane_tile(
                held, tiles * k + q, rows, span
            )


def assemble_first(held, out, flat, rows, extra):
    cs, span = held.shape[1] * held.shape[3], held.shape[4]
    c_in = out.shape[1]
    tiles = flat.shape[1] // 128
    for tile in range(tiles):
        flat[:, tile * 128 : (tile + 1) * 128] = lane_tile(held, tile, rows, span)
    for k in range(9):
        begin = k * c_in
        base = begin // 128 * 128
        reach = min(-(-(begin + c_in) // 128) * 128, flat.shape[1])
        move = one_hot(c_in, reach - base, begin - base)
        out[row_of(k, cs), :] = pick(flat[:, base:reach], move, ((1,), (1,)))
    total = None
    for v in range(2 * held.shape[2]):
        row = lax.broadcasted_iota(jnp.int32, (span, c_in), 0)
        col = lax.broadcasted_iota(jnp.int32, (span, c_in), 1)
        at = col - extra * v
        begin = rows * v % 128 + rows
        place = (at >= 0) & (at < extra) & ((row == at + begin) | (row == at + begin - span))
        part = jnp.concatenate(
            [
                pick32(held[v % 2, x, v // 2], place.astype(BF16))
                for x in range(held.shape[1])
            ],
            axis=0,
        )
        total = part if total is None else total + part
    out[row_of(9, cs), :] = total.astype(BF16)


def entry_stats(area, idx, *refs):
    images, out = refs[:PEERS], refs[PEERS]
    lanes = out.shape[1]
    first = jnp.zeros((1, lanes), F32)
    wide = jnp.zeros((1, 1), F32)
    narrow = jnp.zeros((1, 1), F32)
    c_in = lanes - 64
    for ref in images:
        x = ref[...].astype(F32)
        w = x[:, c_in : c_in + 1]
        first += jnp.sum(x * w, axis=0, keepdims=True)
        wide += jnp.sum(w, axis=0, keepdims=True)
        narrow += jnp.sum(w[:area], axis=0, keepdims=True)
    mean = first / wide
    squares = jnp.zeros((1, lanes), F32)
    for ref in images:
        x = ref[...].astype(F32)
        w = x[:, c_in : c_in + 1]
        d = x - mean
        squares += jnp.sum(d * d * w, axis=0, keepdims=True)
    out[...] = jnp.zeros_like(out)
    out[0:1, :] = mean
    out[1:2, :] = squares
    out[2:3, :] = jnp.broadcast_to(wide, (1, lanes))
    out[3:4, :] = jnp.broadcast_to(narrow, (1, lanes))


def entry_block(nz, nx, rows, extra, area, small, idx, *refs):
    images = refs[:PEERS]
    stats, rest = refs[PEERS : PEERS + nz], refs[PEERS + nz :]
    gain, shift, messages, rest = rest[0], rest[1], rest[2 : 2 + nx], rest[2 + nx :]
    first, skipped, out_stats, norm, narrow, act, w_first = rest[:7]
    order, masks, flat, held = rest[7:]
    me, mine = idx[0], idx[1]
    c_in = gain.shape[1]
    lanes = norm.shape[1]
    cs = first.shape[0]
    width = first.shape[1]
    hold(idx[2], messages, held)
    assemble_first(held, w_first, flat, rows, extra)
    send(w_first)
    mean, squares, total, count = merge_rows(in_order(stats, mine, order))
    scale = lax.rsqrt(squares / total + EPS)
    norm[...] = jnp.zeros_like(norm)
    norm[0:1, :] = mean
    norm[1:2, :] = scale
    norm[2:3, :] = total
    norm[3:4, :] = count
    for k, ref in enumerate(images):
        x = ref[...]
        v = x[:, :c_in].astype(F32)
        pre = gain[...] * ((v - mean[:, :c_in]) * scale[:, :c_in]) + shift[...]
        a = gelu(pre).astype(BF16)
        for phase in range(4):
            act[phase, rows_at(me ^ k, area), :] = a[phase * area : (phase + 1) * area]
        masks[rows_at(me ^ k, area), :] = x[:area]
    send(act)
    send(norm)
    ones = (lax.broadcasted_iota(jnp.int32, (8, lanes), 1) == c_in).astype(BF16)
    weight8 = lax.dot_general(
        ones, masks[...], (((1,), (1,)), ((), ())), preferred_element_type=F32
    )
    narrow[...] = weight8
    weight = weight8[0:1]
    row, col = pixel(width, area, small)
    total_first = jnp.zeros((cs, width), F32)
    for phase in range(4):
        group = lax.dot_general(
            w_first[phase_rows(phase, cs), :],
            act[phase],
            (((1,), (1,)), ((), ())),
            preferred_element_type=F32,
        )
        for at, k in enumerate(PHASES[phase]):
            y = group[at * cs : (at + 1) * cs]
            if k == 9:
                skipped[...] = y
                continue
            _, drow, dcol = STRIDED[k]
            y = moved(y, drow * small + dcol)
            total_first += jnp.where(inside(row, col, drow, dcol, small), y, 0.0)
    first[...] = total_first
    n = jnp.sum(weight, axis=1, keepdims=True)
    mean2, squares = masked_stats(total_first, weight, n)
    out_stats[...] = as_rows((mean2, squares, n))


def merge_stats(idx, *refs):
    out, order = refs[-2:]
    mean, squares, total, count = merge_rows(in_order(refs[:-2], idx[2], order))
    out[...] = jnp.zeros_like(out)
    out[0:1] = mean
    out[1:2] = squares
    out[2:3] = total
    out[3:4] = count


def add_rows(which, idx, *refs):
    out, order = refs[-2:]
    got = in_order(refs[:-2], idx[which], order)
    total = got[0]
    for g in got[1:]:
        total = total + g
    out[...] = total


def act_block(nz, idx, *refs):
    value, params = refs[:2]
    stats, rest = refs[2 : 2 + nz], refs[2 + nz :]
    if rest[-1].shape[1] == 128:
        cot, normed, scales, outs, order, stack = (*rest[:3], rest[3:-2], *rest[-2:])
    else:
        cot, normed, scales, outs, order = (None, *rest[:2], rest[2:-1], rest[-1])
    mean, squares, total, _ = merge_rows(in_order(stats, idx[1], order))
    rows = jnp.concatenate(
        [mean, lax.rsqrt(squares / total + EPS), total, jnp.zeros((5, mean.shape[1]), F32)], axis=0
    )
    cols = as_columns(rows)
    norm = (value[...] - cols[:, 0:1]) * cols[:, 1:2]
    normed[...] = norm
    send(normed)
    scales[...] = cols
    send(scales)
    act = gelu(params[:, 0:1] * norm + params[:, 1:2]).astype(BF16)
    cs, width = norm.shape
    if cot is not None:
        c = cot[...].astype(F32)
        stack[...] = jnp.concatenate([c, c], axis=0).T
    for k, out in enumerate(outs):
        out[:, :width] = act
        if cot is not None:
            out[:, width:] = stack[rows_at(idx[0] ^ k, cs), :].astype(BF16)


def conv_block(nx, added, last, rows, section, area, small, idx, *refs):
    pieces = refs[:PEERS]
    narrow, rest = refs[PEERS], refs[PEERS + 1 :]
    if last:
        weights, rest = rest[0], rest[1:]
    else:
        messages, rest = rest[:nx], rest[nx:]
    base, rest = (rest[0], rest[1:]) if added else (None, rest)
    me = idx[0]
    cs, width = pieces[0].shape[0], narrow.shape[1]
    if last:
        outs, act, spread = rest[:PEERS], rest[PEERS], rest[PEERS + 1]
    else:
        value, out_stats, act, whole, spread, held = rest
        hold(idx[2], messages, held, section)
        assemble(held, whole, rows)
        send(whole)
        weights = whole
    for k, ref in enumerate(pieces):
        act[rows_at(me ^ k, cs), :] = ref[:, :width]
    send(act)
    spread[...] = jnp.dot(weights[...], act[...], preferred_element_type=F32)
    row, col = pixel(width, area, small)
    total = base[...] if added else jnp.zeros((cs, width), F32)
    for k, (_, drow, dcol) in enumerate(OFFSETS):
        y = moved(spread[k * cs : (k + 1) * cs, :], drow * small + dcol)
        total += jnp.where(inside(row, col, drow, dcol, small), y, 0.0)
    if last:
        result = total.astype(BF16)
        lane = lax.broadcasted_iota(jnp.int32, (width, 128), 0)
        slot = lax.broadcasted_iota(jnp.int32, (width, 128), 1)
        for k, out in enumerate(outs):
            out[...] = pick(result, (lane == (me ^ k) * area + slot).astype(BF16))
    else:
        value[...] = total
        weight = narrow[0:1, :]
        n = jnp.sum(weight, axis=1, keepdims=True)
        mean, squares = masked_stats(total, weight, n)
        out_stats[...] = as_rows((mean, squares, n))


def join_result(idx, *refs):
    pieces, (out, stack) = refs[:PEERS], refs[PEERS:]
    cs = pieces[0].shape[0]
    for k, ref in enumerate(pieces):
        stack[rows_at(idx[0] ^ k, cs), :] = ref[:, -128:].astype(F32)
    out[...] = stack[...].T[: out.shape[0]].astype(BF16)


def spread_grad(grad, shifted, area, small, offs, row_at):
    cs, width = grad.shape
    row, col = pixel(width, area, small)
    for k, (_, drow, dcol) in enumerate(offs):
        g = moved(grad, -(drow * small + dcol))
        g = jnp.where(inside(row, col, -drow, -dcol, small), g, 0.0)
        shifted[row_at(k, cs), :] = g.astype(BF16)


def plain_rows(k, cs):
    return slice(k * cs, (k + 1) * cs)


def push_back(me, weights, shifted, partial, outs):
    cs, width = outs[0].shape[0], shifted.shape[1]
    partial[...] = lax.dot_general(
        weights[...], shifted[...], (((0,), (0,)), ((), ())), preferred_element_type=F32
    )
    for k, out in enumerate(outs):
        out[:, :width] = partial[rows_at(me ^ k, cs), :].astype(BF16)


def last_back(nx, rows, section, area, small, idx, *refs):
    pieces, messages, rest = refs[:PEERS], refs[PEERS : PEERS + nx], refs[PEERS + nx :]
    cot, shifted, weights = rest[:3]
    outs = rest[3 : PEERS + 3]
    partial, held = rest[PEERS + 3 :]
    hold(idx[2], messages, held, section)
    assemble(held, weights, rows)
    send(weights)
    me = idx[0]
    cs, width = cot.shape
    image = lax.broadcasted_iota(jnp.int32, (1, width), 1) // area
    grad = jnp.zeros((cs, width), F32)
    for k, ref in enumerate(pieces):
        tiled = jnp.concatenate([ref[:, width:].astype(F32)] * (width // 128), axis=1)
        grad = jnp.where(image == (me ^ k), tiled, grad)
    cot[...] = grad
    send(cot)
    spread_grad(grad, shifted, area, small, OFFSETS, plain_rows)
    send(shifted)
    push_back(me, weights, shifted, partial, outs)


def gelu_back(idx, *refs):
    pieces = refs[:PEERS]
    normed, params, grad_pre, sums = refs[PEERS:]
    width = normed.shape[1]
    grad = pieces[0][:, :width].astype(F32)
    for ref in pieces[1:]:
        grad += ref[:, :width].astype(F32)
    norm = normed[...]
    g = gelu_slope(params[:, 0:1] * norm + params[:, 1:2]) * grad
    grad_pre[...] = g
    sums[...] = as_rows(
        (jnp.sum(g * norm, axis=1, keepdims=True), jnp.sum(g, axis=1, keepdims=True))
    )


def norm_back(nz, added, last, area, small, idx, *refs):
    grad_pre, normed, scales, params, narrow = refs[:5]
    sums = refs[5 : 5 + nz]
    rest = refs[5 + nz :]
    base, rest = (rest[0], rest[1:]) if added else (None, rest)
    me = idx[0]
    cs, width = grad_pre.shape
    order = rest[-1]
    got = in_order(sums, idx[1], order)
    total = got[0]
    for g in got[1:]:
        total = total + g
    cols = as_columns(total)
    gain_grad, shift_grad = cols[:, 0:1], cols[:, 1:2]
    norm = normed[...]
    back = params[:, 0:1] * scales[:, 1:2] * (
        grad_pre[...]
        - narrow[0:1, :] * (shift_grad + norm * gain_grad) / scales[:, 2:3]
    )
    if added:
        back = base[...] + back
    grad = back.astype(BF16).astype(F32)
    if not last:
        riders = ()
        if not added:
            riders, rest = rest[:PEERS], rest[PEERS:]
        weights, sums_out, shifted = rest[:3]
        outs, partial = rest[3 : 3 + PEERS], rest[3 + PEERS]
        for rider, out in zip(riders, outs):
            out[:, width:] = rider[...]
        if added:
            grad_out, outs, partial = rest[3], rest[4 : 4 + PEERS], rest[4 + PEERS]
            grad_out[...] = grad.astype(BF16)
        sums_out[...] = total
        spread_grad(grad, shifted, area, small, OFFSETS, plain_rows)
        push_back(me, weights, shifted, partial, outs)
    else:
        weights, grad_skip, sums_out, shifted = rest[:4]
        outs, partial = rest[4 : 4 + PEERS], rest[4 + PEERS]
        sums_out[...] = total
        spread_grad(grad, shifted, area, small, STRIDED[:9], row_of)
        shifted[row_of(9, cs), :] = grad_skip[...]
        for phase in range(4):
            partial[phase] = lax.dot_general(
                shifted[phase_rows(phase, cs), :],
                weights[phase_rows(phase, cs), :],
                (((0,), (0,)), ((), ())),
                preferred_element_type=F32,
            )
        for k, out in enumerate(outs):
            for phase in range(4):
                out[phase * area : (phase + 1) * area, :] = partial[
                    phase, rows_at(me ^ k, area), :
                ].astype(BF16)


def part_halves(core, units, own, other):
    own[...] = units[core]
    other[...] = units[1 - core].astype(BF16)


def weight_grad(rows, idx, shifted, act, own, other, full, units):
    full[...] = lax.dot_general(
        shifted[...], act[...], (((1,), (1,)), ((), ())), preferred_element_type=F32
    )
    ny, cs, span = own.shape
    tiles = full.shape[1] // 128
    for v in range(2 * ny):
        begin = rows * v % 128
        parts = []
        for q in range((begin + rows + 127) // 128):
            k, p = divmod(rows * v // 128 + q, tiles)
            parts.append(full[k * cs : (k + 1) * cs, p * 128 : (p + 1) * 128])
        window = jnp.concatenate(parts, axis=1)
        units[v % 2, v // 2] = moved(window, begin)[:, :span]
    part_halves(idx[2] % 2, units, own, other)


def weight_grad_first(rows, extra, idx, shifted, act, own, other, flat, units):
    ny, cs, span = own.shape
    c_in = act.shape[2]
    flat[...] = jnp.zeros_like(flat)
    skip = None
    for phase in range(4):
        group = jnp.dot(
            shifted[phase_rows(phase, cs), :], act[phase], preferred_element_type=F32
        ).astype(BF16)
        for at, k in enumerate(PHASES[phase]):
            grad = group[at * cs : (at + 1) * cs]
            if k == 9:
                skip = grad
                continue
            begin = k * c_in
            base = begin // 128 * 128
            reach = -(-(begin + c_in) // 128) * 128
            move = one_hot(c_in, reach - base, begin - base)
            flat[:, base:reach] += jnp.dot(grad, move, preferred_element_type=F32)
    lane = lax.broadcasted_iota(jnp.int32, (1, span), 1)
    for v in range(2 * ny):
        begin = rows * v % 128
        base = rows * v - begin
        window = moved(flat[:, base : base + span + 128], begin)[:, :span]
        row = lax.broadcasted_iota(jnp.int32, (c_in, span), 0)
        col = lax.broadcasted_iota(jnp.int32, (c_in, span), 1)
        place = (row >= extra * v) & (row < extra * (v + 1)) & (col == row - extra * v + rows)
        tail = pick32(skip, place.astype(BF16))
        units[v % 2, v // 2] = jnp.where(lane < rows, window, 0.0) + tail
    part_halves(idx[2] % 2, units, own, other)


def reduce_core(count, idx, *refs):
    own, other, outs, total = refs[:count], refs[count : 2 * count], refs[2 * count : -1], refs[-1]
    cb = outs[0].shape[1]
    at = 0
    for a, b in zip(own, other):
        span = a.shape[2]
        total[:, :, at : at + span] = a[...] + b[...].astype(F32)
        at += span
    for k, out in enumerate(outs):
        for j in range(total.shape[0]):
            out[j] = total[j, rows_at(idx[2] // 2 ^ k, cb), :].astype(out.dtype)


def reduce_side(sizes, idx, *refs):
    refs, out = refs[:-1], refs[-1]
    at = 0
    for size in sizes:
        total = refs[0][...].astype(F32)
        for ref in refs[1:size]:
            total += ref[...].astype(F32)
        out[:, :, at : at + total.shape[2]] = total.astype(BF16)
        refs = refs[size:]
        at += total.shape[2]


def fold(nz, fy, idx, got, out):
    cs = got.shape[1]
    for f in range(fy):
        total = got[f].astype(F32)
        for z in range(1, nz):
            total += got[z * fy + f].astype(F32)
        out[f * cs : (f + 1) * cs, :] = total.astype(BF16)


def own_rows(count, spans, idx, *refs):
    pieces, outs, stack = refs[:count], refs[count:-1], refs[-1]
    for k, ref in enumerate(pieces):
        at = idx[2] ^ k
        stack[at % 2, at // 2] = ref[...]
    sides, height = stack.shape[1], stack.shape[2]
    fy_cb = [(f, x) for f in range(PEERS) for x in range(sides)]
    cb = height // PEERS
    for half in range(2):
        whole = jnp.concatenate(
            [stack[half, x, f * cb : (f + 1) * cb, :].astype(F32) for f, x in fy_cb], axis=0
        ).T
        at = 0
        for span, group in spans:
            begin = at
            for n in group:
                out = outs[n]
                rows = out.shape[0] // 2
                out[half * rows : (half + 1) * rows, :] = whole[begin : begin + rows]
                begin += rows
            at += span


def entry_back(small, idx, *refs):
    pieces = refs[:PEERS]
    image, norm, gain, shift, grad_pre, sums = refs[PEERS:]
    c_in = gain.shape[1]
    side = 2 * small
    grad = pieces[0][...].astype(F32)
    for ref in pieces[1:]:
        grad += ref[...].astype(F32)
    order = pixel_order(small, side * side, lambda y, x: y * side + x)
    high = grad.astype(BF16)
    low = (grad - high.astype(F32)).astype(BF16)
    grad = sum(
        lax.dot_general(order, part, (((0,), (0,)), ((), ())), preferred_element_type=F32)
        for part in (high, low)
    )
    normed = (image[...].astype(F32) - norm[0:1, :c_in]) * norm[1:2, :c_in]
    g = gelu_slope(gain[...] * normed + shift[...]) * grad
    grad_pre[...] = g
    sums[...] = jnp.zeros_like(sums)
    sums[0:1, :c_in] = jnp.sum(g * normed, axis=0, keepdims=True)
    sums[1:2, :c_in] = jnp.sum(g, axis=0, keepdims=True)


def bundle(idx, first, second, third, sums, out):
    out[...] = jnp.zeros_like(out)
    out[0:8, :] = sums[...]
    for k, ref in enumerate((first, second, third)):
        out[8 + 2 * k : 10 + 2 * k, : ref.shape[1]] = ref[0:2]


def unbundle(idx, *refs):
    out, six, order = refs[-3:]
    got = in_order(refs[:-3], idx[0], order)
    total = got[0][0:8]
    for g in got[1:]:
        total = total + g[0:8]
    out[...] = total
    cs = six.shape[1] // PEERS
    six[...] = jnp.concatenate([g[8:16, :cs] for g in got], axis=1)


def entry_grad(nz, idx, *refs):
    sums = refs[:nz]
    grad_pre, image, weight, norm, gain, gain_grad, shift_grad, out, order = refs[nz:]
    got = in_order(sums, idx[1], order)
    total = got[0]
    for g in got[1:]:
        total = total + g
    gain_grad[...] = total[0:1]
    shift_grad[...] = total[1:2]
    c_in = gain.shape[1]
    scale = norm[1:2, :c_in]
    normed = (image[...].astype(F32) - norm[0:1, :c_in]) * scale
    out[...] = gain[...] * scale * (
        grad_pre[...]
        - weight[:, 0:1]
        * (shift_grad[0:1, :c_in] + normed * gain_grad[0:1, :c_in])
        / norm[2:3, :c_in]
    )


def program(
    nx,
    ny,
    images,
    valid_count,
    pixel_mask,
    gain_entry,
    shift_entry,
    conv_first,
    gain_middle,
    shift_middle,
    conv_second,
    projection,
    gain_inner,
    shift_inner,
    conv_third,
    gain_last,
    shift_last,
    conv_fourth,
    cotangent,
):
    fy = PEERS
    nz = ny // fy
    sides = nx // 2
    side, c_in = images.shape[1], images.shape[3]
    small = side // 2
    area = small * small
    c_out = conv_first.shape[1]
    cs = c_out // PEERS
    cb = cs // sides
    width = PEERS * area
    lanes = c_in + 64
    padded = span_of(c_in)
    gx, gy = lax.axis_index("gx"), lax.axis_index("gy")
    me = gy % fy
    mine = gy // fy
    run = Order(jnp.stack([me, mine, gx, gy]).astype(jnp.int32))
    part = functools.partial

    def to_slice(piece, k):
        return lax.ppermute(piece, "gy", [(j, j // fy * fy + (j % fy ^ k)) for j in range(ny)])

    def share(pieces):
        return [pieces[0]] + [to_slice(pieces[k], k) for k in range(1, PEERS)]

    def to_gx(piece, k):
        return lax.ppermute(piece, "gx", [(i, i ^ k) for i in range(nx)])

    def pool_gx(piece):
        return [piece] + [to_gx(piece, k) for k in range(1, nx)]

    def pool_z(piece):
        out = [piece]
        for k in range(1, nz):
            perm = [(j, (j // fy ^ k) * fy + j % fy) for j in range(ny)]
            out.append(lax.ppermute(piece, "gy", perm))
        return out

    def over_x(block):
        return {0: block, **{k: to_gx(block, k) for k in range(2, nx, 2)}}

    def over_core(held, *then):
        held = {k: after(v, *then) for k, v in held.items()} if then else dict(held)
        for k in list(held):
            held[k + 1] = to_gx(held[k], 1)
        return [held[k] for k in sorted(held)]

    def turn(block):
        return lax.all_to_all(block, "gy", 0, 0, tiled=True)

    unit_first, unit_skip = conv_first.shape[0] // 2, projection.shape[0] // 2
    unit_mid = conv_second.shape[0] // 2
    span_first, span_mid = span_of(unit_first + unit_skip), span_of(unit_mid)
    tile, tile16 = shape((cs, width)), shape((cs, width), BF16)
    long16 = shape((cs, width + 128), BF16)
    cols, stat, entry_stat = shape((cs, 128)), shape((8, cs)), shape((8, lanes))
    shifted16 = shape((9 * cs, width), BF16)
    full16 = shape((c_out, width), BF16)
    whole16 = shape((9 * cs, c_out), BF16)

    def halves(span, channels):
        return pltpu.VMEM((2, cs // channels, ny, channels, span), BF16)

    def ready(span, sections, *weights):
        out = shape((ny, cb, span * len(sections)), BF16)
        return run(
            part(entry_weights, cs, fy, sections), out, weights, cost=24 * len(sections)
        )

    def merge(pieces, kernel):
        like = pieces[0].shape
        return run(kernel, shape(like), pieces, [pltpu.VMEM((nx, *like), F32)])

    add_gx = part(add_rows, 2)

    def activate(value, params, pooled, cot=None):
        more = [] if cot is None else [cot]
        outs = [tile16] if cot is None else [long16] * PEERS
        return run(
            part(act_block, nz),
            [tile, cols] + outs,
            [value, params, *pooled, *more],
            [pltpu.VMEM((nz, 8, cs), F32)]
            + ([] if cot is None else [pltpu.VMEM((c_out, 128), F32)]),
            far=(0, 1),
        )

    def convolve(pieces, weights, base, section=0, last=False):
        more = [] if base is None else [base]
        outs = [shape((cs, 128), BF16)] * PEERS + [full16]
        return run(
            part(conv_block, nx, base is not None, last, unit_mid, section, area, small),
            outs if last else [tile, stat, full16, whole16],
            [*pieces, narrow, *weights, *more],
            [pltpu.VMEM((9 * cs, width), F32)] + ([] if last else [halves(span_mid, cb)]),
            cost=25,
            far=() if last else (2, 3),
        )

    def slope(parts, normed, params):
        return run(gelu_back, [tile, stat], [*parts, normed, params])

    def back(grad_pre, normed, scales, params, pooled, weights, base, riders=()):
        more = list(riders) if base is None else [base]
        return run(
            part(norm_back, nz, base is not None, False, area, small),
            [stat, shifted16]
            + ([long16] * PEERS if base is None else [tile16] * (PEERS + 1)),
            [grad_pre, normed, scales, params, narrow, *pooled, *more, weights],
            [pltpu.VMEM((c_out, width), F32), pltpu.VMEM((nz, 8, cs), F32)],
            cost=18,
        )

    def grad_of(kernel, span, shifted, act, scratch):
        own, other = run(
            kernel,
            [shape((ny, cs, span)), shape((ny, cs, span), BF16)],
            [shifted, act],
            [scratch, pltpu.VMEM((2, ny, cs, span), F32)],
            cost=28,
        )
        return own, to_gx(other, 1)

    def grad_mid(shifted, act):
        return grad_of(
            part(weight_grad, unit_mid), span_mid, shifted, act, pltpu.VMEM((9 * cs, c_out), F32)
        )

    def over_pair(own, other):
        span = own.shape[2]
        return run(
            part(reduce_core, 1),
            [shape((ny, cb, span))] + [shape((ny, cb, span), BF16)] * (sides - 1),
            [own, other],
            [pltpu.VMEM((ny, cs, span), F32)],
        )

    def to_sides(parts, *then):
        parts = [after(p, *then) for p in parts] if then else parts
        return [parts[0]] + [to_gx(parts[k], 2 * k) for k in range(1, sides)]

    def over_sides(*groups):
        span = sum(parts[0].shape[2] for parts in groups)
        return run(
            part(reduce_side, tuple(len(parts) for parts in groups)),
            shape((ny, cb, span), BF16),
            [p for parts in groups for p in parts],
        )

    def folded(got):
        out = shape((fy * cb, got.shape[2]), BF16)
        return over_x(run(part(fold, nz, fy), out, [got]))

    def rows_of(pieces, spans, *rows):
        return run(
            part(own_rows, nx, spans),
            [shape((r, c_out)) for r in rows],
            pieces,
            [pltpu.VMEM((2, sides, fy * cb, pieces[0].shape[1]), BF16)],
            cost=30,
        )

    def own(gain, shift):
        pair = jnp.stack([gain, shift], axis=1)
        return lax.dynamic_slice_in_dim(pair, me * cs, cs, axis=0)

    p_middle = own(gain_middle, shift_middle)
    p_inner = own(gain_inner, shift_inner)
    p_last = own(gain_last, shift_last)
    g_entry, s_entry = gain_entry[None], shift_entry[None]
    pixels = images.reshape(side * side, c_in)

    image, wide = run(
        part(entry_image, small),
        [shape((4 * area, lanes), BF16), shape((4 * area, 128))],
        [pixels, pixel_mask.reshape(side, side), valid_count],
        scalars=1,
    )
    group = share([image] * PEERS)
    out_first = ready(span_first, (2,), conv_first, projection)
    stats = run(part(entry_stats, area), entry_stat, group)
    pieces = pool_gx(stats)
    got_first = turn(after(out_first, *group[1:]))
    got_first = over_core(over_x(after(got_first, *pieces[1:])))
    pooled = pool_z(merge(pieces, merge_stats))
    out_middle = ready(span_mid, (1, 1), conv_second, conv_third)
    got_middle = turn(after(out_middle, pooled[-1]))
    out_fourth = ready(span_mid, (1,), conv_fourth)
    first, skipped, stats, norm_one, narrow, act_one, w_first = run(
        part(entry_block, nz, nx, unit_first, unit_skip, area, small),
        [
            tile,
            tile,
            stat,
            entry_stat,
            shape((8, width)),
            shape((4, width, c_in), BF16),
            shape((10 * cs, c_in), BF16),
        ],
        [*group, *pooled, g_entry, s_entry, *got_first],
        [
            pltpu.VMEM((nz, 8, lanes), F32),
            pltpu.VMEM((width, lanes), BF16),
            pltpu.VMEM((cs, span_of(9 * c_in)), BF16),
            halves(span_first, cb),
        ],
        cost=40,
        far=(3, 5, 6),
    )

    merged = merge(pool_gx(stats), merge_stats)
    got_middle = over_x(after(got_middle, merged))
    pooled = pool_z(merged)
    got_fourth = turn(after(out_fourth, pooled[-1]))
    normed_two, scale_two, *messages = activate(
        first, p_middle, pooled, cotangent.reshape(area, c_out)
    )
    pieces = share(messages)
    got_middle = over_core(got_middle, *pieces[1:])
    hidden, stats, act_two, w_second = convolve(pieces, got_middle, skipped)
    cot_parts = pieces
    merged = merge(pool_gx(stats), merge_stats)
    pooled = pool_z(merged)
    got_fourth = over_x(after(got_fourth, pooled[-1]))
    normed_three, scale_three, act = activate(hidden, p_inner, pooled)
    pieces = share([act] * PEERS)
    third, stats, act_three, w_third = convolve(pieces, got_middle, None, section=1)
    got_fourth = over_core(got_fourth, stats)
    merged = merge(pool_gx(stats), merge_stats)

    cot, shifted_four, w_fourth, *parts = run(
        part(last_back, nx, unit_mid, 0, area, small),
        [tile, shifted16, whole16] + [tile16] * PEERS,
        [*cot_parts, *got_fourth],
        [pltpu.VMEM((c_out, width), F32), halves(span_mid, cb)],
        cost=18,
        far=(0, 1, 2),
    )
    parts = share(parts)
    normed_four, scale_four, act = activate(third, p_last, pool_z(merged))
    pieces = share([act] * PEERS)
    grad_pre, sums = slope(parts, normed_four, p_last)
    sums = pool_gx(sums)
    *riders, act_four = convolve(pieces, [w_fourth], hidden, last=True)
    sums = pool_z(merge(sums, add_gx))
    fourth = grad_mid(shifted_four, act_four)
    last_sums, shifted_three, *parts = back(
        grad_pre, normed_four, scale_four, p_last, sums, w_third, None, riders
    )
    parts = share(parts)
    fourth = over_pair(*fourth)
    grad_pre, sums = slope(parts, normed_three, p_inner)
    sums = pool_gx(sums)
    third = grad_mid(shifted_three, act_three)
    merged = merge(sums, add_gx)
    fourth = to_sides(fourth, merged)
    sums = pool_z(merged)
    out = run(
        join_result, shape((area, c_out), BF16), parts, [pltpu.VMEM((c_out, 128), F32)]
    )
    inner_sums, shifted_two, grad_hidden, *parts = back(
        grad_pre, normed_three, scale_three, p_inner, sums, w_second, cot
    )
    parts = share(parts)
    third = over_pair(*third)
    grad_pre, sums = slope(parts, normed_two, p_middle)
    sums = pool_gx(sums)
    fourth = over_sides(fourth)
    second = grad_mid(shifted_two, act_two)
    merged = merge(sums, add_gx)
    third = to_sides(third, merged)
    sums = pool_z(merged)
    second = to_sides(over_pair(*second), merged)
    middle_sums, shifted_one, *parts = run(
        part(norm_back, nz, False, True, area, small),
        [stat, shape((10 * cs, width), BF16)] + [shape((4 * area, c_in), BF16)] * PEERS,
        [
            grad_pre,
            normed_two,
            scale_two,
            p_middle,
            narrow,
            *sums,
            w_first,
            grad_hidden,
        ],
        [pltpu.VMEM((4, width, c_in), F32), pltpu.VMEM((nz, 8, cs), F32)],
        cost=18,
    )

    parts = share(parts)
    first = grad_of(
        part(weight_grad_first, unit_first, unit_skip),
        span_first,
        shifted_one,
        act_one,
        pltpu.VMEM((cs, span_of(9 * c_in + span_first + 128)), F32),
    )
    first = to_sides(over_pair(*first))
    second = over_sides(second)
    late = turn(over_sides([after(fourth, *parts[1:])], third))
    grad_pre, sums = run(
        part(entry_back, small),
        [shape((4 * area, c_in)), shape((8, padded))],
        [*parts, pixels, norm_one, g_entry, s_entry],
        cost=13,
    )
    message = run(bundle, shape((16, padded)), [middle_sums, inner_sums, last_sums, sums])
    message = share([message] * PEERS)
    early = over_sides([second], first)
    early = turn(after(early, *message[1:]))
    late = folded(late)
    sums, six = run(
        unbundle,
        [shape((8, padded)), shape((8, c_out))],
        message,
        [pltpu.VMEM((PEERS, 16, padded), F32)],
    )
    sums = pool_gx(sums)
    early = folded(early)
    merged = merge(sums, add_gx)
    sums = pool_z(merged)
    gain_entry_grad, shift_entry_grad, image_grad = run(
        part(entry_grad, nz),
        [shape((1, padded)), shape((1, padded)), shape((4 * area, c_in))],
        [*sums, grad_pre, pixels, wide, norm_one, g_entry],
        [pltpu.VMEM((nz, 8, padded), F32)],
    )
    fourth_grad, third_grad = rows_of(
        over_core(late, merged),
        ((span_mid, (0,)), (span_mid, (1,))),
        2 * unit_mid,
        2 * unit_mid,
    )
    second_grad, first_grad, skip_grad = rows_of(
        over_core(early, fourth_grad),
        ((span_mid, (0,)), (span_first, (1, 2))),
        2 * unit_mid,
        2 * unit_first,
        2 * unit_skip,
    )
    return (
        out.reshape(1, small, small, c_out),
        image_grad.reshape(1, side, side, c_in),
        gain_entry_grad[0, :c_in],
        shift_entry_grad[0, :c_in],
        first_grad,
        six[0],
        six[1],
        second_grad,
        skip_grad,
        six[2],
        six[3],
        third_grad,
        six[4],
        six[5],
        fourth_grad,
    )


def solution(mesh):
    whole = P(("gx", "gy"), None, None, None)
    rows = P("gy", None)
    return jax.shard_map(
        functools.partial(program, mesh.shape["gx"], mesh.shape["gy"]),
        mesh=mesh,
        in_specs=(
            whole,
            P(("gx", "gy")),
            P(("gx", "gy"), None, None),
            P(),
            P(),
            rows,
            P(),
            P(),
            rows,
            rows,
            P(),
            P(),
            rows,
            P(),
            P(),
            rows,
            whole,
        ),
        out_specs=(
            whole, whole, P(), P(), rows, P(), P(), rows, rows, P(), P(), rows, P(), P(), rows,
        ),
        check_vma=False,
    )
```
